32 devices in a mesh: seq: 4 (over z), chan: 4 (over y, x), dp: 2 (over core).
Axes of the slice: x: 2, y: 2, z: 4, core: 2. Of those that a mesh axis runs over, the one named last changes fastest.
Arguments:
- mr_query: bfloat16 [2, 8192, 512], P('dp', 'chan', 'seq'), may hold values from -6 to 6
- mr_key: bfloat16 [2, 8192, 512], P('dp', 'chan', 'seq'), may hold values from -6 to 6
- mr_value: bfloat16 [2, 8192, 512], P('dp', 'chan', 'seq'), may hold values from -6 to 6
- li_key: bfloat16 [2, 8192, 512], P('dp', 'chan', 'seq'), may hold values from -6 to 6
- li_value: bfloat16 [2, 8192, 512], P('dp', 'chan', 'seq'), may hold values from -6 to 6
- grad_out: bfloat16 [2, 8192, 512], P('dp', 'chan', 'seq'), may hold values from -6 to 6
- mr_filter: bfloat16 [512, 128], P('chan'), may hold values from -0.5 to 0.5
- li_residue: float32 [512, 16], P('chan'), may hold values from -1.5 to 1.5
- li_rate: float32 [512, 16], P('chan'), may hold values from 1.953125e-05 to 0.05
Outputs:
- grad_mr_query: bfloat16 [2, 8192, 512], P('dp', 'chan', 'seq')
- grad_mr_key: bfloat16 [2, 8192, 512], P('dp', 'chan', 'seq')
- grad_mr_value: bfloat16 [2, 8192, 512], P('dp', 'chan', 'seq')
- grad_li_key: bfloat16 [2, 8192, 512], P('dp', 'chan', 'seq')
- grad_li_value: bfloat16 [2, 8192, 512], P('dp', 'chan', 'seq')
- grad_filter: float32 [512, 128], P('chan')
- grad_residue: float32 [512, 16], P('chan')
The draws below stay inside these ranges and needn't reach their ends.
All inputs are finite; a program needn't handle non-finite values.
Results may differ from the reference program's by a relative error of at most 0.012.
Values may be sent and summed in bfloat16 or wider, within the bound.
No kernel may reach another device: no remote copies, remote signals or barrier semaphores. Data moves between devices by JAX's collectives and lax.ppermute only.
A program may use at most 128 MiB of HBM per device.

```python
import math
import jax
import jax.numpy as jnp
from jax import lax

CH = 8192
FILT = 128
MODES = 16
GROUPS = 512
SEQ_LEN = 512
BATCH = 2


def levels(key, shape, shards, low, top_value):
    loudness, own = 1.0, jax.random.fold_in(key, 6)
    for axis_at, shards_of in shards:
        heights = jnp.exp(jax.random.uniform(jax.random.fold_in(own, axis_at), (shards_of,), jnp.float32, low / len(shards), top_value / len(shards)))
        loudness = loudness * jnp.repeat(heights, shape[axis_at] // shards_of).reshape([-1 if axis == axis_at else 1 for axis in range(len(shape))])
    return loudness


def normal_values(key, shape, scale, most, split=(), kind=jnp.bfloat16):
    values = scale * jax.random.normal(key, shape, jnp.float32)
    if split:
        values = values * levels(key, shape, split, -0.22, 0.18)
    return jnp.clip(values, -most, most).astype(kind)


def setup_inputs(seed: int = 0) -> dict:
    splits = jax.random.split(jax.random.key(seed), 10)
    return {
        "mr_query": normal_values(splits[0], (BATCH, CH, SEQ_LEN), 1.0, 6.0, ((0, 2), (1, 4), (2, 4))),
        "mr_key": normal_values(splits[1], (BATCH, CH, SEQ_LEN), 1.0, 6.0, ((0, 2), (1, 4), (2, 4))),
        "mr_value": normal_values(splits[2], (BATCH, CH, SEQ_LEN), 1.0, 6.0, ((0, 2), (1, 4), (2, 4))),
        "li_key": normal_values(splits[3], (BATCH, CH, SEQ_LEN), 1.0, 6.0, ((0, 2), (1, 4), (2, 4))),
        "li_value": normal_values(splits[4], (BATCH, CH, SEQ_LEN), 1.0, 6.0, ((0, 2), (1, 4), (2, 4))),
        "grad_out": normal_values(splits[5], (BATCH, CH, SEQ_LEN), 1.0, 6.0, ((0, 2), (1, 4), (2, 4))),
        "mr_filter": normal_values(splits[6], (GROUPS, FILT), FILT ** -0.5, 0.5, ((0, 4),)),
        "li_residue": normal_values(splits[7], (GROUPS, MODES), MODES ** -0.5, 1.5, ((0, 4),), jnp.float32),
        "li_rate": jnp.clip(jnp.exp(math.log(0.05) - 7.8477626 * jax.random.uniform(splits[8], (GROUPS, MODES), jnp.float32) ** levels(splits[8], (GROUPS, MODES), ((0, 4),), -0.2, 0.2)), 1.9531249563442543e-05, 0.05),
    }


exact_mode = lax.Precision.HIGHEST

def circulant_ref(entries):
    extent = entries.shape[-1]
    index = (jnp.arange(extent)[:, None] - jnp.arange(extent)[None, :]) % extent
    return entries[..., index]

def diagonal_ref(matrix):
    extent = matrix.shape[-1]
    index = (jnp.arange(extent)[:, None] - jnp.arange(extent)[None, :]) % extent
    picked = jnp.take_along_axis(matrix, jnp.broadcast_to(index, matrix.shape), axis=-1)
    return lax.optimization_barrier(jnp.sum(picked, axis=-2))

def sequence_grads(mr_query, mr_key, mr_value, li_key, li_value, grad_out, mr_filter, li_residue, li_rate):
    groups, filt_len = mr_filter.shape
    channels = mr_query.shape[0]
    group_size = channels // groups
    tile_count = mr_query.shape[1] // filt_len
    mode_count = li_rate.shape[1]
    shape_tiles = (groups, group_size, tile_count, filt_len)
    query_f = mr_query.reshape(shape_tiles).astype(jnp.float32)
    key_f = mr_key.reshape(shape_tiles).astype(jnp.float32)
    value_f = mr_value.reshape(shape_tiles).astype(jnp.float32)
    key_two = li_key.reshape(shape_tiles).astype(jnp.float32)
    value_two = li_value.reshape(shape_tiles).astype(jnp.float32)
    grad_f = grad_out.reshape(shape_tiles).astype(jnp.float32)
    lower_mask = jnp.arange(filt_len)[:, None] >= jnp.arange(filt_len)[None, :]
    circ = circulant_ref(mr_filter).astype(jnp.float32)
    toeplitz_now = jnp.where(lower_mask, circ, jnp.float32(0.0))
    toeplitz_prev = jnp.where(lower_mask, jnp.float32(0.0), circ)
    product_one = (mr_query * mr_key).reshape(shape_tiles).astype(jnp.float32)
    zero_tile = jnp.zeros_like(product_one[:, :, :1])
    product_prev = jnp.concatenate([zero_tile, product_one[:, :, :-1]], 2)
    conv_one = jnp.einsum('gcnb,gab->gcna', product_one, toeplitz_now, precision=exact_mode) + jnp.einsum('gcnb,gab->gcna', product_prev, toeplitz_prev, precision=exact_mode)
    output_one = (value_f * conv_one).astype(jnp.bfloat16)
    output_f = output_one.astype(jnp.float32)
    input_two = output_f * key_two
    offsets = jnp.arange(filt_len).astype(jnp.float32)
    gains = jnp.sqrt(-jnp.expm1(-2.0 * li_rate))
    coeffs = li_residue * gains
    powers = jnp.exp(-li_rate[:, :, None] * offsets)
    to_end = jnp.exp(-li_rate[:, :, None] * (filt_len - 1 - offsets))
    after_one = jnp.exp(-li_rate[:, :, None] * (offsets + 1))
    to_next = jnp.exp(-li_rate[:, :, None] * (filt_len - offsets))
    tile_decay = jnp.exp(-li_rate * filt_len)[:, None, :]
    local_filter = jnp.einsum('gm,gmk->gk', coeffs, powers, precision=exact_mode)
    toeplitz_li = jnp.where(lower_mask, circulant_ref(local_filter), jnp.float32(0.0))
    conv_intra = jnp.einsum('gcnb,gab->gcna', input_two, toeplitz_li, precision=exact_mode)
    tile_sums = jnp.einsum('gcnb,gmb->ngcm', input_two, to_end, precision=exact_mode)

    def forward(state, piece):
        return (tile_decay * state + piece, state)
    start = jnp.zeros((groups, group_size, mode_count), jnp.float32)
    _, state_before = lax.scan(forward, start, tile_sums)
    conv_cross = jnp.einsum('ngcm,gma->gcna', state_before, coeffs[:, :, None] * after_one, precision=exact_mode)
    conv_two = conv_intra + conv_cross
    grad_value_two = (grad_f * conv_two).astype(jnp.bfloat16)
    grad_conv_two = grad_f * value_two
    back_sums = jnp.einsum('gcna,gma->ngcm', grad_conv_two, powers, precision=exact_mode)

    def backward(state, piece):
        return (piece + tile_decay * state, state)
    _, state_after = lax.scan(backward, start, back_sums, reverse=True)
    grad_input_two = jnp.einsum('gcna,gab->gcnb', grad_conv_two, toeplitz_li, precision=exact_mode) + jnp.einsum('ngcm,gmb->gcnb', state_after, coeffs[:, :, None] * to_next, precision=exact_mode)
    grad_key_two = (grad_input_two * output_f).astype(jnp.bfloat16)
    grad_mid = grad_input_two * key_two
    energy = jnp.einsum('gcna,gcnb->gab', grad_conv_two, input_two, precision=exact_mode)
    lag_sums = diagonal_ref(jnp.where(lower_mask, energy, jnp.float32(0.0)))
    intra_term = jnp.einsum('gk,gmk->gm', lag_sums, powers, precision=exact_mode)
    cross_weight = jnp.einsum('gcna,gma->ngcm', grad_conv_two, after_one, precision=exact_mode)
    cross_term = lax.optimization_barrier(jnp.sum(state_before * cross_weight, axis=(0, 2)))
    residue_part = gains * (intra_term + cross_term)
    grad_conv_one = (grad_mid * value_f).astype(jnp.bfloat16).astype(jnp.float32)
    grad_value_one = (grad_mid * conv_one).astype(jnp.bfloat16)
    grad_next = jnp.concatenate([grad_conv_one[:, :, 1:], zero_tile], 2)
    grad_product = jnp.einsum('gcna,gab->gcnb', grad_conv_one, toeplitz_now, precision=exact_mode) + jnp.einsum('gcna,gab->gcnb', grad_next, toeplitz_prev, precision=exact_mode)
    grad_query = (grad_product * key_f).astype(jnp.bfloat16)
    grad_key = (grad_product * query_f).astype(jnp.bfloat16)
    lag_now = jnp.einsum('gcna,gcnb->gab', grad_conv_one, product_one, precision=exact_mode)
    lag_prev = jnp.einsum('gcna,gcnb->gab', grad_conv_one, product_prev, precision=exact_mode)
    filter_part = diagonal_ref(jnp.where(lower_mask, lag_now, lag_prev))
    flat_shape = mr_query.shape
    return (grad_query.reshape(flat_shape), grad_key.reshape(flat_shape), grad_value_one.reshape(flat_shape), grad_key_two.reshape(flat_shape), grad_value_two.reshape(flat_shape), filter_part, residue_part)

def reference(mr_query, mr_key, mr_value, li_key, li_value, grad_out, mr_filter, li_residue, li_rate):

    def one_sequence(streams):
        return sequence_grads(streams[0], streams[1], streams[2], streams[3], streams[4], streams[5], mr_filter, li_residue, li_rate)
    results = lax.map(one_sequence, (mr_query, mr_key, mr_value, li_key, li_value, grad_out))
    return (results[0], results[1], results[2], results[3], results[4], lax.optimization_barrier(jnp.sum(results[5], axis=0)), lax.optimization_barrier(jnp.sum(results[6], axis=0)))
```

```python
import functools

import jax
import jax.numpy as jnp
from jax import lax
from jax.experimental import pallas as pl
from jax.experimental.pallas import tpu as pltpu
from jax.sharding import PartitionSpec as P

F32 = jnp.float32
BF16 = jnp.bfloat16
TILE = 128
LANES = 16
PACK = TILE // LANES
VMEM_LIMIT = 48 * 1024 * 1024


def nn(lhs, rhs, precision=None):
    return lax.dot_general(
        lhs, rhs, (((1,), (0,)), ((), ())), precision=precision, preferred_element_type=F32
    )


def nt(lhs, rhs, precision=None):
    return lax.dot_general(
        lhs, rhs, (((1,), (1,)), ((), ())), precision=precision, preferred_element_type=F32
    )


def iotas():
    rows = lax.broadcasted_iota(jnp.int32, (TILE, TILE), 0)
    cols = lax.broadcasted_iota(jnp.int32, (TILE, TILE), 1)
    return rows, cols


def column(block):
    wide = jnp.concatenate(
        [jnp.broadcast_to(block[g : g + 1, :], (LANES, LANES)) for g in range(PACK)], axis=0
    )
    rows = lax.broadcasted_iota(jnp.int32, (TILE, LANES), 0)
    cols = lax.broadcasted_iota(jnp.int32, (TILE, LANES), 1)
    return jnp.sum(jnp.where(rows % LANES == cols, wide, 0.0), axis=1, keepdims=True)


def same_group():
    rows, cols = iotas()
    return (rows // LANES) == (cols // LANES)


def squeeze_groups(wide, mask):
    kept = jnp.where(mask, wide, 0.0)
    total = kept[:LANES]
    for g in range(1, PACK):
        total = total + kept[g * LANES : (g + 1) * LANES]
    return total


def spread_groups(narrow, mask):
    return jnp.where(mask, jnp.concatenate([narrow] * PACK, axis=0), 0.0)


def circulant(row):
    return pltpu.roll(jnp.broadcast_to(row, (TILE, TILE)), 0, 1, stride=1, stride_axis=0)


def one_minus_exp(value):
    series = jnp.full_like(value, 1.0)
    for order in (7, 6, 5, 4, 3, 2):
        series = 1.0 - value * series / order
    return jnp.where(value < 0.125, value * series, 1.0 - jnp.exp(-value))


def diagonal_rows(matrix):
    total = matrix[:8]
    for j in range(1, TILE // 8):
        total = total + pltpu.roll(matrix[8 * j : 8 * j + 8], TILE - 8 * j, 1)
    return total


def finish_diagonals(partial):
    sub = lax.broadcasted_iota(jnp.int32, partial.shape, 0) % 8
    for bit in (1, 2, 4):
        partial = jnp.where((sub & bit) != 0, pltpu.roll(partial, TILE - bit, 1), partial)
    return jnp.sum(partial.reshape(PACK, 8, TILE), axis=1)


def first_kernel(query, key, grad, value, rate, product, state):
    _, cols = iotas()
    offsets = cols.astype(F32)
    mask = same_group()
    for block in range(query.shape[0] // TILE):
        span = pl.ds(block * TILE, TILE)
        product[span, :] = query[span, :] * key[span, :]
        rates = column(rate[pl.ds(block * PACK, PACK), :])
        powers = jnp.exp(-rates * offsets).astype(BF16)
        dz2 = grad[span, :] * value[span, :]
        state[:, span] = squeeze_groups(nt(powers, dz2), mask).astype(BF16)


def local_kernel(grad, value, rate, residue, du2, to_next, after, to_end, power, taps, decay):
    rows, cols = iotas()
    offsets = cols.astype(F32)
    mask = same_group()
    upper = cols >= rows
    for block in range(grad.shape[0] // TILE):
        span = pl.ds(block * TILE, TILE)
        few = pl.ds(block * PACK, PACK)
        rates = column(rate[few, :])
        gains = jnp.sqrt(one_minus_exp(2.0 * rates))
        coeffs = column(residue[few, :]) * gains
        powers = jnp.exp(-rates * offsets)
        ends = jnp.exp(-rates * (TILE - 1 - offsets))
        step = jnp.exp(-rates)
        power[span, :] = powers.astype(BF16)
        to_end[span, :] = ends.astype(BF16)
        after[span, :] = (powers * (coeffs * step)).astype(BF16)
        to_next[span, :] = (ends * (coeffs * step)).astype(BF16)
        decay[:, span] = squeeze_groups(
            jnp.broadcast_to(jnp.exp(-rates * TILE), (TILE, TILE)), mask
        )
        filt = jnp.sum((powers * coeffs).reshape(PACK, LANES, TILE), axis=1)
        taps[few, :] = filt
        dz2 = grad[span, :] * value[span, :]
        pieces = []
        for g in range(PACK):
            weights = jnp.where(upper, circulant(filt[g : g + 1, :]), 0.0).astype(BF16)
            pieces.append(nt(dz2[g * LANES : (g + 1) * LANES, :], weights))
        du2[span, :] = jnp.concatenate(pieces, axis=0)


def middle_kernel(count, *refs):
    states = refs[: count - 1]
    local, to_next, decay, li_key, value, dz1, du2, after_shard = refs[count - 1 :]
    mask = same_group()
    for block in range(local.shape[0] // TILE):
        span = pl.ds(block * TILE, TILE)
        fade = decay[:, span]
        carried = states[-1][:, span].astype(F32)
        for state in states[-2::-1]:
            carried = state[:, span].astype(F32) + fade * carried
        after_shard[:, span] = carried
        wide = spread_groups(carried, mask).T.astype(BF16)
        total = local[span, :] + nn(wide, to_next[span, :])
        du2[span, :] = total
        dy1 = total * li_key[span, :].astype(F32)
        dz1[span, :] = (dy1 * value[span, :].astype(F32)).astype(BF16)


def forward_kernel(
    steps, before, now, filters, value, li_key, grad, li_value, taps, to_end, power, rate, after_shard, dz1, du2,
    grad_value, grad_key, z2, packed, filter_sums, residue_sums,
):
    rows, cols = iotas()
    mask = same_group()
    upper = cols >= rows
    upper_half = upper.astype(F32).astype(BF16)
    blocks = now.shape[0] // TILE
    at = pl.program_id(0)
    spot = lax.broadcasted_iota(jnp.int32, (PACK, TILE), 0) == (
        lax.broadcasted_iota(jnp.int32, (PACK, TILE), 1) // LANES
    )
    one_mode = (
        lax.broadcasted_iota(jnp.int32, (LANES, TILE), 1) % LANES
        == lax.broadcasted_iota(jnp.int32, (LANES, TILE), 0)
    ).astype(F32)
    own_group = mask.astype(F32)
    exact = lax.Precision.HIGHEST
    zeros = jnp.zeros((LANES, TILE), BF16)
    for block in range(blocks):
        span = pl.ds(block * TILE, TILE)
        few = pl.ds(block * PACK, PACK)
        u1 = now[span, :]
        u1_before = before[span, :]
        filt = filters[few, :].astype(F32)
        lag_taps = taps[few, :]
        pieces = []
        for g in range(PACK):
            part = slice(g * LANES, (g + 1) * LANES)
            circ = circulant(filt[g : g + 1, :]).astype(BF16)
            w_now = circ * upper_half
            w_before = circ - w_now
            pieces.append(nn(u1[part, :], w_now) + nn(u1_before[part, :], w_before))
        z1 = jnp.concatenate(pieces, axis=0)
        y1 = (value[span, :].astype(F32) * z1).astype(BF16).astype(F32)
        key_two = li_key[span, :].astype(F32)
        u2 = y1 * key_two
        u2_half = u2.astype(BF16)
        du2_here = du2[span, :]
        grad_key[span, :] = (du2_here * y1).astype(BF16)
        grad_value[span, :] = (du2_here * key_two * z1).astype(BF16)
        state = squeeze_groups(nt(to_end[span, :], u2_half), mask)
        packed[at * blocks + block] = state.astype(BF16)

        dz2 = grad[span, :] * li_value[span, :]
        dz1_here = dz1[span, :]
        u1_turned = u1.T
        before_turned = u1_before.T
        u2_turned = u2.T.astype(BF16)
        pieces, lag_parts, energy_parts = [], [], []
        for g in range(PACK):
            part = slice(g * LANES, (g + 1) * LANES)
            weights = circulant(lag_taps[g : g + 1, :]).astype(BF16) * upper_half
            pieces.append(nn(u2_half[part, :], weights))

            def alone(array):
                above = [zeros] * g
                below = [zeros] * (PACK - 1 - g)
                return jnp.concatenate(above + [array[part, :]] + below, axis=0)

            dz1_alone = alone(dz1_here)
            lag = jnp.where(upper, nn(u1_turned, dz1_alone), nn(before_turned, dz1_alone))
            lag_parts.append(diagonal_rows(lag))
            energy = jnp.where(upper, nn(u2_turned, alone(dz2)), 0.0)
            energy_parts.append(diagonal_rows(energy))
        z2[span, :] = jnp.concatenate(pieces, axis=0)
        filter_sums[pl.ds(pl.multiple_of((at * blocks + block) * PACK, PACK), PACK), :] = (
            finish_diagonals(jnp.concatenate(lag_parts, axis=0))
        )
        energies = finish_diagonals(jnp.concatenate(energy_parts, axis=0))
        within = nt(energies, power[span, :].astype(F32), exact)
        within = jnp.sum(jnp.where(spot, within, 0.0), axis=0, keepdims=True)
        across = nn(state * after_shard[:, span], own_group, exact)
        across = jnp.sum(across * one_mode, axis=0, keepdims=True)
        rates = jnp.where(spot, nn(rate[few, :], one_mode, exact), 0.0)
        rates = jnp.sum(rates, axis=0, keepdims=True)
        gains = jnp.sqrt(one_minus_exp(2.0 * rates))
        residue_sums[pl.ds(at * blocks + block, 1), :] = gains * (within + jnp.exp(-rates) * across)

    @pl.when(at == steps - 1)
    def _():
        shift = steps * blocks
        sums = filter_sums[...].astype(BF16)
        for chunk in range(filter_sums.shape[0] // LANES):
            packed[shift + chunk] = sums[chunk * LANES : (chunk + 1) * LANES]
        shift += filter_sums.shape[0] // LANES
        sums = residue_sums[...].astype(BF16)
        for chunk in range(residue_sums.shape[0] // LANES):
            packed[shift + chunk] = sums[chunk * LANES : (chunk + 1) * LANES]


def product_kernel(dz1, later, filters, query, key, grad_query, grad_key):
    rows, cols = iotas()
    upper_half = (cols >= rows).astype(F32).astype(BF16)
    for block in range(dz1.shape[0] // TILE):
        span = pl.ds(block * TILE, TILE)
        filt = filters[pl.ds(block * PACK, PACK), :].astype(F32)
        here = dz1[span, :]
        there = later[span, :]
        pieces = []
        for g in range(PACK):
            part = slice(g * LANES, (g + 1) * LANES)
            circ = circulant(filt[g : g + 1, :]).astype(BF16)
            w_now = circ * upper_half
            pieces.append(nt(here[part, :], w_now) + nt(there[part, :], circ - w_now))
        du1 = jnp.concatenate(pieces, axis=0)
        grad_query[span, :] = (du1 * key[span, :].astype(F32)).astype(BF16)
        grad_key[span, :] = (du1 * query[span, :].astype(F32)).astype(BF16)


def value_kernel(count, *refs):
    states = refs[: count - 1]
    after, decay, z2, grad, grad_value = refs[count - 1 :]
    mask = same_group()
    place = lax.axis_index("seq")
    blocks = z2.shape[0] // TILE
    for block in range(blocks):
        span = pl.ds(block * TILE, TILE)
        fade = decay[:, span]
        carried = jnp.zeros((LANES, TILE), F32)
        for gap in range(count - 1, 0, -1):
            state = states[gap - 1][block].astype(F32)
            carried = jnp.where(place >= gap, state, 0.0) + fade * carried
        wide = spread_groups(carried, mask).T.astype(BF16)
        total = z2[span, :] + nn(wide, after[span, :])
        grad_value[span, :] = (grad[span, :].astype(F32) * total).astype(BF16)


def shifted(value, axis, steps, around=False):
    count = lax.axis_size(axis)
    pairs = [(source, (source + steps) % count) for source in range(count)]
    if not around:
        pairs = [pair for pair in pairs if pair[1] - pair[0] == steps]
    return lax.ppermute(value, axis, pairs)


def per_device(
    mr_query, mr_key, mr_value, li_key, li_value, grad_out, mr_filter, li_residue, li_rate
):
    query, key, value, key_two, value_two, grad = (
        array[0] for array in (mr_query, mr_key, mr_value, li_key, li_value, grad_out)
    )
    groups, filt_len = mr_filter.shape
    channels, seq_local = query.shape
    assert filt_len == TILE and seq_local == TILE
    assert channels == groups * LANES and li_rate.shape[1] == LANES
    count = lax.axis_size("seq")
    steps = 4
    rows = channels // steps
    few = groups // steps
    blocks = channels // TILE

    wide = pl.BlockSpec((rows, TILE), lambda i: (i, 0))
    modes = pl.BlockSpec((few, LANES), lambda i: (i, 0))
    table = pl.BlockSpec((few, TILE), lambda i: (i, 0))
    narrow = pl.BlockSpec((LANES, rows), lambda i: (0, i))
    wide_half = jax.ShapeDtypeStruct((channels, TILE), BF16)
    wide_full = jax.ShapeDtypeStruct((channels, TILE), F32)
    narrow_half = jax.ShapeDtypeStruct((LANES, channels), BF16)
    narrow_full = jax.ShapeDtypeStruct((LANES, channels), F32)

    def call(kernel, name, in_specs, out_specs, out_shape, work, scratch=()):
        size = sum(leaf.size * leaf.dtype.itemsize for leaf in out_shape)
        return pl.pallas_call(
            kernel,
            grid=(steps,),
            in_specs=in_specs,
            out_specs=out_specs,
            out_shape=out_shape,
            scratch_shapes=scratch,
            name=name,
            cost_estimate=pl.CostEstimate(
                flops=work * 2 * channels * TILE * TILE,
                bytes_accessed=size + len(in_specs) * channels * TILE * 2,
                transcendentals=channels * TILE,
            ),
            compiler_params=pltpu.CompilerParams(vmem_limit_bytes=VMEM_LIMIT),
        )

    product, back = call(
        first_kernel, "first",
        [wide] * 4 + [modes],
        [wide, narrow], [wide_half, narrow_half], 4,
    )(query, key, grad, value_two, li_rate)
    product_before = shifted(product, "seq", 1)
    later_backs = [shifted(back, "seq", -gap) for gap in range(1, count)]

    du2_local, to_next, after, to_end, power, taps, decay = call(
        local_kernel, "local",
        [wide, wide, modes, modes],
        [wide] * 5 + [table, narrow],
        [wide_full] + [wide_half] * 4 + [jax.ShapeDtypeStruct((groups, TILE), F32), narrow_full],
        20,
    )(grad, value_two, li_rate, li_residue)

    dz1, du2, after_shard = call(
        functools.partial(middle_kernel, count), "middle",
        [narrow] * (count - 1) + [wide, wide, narrow, wide, wide],
        [wide, wide, narrow], [wide_half, wide_full, narrow_full], 4,
    )(*later_backs, du2_local, to_next, decay, key_two, value)
    dz1_later = shifted(dz1, "seq", -1)

    filter_chunks = groups // LANES
    residue_chunks = pl.cdiv(blocks, LANES)
    chunks = blocks + filter_chunks + residue_chunks
    grad_mr_value, grad_li_key, z2, packed = call(
        functools.partial(forward_kernel, steps), "forward",
        [wide, wide, table, wide, wide, wide, wide, table, wide, wide, modes, narrow, wide, wide],
        [wide, wide, wide, pl.BlockSpec((chunks, LANES, TILE), lambda i: (0, 0, 0))],
        [
            wide_half, wide_half, wide_full,
            jax.ShapeDtypeStruct((chunks, LANES, TILE), BF16),
        ],
        40,
        [pltpu.VMEM((groups, TILE), F32), pltpu.VMEM((residue_chunks * LANES, TILE), F32)],
    )(
        product_before, product, mr_filter, value, key_two, grad, value_two, taps, to_end, power,
        li_rate, after_shard, dz1, du2,
    )
    others = [shifted(packed, "seq", gap, around=True) for gap in range(1, count)]

    sums = packed[blocks:].astype(F32)
    for other in others:
        sums = sums + other[blocks:].astype(F32)
    partners = [
        shifted(sums, "dp", gap, around=True) for gap in range(1, lax.axis_size("dp"))
    ]

    grad_query, grad_key = call(
        product_kernel, "product",
        [wide, wide, table, wide, wide], [wide, wide], [wide_half, wide_half], 20,
    )(dz1, dz1_later, mr_filter, query, key)

    state_block = pl.BlockSpec((rows // TILE, LANES, TILE), lambda i: (i, 0, 0))
    (grad_li_value,) = call(
        functools.partial(value_kernel, count), "value",
        [state_block] * (count - 1) + [wide, narrow, wide, wide], [wide], [wide_half], 4,
    )(*others, after, decay, z2, grad)

    for partner in partners:
        sums = sums + partner
    grad_filter = sums[:filter_chunks].reshape(groups, TILE)
    grad_residue = sums[filter_chunks:].reshape(-1, TILE)[:blocks].reshape(groups, LANES)
    return (
        grad_query[None],
        grad_key[None],
        grad_mr_value[None],
        grad_li_key[None],
        grad_li_value[None],
        grad_filter,
        grad_residue,
    )


def solution(mesh):
    streams = (P("dp", "chan", "seq"),)
    tables = (P("chan", None),)
    return jax.shard_map(
        per_device,
        mesh=mesh,
        in_specs=streams * 6 + tables * 3,
        out_specs=streams * 5 + tables * 2,
        check_vma=False,
    )
```

```python
import functools

import jax
import jax.numpy as jnp
from jax import lax
from jax.experimental import pallas as pl
from jax.experimental.pallas import tpu as pltpu
from jax.sharding import PartitionSpec as P

F32 = jnp.float32
BF16 = jnp.bfloat16
TILE = 128
LANES = 16
PACK = TILE // LANES
STEPS = 4
VMEM_LIMIT = 24 * 1024 * 1024


def nn(lhs, rhs):
    return lax.dot_general(lhs, rhs, (((1,), (0,)), ((), ())), preferred_element_type=F32)


def nt(lhs, rhs):
    return lax.dot_general(lhs, rhs, (((1,), (1,)), ((), ())), preferred_element_type=F32)


def iotas():
    rows = lax.broadcasted_iota(jnp.int32, (TILE, TILE), 0)
    cols = lax.broadcasted_iota(jnp.int32, (TILE, TILE), 1)
    return rows, cols


def ones_where(mask):
    return jnp.where(mask, 1.0, 0.0).astype(BF16)


def column(turned, mask):
    wide = jnp.concatenate([turned] * PACK, axis=0)
    return jnp.sum(jnp.where(mask, wide, 0.0), axis=1, keepdims=True)


def squeeze_groups(wide, mask):
    kept = jnp.where(mask, wide, 0.0)
    total = kept[:LANES]
    for g in range(1, PACK):
        total = total + kept[g * LANES : (g + 1) * LANES]
    return total


def spread_groups(narrow, mask):
    return jnp.where(mask, jnp.concatenate([narrow] * PACK, axis=0), 0.0)


def circulant(row):
    base = jnp.broadcast_to(row, (LANES, TILE))
    base = pltpu.roll(base, 0, 1, stride=1, stride_axis=0).astype(BF16)
    return jnp.concatenate(
        [base] + [pltpu.roll(base, LANES * j, 1) for j in range(1, PACK)], axis=0
    )


def reversal():
    rows, cols = iotas()
    return ones_where((rows + cols) % TILE == 0)


def one_minus_exp(value):
    series = jnp.full_like(value, 1.0)
    for order in (7, 6, 5, 4, 3, 2):
        series = 1.0 - value * series / order
    return jnp.where(value < 0.125, value * series, 1.0 - jnp.exp(-value))


def diagonals(matrix):
    total = matrix[:LANES].astype(F32)
    for j in range(1, PACK):
        piece = matrix[LANES * j : LANES * (j + 1)]
        total = total + pltpu.roll(piece, TILE - LANES * j, 1).astype(F32)
    total = pltpu.roll(total, 0, 1, stride=1, stride_axis=0)
    return jnp.sum(total, axis=0, keepdims=True)


def block_groups(at, blocks, block):
    rows, cols = iotas()
    return cols == rows // LANES + (at * blocks + block) * PACK


def first_kernel(query_hbm, key_hbm, grad_hbm, value_hbm, rate, product, state, held, arrived):
    _, cols = iotas()
    offsets = cols.astype(F32)
    rows, cols = iotas()
    mask = rows // LANES == cols // LANES
    at = pl.program_id(0)
    size = product.shape[0]
    blocks = size // TILE

    def fetch(array, step):
        span = pl.ds(step * size, size)
        source = (grad_hbm, value_hbm, query_hbm, key_hbm)[array]
        return pltpu.make_async_copy(
            source.at[span, :], held.at[array, span, :], arrived.at[array, step]
        )

    @pl.when(at == 0)
    def _():
        for step in range(STEPS):
            for array in range(4):
                fetch(array, step).start()

    for array in range(4):
        fetch(array, at).wait()
    for block in range(blocks):
        span = pl.ds(block * TILE, TILE)
        here = pl.ds(pl.multiple_of(at * size + block * TILE, TILE), TILE)
        rates = column(rate[...], block_groups(at, blocks, block))
        powers = jnp.exp(-rates * offsets).astype(BF16)
        dz2 = held[0, here, :] * held[1, here, :]
        state[:, span] = squeeze_groups(nt(powers, dz2), mask).astype(BF16)
        product[span, :] = held[2, here, :] * held[3, here, :]


def local_kernel(grad, value, rate, residue, du2, to_next, after, to_end, power, taps, decay):
    rows, cols = iotas()
    offsets = cols.astype(F32)
    mask = rows // LANES == cols // LANES
    lower_half = ones_where(rows >= cols)
    turn = reversal()
    at = pl.program_id(0)
    blocks = grad.shape[0] // TILE
    for block in range(blocks):
        span = pl.ds(block * TILE, TILE)
        own = block_groups(at, blocks, block)
        rates = column(rate[...], own)
        gains = jnp.sqrt(one_minus_exp(2.0 * rates))
        coeffs = column(residue[...], own) * gains
        powers = jnp.exp(-rates * offsets)
        ends = jnp.exp(-rates * (TILE - 1 - offsets))
        stepped = coeffs * jnp.exp(-rates)
        power[span, :] = powers.astype(BF16)
        to_end[span, :] = ends.astype(BF16)
        after[span, :] = (powers * stepped).astype(BF16)
        to_next[span, :] = (ends * stepped).astype(BF16)
        fades = jnp.broadcast_to(jnp.exp(-rates * TILE), (TILE, TILE))
        decay[:, span] = squeeze_groups(fades, mask)
        filt = jnp.sum((powers * coeffs).reshape(PACK, LANES, TILE), axis=1)
        taps[pl.ds(block * PACK, PACK), :] = filt
        turned = nn(filt.astype(BF16), turn)
        dz2 = grad[span, :] * value[span, :]
        pieces = []
        for g in range(PACK):
            weights = circulant(turned[g : g + 1, :]) * lower_half
            pieces.append(nn(dz2[g * LANES : (g + 1) * LANES, :], weights))
        du2[span, :] = jnp.concatenate(pieces, axis=0)


def middle_kernel(count, *refs):
    states = refs[: count - 1]
    local, to_next, decay, li_key, value, dz1, du2, after_shard = refs[count - 1 :]
    rows, cols = iotas()
    mask = rows // LANES == cols // LANES
    for block in range(local.shape[0] // TILE):
        span = pl.ds(block * TILE, TILE)
        fade = decay[:, span]
        carried = states[-1][:, span].astype(F32)
        for state in states[-2::-1]:
            carried = state[:, span].astype(F32) + fade * carried
        after_shard[:, span] = carried
        wide = spread_groups(carried, mask).T.astype(BF16)
        total = local[span, :] + nn(wide, to_next[span, :])
        du2[span, :] = total
        dy1 = total * li_key[span, :].astype(F32)
        dz1[span, :] = (dy1 * value[span, :].astype(F32)).astype(BF16)


def forward_kernel(
    before, now, filters, value, li_key, to_end, du2, grad_value, grad_key, u2, state
):
    rows, cols = iotas()
    mask = rows // LANES == cols // LANES
    upper_half = ones_where(cols >= rows)
    for block in range(now.shape[0] // TILE):
        span = pl.ds(block * TILE, TILE)
        both = jnp.concatenate([now[span, :], before[span, :]], axis=1)
        filt = filters[pl.ds(block * PACK, PACK), :].astype(F32)
        pieces = []
        for g in range(PACK):
            circ = circulant(filt[g : g + 1, :])
            w_now = circ * upper_half
            weights = jnp.concatenate([w_now, circ - w_now], axis=0)
            pieces.append(nn(both[g * LANES : (g + 1) * LANES, :], weights))
        z1 = jnp.concatenate(pieces, axis=0)
        y1 = (value[span, :].astype(F32) * z1).astype(BF16).astype(F32)
        key_two = li_key[span, :].astype(F32)
        u2_half = (y1 * key_two).astype(BF16)
        u2[span, :] = u2_half
        state[:, span] = squeeze_groups(nt(to_end[span, :], u2_half), mask).astype(BF16)
        du2_here = du2[span, :]
        grad_key[span, :] = (du2_here * y1).astype(BF16)
        grad_value[span, :] = (du2_here * key_two * z1).astype(BF16)


def sums_kernel(
    before, now, u2, dz1, grad, li_value, taps, power, state, after_shard, rate,
    z2, packed, filter_sums, within_sums, across_sums,
):
    rows, cols = iotas()
    upper_half = ones_where(cols >= rows)
    place = rows - rows % LANES + (LANES - 1 - rows % LANES)
    turn = ones_where(place == cols)
    keep = cols >= place
    keep_half = ones_where(keep)
    drop_half = ones_where(jnp.logical_not(keep))
    at = pl.program_id(0)
    blocks = now.shape[0] // TILE
    zeros = jnp.zeros((LANES, TILE), BF16)

    @pl.when(at == 0)
    def _():
        within_sums[...] = jnp.zeros_like(within_sums)
        across_sums[...] = jnp.zeros_like(across_sums)

    for block in range(blocks):
        span = pl.ds(block * TILE, TILE)
        u2_here = u2[span, :]
        dz2 = grad[span, :] * li_value[span, :]
        dz1_here = dz1[span, :]
        u1_turned = nt(turn, now[span, :]).astype(BF16)
        before_turned = nt(turn, before[span, :]).astype(BF16)
        u2_turned = nt(turn, u2_here).astype(BF16)
        lag_taps = taps[pl.ds(block * PACK, PACK), :]
        pieces, lags, energies = [], [], []
        for g in range(PACK):
            part = slice(g * LANES, (g + 1) * LANES)
            weights = circulant(lag_taps[g : g + 1, :]) * upper_half
            pieces.append(nn(u2_here[part, :], weights))

            def alone(array):
                above = [zeros] * g
                below = [zeros] * (PACK - 1 - g)
                return jnp.concatenate(above + [array[part, :]] + below, axis=0)

            dz1_alone = alone(dz1_here)
            lag = nn(u1_turned, dz1_alone).astype(BF16) * keep_half
            lag = lag + nn(before_turned, dz1_alone).astype(BF16) * drop_half
            lags.append(diagonals(lag))
            energy = nn(u2_turned, alone(dz2)).astype(BF16) * keep_half
            energies.append(diagonals(energy))
        z2[span, :] = jnp.concatenate(pieces, axis=0)
        few = pl.ds(pl.multiple_of((at * blocks + block) * PACK, PACK), PACK)
        filter_sums[few, :] = jnp.concatenate(lags, axis=0)
        energies = pltpu.roll(jnp.concatenate(energies, axis=0), TILE - LANES + 1, 1)
        energies = jnp.concatenate([energies.astype(BF16)] * LANES, axis=0)
        own = block_groups(at, blocks, block)
        within_sums[...] += squeeze_groups(nt(power[span, :], energies), own)
        across = state[:, span].astype(F32) * after_shard[:, span]
        across_sums[...] += nn(across.astype(BF16), ones_where(own))

    @pl.when(at == STEPS - 1)
    def _():
        sums = pltpu.roll(filter_sums[...], TILE - LANES + 1, 1)
        for chunk in range(filter_sums.shape[0] // LANES):
            packed[chunk] = sums[chunk * LANES : (chunk + 1) * LANES]
        rates = rate[...]
        gains = jnp.sqrt(one_minus_exp(2.0 * rates))
        total = gains * (within_sums[...] + jnp.exp(-rates) * across_sums[...])
        packed[filter_sums.shape[0] // LANES] = total


def product_kernel(dz1, later, filters, query, key, grad_query, grad_key):
    rows, cols = iotas()
    lower_half = ones_where(rows >= cols)
    turn = reversal()
    for block in range(dz1.shape[0] // TILE):
        span = pl.ds(block * TILE, TILE)
        filt = nn(filters[pl.ds(block * PACK, PACK), :], turn)
        both = jnp.concatenate([dz1[span, :], later[span, :]], axis=1)
        pieces = []
        for g in range(PACK):
            circ = circulant(filt[g : g + 1, :])
            w_now = circ * lower_half
            weights = jnp.concatenate([w_now, circ - w_now], axis=0)
            pieces.append(nn(both[g * LANES : (g + 1) * LANES, :], weights))
        du1 = jnp.concatenate(pieces, axis=0)
        grad_query[span, :] = (du1 * key[span, :].astype(F32)).astype(BF16)
        grad_key[span, :] = (du1 * query[span, :].astype(F32)).astype(BF16)


def value_kernel(count, *refs):
    states = refs[: count - 1]
    after, decay, z2, grad, grad_value = refs[count - 1 :]
    rows, cols = iotas()
    mask = rows // LANES == cols // LANES
    for block in range(z2.shape[0] // TILE):
        span = pl.ds(block * TILE, TILE)
        fade = decay[:, span]
        carried = states[-1][:, span].astype(F32)
        for state in states[-2::-1]:
            carried = state[:, span].astype(F32) + fade * carried
        wide = spread_groups(carried, mask).T.astype(BF16)
        total = z2[span, :] + nn(wide, after[span, :])
        grad_value[span, :] = (grad[span, :].astype(F32) * total).astype(BF16)


def shifted(value, axis, steps):
    count = lax.axis_size(axis)
    first, last = max(0, -steps), min(count, count - steps)
    return lax.ppermute(value, axis, [(source, source + steps) for source in range(first, last)])


def exchange_sum(value, axis):
    count, bit = lax.axis_size(axis), 1
    assert count & (count - 1) == 0
    while bit < count:
        half = value.astype(BF16)
        other = lax.ppermute(half, axis, [(source, source ^ bit) for source in range(count)])
        value = half.astype(F32) + other.astype(F32)
        bit *= 2
    return value


def per_device(
    mr_query, mr_key, mr_value, li_key, li_value, grad_out, mr_filter, li_residue, li_rate
):
    query, key, value, key_two, value_two, grad = (
        array[0] for array in (mr_query, mr_key, mr_value, li_key, li_value, grad_out)
    )
    groups, filt_len = mr_filter.shape
    channels, seq_local = query.shape
    assert filt_len == TILE and seq_local == TILE and groups <= TILE
    assert channels == groups * LANES and li_rate.shape[1] == LANES
    count = lax.axis_size("seq")
    rows = channels // STEPS
    few = groups // STEPS
    spare = ((0, 0), (0, TILE - groups))
    rate = jnp.pad(li_rate.T, spare)
    residue = jnp.pad(li_residue.T, spare)

    wide = pl.BlockSpec((rows, TILE), lambda i: (i, 0))
    table = pl.BlockSpec((few, TILE), lambda i: (i, 0))
    narrow = pl.BlockSpec((LANES, rows), lambda i: (0, i))
    modes = pl.BlockSpec((LANES, TILE), lambda i: (0, 0))
    distant = pl.BlockSpec(memory_space=pltpu.HBM)
    wide_half = jax.ShapeDtypeStruct((channels, TILE), BF16)
    wide_full = jax.ShapeDtypeStruct((channels, TILE), F32)
    narrow_half = jax.ShapeDtypeStruct((LANES, channels), BF16)
    narrow_full = jax.ShapeDtypeStruct((LANES, channels), F32)

    def call(kernel, name, in_specs, out_specs, out_shape, work, scratch=()):
        size = sum(leaf.size * leaf.dtype.itemsize for leaf in out_shape)
        return pl.pallas_call(
            kernel,
            grid=(STEPS,),
            in_specs=in_specs,
            out_specs=out_specs,
            out_shape=out_shape,
            scratch_shapes=scratch,
            name=name,
            cost_estimate=pl.CostEstimate(
                flops=work * 2 * channels * TILE * TILE,
                bytes_accessed=size + len(in_specs) * channels * TILE * 2,
                transcendentals=channels * TILE,
            ),
            compiler_params=pltpu.CompilerParams(vmem_limit_bytes=VMEM_LIMIT),
        )

    product, back = call(
        first_kernel, "first",
        [distant] * 4 + [modes],
        [wide, narrow], [wide_half, narrow_half], 4,
        [pltpu.VMEM((4, channels, TILE), BF16), pltpu.SemaphoreType.DMA((4, STEPS))],
    )(query, key, grad, value_two, rate)
    product_before = shifted(product, "seq", 1)
    later_backs = [shifted(back, "seq", -gap) for gap in range(1, count)]

    du2_local, to_next, after, to_end, power, taps, decay = call(
        local_kernel, "local",
        [wide, wide, modes, modes],
        [wide] * 5 + [table, narrow],
        [wide_full] + [wide_half] * 4 + [jax.ShapeDtypeStruct((groups, TILE), F32), narrow_full],
        20,
    )(grad, value_two, rate, residue)

    dz1, du2, after_shard = call(
        functools.partial(middle_kernel, count), "middle",
        [narrow] * (count - 1) + [wide, wide, narrow, wide, wide],
        [wide, wide, narrow], [wide_half, wide_full, narrow_full], 4,
    )(*later_backs, du2_local, to_next, decay, key_two, value)
    dz1_later = shifted(dz1, "seq", -1)

    grad_mr_value, grad_li_key, u2, state = call(
        forward_kernel, "forward",
        [wide, wide, table, wide, wide, wide, wide],
        [wide, wide, wide, narrow], [wide_half] * 3 + [narrow_half], 20,
    )(product_before, product, mr_filter, value, key_two, to_end, du2)
    earlier_states = [shifted(state, "seq", gap) for gap in range(1, count)]

    chunks = groups // LANES + 1
    z2, packed = call(
        sums_kernel, "sums",
        [wide] * 6 + [table, wide, narrow, narrow, modes],
        [wide, pl.BlockSpec((chunks, LANES, TILE), lambda i: (0, 0, 0))],
        [wide_full, jax.ShapeDtypeStruct((chunks, LANES, TILE), F32)],
        40,
        [pltpu.VMEM((groups, TILE), F32)] + [pltpu.VMEM((LANES, TILE), F32)] * 2,
    )(product_before, product, u2, dz1, grad, value_two, taps, power, state, after_shard, rate)

    grad_query, grad_key = call(
        product_kernel, "product",
        [wide, wide, table, wide, wide], [wide, wide], [wide_half, wide_half], 20,
    )(dz1, dz1_later, mr_filter, query, key)

    (grad_li_value,) = call(
        functools.partial(value_kernel, count), "value",
        [narrow] * (count - 1) + [wide, narrow, wide, wide], [wide], [wide_half], 4,
    )(*earlier_states, after, decay, z2, grad)

    sums = exchange_sum(exchange_sum(packed, "dp"), "seq")
    return (
        grad_query[None],
        grad_key[None],
        grad_mr_value[None],
        grad_li_key[None],
        grad_li_value[None],
        sums[:-1].reshape(groups, TILE),
        sums[-1][:, :groups].T,
    )


def solution(mesh):
    streams = (P("dp", "chan", "seq"),)
    tables = (P("chan", None),)
    return jax.shard_map(
        per_device,
        mesh=mesh,
        in_specs=streams * 6 + tables * 3,
        out_specs=streams * 5 + tables * 2,
        check_vma=False,
    )
```

```python
import functools

import jax
import jax.numpy as jnp
from jax import lax
from jax.experimental import pallas as pl
from jax.experimental.pallas import tpu as pltpu
from jax.sharding import PartitionSpec as P

F32 = jnp.float32
BF16 = jnp.bfloat16
TILE = 128
LANES = 16
PACK = TILE // LANES
CHUNK = 32
STEPS = 4
VMEM_LIMIT = 24 * 1024 * 1024


def nn(lhs, rhs):
    return lax.dot_general(lhs, rhs, (((1,), (0,)), ((), ())), preferred_element_type=F32)


def nt(lhs, rhs):
    return lax.dot_general(lhs, rhs, (((1,), (1,)), ((), ())), preferred_element_type=F32)


def iotas():
    rows = lax.broadcasted_iota(jnp.int32, (TILE, TILE), 0)
    cols = lax.broadcasted_iota(jnp.int32, (TILE, TILE), 1)
    return rows, cols


def ones_where(mask):
    return jnp.where(mask, 1.0, 0.0).astype(BF16)


def column(turned, mask):
    wide = jnp.concatenate([turned] * PACK, axis=0)
    return jnp.sum(jnp.where(mask, wide, 0.0), axis=1, keepdims=True)


def squeeze_groups(wide, mask):
    kept = jnp.where(mask, wide, 0.0)
    total = kept[:LANES]
    for g in range(1, PACK):
        total = total + kept[g * LANES : (g + 1) * LANES]
    return total


def spread_groups(narrow, mask):
    return jnp.where(mask, jnp.concatenate([narrow] * PACK, axis=0), 0.0)


def circulant(row):
    base = jnp.broadcast_to(row, (LANES, TILE))
    base = pltpu.roll(base, 0, 1, stride=1, stride_axis=0).astype(BF16)
    return jnp.concatenate(
        [base] + [pltpu.roll(base, LANES * j, 1) for j in range(1, PACK)], axis=0
    )


def reversal():
    rows, cols = iotas()
    return ones_where((rows + cols) % TILE == 0)


def one_minus_exp(value):
    series = jnp.full_like(value, 1.0)
    for order in (7, 6, 5, 4, 3, 2):
        series = 1.0 - value * series / order
    return jnp.where(value < 0.125, value * series, 1.0 - jnp.exp(-value))


def chunk_mask(shape, bit):
    return (lax.broadcasted_iota(jnp.int32, shape, 1) // CHUNK) & bit == 0


def pair_chunks(turned):
    parts = [turned[CHUNK * j : CHUNK * (j + 1), :] for j in range(TILE // CHUNK)]
    for bit in (1, 2):
        keep = chunk_mask((CHUNK, TILE), bit)
        for j in range(len(parts)):
            if j & bit == 0:
                low, high = parts[j], parts[j + bit]
                parts[j] = jnp.where(keep, low, pltpu.roll(high, CHUNK * bit, 1))
                parts[j + bit] = jnp.where(keep, pltpu.roll(low, TILE - CHUNK * bit, 1), high)
    return parts


def windows(before, now):
    lanes = lax.broadcasted_iota(jnp.int32, now.shape, 1)
    none = jnp.zeros_like(now)
    first, second = [none if before is None else before], [now]
    for j in range(1, TILE // CHUNK):
        left = TILE - CHUNK * j
        moved = pltpu.roll(now, left, 1)
        older = none if before is None else pltpu.roll(before, left, 1)
        first.append(jnp.where(lanes < left, older, moved))
        second.append(moved)
    return jnp.concatenate(
        [jnp.concatenate(first, axis=0), jnp.concatenate(second, axis=0)], axis=1
    )


def lag_rows(chunks, shifted_rows, own_rows):
    left = jnp.concatenate([chunks * own for own in own_rows], axis=0)
    wide = nn(left, shifted_rows)
    rows = lax.broadcasted_iota(jnp.int32, (2 * CHUNK, TILE), 0) % CHUNK
    lanes = lax.broadcasted_iota(jnp.int32, (2 * CHUNK, TILE), 1)
    sums = jnp.where(lanes + rows < CHUNK, wide[:, TILE:], wide[:, :TILE])
    sums = [
        pltpu.roll(sums[CHUNK * i : CHUNK * (i + 1)], 0, 1, stride=1, stride_axis=0)
        for i in range(2)
    ]
    return jnp.concatenate([jnp.sum(part, axis=0, keepdims=True) for part in sums], axis=0)


def crossed(left, weights):
    wide = nn(left, weights)
    return wide[:LANES, :TILE], wide[LANES:, TILE:]


def now_and_before(now, before, rows, half):
    pieces = []
    for g in range(PACK):
        part = slice(g * LANES, (g + 1) * LANES)
        circ = circulant(rows[g : g + 1, :])
        w_now = circ * half
        weights = jnp.concatenate([w_now, circ - w_now], axis=1)
        pair = crossed(jnp.concatenate([now[part, :], before[part, :]], axis=0), weights)
        pieces.append(pair[0] + pair[1])
    return jnp.concatenate(pieces, axis=0)


def within_shard(array, rows, half):
    pieces = []
    for g in range(0, PACK, 2):
        weights = [circulant(rows[h : h + 1, :]) * half for h in (g, g + 1)]
        part = slice(g * LANES, (g + 2) * LANES)
        pieces += crossed(array[part, :], jnp.concatenate(weights, axis=1))
    return jnp.concatenate(pieces, axis=0)


def block_groups(at, blocks, block):
    rows, cols = iotas()
    return cols == rows // LANES + (at * blocks + block) * PACK


def first_kernel(query, key, grad, value, rate, product, state):
    rows, cols = iotas()
    offsets = cols.astype(F32)
    mask = rows // LANES == cols // LANES
    at = pl.program_id(0)
    blocks = product.shape[0] // TILE
    for block in range(blocks):
        span = pl.ds(block * TILE, TILE)
        rates = column(rate[...], block_groups(at, blocks, block))
        powers = jnp.exp(-rates * offsets).astype(BF16)
        dz2 = grad[span, :] * value[span, :]
        state[:, span] = squeeze_groups(nt(powers, dz2), mask).astype(BF16)
        product[span, :] = query[span, :] * key[span, :]


def local_kernel(grad, value, rate, residue, du2, to_next, after, to_end, power, taps, decay):
    rows, cols = iotas()
    offsets = cols.astype(F32)
    mask = rows // LANES == cols // LANES
    lower_half = ones_where(rows >= cols)
    lags = ((CHUNK - 1 - cols) % TILE).astype(F32)
    at = pl.program_id(0)
    blocks = grad.shape[0] // TILE
    filters = []
    for block in range(blocks):
        span = pl.ds(block * TILE, TILE)
        own = block_groups(at, blocks, block)
        rates = column(rate[...], own)
        gains = jnp.sqrt(one_minus_exp(2.0 * rates))
        coeffs = column(residue[...], own) * gains
        powers = jnp.exp(-rates * offsets)
        ends = jnp.exp(-rates * (TILE - 1 - offsets))
        stepped = coeffs * jnp.exp(-rates)
        power[span, :] = jnp.exp(-rates * lags).astype(BF16)
        to_end[span, :] = ends.astype(BF16)
        after[span, :] = (powers * stepped).astype(BF16)
        to_next[span, :] = (ends * stepped).astype(BF16)
        fades = jnp.broadcast_to(jnp.exp(-rates * TILE), (TILE, TILE))
        decay[:, span] = squeeze_groups(fades, mask)
        filters.append(jnp.sum((powers * coeffs).reshape(PACK, LANES, TILE), axis=1))
    filters = jnp.concatenate(filters, axis=0)
    taps[...] = filters
    turned = nn(filters.astype(BF16), reversal())
    for block in range(blocks):
        span = pl.ds(block * TILE, TILE)
        dz2 = grad[span, :] * value[span, :]
        du2[span, :] = within_shard(dz2, turned[block * PACK : (block + 1) * PACK], lower_half)


def middle_kernel(count, *refs):
    states = refs[: count - 1]
    local, to_next, decay, li_key, value, dz1, du2, after_shard = refs[count - 1 :]
    rows, cols = iotas()
    mask = rows // LANES == cols // LANES
    for block in range(local.shape[0] // TILE):
        span = pl.ds(block * TILE, TILE)
        fade = decay[:, span]
        carried = states[-1][:, span].astype(F32)
        for state in states[-2::-1]:
            carried = state[:, span].astype(F32) + fade * carried
        after_shard[:, span] = carried
        wide = spread_groups(carried, mask).T.astype(BF16)
        total = local[span, :] + nn(wide, to_next[span, :])
        du2[span, :] = total
        dy1 = total * li_key[span, :].astype(F32)
        dz1[span, :] = (dy1 * value[span, :].astype(F32)).astype(BF16)


def forward_kernel(
    before, now, filters, value, li_key, to_end, du2, grad_value, grad_key, u2, state
):
    rows, cols = iotas()
    mask = rows // LANES == cols // LANES
    upper_half = ones_where(cols >= rows)
    for block in range(now.shape[0] // TILE):
        span = pl.ds(block * TILE, TILE)
        filt = filters[pl.ds(block * PACK, PACK), :].astype(F32)
        z1 = now_and_before(now[span, :], before[span, :], filt, upper_half)
        y1 = (value[span, :].astype(F32) * z1).astype(BF16).astype(F32)
        key_two = li_key[span, :].astype(F32)
        u2_half = (y1 * key_two).astype(BF16)
        u2[span, :] = u2_half
        state[:, span] = squeeze_groups(nt(to_end[span, :], u2_half), mask).astype(BF16)
        du2_here = du2[span, :]
        grad_key[span, :] = (du2_here * y1).astype(BF16)
        grad_value[span, :] = (du2_here * key_two * z1).astype(BF16)


def sums_kernel(
    before, now, u2, dz1, grad, li_value, power, state, after_shard, rate,
    packed, filter_sums, within_sums, across_sums,
):
    rows, cols = iotas()
    turn = ones_where(cols == rows - rows % CHUNK + (CHUNK - 1 - rows % CHUNK))
    lanes = lax.broadcasted_iota(jnp.int32, (CHUNK, TILE), 1)
    own_rows = [ones_where((lanes // LANES) % 2 == i) for i in range(2)]
    at = pl.program_id(0)
    blocks = now.shape[0] // TILE

    @pl.when(at == 0)
    def _():
        within_sums[...] = jnp.zeros_like(within_sums)
        across_sums[...] = jnp.zeros_like(across_sums)

    for block in range(blocks):
        span = pl.ds(block * TILE, TILE)
        dz2 = grad[span, :] * li_value[span, :]
        turned = nt(turn, jnp.concatenate([dz1[span, :], dz2], axis=0)).astype(BF16)
        lag_chunks = pair_chunks(turned[:, :TILE])
        energy_chunks = pair_chunks(turned[:, TILE:])
        lags, energies = [], []
        for p in range(TILE // CHUNK):
            pair = pl.ds(block * TILE + p * CHUNK, CHUNK)
            lags.append(lag_rows(lag_chunks[p], windows(before[pair, :], now[pair, :]), own_rows))
            energies.append(lag_rows(energy_chunks[p], windows(None, u2[pair, :]), own_rows))
        few = pl.ds(pl.multiple_of((at * blocks + block) * PACK, PACK), PACK)
        filter_sums[few, :] = jnp.concatenate(lags, axis=0)
        energies = jnp.concatenate(energies, axis=0).astype(BF16)
        energies = jnp.concatenate([energies] * LANES, axis=0)
        own = block_groups(at, blocks, block)
        within_sums[...] += squeeze_groups(nt(power[span, :], energies), own)
        across = state[:, span].astype(F32) * after_shard[:, span]
        across_sums[...] += nn(across.astype(BF16), ones_where(own))

    @pl.when(at == STEPS - 1)
    def _():
        place = ones_where((rows + cols) % TILE == CHUNK - 1)
        sums = nn(filter_sums[...].astype(BF16), place).astype(BF16)
        for chunk in range(filter_sums.shape[0] // LANES):
            packed[chunk] = sums[chunk * LANES : (chunk + 1) * LANES]
        rates = rate[...]
        gains = jnp.sqrt(one_minus_exp(2.0 * rates))
        total = gains * (within_sums[...] + jnp.exp(-rates) * across_sums[...])
        packed[filter_sums.shape[0] // LANES] = total.astype(BF16)


def within_kernel(u2, taps, z2):
    rows, cols = iotas()
    upper_half = ones_where(cols >= rows)
    for block in range(u2.shape[0] // TILE):
        span = pl.ds(block * TILE, TILE)
        z2[span, :] = within_shard(u2[span, :], taps[pl.ds(block * PACK, PACK), :], upper_half)


def last_kernel(half, other, grad_filter, grad_residue):
    chunks = half.shape[0] - 1
    for chunk in range(chunks):
        grad_filter[pl.ds(chunk * LANES, LANES), :] = half[chunk].astype(F32) + other[chunk].astype(F32)
    grad_residue[...] = half[chunks].astype(F32) + other[chunks].astype(F32)


def product_kernel(dz1, later, filters, query, key, grad_query, grad_key):
    rows, cols = iotas()
    lower_half = ones_where(rows >= cols)
    turned = nn(filters[...], reversal())
    for block in range(dz1.shape[0] // TILE):
        span = pl.ds(block * TILE, TILE)
        filt = turned[block * PACK : (block + 1) * PACK]
        du1 = now_and_before(dz1[span, :], later[span, :], filt, lower_half)
        grad_query[span, :] = (du1 * key[span, :].astype(F32)).astype(BF16)
        grad_key[span, :] = (du1 * query[span, :].astype(F32)).astype(BF16)


def value_kernel(count, *refs):
    states = refs[: count - 1]
    after, decay, z2, grad, grad_value = refs[count - 1 :]
    rows, cols = iotas()
    mask = rows // LANES == cols // LANES
    for block in range(z2.shape[0] // TILE):
        span = pl.ds(block * TILE, TILE)
        fade = decay[:, span]
        carried = states[-1][:, span].astype(F32)
        for state in states[-2::-1]:
            carried = state[:, span].astype(F32) + fade * carried
        wide = spread_groups(carried, mask).T.astype(BF16)
        total = z2[span, :] + nn(wide, after[span, :])
        grad_value[span, :] = (grad[span, :].astype(F32) * total).astype(BF16)


def shifted(value, axis, steps):
    count = lax.axis_size(axis)
    first, last = max(0, -steps), min(count, count - steps)
    return lax.ppermute(value, axis, [(source, source + steps) for source in range(first, last)])


def exchanged(half, axes, beside):
    partners = []
    for axis in axes:
        count, bit = lax.axis_size(axis), 1
        assert count & (count - 1) == 0
        while bit < count:
            partners.append((axis, [(source, source ^ bit) for source in range(count)]))
            bit *= 2
    made = []
    for at, (axis, pairs) in enumerate(partners):
        other = lax.ppermute(half, axis, pairs)
        if at < len(partners) - 1:
            half = (half.astype(F32) + other.astype(F32)).astype(BF16)
            if at < len(beside):
                half, arrays = lax.optimization_barrier((half, beside[at]))
                made.append(arrays)
    return half, other, made


def per_device(
    mr_query, mr_key, mr_value, li_key, li_value, grad_out, mr_filter, li_residue, li_rate
):
    query, key, value, key_two, value_two, grad = (
        array[0] for array in (mr_query, mr_key, mr_value, li_key, li_value, grad_out)
    )
    groups, filt_len = mr_filter.shape
    channels, seq_local = query.shape
    assert filt_len == TILE and seq_local == TILE and groups <= TILE
    assert channels == groups * LANES and li_rate.shape[1] == LANES
    count = lax.axis_size("seq")
    rows = channels // STEPS
    few = groups // STEPS
    spare = ((0, 0), (0, TILE - groups))
    rate = jnp.pad(li_rate.T, spare)
    residue = jnp.pad(li_residue.T, spare)

    wide = pl.BlockSpec((rows, TILE), lambda i: (i, 0))
    table = pl.BlockSpec((few, TILE), lambda i: (i, 0))
    narrow = pl.BlockSpec((LANES, rows), lambda i: (0, i))
    modes = pl.BlockSpec((LANES, TILE), lambda i: (0, 0))
    wide_half = jax.ShapeDtypeStruct((channels, TILE), BF16)
    wide_full = jax.ShapeDtypeStruct((channels, TILE), F32)
    narrow_half = jax.ShapeDtypeStruct((LANES, channels), BF16)
    narrow_full = jax.ShapeDtypeStruct((LANES, channels), F32)

    def call(kernel, name, in_specs, out_specs, out_shape, scratch=(), limit=VMEM_LIMIT, grid=STEPS):
        return pl.pallas_call(
            kernel,
            grid=(grid,),
            in_specs=in_specs,
            out_specs=out_specs,
            out_shape=out_shape,
            scratch_shapes=scratch,
            name=name,
            cost_estimate=pl.CostEstimate(flops=1, bytes_accessed=1, transcendentals=0),
            compiler_params=pltpu.CompilerParams(vmem_limit_bytes=limit),
        )

    product, back = call(
        first_kernel, "first",
        [wide] * 4 + [modes], [wide, narrow], [wide_half, narrow_half], limit=60 * 1024 * 1024,
    )(query, key, grad, value_two, rate)
    product_before = shifted(product, "seq", 1)
    later_backs = [shifted(back, "seq", -gap) for gap in range(1, count)]

    du2_local, to_next, after, to_end, power, taps, decay = call(
        local_kernel, "local",
        [wide, wide, modes, modes],
        [wide] * 5 + [table, narrow],
        [wide_full] + [wide_half] * 4 + [jax.ShapeDtypeStruct((groups, TILE), F32), narrow_full],
    )(grad, value_two, rate, residue)

    dz1, du2, after_shard = call(
        functools.partial(middle_kernel, count), "middle",
        [narrow] * (count - 1) + [wide, wide, narrow, wide, wide],
        [wide, wide, narrow], [wide_half, wide_full, narrow_full],
    )(*later_backs, du2_local, to_next, decay, key_two, value)
    dz1_later = shifted(dz1, "seq", -1)

    grad_mr_value, grad_li_key, u2, state = call(
        forward_kernel, "forward",
        [wide, wide, table, wide, wide, wide, wide],
        [wide, wide, wide, narrow], [wide_half] * 3 + [narrow_half],
    )(product_before, product, mr_filter, value, key_two, to_end, du2)
    earlier_states = [shifted(state, "seq", gap) for gap in range(1, count)]

    chunks = groups // LANES + 1
    whole = pl.BlockSpec((chunks, LANES, TILE), lambda i: (0, 0, 0))
    (packed,) = call(
        sums_kernel, "sums",
        [wide] * 7 + [narrow, narrow, modes],
        [whole], [jax.ShapeDtypeStruct((chunks, LANES, TILE), BF16)],
        [pltpu.VMEM((groups, TILE), F32)] + [pltpu.VMEM((LANES, TILE), F32)] * 2,
    )(product_before, product, u2, dz1, grad, value_two, power, state, after_shard, rate)
    packed, dz1_later, *earlier_states = lax.optimization_barrier(
        (packed, dz1_later, *earlier_states)
    )

    (z2,) = call(within_kernel, "within", [wide, table], [wide], [wide_full])(u2, taps)

    products = call(
        product_kernel, "product",
        [wide, wide, table, wide, wide], [wide, wide], [wide_half, wide_half],
    )(dz1, dz1_later, mr_filter, query, key)

    half, other, ((z2,), (grad_query, grad_key)) = exchanged(
        packed, ("dp", "seq"), [[z2], products]
    )

    (grad_li_value,) = call(
        functools.partial(value_kernel, count), "value",
        [narrow] * (count - 1) + [wide, narrow, wide, wide], [wide], [wide_half],
    )(*earlier_states, after, decay, z2, grad)

    all_groups = pl.BlockSpec((groups, TILE), lambda i: (0, 0))
    grad_filter, grad_residue = call(
        last_kernel, "last", [whole, whole], [all_groups, modes],
        [jax.ShapeDtypeStruct((groups, TILE), F32), jax.ShapeDtypeStruct((LANES, TILE), F32)],
        grid=1,
    )(half, other)
    return (
        grad_query[None],
        grad_key[None],
        grad_mr_value[None],
        grad_li_key[None],
        grad_li_value[None],
        grad_filter,
        grad_residue[:, :groups].T,
    )


def solution(mesh):
    streams = (P("dp", "chan", "seq"),)
    tables = (P("chan", None),)
    return jax.shard_map(
        per_device,
        mesh=mesh,
        in_specs=streams * 6 + tables * 3,
        out_specs=streams * 5 + tables * 2,
        check_vma=False,
    )
```

```python
import functools

import jax
import jax.numpy as jnp
from jax import lax
from jax.experimental import pallas as pl
from jax.experimental.pallas import tpu as pltpu
from jax.sharding import PartitionSpec as P

F32 = jnp.float32
BF16 = jnp.bfloat16
TILE = 128
LANES = 16
PACK = TILE // LANES
CHUNK = 32
STEPS = 4
VMEM_LIMIT = 24 * 1024 * 1024


def nn(lhs, rhs):
    return lax.dot_general(lhs, rhs, (((1,), (0,)), ((), ())), preferred_element_type=F32)


def nt(lhs, rhs):
    return lax.dot_general(lhs, rhs, (((1,), (1,)), ((), ())), preferred_element_type=F32)


def iotas():
    rows = lax.broadcasted_iota(jnp.int32, (TILE, TILE), 0)
    cols = lax.broadcasted_iota(jnp.int32, (TILE, TILE), 1)
    return rows, cols


def ones_where(mask):
    return jnp.where(mask, 1.0, 0.0).astype(BF16)


def column(turned, mask):
    wide = jnp.concatenate([turned] * PACK, axis=0)
    return jnp.sum(jnp.where(mask, wide, 0.0), axis=1, keepdims=True)


def squeeze_groups(wide, mask):
    kept = jnp.where(mask, wide, 0.0)
    total = kept[:LANES]
    for g in range(1, PACK):
        total = total + kept[g * LANES : (g + 1) * LANES]
    return total


def spread_groups(narrow, mask):
    return jnp.where(mask, jnp.concatenate([narrow] * PACK, axis=0), 0.0)


def circulant(row):
    base = jnp.broadcast_to(row, (LANES, TILE))
    base = pltpu.roll(base, 0, 1, stride=1, stride_axis=0).astype(BF16)
    return jnp.concatenate(
        [base] + [pltpu.roll(base, LANES * j, 1) for j in range(1, PACK)], axis=0
    )


def reversal():
    rows, cols = iotas()
    return ones_where((rows + cols) % TILE == 0)


def one_minus_exp(value):
    series = jnp.full_like(value, 1.0)
    for order in (7, 6, 5, 4, 3, 2):
        series = 1.0 - value * series / order
    return jnp.where(value < 0.125, value * series, 1.0 - jnp.exp(-value))


def chunk_mask(shape, bit):
    return (lax.broadcasted_iota(jnp.int32, shape, 1) // CHUNK) & bit == 0


def pair_chunks(turned):
    parts = [turned[CHUNK * j : CHUNK * (j + 1), :] for j in range(TILE // CHUNK)]
    for bit in (1, 2):
        keep = chunk_mask((CHUNK, TILE), bit)
        for j in range(len(parts)):
            if j & bit == 0:
                low, high = parts[j], parts[j + bit]
                parts[j] = jnp.where(keep, low, pltpu.roll(high, CHUNK * bit, 1))
                parts[j + bit] = jnp.where(keep, pltpu.roll(low, TILE - CHUNK * bit, 1), high)
    return parts


def windows(before, now):
    lanes = lax.broadcasted_iota(jnp.int32, now.shape, 1)
    none = jnp.zeros_like(now)
    first, second = [none if before is None else before], [now]
    for j in range(1, TILE // CHUNK):
        left = TILE - CHUNK * j
        moved = pltpu.roll(now, left, 1)
        older = none if before is None else pltpu.roll(before, left, 1)
        first.append(jnp.where(lanes < left, older, moved))
        second.append(moved)
    return jnp.concatenate(
        [jnp.concatenate(first, axis=0), jnp.concatenate(second, axis=0)], axis=1
    )


def lag_rows(chunks, shifted_rows, own_rows):
    left = jnp.concatenate([chunks * own for own in own_rows], axis=0)
    wide = nn(left, shifted_rows)
    rows = lax.broadcasted_iota(jnp.int32, (2 * CHUNK, TILE), 0) % CHUNK
    lanes = lax.broadcasted_iota(jnp.int32, (2 * CHUNK, TILE), 1)
    sums = jnp.where(lanes + rows < CHUNK, wide[:, TILE:], wide[:, :TILE])
    sums = [
        pltpu.roll(sums[CHUNK * i : CHUNK * (i + 1)], 0, 1, stride=1, stride_axis=0)
        for i in range(2)
    ]
    return jnp.concatenate([jnp.sum(part, axis=0, keepdims=True) for part in sums], axis=0)


def crossed(left, weights):
    wide = nn(left, weights)
    return wide[:LANES, :TILE], wide[LANES:, TILE:]


def now_and_before(now, before, rows, half):
    pieces = []
    for g in range(PACK):
        part = slice(g * LANES, (g + 1) * LANES)
        circ = circulant(rows[g : g + 1, :])
        w_now = circ * half
        weights = jnp.concatenate([w_now, circ - w_now], axis=1)
        pair = crossed(jnp.concatenate([now[part, :], before[part, :]], axis=0), weights)
        pieces.append(pair[0] + pair[1])
    return jnp.concatenate(pieces, axis=0)


def within_shard(array, rows, half):
    pieces = []
    for g in range(0, PACK, 2):
        weights = [circulant(rows[h : h + 1, :]) * half for h in (g, g + 1)]
        part = slice(g * LANES, (g + 2) * LANES)
        pieces += crossed(array[part, :], jnp.concatenate(weights, axis=1))
    return jnp.concatenate(pieces, axis=0)


def block_groups(at, blocks, block):
    rows, cols = iotas()
    return cols == rows // LANES + (at * blocks + block) * PACK


def first_kernel(query, key, grad, value, rate, product, states, held, arrived):
    rows, cols = iotas()
    offsets = cols.astype(F32)
    mask = rows // LANES == cols // LANES
    size = held.shape[1] // STEPS
    blocks = size // TILE
    streams = (grad, value, query, key)

    def fetch(array, step):
        span = pl.ds(step * size, size)
        return pltpu.make_async_copy(
            streams[array].at[span, :], held.at[array, span, :], arrived.at[array, step]
        )

    for step in range(STEPS):
        for array in range(2):
            fetch(array, step).start()
    for step in range(STEPS):
        for array in range(2, 4):
            fetch(array, step).start()
    for step in range(STEPS):
        for array in range(2):
            fetch(array, step).wait()
        for block in range(step * blocks, (step + 1) * blocks):
            span = pl.ds(block * TILE, TILE)
            rates = column(rate[...], block_groups(0, 0, block))
            powers = jnp.exp(-rates * offsets).astype(BF16)
            dz2 = held[0, span, :] * held[1, span, :]
            state = squeeze_groups(nt(powers, dz2), mask).astype(BF16)
            for place in range(states.shape[0]):
                states[place, :, span] = state
    for step in range(STEPS):
        for array in range(2, 4):
            fetch(array, step).wait()
        span = pl.ds(step * size, size)
        product[span, :] = held[2, span, :] * held[3, span, :]


def local_kernel(grad, value, rate, residue, du2, to_next, after, to_end, power, taps, decay):
    rows, cols = iotas()
    offsets = cols.astype(F32)
    mask = rows // LANES == cols // LANES
    lower_half = ones_where(rows >= cols)
    lags = ((CHUNK - 1 - cols) % TILE).astype(F32)
    at = pl.program_id(0)
    blocks = grad.shape[0] // TILE
    filters = []
    for block in range(blocks):
        span = pl.ds(block * TILE, TILE)
        own = block_groups(at, blocks, block)
        rates = column(rate[...], own)
        gains = jnp.sqrt(one_minus_exp(2.0 * rates))
        coeffs = column(residue[...], own) * gains
        powers = jnp.exp(-rates * offsets)
        ends = jnp.exp(-rates * (TILE - 1 - offsets))
        stepped = coeffs * jnp.exp(-rates)
        power[span, :] = jnp.exp(-rates * lags).astype(BF16)
        to_end[span, :] = ends.astype(BF16)
        after[span, :] = (powers * stepped).astype(BF16)
        to_next[span, :] = (ends * stepped).astype(BF16)
        fades = jnp.broadcast_to(jnp.exp(-rates * TILE), (TILE, TILE))
        decay[:, span] = squeeze_groups(fades, mask)
        filters.append(jnp.sum((powers * coeffs).reshape(PACK, LANES, TILE), axis=1))
    filters = jnp.concatenate(filters, axis=0)
    taps[...] = filters
    turned = nn(filters.astype(BF16), reversal())
    for block in range(blocks):
        span = pl.ds(block * TILE, TILE)
        dz2 = grad[span, :] * value[span, :]
        du2[span, :] = within_shard(dz2, turned[block * PACK : (block + 1) * PACK], lower_half)


def middle_kernel(states, local, to_next, decay, li_key, value, dz1, du2, after_shard):
    rows, cols = iotas()
    mask = rows // LANES == cols // LANES
    place = lax.axis_index("seq")
    for block in range(local.shape[0] // TILE):
        span = pl.ds(block * TILE, TILE)
        fade = decay[:, span]
        carried = jnp.zeros((LANES, TILE), F32)
        for source in range(states.shape[0] - 1, 0, -1):
            longer = states[source, :, span].astype(F32) + fade * carried
            carried = jnp.where(place < source, longer, carried)
        after_shard[:, span] = carried
        wide = spread_groups(carried, mask).T.astype(BF16)
        total = local[span, :] + nn(wide, to_next[span, :])
        du2[span, :] = total
        dy1 = total * li_key[span, :].astype(F32)
        dz1[span, :] = (dy1 * value[span, :].astype(F32)).astype(BF16)


def forward_kernel(
    before, now, filters, value, li_key, to_end, du2, grad_value, grad_key, u2, states
):
    rows, cols = iotas()
    mask = rows // LANES == cols // LANES
    upper_half = ones_where(cols >= rows)
    for block in range(now.shape[0] // TILE):
        span = pl.ds(block * TILE, TILE)
        filt = filters[pl.ds(block * PACK, PACK), :].astype(F32)
        z1 = now_and_before(now[span, :], before[span, :], filt, upper_half)
        y1 = (value[span, :].astype(F32) * z1).astype(BF16).astype(F32)
        key_two = li_key[span, :].astype(F32)
        u2_half = (y1 * key_two).astype(BF16)
        u2[span, :] = u2_half
        state = squeeze_groups(nt(to_end[span, :], u2_half), mask).astype(BF16)
        for place in range(states.shape[0]):
            states[place, :, span] = state
        du2_here = du2[span, :]
        grad_key[span, :] = (du2_here * y1).astype(BF16)
        grad_value[span, :] = (du2_here * key_two * z1).astype(BF16)


def sums_kernel(
    before, now, u2, dz1, grad, li_value, power, states, after_shard, rate,
    packed, filter_sums, within_sums, across_sums,
):
    rows, cols = iotas()
    turn = ones_where(cols == rows - rows % CHUNK + (CHUNK - 1 - rows % CHUNK))
    lanes = lax.broadcasted_iota(jnp.int32, (CHUNK, TILE), 1)
    own_rows = [ones_where((lanes // LANES) % 2 == i) for i in range(2)]
    at = pl.program_id(0)
    blocks = now.shape[0] // TILE

    @pl.when(at == 0)
    def _():
        within_sums[...] = jnp.zeros_like(within_sums)
        across_sums[...] = jnp.zeros_like(across_sums)

    for block in range(blocks):
        span = pl.ds(block * TILE, TILE)
        dz2 = grad[span, :] * li_value[span, :]
        turned = nt(turn, jnp.concatenate([dz1[span, :], dz2], axis=0)).astype(BF16)
        lag_chunks = pair_chunks(turned[:, :TILE])
        energy_chunks = pair_chunks(turned[:, TILE:])
        lags, energies = [], []
        for p in range(TILE // CHUNK):
            pair = pl.ds(block * TILE + p * CHUNK, CHUNK)
            lags.append(lag_rows(lag_chunks[p], windows(before[pair, :], now[pair, :]), own_rows))
            energies.append(lag_rows(energy_chunks[p], windows(None, u2[pair, :]), own_rows))
        few = pl.ds(pl.multiple_of((at * blocks + block) * PACK, PACK), PACK)
        filter_sums[few, :] = jnp.concatenate(lags, axis=0)
        energies = jnp.concatenate(energies, axis=0).astype(BF16)
        energies = jnp.concatenate([energies] * LANES, axis=0)
        own = block_groups(at, blocks, block)
        within_sums[...] += squeeze_groups(nt(power[span, :], energies), own)
        across = states[0, :, span].astype(F32) * after_shard[:, span]
        across_sums[...] += nn(across.astype(BF16), ones_where(own))

    @pl.when(at == STEPS - 1)
    def _():
        place = ones_where((rows + cols) % TILE == CHUNK - 1)
        sums = nn(filter_sums[...].astype(BF16), place).astype(BF16)
        for chunk in range(filter_sums.shape[0] // LANES):
            packed[chunk] = sums[chunk * LANES : (chunk + 1) * LANES]
        rates = rate[...]
        gains = jnp.sqrt(one_minus_exp(2.0 * rates))
        total = gains * (within_sums[...] + jnp.exp(-rates) * across_sums[...])
        packed[filter_sums.shape[0] // LANES] = total.astype(BF16)


def within_kernel(u2, taps, z2):
    rows, cols = iotas()
    upper_half = ones_where(cols >= rows)
    for block in range(u2.shape[0] // TILE):
        span = pl.ds(block * TILE, TILE)
        z2[span, :] = within_shard(u2[span, :], taps[pl.ds(block * PACK, PACK), :], upper_half)


def last_kernel(half, other, grad_filter, grad_residue):
    chunks = half.shape[0] - 1
    for chunk in range(chunks):
        grad_filter[pl.ds(chunk * LANES, LANES), :] = half[chunk].astype(F32) + other[chunk].astype(F32)
    grad_residue[...] = half[chunks].astype(F32) + other[chunks].astype(F32)


def product_kernel(dz1, later, filters, query, key, *refs):
    grad_query, grad_key = refs[-2:]
    rows, cols = iotas()
    lower_half = ones_where(rows >= cols)
    turned = nn(filters[...], reversal())
    for block in range(dz1.shape[0] // TILE):
        span = pl.ds(block * TILE, TILE)
        filt = turned[block * PACK : (block + 1) * PACK]
        du1 = now_and_before(dz1[span, :], later[span, :], filt, lower_half)
        grad_query[span, :] = (du1 * key[span, :].astype(F32)).astype(BF16)
        grad_key[span, :] = (du1 * query[span, :].astype(F32)).astype(BF16)


def value_kernel(states, after, decay, z2, grad, grad_value):
    rows, cols = iotas()
    mask = rows // LANES == cols // LANES
    place = lax.axis_index("seq")
    for block in range(z2.shape[0] // TILE):
        span = pl.ds(block * TILE, TILE)
        fade = decay[:, span]
        carried = jnp.zeros((LANES, TILE), F32)
        for source in range(states.shape[0] - 1):
            longer = states[source, :, span].astype(F32) + fade * carried
            carried = jnp.where(place > source, longer, carried)
        wide = spread_groups(carried, mask).T.astype(BF16)
        total = z2[span, :] + nn(wide, after[span, :])
        grad_value[span, :] = (grad[span, :].astype(F32) * total).astype(BF16)


def shifted(value, axis, steps):
    count = lax.axis_size(axis)
    first, last = max(0, -steps), min(count, count - steps)
    return lax.ppermute(value, axis, [(source, source + steps) for source in range(first, last)])


def to_all(states):
    return lax.all_to_all(states, "seq", 0, 0, tiled=True)


def exchanged(half, axes, makers):
    partners = []
    for axis in axes:
        count, bit = lax.axis_size(axis), 1
        assert count & (count - 1) == 0
        while bit < count:
            partners.append((axis, [(source, source ^ bit) for source in range(count)]))
            bit *= 2
    made = []
    for at, (axis, pairs) in enumerate(partners):
        other = lax.ppermute(half, axis, pairs)
        if at < len(makers):
            made.append(makers[at](*made[-1:]))
        if at < len(partners) - 1:
            half = (half.astype(F32) + other.astype(F32)).astype(BF16)
            if at < len(makers):
                half, made[-1] = lax.optimization_barrier((half, made[-1]))
    return half, other, made


def per_device(
    mr_query, mr_key, mr_value, li_key, li_value, grad_out, mr_filter, li_residue, li_rate
):
    query, key, value, key_two, value_two, grad = (
        array[0] for array in (mr_query, mr_key, mr_value, li_key, li_value, grad_out)
    )
    groups, filt_len = mr_filter.shape
    channels, seq_local = query.shape
    assert filt_len == TILE and seq_local == TILE and groups <= TILE
    assert channels == groups * LANES and li_rate.shape[1] == LANES
    count = lax.axis_size("seq")
    rows = channels // STEPS
    few = groups // STEPS
    spare = ((0, 0), (0, TILE - groups))
    rate = jnp.pad(li_rate.T, spare)
    residue = jnp.pad(li_residue.T, spare)

    wide = pl.BlockSpec((rows, TILE), lambda i: (i, 0))
    table = pl.BlockSpec((few, TILE), lambda i: (i, 0))
    narrow = pl.BlockSpec((LANES, rows), lambda i: (0, i))
    modes = pl.BlockSpec((LANES, TILE), lambda i: (0, 0))
    wide_half = jax.ShapeDtypeStruct((channels, TILE), BF16)
    wide_full = jax.ShapeDtypeStruct((channels, TILE), F32)
    narrow_full = jax.ShapeDtypeStruct((LANES, channels), F32)

    copies = pl.BlockSpec((count, LANES, rows), lambda i: (0, 0, i))
    all_copies = jax.ShapeDtypeStruct((count, LANES, channels), BF16)

    def call(kernel, name, in_specs, out_specs, out_shape, scratch=(), grid=STEPS, work=0, **more):
        return pl.pallas_call(
            kernel,
            grid=(grid,),
            in_specs=in_specs,
            out_specs=out_specs,
            out_shape=out_shape,
            scratch_shapes=scratch,
            name=name,
            cost_estimate=pl.CostEstimate(
                flops=work * 2 * channels * TILE * TILE, bytes_accessed=1, transcendentals=0
            ),
            compiler_params=pltpu.CompilerParams(vmem_limit_bytes=more.pop("limit", VMEM_LIMIT)),
            **more,
        )

    def whole(leaf):
        return pl.BlockSpec(leaf.shape, lambda i: (0,) * len(leaf.shape))

    product, backs = call(
        first_kernel, "first",
        [pl.BlockSpec(memory_space=pltpu.HBM)] * 4 + [modes],
        [whole(wide_half), whole(all_copies)], [wide_half, all_copies],
        [pltpu.VMEM((4, channels, TILE), BF16), pltpu.SemaphoreType.DMA((4, STEPS))],
        grid=1, limit=60 * 1024 * 1024,
    )(query, key, grad, value_two, rate)
    product_before = shifted(product, "seq", 1)
    all_backs = to_all(backs)

    du2_local, to_next, after, to_end, power, taps, decay = call(
        local_kernel, "local",
        [wide, wide, modes, modes],
        [wide] * 5 + [table, narrow],
        [wide_full] + [wide_half] * 4 + [jax.ShapeDtypeStruct((groups, TILE), F32), narrow_full],
        work=20,
    )(grad, value_two, rate, residue)

    dz1, du2, after_shard = call(
        middle_kernel, "middle",
        [copies, wide, wide, narrow, wide, wide],
        [wide, wide, narrow], [wide_half, wide_full, narrow_full],
    )(all_backs, du2_local, to_next, decay, key_two, value)

    grad_mr_value, grad_li_key, u2, states = call(
        forward_kernel, "forward",
        [wide, wide, table, wide, wide, wide, wide],
        [wide, wide, wide, copies], [wide_half] * 3 + [all_copies],
    )(product_before, product, mr_filter, value, key_two, to_end, du2)
    all_states = to_all(states)

    (z2,) = call(within_kernel, "within", [wide, table], [wide], [wide_full])(u2, taps)

    dz1_sent, u2_kept, z2, all_states = lax.optimization_barrier((dz1, u2, z2, all_states))
    dz1_later = shifted(dz1_sent, "seq", -1)

    sums_shape = jax.ShapeDtypeStruct((groups // LANES + 1, LANES, TILE), BF16)
    (packed,) = call(
        sums_kernel, "sums",
        [wide] * 7 + [copies, narrow, modes],
        [whole(sums_shape)], [sums_shape],
        [pltpu.VMEM((groups, TILE), F32)] + [pltpu.VMEM((LANES, TILE), F32)] * 2,
    )(product_before, product, u2_kept, dz1, grad, value_two, power, states, after_shard, rate)
    all_states, dz1_later = lax.optimization_barrier((all_states, dz1_later))

    def make_value():
        return call(
            value_kernel, "value", [copies, wide, narrow, wide, wide], [wide], [wide_half]
        )(all_states, after, decay, z2, grad)

    def make_products(part, *halves):
        def blocks(spec):
            return pl.BlockSpec(spec.block_shape, lambda i: (i + part * (STEPS // 2), 0))

        kept = [pl.BlockSpec(memory_space=pl.ANY)] * len(halves)
        return call(
            product_kernel, "product",
            [blocks(spec) for spec in (wide, wide, table, wide, wide)] + kept,
            [blocks(wide)] * 2, [wide_half, wide_half], grid=STEPS // 2,
            input_output_aliases={5 + at: at for at in range(len(halves))},
        )(dz1, dz1_later, mr_filter, query, key, *halves)

    half, other, ((grad_li_value,), _, (grad_query, grad_key)) = exchanged(
        packed, ("dp", "seq"),
        [lambda: make_value(), lambda _: make_products(0), lambda halves: make_products(1, *halves)],
    )

    filter_shape = jax.ShapeDtypeStruct((groups, TILE), F32)
    residue_shape = jax.ShapeDtypeStruct((LANES, TILE), F32)
    grad_filter, grad_residue = call(
        last_kernel, "last", [whole(sums_shape)] * 2,
        [whole(filter_shape), whole(residue_shape)], [filter_shape, residue_shape], grid=1,
    )(half, other)
    return (
        grad_query[None],
        grad_key[None],
        grad_mr_value[None],
        grad_li_key[None],
        grad_li_value[None],
        grad_filter,
        grad_residue[:, :groups].T,
    )


def solution(mesh):
    streams = (P("dp", "chan", "seq"),)
    tables = (P("chan", None),)
    return jax.shard_map(
        per_device,
        mesh=mesh,
        in_specs=streams * 6 + tables * 3,
        out_specs=streams * 5 + tables * 2,
        check_vma=False,
    )
```

```python
import functools

import jax
import jax.numpy as jnp
from jax import lax
from jax.experimental import pallas as pl
from jax.experimental.pallas import tpu as pltpu
from jax.sharding import PartitionSpec as P

F32 = jnp.float32
BF16 = jnp.bfloat16
TILE = 128
LANES = 16
PACK = TILE // LANES
CHUNK = 32
STEPS = 4
VMEM_LIMIT = 24 * 1024 * 1024


def nn(lhs, rhs):
    return lax.dot_general(lhs, rhs, (((1,), (0,)), ((), ())), preferred_element_type=F32)


def nt(lhs, rhs):
    return lax.dot_general(lhs, rhs, (((1,), (1,)), ((), ())), preferred_element_type=F32)


def iotas():
    rows = lax.broadcasted_iota(jnp.int32, (TILE, TILE), 0)
    cols = lax.broadcasted_iota(jnp.int32, (TILE, TILE), 1)
    return rows, cols


def ones_where(mask):
    return jnp.where(mask, 1.0, 0.0).astype(BF16)


def column(turned, mask):
    wide = jnp.concatenate([turned] * PACK, axis=0)
    return jnp.sum(jnp.where(mask, wide, 0.0), axis=1, keepdims=True)


def squeeze_groups(wide, mask):
    kept = jnp.where(mask, wide, 0.0)
    total = kept[:LANES]
    for g in range(1, PACK):
        total = total + kept[g * LANES : (g + 1) * LANES]
    return total


def spread_groups(narrow, mask):
    return jnp.where(mask, jnp.concatenate([narrow] * PACK, axis=0), 0.0)


def circulant(row):
    base = jnp.broadcast_to(row, (LANES, TILE))
    base = pltpu.roll(base, 0, 1, stride=1, stride_axis=0).astype(BF16)
    return jnp.concatenate(
        [base] + [pltpu.roll(base, LANES * j, 1) for j in range(1, PACK)], axis=0
    )


def reversal():
    rows, cols = iotas()
    return ones_where((rows + cols) % TILE == 0)


def one_minus_exp(value):
    series = jnp.full_like(value, 1.0)
    for order in (7, 6, 5, 4, 3, 2):
        series = 1.0 - value * series / order
    return jnp.where(value < 0.125, value * series, 1.0 - jnp.exp(-value))


def chunk_mask(shape, bit):
    return (lax.broadcasted_iota(jnp.int32, shape, 1) // CHUNK) & bit == 0


def pair_chunks(turned):
    parts = [turned[CHUNK * j : CHUNK * (j + 1), :] for j in range(TILE // CHUNK)]
    for bit in (1, 2):
        keep = chunk_mask((CHUNK, TILE), bit)
        for j in range(len(parts)):
            if j & bit == 0:
                low, high = parts[j], parts[j + bit]
                parts[j] = jnp.where(keep, low, pltpu.roll(high, CHUNK * bit, 1))
                parts[j + bit] = jnp.where(keep, pltpu.roll(low, TILE - CHUNK * bit, 1), high)
    return parts


def windows(before, now):
    lanes = lax.broadcasted_iota(jnp.int32, now.shape, 1)
    none = jnp.zeros_like(now)
    first, second = [none if before is None else before], [now]
    for j in range(1, TILE // CHUNK):
        left = TILE - CHUNK * j
        moved = pltpu.roll(now, left, 1)
        older = none if before is None else pltpu.roll(before, left, 1)
        first.append(jnp.where(lanes < left, older, moved))
        second.append(moved)
    return jnp.concatenate(
        [jnp.concatenate(first, axis=0), jnp.concatenate(second, axis=0)], axis=1
    )


def beside(first, second):
    return jnp.concatenate([first, second], axis=1)


def above(first, second):
    return jnp.concatenate([first, second], axis=0)


def apart(first, second):
    none = jnp.zeros_like(first)
    return above(beside(first, none), beside(none, second))


def lag_rows(chunks, others, shifted_rows, other_rows, own_rows):
    left = [jnp.concatenate([part * own for own in own_rows], axis=0) for part in (chunks, others)]
    wide = nn(apart(*left), above(shifted_rows, other_rows))
    rows = lax.broadcasted_iota(jnp.int32, wide[:, :TILE].shape, 0) % CHUNK
    lanes = lax.broadcasted_iota(jnp.int32, wide[:, :TILE].shape, 1)
    sums = jnp.where(lanes + rows < CHUNK, wide[:, TILE:], wide[:, :TILE])
    sums = [
        jnp.sum(
            pltpu.roll(sums[CHUNK * i : CHUNK * (i + 1)], 0, 1, stride=1, stride_axis=0),
            axis=0, keepdims=True,
        )
        for i in range(4)
    ]
    return above(*sums[:2]), above(*sums[2:])


def now_and_before(now, before, rows, half):
    both = beside(now, before)
    pieces = []
    for g in range(0, PACK, 2):
        circs = beside(*[circulant(rows[h : h + 1, :]) for h in (g, g + 1)])
        w_now = circs * half
        wide = nn(both[g * LANES : (g + 2) * LANES, :], above(w_now, circs - w_now))
        pieces += [wide[:LANES, :TILE], wide[LANES:, TILE:]]
    return jnp.concatenate(pieces, axis=0)


def within_shard(array, rows, half):
    pieces = []
    for g in range(0, PACK, 4):
        weights = [
            beside(*[circulant(rows[h : h + 1, :]) for h in (k, k + 1)]) * half
            for k in (g, g + 2)
        ]
        parts = [array[k * LANES : (k + 2) * LANES, :] for k in (g, g + 2)]
        wide = nn(apart(*parts), above(*weights))
        for k in range(4):
            column_at = (k % 2) * TILE
            pieces.append(wide[k * LANES : (k + 1) * LANES, column_at : column_at + TILE])
    return jnp.concatenate(pieces, axis=0)


def block_groups(at, blocks, block):
    rows, cols = iotas()
    return cols == rows // LANES + (at * blocks + block) * PACK


def gate_kernel(query, key, product, held, made, arrived, left):
    size = held.shape[1] // STEPS

    def fetch(array, step):
        span = pl.ds(step * size, size)
        return pltpu.make_async_copy(
            (query, key)[array].at[span, :], held.at[array, span, :], arrived.at[array, step]
        )

    def store(step):
        span = pl.ds(step * size, size)
        return pltpu.make_async_copy(made.at[span, :], product.at[span, :], left.at[step])

    for step in range(STEPS):
        for array in range(2):
            fetch(array, step).start()
    for step in range(STEPS):
        for array in range(2):
            fetch(array, step).wait()
        span = pl.ds(step * size, size)
        made[span, :] = held[0, span, :] * held[1, span, :]
        store(step).start()
    for step in range(STEPS):
        store(step).wait()


def state_kernel(grad, value, rate, state, wide_rate):
    rows, cols = iotas()
    offsets = cols.astype(F32)
    mask = rows // LANES == cols // LANES
    at = pl.program_id(0)
    blocks = state.shape[0]
    for block in range(blocks):
        span = pl.ds(block * TILE, TILE)
        rates = column(rate[...], block_groups(at, blocks, block))
        powers = jnp.exp(-rates * offsets).astype(BF16)
        wide_rate[block] = squeeze_groups(jnp.broadcast_to(rates, (TILE, TILE)), mask)
        dz2 = grad[span, :] * value[span, :]
        state[block] = squeeze_groups(nt(powers, dz2), mask).astype(BF16)


def table_kernel(rate, residue, to_next, after, to_end, power, taps, turned):
    rows, cols = iotas()
    offsets = cols.astype(F32)
    lags = ((CHUNK - 1 - cols) % TILE).astype(F32)
    at = pl.program_id(0)
    blocks = power.shape[0] // TILE
    coeffs = residue[...] * jnp.sqrt(one_minus_exp(2.0 * rate[...]))
    filters = []
    for block in range(blocks):
        span = pl.ds(block * TILE, TILE)
        own = block_groups(at, blocks, block)
        rates = column(rate[...], own)
        scale = column(coeffs, own)
        powers = jnp.exp(-rates * offsets)
        scaled = powers * scale
        ends = jnp.exp(-rates * (TILE - 1 - offsets))
        power[span, :] = jnp.exp(-rates * lags).astype(BF16)
        to_end[span, :] = ends.astype(BF16)
        after[span, :] = scaled.astype(BF16)
        to_next[span, :] = (ends * scale).astype(BF16)
        filters.append(jnp.sum(scaled.reshape(PACK, LANES, TILE), axis=1))
    filters = jnp.concatenate(filters, axis=0)
    taps[...] = filters
    turned[...] = nn(filters.astype(BF16), reversal())


def local_kernel(grad, value, turned, du2):
    rows, cols = iotas()
    lower = ones_where(rows >= cols)
    lower_half = beside(lower, lower)
    for block in range(grad.shape[0] // TILE):
        span = pl.ds(block * TILE, TILE)
        dz2 = grad[span, :] * value[span, :]
        du2[span, :] = within_shard(dz2, turned[pl.ds(block * PACK, PACK), :], lower_half)


def middle_kernel(states, local, to_next, li_key, value, dz1, du2):
    rows, cols = iotas()
    mask = rows // LANES == cols // LANES
    for block in range(local.shape[0] // TILE):
        span = pl.ds(block * TILE, TILE)
        wide = spread_groups(states[block], mask).T.astype(BF16)
        total = local[span, :] + nn(wide, to_next[span, :])
        du2[span, :] = total
        dy1 = total * li_key[span, :].astype(F32)
        dz1[span, :] = (dy1 * value[span, :].astype(F32)).astype(BF16)


def forward_kernel(
    before, now, filters, value, li_key, to_end, du2, grad_value, grad_key, u2, state
):
    rows, cols = iotas()
    mask = rows // LANES == cols // LANES
    upper = ones_where(cols >= rows)
    upper_half = beside(upper, upper)
    for block in range(now.shape[0] // TILE):
        span = pl.ds(block * TILE, TILE)
        filt = filters[pl.ds(block * PACK, PACK), :].astype(F32)
        z1 = now_and_before(now[span, :], before[span, :], filt, upper_half)
        y1 = (value[span, :].astype(F32) * z1).astype(BF16).astype(F32)
        key_two = li_key[span, :].astype(F32)
        u2_half = (y1 * key_two).astype(BF16)
        u2[span, :] = u2_half
        state[block] = squeeze_groups(nt(to_end[span, :], u2_half), mask).astype(BF16)
        du2_here = du2[span, :]
        grad_key[span, :] = (du2_here * y1).astype(BF16)
        grad_value[span, :] = (du2_here * key_two * z1).astype(BF16)


def sums_kernel(
    before, now, u2, dz1, grad, li_value, power, state, after_shard, rate,
    packed, filter_sums, within_sums, across_sums,
):
    rows, cols = iotas()
    turn = ones_where(cols == rows - rows % CHUNK + (CHUNK - 1 - rows % CHUNK))
    lanes = lax.broadcasted_iota(jnp.int32, (CHUNK, TILE), 1)
    own_rows = [ones_where((lanes // LANES) % 2 == i) for i in range(2)]
    at = pl.program_id(0)
    blocks = now.shape[0] // TILE

    @pl.when(at == 0)
    def _():
        within_sums[...] = jnp.zeros_like(within_sums)
        across_sums[...] = jnp.zeros_like(across_sums)

    for block in range(blocks):
        span = pl.ds(block * TILE, TILE)
        dz2 = grad[span, :] * li_value[span, :]
        turned = nt(turn, jnp.concatenate([dz1[span, :], dz2], axis=0)).astype(BF16)
        lag_chunks = pair_chunks(turned[:, :TILE])
        energy_chunks = pair_chunks(turned[:, TILE:])
        lags, energies = [], []
        for p in range(TILE // CHUNK):
            pair = pl.ds(block * TILE + p * CHUNK, CHUNK)
            lag, energy = lag_rows(
                lag_chunks[p], energy_chunks[p],
                windows(before[pair, :], now[pair, :]), windows(None, u2[pair, :]), own_rows,
            )
            lags.append(lag)
            energies.append(energy)
        few = pl.ds(pl.multiple_of((at * blocks + block) * PACK, PACK), PACK)
        filter_sums[few, :] = jnp.concatenate(lags, axis=0)
        energies = jnp.concatenate(energies, axis=0).astype(BF16)
        energies = jnp.concatenate([energies] * LANES, axis=0)
        own = block_groups(at, blocks, block)
        within_sums[...] += squeeze_groups(nt(power[span, :], energies), own)
        packed[at * blocks + block] = state[block]
        across = state[block].astype(F32) * after_shard[block]
        across_sums[...] += nn(across.astype(BF16), ones_where(own))

    @pl.when(at == STEPS - 1)
    def _():
        place = ones_where((rows + cols) % TILE == CHUNK - 1)
        sums = nn(filter_sums[...].astype(BF16), place).astype(BF16)
        for chunk in range(filter_sums.shape[0] // LANES):
            packed[STEPS * blocks + chunk] = sums[chunk * LANES : (chunk + 1) * LANES]
        gains = jnp.sqrt(one_minus_exp(2.0 * rate[...]))
        total = gains * (within_sums[...] + across_sums[...])
        packed[STEPS * blocks + filter_sums.shape[0] // LANES] = total.astype(BF16)


def within_kernel(u2, taps, z2):
    rows, cols = iotas()
    upper = ones_where(cols >= rows)
    upper_half = beside(upper, upper)
    for block in range(u2.shape[0] // TILE):
        span = pl.ds(block * TILE, TILE)
        z2[span, :] = within_shard(u2[span, :], taps[pl.ds(block * PACK, PACK), :], upper_half)


def last_kernel(half, other, grad_filter, grad_residue):
    chunks = half.shape[0] - 1
    for chunk in range(chunks):
        grad_filter[pl.ds(chunk * LANES, LANES), :] = half[chunk].astype(F32) + other[chunk].astype(F32)
    grad_residue[...] = half[chunks].astype(F32) + other[chunks].astype(F32)


def product_kernel(dz1, later, filters, query, key, grad_query, grad_key):
    rows, cols = iotas()
    lower = ones_where(rows >= cols)
    lower_half = beside(lower, lower)
    turned = nn(filters[...], reversal())
    for block in range(dz1.shape[0] // TILE):
        span = pl.ds(block * TILE, TILE)
        filt = turned[block * PACK : (block + 1) * PACK]
        du1 = now_and_before(dz1[span, :], later[span, :], filt, lower_half)
        grad_query[span, :] = (du1 * key[span, :].astype(F32)).astype(BF16)
        grad_key[span, :] = (du1 * query[span, :].astype(F32)).astype(BF16)


def value_kernel(states, after, z2, grad, grad_value):
    rows, cols = iotas()
    mask = rows // LANES == cols // LANES
    for block in range(z2.shape[0] // TILE):
        span = pl.ds(block * TILE, TILE)
        wide = spread_groups(states[block], mask).T.astype(BF16)
        total = z2[span, :] + nn(wide, after[span, :])
        grad_value[span, :] = (grad[span, :].astype(F32) * total).astype(BF16)


def shifted(value, axis, steps):
    count = lax.axis_size(axis)
    first, last = max(0, -steps), min(count, count - steps)
    return lax.ppermute(value, axis, [(source, source + steps) for source in range(first, last)])


def swapped(value, axis, bit):
    count = lax.axis_size(axis)
    return lax.ppermute(value, axis, [(source, source ^ bit) for source in range(count)])


def scan_rounds():
    count, bit, bits = lax.axis_size("seq"), 1, []
    assert count & (count - 1) == 0
    while bit < count:
        bits.append(bit)
        bit *= 2
    return bits


def merged(outside, total, other, bit, wide_rate, earlier):
    place = lax.axis_index("seq")
    low = (place & bit) == 0
    at = place & (bit - 1)

    def fade(shards):
        return jnp.exp(-wide_rate * (TILE * shards).astype(F32))

    run = fade(jnp.int32(bit))
    if earlier:
        outside = outside + jnp.where(low, 0.0, fade(at) * other)
        total = jnp.where(low, other + run * total, total + run * other)
    else:
        outside = outside + jnp.where(low, fade(bit - 1 - at) * other, 0.0)
        total = jnp.where(low, total + run * other, other + run * total)
    return outside, total


def per_device(
    mr_query, mr_key, mr_value, li_key, li_value, grad_out, mr_filter, li_residue, li_rate
):
    query, key, value, key_two, value_two, grad = (
        array[0] for array in (mr_query, mr_key, mr_value, li_key, li_value, grad_out)
    )
    groups, filt_len = mr_filter.shape
    channels, seq_local = query.shape
    assert filt_len == TILE and seq_local == TILE and groups <= TILE
    assert channels == groups * LANES and li_rate.shape[1] == LANES
    rows = channels // STEPS
    few = groups // STEPS
    spare = ((0, 0), (0, TILE - groups))
    rate = jnp.pad(li_rate.T, spare)
    residue = jnp.pad(li_residue.T, spare)

    blocks = channels // TILE

    wide = pl.BlockSpec((rows, TILE), lambda i: (i, 0))
    table = pl.BlockSpec((few, TILE), lambda i: (i, 0))
    chunk = pl.BlockSpec((blocks // STEPS, LANES, TILE), lambda i: (i, 0, 0))
    modes = pl.BlockSpec((LANES, TILE), lambda i: (0, 0))
    distant = pl.BlockSpec(memory_space=pltpu.HBM)
    wide_half = jax.ShapeDtypeStruct((channels, TILE), BF16)
    wide_full = jax.ShapeDtypeStruct((channels, TILE), F32)
    table_full = jax.ShapeDtypeStruct((groups, TILE), F32)
    chunk_half = jax.ShapeDtypeStruct((blocks, LANES, TILE), BF16)
    chunk_full = jax.ShapeDtypeStruct((blocks, LANES, TILE), F32)

    def call(kernel, name, in_specs, out_specs, out_shape, scratch=(), grid=STEPS, limit=VMEM_LIMIT):
        return pl.pallas_call(
            kernel,
            grid=(grid,),
            in_specs=in_specs,
            out_specs=out_specs,
            out_shape=out_shape,
            scratch_shapes=scratch,
            name=name,
            cost_estimate=pl.CostEstimate(flops=1, bytes_accessed=1, transcendentals=0),
            compiler_params=pltpu.CompilerParams(vmem_limit_bytes=limit),
        )

    def whole(leaf):
        return pl.BlockSpec(leaf.shape, lambda i: (0,) * len(leaf.shape))

    (product,) = call(
        gate_kernel, "gate", [distant] * 2, [distant], [wide_half],
        [
            pltpu.VMEM((2, channels, TILE), BF16), pltpu.VMEM((channels, TILE), BF16),
            pltpu.SemaphoreType.DMA((2, STEPS)), pltpu.SemaphoreType.DMA((STEPS,)),
        ],
        grid=1, limit=60 * 1024 * 1024,
    )(query, key)
    product_before = shifted(product, "seq", 1)

    grad_kept, _ = lax.optimization_barrier((grad, product))
    back, wide_rate = call(
        state_kernel, "state", [wide, wide, modes], [chunk, chunk], [chunk_half, chunk_full]
    )(grad_kept, value_two, rate)

    def make_tables():
        return call(
            table_kernel, "table", [modes, modes], [wide] * 4 + [table] * 2,
            [wide_half] * 4 + [table_full] * 2,
        )(rate, residue)

    def make_local(tables):
        return call(local_kernel, "local", [wide, wide, table], [wide], [wide_full])(
            grad, value_two, tables[-1]
        )

    outside, total = jnp.zeros(back.shape, F32), back.astype(F32)
    tables, local = None, None
    for bit in scan_rounds():
        other = swapped(total.astype(BF16), "seq", bit).astype(F32)
        outside, total = merged(outside, total, other, bit, wide_rate, False)
        if tables is None:
            tables = make_tables()
            total, tables = lax.optimization_barrier((total, tables))
        elif local is None:
            local = make_local(tables)
    to_next, after, to_end, power, taps, _ = tables
    (du2_local,) = local
    after_shard = outside * jnp.exp(-wide_rate)
    after_shard, product_before = lax.optimization_barrier((after_shard, product_before))

    dz1, du2 = call(
        middle_kernel, "middle", [chunk, wide, wide, wide, wide], [wide, wide],
        [wide_half, wide_full],
    )(after_shard, du2_local, to_next, key_two, value)
    dz1_later = shifted(dz1, "seq", -1)

    grad_mr_value, grad_li_key, u2, state = call(
        forward_kernel, "forward",
        [wide, wide, table, wide, wide, wide, wide],
        [wide, wide, wide, chunk], [wide_half] * 3 + [chunk_half],
    )(product_before, product, mr_filter, value, key_two, to_end, du2)

    filter_chunks = groups // LANES
    packed_shape = jax.ShapeDtypeStruct((blocks + filter_chunks + 1, LANES, TILE), BF16)
    (packed,) = call(
        sums_kernel, "sums",
        [wide] * 7 + [chunk, chunk, modes],
        [whole(packed_shape)], [packed_shape],
        [pltpu.VMEM((groups, TILE), F32)] + [pltpu.VMEM((LANES, TILE), F32)] * 2,
    )(product_before, product, u2, dz1, grad, value_two, power, state, after_shard, rate)

    packed, dz1_later = lax.optimization_barrier((packed, dz1_later))

    def make_within():
        return call(within_kernel, "within", [wide, table], [wide], [wide_full])(u2, taps)

    def make_products():
        return call(
            product_kernel, "product",
            [wide, wide, table, wide, wide], [wide, wide], [wide_half, wide_half],
        )(dz1, dz1_later, mr_filter, query, key)

    outside, total = jnp.zeros(back.shape, F32), packed[:blocks].astype(F32)
    within, products = None, None
    for bit in scan_rounds():
        other = swapped(packed, "seq", bit)
        sums = (packed[blocks:].astype(F32) + other[blocks:].astype(F32)).astype(BF16)
        outside, total = merged(
            outside, total, other[:blocks].astype(F32), bit, wide_rate, True
        )
        if within is None:
            within = make_within()
            total, within = lax.optimization_barrier((total, within))
        elif products is None:
            products = make_products()
            sums, products = lax.optimization_barrier((sums, products))
        packed = jnp.concatenate([total.astype(BF16), sums], axis=0)
    (z2,), (grad_query, grad_key) = within, products
    before_shard = outside * jnp.exp(-wide_rate)

    assert lax.axis_size("dp") == 2
    partner = swapped(sums, "dp", 1)
    (grad_li_value,) = call(
        value_kernel, "value", [chunk, wide, wide, wide], [wide], [wide_half]
    )(before_shard, after, z2, grad)

    residue_full = jax.ShapeDtypeStruct((LANES, TILE), F32)
    grad_filter, grad_residue = call(
        last_kernel, "last", [whole(sums)] * 2,
        [whole(table_full), whole(residue_full)], [table_full, residue_full], grid=1,
    )(sums, partner)
    return (
        grad_query[None],
        grad_key[None],
        grad_mr_value[None],
        grad_li_key[None],
        grad_li_value[None],
        grad_filter,
        grad_residue[:, :groups].T,
    )


def solution(mesh):
    streams = (P("dp", "chan", "seq"),)
    tables = (P("chan", None),)
    return jax.shard_map(
        per_device,
        mesh=mesh,
        in_specs=streams * 6 + tables * 3,
        out_specs=streams * 5 + tables * 2,
        check_vma=False,
    )
```

```python
import functools

import jax
import jax.numpy as jnp
from jax import lax
from jax.experimental import pallas as pl
from jax.experimental.pallas import tpu as pltpu
from jax.sharding import PartitionSpec as P

F32 = jnp.float32
BF16 = jnp.bfloat16
TILE = 128
LANES = 16
PACK = TILE // LANES
CHUNK = 32
STEPS = 4
VMEM_LIMIT = 24 * 1024 * 1024


def nn(lhs, rhs):
    return lax.dot_general(lhs, rhs, (((1,), (0,)), ((), ())), preferred_element_type=F32)


def nt(lhs, rhs):
    return lax.dot_general(lhs, rhs, (((1,), (1,)), ((), ())), preferred_element_type=F32)


def iotas():
    rows = lax.broadcasted_iota(jnp.int32, (TILE, TILE), 0)
    cols = lax.broadcasted_iota(jnp.int32, (TILE, TILE), 1)
    return rows, cols


def ones_where(mask):
    return jnp.where(mask, 1.0, 0.0).astype(BF16)


def column(turned, mask):
    wide = jnp.concatenate([turned] * PACK, axis=0)
    return jnp.sum(jnp.where(mask, wide, 0.0), axis=1, keepdims=True)


def squeeze_groups(wide, mask):
    kept = jnp.where(mask, wide, 0.0)
    total = kept[:LANES]
    for g in range(1, PACK):
        total = total + kept[g * LANES : (g + 1) * LANES]
    return total


def spread_groups(narrow, mask):
    return jnp.where(mask, jnp.concatenate([narrow] * PACK, axis=0), 0.0)


def circulant(row):
    base = jnp.broadcast_to(row, (LANES, TILE))
    base = pltpu.roll(base, 0, 1, stride=1, stride_axis=0).astype(BF16)
    return jnp.concatenate(
        [base] + [pltpu.roll(base, LANES * j, 1) for j in range(1, PACK)], axis=0
    )


def reversal():
    rows, cols = iotas()
    return ones_where((rows + cols) % TILE == 0)


def one_minus_exp(value):
    series = jnp.full_like(value, 1.0)
    for order in (7, 6, 5, 4, 3, 2):
        series = 1.0 - value * series / order
    return jnp.where(value < 0.125, value * series, 1.0 - jnp.exp(-value))


def chunk_mask(shape, bit):
    return (lax.broadcasted_iota(jnp.int32, shape, 1) // CHUNK) & bit == 0


def pair_chunks(turned):
    parts = [turned[CHUNK * j : CHUNK * (j + 1), :] for j in range(TILE // CHUNK)]
    for bit in (1, 2):
        keep = chunk_mask((CHUNK, TILE), bit)
        for j in range(len(parts)):
            if j & bit == 0:
                low, high = parts[j], parts[j + bit]
                parts[j] = jnp.where(keep, low, pltpu.roll(high, CHUNK * bit, 1))
                parts[j + bit] = jnp.where(keep, pltpu.roll(low, TILE - CHUNK * bit, 1), high)
    return parts


def windows(before, now):
    lanes = lax.broadcasted_iota(jnp.int32, now.shape, 1)
    none = jnp.zeros_like(now)
    first, second = [none if before is None else before], [now]
    for j in range(1, TILE // CHUNK):
        left = TILE - CHUNK * j
        moved = pltpu.roll(now, left, 1)
        older = none if before is None else pltpu.roll(before, left, 1)
        first.append(jnp.where(lanes < left, older, moved))
        second.append(moved)
    return jnp.concatenate(
        [jnp.concatenate(first, axis=0), jnp.concatenate(second, axis=0)], axis=1
    )


def beside(first, second):
    return jnp.concatenate([first, second], axis=1)


def above(first, second):
    return jnp.concatenate([first, second], axis=0)


def apart(first, second):
    none = jnp.zeros_like(first)
    return above(beside(first, none), beside(none, second))


def lag_rows(chunks, shifted_rows, own_rows):
    wide = nn(above(*[chunks * own for own in own_rows]), shifted_rows)
    rows = lax.broadcasted_iota(jnp.int32, (2 * CHUNK, TILE), 0) % CHUNK
    lanes = lax.broadcasted_iota(jnp.int32, (2 * CHUNK, TILE), 1)
    sums = jnp.where(lanes + rows < CHUNK, wide[:, TILE:], wide[:, :TILE])
    sums = [
        pltpu.roll(sums[CHUNK * i : CHUNK * (i + 1)], 0, 1, stride=1, stride_axis=0)
        for i in range(2)
    ]
    return above(*[jnp.sum(part, axis=0, keepdims=True) for part in sums])


def now_and_before(now, before, rows, half):
    both = beside(now, before)
    pieces = []
    for g in range(0, PACK, 2):
        circs = beside(*[circulant(rows[h : h + 1, :]) for h in (g, g + 1)])
        w_now = circs * half
        wide = nn(both[g * LANES : (g + 2) * LANES, :], above(w_now, circs - w_now))
        pieces += [wide[:LANES, :TILE], wide[LANES:, TILE:]]
    return jnp.concatenate(pieces, axis=0)


def within_shard(array, rows, half):
    pieces = []
    for g in range(0, PACK, 4):
        weights = [
            beside(*[circulant(rows[h : h + 1, :]) for h in (k, k + 1)]) * half
            for k in (g, g + 2)
        ]
        parts = [array[k * LANES : (k + 2) * LANES, :] for k in (g, g + 2)]
        wide = nn(apart(*parts), above(*weights))
        for k in range(4):
            column_at = (k % 2) * TILE
            pieces.append(wide[k * LANES : (k + 1) * LANES, column_at : column_at + TILE])
    return jnp.concatenate(pieces, axis=0)


def block_groups(at, blocks, block):
    rows, cols = iotas()
    return cols == rows // LANES + (at * blocks + block) * PACK


def gate_kernel(query, key, product, held, made, arrived, left):
    size = held.shape[1] // STEPS

    def fetch(array, step):
        span = pl.ds(step * size, size)
        return pltpu.make_async_copy(
            (query, key)[array].at[span, :], held.at[array, span, :], arrived.at[array, step]
        )

    def store(step):
        span = pl.ds(step * size, size)
        return pltpu.make_async_copy(made.at[span, :], product.at[span, :], left.at[step])

    for step in range(STEPS):
        for array in range(2):
            fetch(array, step).start()
    for step in range(STEPS):
        for array in range(2):
            fetch(array, step).wait()
        span = pl.ds(step * size, size)
        made[span, :] = held[0, span, :] * held[1, span, :]
        store(step).start()
    for step in range(STEPS):
        store(step).wait()


def state_kernel(grad, value, rate, product, state):
    rows, cols = iotas()
    offsets = cols.astype(F32)
    mask = rows // LANES == cols // LANES
    at = pl.program_id(0)
    blocks = state.shape[0]
    for block in range(blocks):
        span = pl.ds(block * TILE, TILE)
        rates = column(rate[...], block_groups(at, blocks, block))
        powers = jnp.exp(-rates * offsets).astype(BF16)
        dz2 = grad[span, :] * value[span, :]
        state[block] = squeeze_groups(nt(powers, dz2), mask).astype(BF16)


def table_kernel(rate, residue, to_next, after, to_end, power, taps, turned, wide_rate):
    rows, cols = iotas()
    mask = rows // LANES == cols // LANES
    offsets = cols.astype(F32)
    lags = ((CHUNK - 1 - cols) % TILE).astype(F32)
    at = pl.program_id(0)
    blocks = power.shape[0] // TILE
    coeffs = residue[...] * jnp.sqrt(one_minus_exp(2.0 * rate[...]))
    filters = []
    for block in range(blocks):
        span = pl.ds(block * TILE, TILE)
        own = block_groups(at, blocks, block)
        rates = column(rate[...], own)
        scale = column(coeffs, own)
        wide_rate[block] = squeeze_groups(jnp.broadcast_to(rates, (TILE, TILE)), mask)
        powers = jnp.exp(-rates * offsets)
        scaled = powers * scale
        ends = jnp.exp(-rates * (TILE - 1 - offsets))
        power[span, :] = jnp.exp(-rates * lags).astype(BF16)
        to_end[span, :] = ends.astype(BF16)
        after[span, :] = scaled.astype(BF16)
        to_next[span, :] = (ends * scale).astype(BF16)
        filters.append(jnp.sum(scaled.reshape(PACK, LANES, TILE), axis=1))
    filters = jnp.concatenate(filters, axis=0)
    taps[...] = filters
    turned[...] = nn(filters.astype(BF16), reversal())


def local_kernel(grad, value, turned, du2):
    rows, cols = iotas()
    lower = ones_where(rows >= cols)
    lower_half = beside(lower, lower)
    for block in range(grad.shape[0] // TILE):
        span = pl.ds(block * TILE, TILE)
        dz2 = grad[span, :] * value[span, :]
        du2[span, :] = within_shard(dz2, turned[pl.ds(block * PACK, PACK), :], lower_half)


def middle_kernel(states, local, to_next, li_key, value, before, dz1, du2):
    rows, cols = iotas()
    mask = rows // LANES == cols // LANES
    for block in range(local.shape[0] // TILE):
        span = pl.ds(block * TILE, TILE)
        wide = spread_groups(states[block], mask).T.astype(BF16)
        total = local[span, :] + nn(wide, to_next[span, :])
        du2[span, :] = total
        dy1 = total * li_key[span, :].astype(F32)
        dz1[span, :] = (dy1 * value[span, :].astype(F32)).astype(BF16)


def forward_kernel(
    before, now, filters, value, li_key, to_end, du2, grad_value, grad_key, u2, state
):
    rows, cols = iotas()
    mask = rows // LANES == cols // LANES
    upper = ones_where(cols >= rows)
    upper_half = beside(upper, upper)
    for block in range(now.shape[0] // TILE):
        span = pl.ds(block * TILE, TILE)
        filt = filters[pl.ds(block * PACK, PACK), :].astype(F32)
        z1 = now_and_before(now[span, :], before[span, :], filt, upper_half)
        y1 = (value[span, :].astype(F32) * z1).astype(BF16).astype(F32)
        key_two = li_key[span, :].astype(F32)
        u2_half = (y1 * key_two).astype(BF16)
        u2[span, :] = u2_half
        state[block] = squeeze_groups(nt(to_end[span, :], u2_half), mask).astype(BF16)
        du2_here = du2[span, :]
        grad_key[span, :] = (du2_here * y1).astype(BF16)
        grad_value[span, :] = (du2_here * key_two * z1).astype(BF16)


def sums_kernel(
    before, now, u2, dz1, grad, li_value, power, state, after_shard, rate,
    packed, filter_sums, within_sums, across_sums,
):
    rows, cols = iotas()
    turn = ones_where(cols == rows - rows % CHUNK + (CHUNK - 1 - rows % CHUNK))
    lanes = lax.broadcasted_iota(jnp.int32, (CHUNK, TILE), 1)
    own_rows = [ones_where((lanes // LANES) % 2 == i) for i in range(2)]
    at = pl.program_id(0)
    blocks = now.shape[0] // TILE

    @pl.when(at == 0)
    def _():
        within_sums[...] = jnp.zeros_like(within_sums)
        across_sums[...] = jnp.zeros_like(across_sums)

    for block in range(blocks):
        span = pl.ds(block * TILE, TILE)
        dz2 = grad[span, :] * li_value[span, :]
        turned = nt(turn, jnp.concatenate([dz1[span, :], dz2], axis=0)).astype(BF16)
        lag_chunks = pair_chunks(turned[:, :TILE])
        energy_chunks = pair_chunks(turned[:, TILE:])
        lags, energies = [], []
        for p in range(TILE // CHUNK):
            pair = pl.ds(block * TILE + p * CHUNK, CHUNK)
            lags.append(lag_rows(lag_chunks[p], windows(before[pair, :], now[pair, :]), own_rows))
            energies.append(lag_rows(energy_chunks[p], windows(None, u2[pair, :]), own_rows))
        few = pl.ds(pl.multiple_of((at * blocks + block) * PACK, PACK), PACK)
        filter_sums[few, :] = jnp.concatenate(lags, axis=0)
        energies = jnp.concatenate(energies, axis=0).astype(BF16)
        energies = jnp.concatenate([energies] * LANES, axis=0)
        own = block_groups(at, blocks, block)
        within_sums[...] += squeeze_groups(nt(power[span, :], energies), own)
        packed[at * blocks + block] = state[block]
        across = state[block].astype(F32) * after_shard[block]
        across_sums[...] += nn(across.astype(BF16), ones_where(own))

    @pl.when(at == STEPS - 1)
    def _():
        place = ones_where((rows + cols) % TILE == CHUNK - 1)
        sums = nn(filter_sums[...].astype(BF16), place).astype(BF16)
        for chunk in range(filter_sums.shape[0] // LANES):
            packed[STEPS * blocks + chunk] = sums[chunk * LANES : (chunk + 1) * LANES]
        gains = jnp.sqrt(one_minus_exp(2.0 * rate[...]))
        total = gains * (within_sums[...] + across_sums[...])
        packed[STEPS * blocks + filter_sums.shape[0] // LANES] = total.astype(BF16)


def within_kernel(u2, taps, wide_rate, later, z2, fade, nothing):
    nothing[...] = jnp.zeros_like(nothing)
    fade[...] = jnp.exp(-TILE * wide_rate[...])
    rows, cols = iotas()
    upper = ones_where(cols >= rows)
    upper_half = beside(upper, upper)
    for block in range(u2.shape[0] // TILE):
        span = pl.ds(block * TILE, TILE)
        z2[span, :] = within_shard(u2[span, :], taps[pl.ds(block * PACK, PACK), :], upper_half)


def last_kernel(half, other, grad_filter, grad_residue):
    chunks = half.shape[0] - 1
    for chunk in range(chunks):
        grad_filter[pl.ds(chunk * LANES, LANES), :] = half[chunk].astype(F32) + other[chunk].astype(F32)
    grad_residue[...] = half[chunks].astype(F32) + other[chunks].astype(F32)


def product_kernel(dz1, later, filters, query, key, grad_query, grad_key, nothing):
    nothing[...] = jnp.zeros_like(nothing)
    rows, cols = iotas()
    lower = ones_where(rows >= cols)
    lower_half = beside(lower, lower)
    turned = nn(filters[...], reversal())
    for block in range(dz1.shape[0] // TILE):
        span = pl.ds(block * TILE, TILE)
        filt = turned[block * PACK : (block + 1) * PACK]
        du1 = now_and_before(dz1[span, :], later[span, :], filt, lower_half)
        grad_query[span, :] = (du1 * key[span, :].astype(F32)).astype(BF16)
        grad_key[span, :] = (du1 * query[span, :].astype(F32)).astype(BF16)


def value_kernel(states, after, z2, grad, grad_value):
    rows, cols = iotas()
    mask = rows // LANES == cols // LANES
    for block in range(z2.shape[0] // TILE):
        span = pl.ds(block * TILE, TILE)
        wide = spread_groups(states[block], mask).T.astype(BF16)
        total = z2[span, :] + nn(wide, after[span, :])
        grad_value[span, :] = (grad[span, :].astype(F32) * total).astype(BF16)


def shifted(value, axis, steps):
    count = lax.axis_size(axis)
    first, last = max(0, -steps), min(count, count - steps)
    return lax.ppermute(value, axis, [(source, source + steps) for source in range(first, last)])


def swapped(value, axis, bit):
    count = lax.axis_size(axis)
    return lax.ppermute(value, axis, [(source, source ^ bit) for source in range(count)])


def scan_bits():
    count, bit, bits = lax.axis_size("seq"), 1, []
    assert count & (count - 1) == 0
    while bit < count:
        bits.append(bit)
        bit *= 2
    return bits


def merged(outside, total, other, bit, fade):
    place = lax.axis_index("seq")
    low = (place & bit) == 0
    reach, run, step = other, fade, 1
    while step < bit:
        reach = jnp.where((place & step) == 0, reach, run * reach)
        run = run * run
        step *= 2
    outside = outside + jnp.where(low, 0.0, reach)
    total = jnp.where(low, other + run * total, total + run * other)
    return outside, total


def per_device(
    mr_query, mr_key, mr_value, li_key, li_value, grad_out, mr_filter, li_residue, li_rate
):
    query, key, value, key_two, value_two, grad = (
        array[0] for array in (mr_query, mr_key, mr_value, li_key, li_value, grad_out)
    )
    groups, filt_len = mr_filter.shape
    channels, seq_local = query.shape
    assert filt_len == TILE and seq_local == TILE and groups <= TILE
    assert channels == groups * LANES and li_rate.shape[1] == LANES
    rows = channels // STEPS
    few = groups // STEPS
    spare = ((0, 0), (0, TILE - groups))
    rate = jnp.pad(li_rate.T, spare)
    residue = jnp.pad(li_residue.T, spare)

    blocks = channels // TILE

    wide = pl.BlockSpec((rows, TILE), lambda i: (i, 0))
    table = pl.BlockSpec((few, TILE), lambda i: (i, 0))
    chunk = pl.BlockSpec((blocks // STEPS, LANES, TILE), lambda i: (i, 0, 0))
    modes = pl.BlockSpec((LANES, TILE), lambda i: (0, 0))
    distant = pl.BlockSpec(memory_space=pltpu.HBM)
    anywhere = pl.BlockSpec(memory_space=pl.ANY)
    wide_half = jax.ShapeDtypeStruct((channels, TILE), BF16)
    wide_full = jax.ShapeDtypeStruct((channels, TILE), F32)
    table_full = jax.ShapeDtypeStruct((groups, TILE), F32)
    chunk_half = jax.ShapeDtypeStruct((blocks, LANES, TILE), BF16)
    chunk_full = jax.ShapeDtypeStruct((blocks, LANES, TILE), F32)

    def call(kernel, name, in_specs, out_specs, out_shape, scratch=(), grid=STEPS, limit=VMEM_LIMIT):
        return pl.pallas_call(
            kernel,
            grid=(grid,),
            in_specs=in_specs,
            out_specs=out_specs,
            out_shape=out_shape,
            scratch_shapes=scratch,
            name=name,
            cost_estimate=pl.CostEstimate(flops=1, bytes_accessed=1, transcendentals=0),
            compiler_params=pltpu.CompilerParams(vmem_limit_bytes=limit),
        )

    def whole(leaf):
        return pl.BlockSpec(leaf.shape, lambda i: (0,) * len(leaf.shape))

    (product,) = call(
        gate_kernel, "gate", [distant] * 2, [distant], [wide_half],
        [
            pltpu.VMEM((2, channels, TILE), BF16), pltpu.VMEM((channels, TILE), BF16),
            pltpu.SemaphoreType.DMA((2, STEPS)), pltpu.SemaphoreType.DMA((STEPS,)),
        ],
        grid=1, limit=60 * 1024 * 1024,
    )(query, key)
    product_before = shifted(product, "seq", 1)

    (back,) = call(
        state_kernel, "state", [wide, wide, modes, anywhere], [chunk], [chunk_half]
    )(grad, value_two, rate, product)

    outside, total = None, back.astype(F32)
    to_next, after, to_end, power, taps, turned, wide_rate = call(
        table_kernel, "table", [modes, modes], [wide] * 4 + [table] * 2 + [chunk],
        [wide_half] * 4 + [table_full] * 2 + [chunk_full],
    )(rate, residue)
    for bit in scan_bits():
        other = shifted(total.astype(BF16), "seq", -bit).astype(F32)
        reach = jnp.exp(-TILE * (bit - 1) * wide_rate) * other if bit > 1 else other
        outside = reach if outside is None else outside + reach
        total = total + jnp.exp(-TILE * bit * wide_rate) * other
    after_shard = outside * jnp.exp(-wide_rate)

    (du2_local,) = call(local_kernel, "local", [wide, wide, table], [wide], [wide_full])(
        grad, value_two, turned
    )

    dz1, du2 = call(
        middle_kernel, "middle", [chunk, wide, wide, wide, wide, anywhere], [wide, wide],
        [wide_half, wide_full],
    )(after_shard, du2_local, to_next, key_two, value, product_before)
    dz1_later = shifted(dz1, "seq", -1)

    grad_mr_value, grad_li_key, u2, state = call(
        forward_kernel, "forward",
        [wide, wide, table, wide, wide, wide, wide],
        [wide, wide, wide, chunk], [wide_half] * 3 + [chunk_half],
    )(product_before, product, mr_filter, value, key_two, to_end, du2)

    filter_chunks = groups // LANES
    packed_shape = jax.ShapeDtypeStruct((blocks + filter_chunks + 1, LANES, TILE), BF16)
    (packed,) = call(
        sums_kernel, "sums",
        [wide] * 7 + [chunk, chunk, modes],
        [whole(packed_shape)], [packed_shape],
        [pltpu.VMEM((groups, TILE), F32)] + [pltpu.VMEM((LANES, TILE), F32)] * 2,
    )(product_before, product, u2, dz1, grad, value_two, power, state, after_shard, rate)

    small = jax.ShapeDtypeStruct((8, TILE), F32)
    z2, fade, *zeros = call(
        within_kernel, "within", [wide, table, chunk, anywhere], [wide, chunk, whole(small)],
        [wide_full, chunk_full, small],
    )(u2, taps, wide_rate, dz1_later)

    grad_query, grad_key, nothing = call(
        product_kernel, "product",
        [wide, wide, table, wide, wide], [wide, wide, whole(small)],
        [wide_half, wide_half, small],
    )(dz1, dz1_later, mr_filter, query, key)

    zeros.append(nothing)
    outside, total = jnp.zeros(back.shape, F32), packed[:blocks].astype(F32)
    for bit in scan_bits():
        other = swapped(packed, "seq", bit)
        sums = packed[blocks:].astype(F32) + other[blocks:].astype(F32)
        if zeros:
            sums = sums + zeros.pop(0)[0, 0]
        outside, total = merged(outside, total, other[:blocks].astype(F32), bit, fade)
        packed = jnp.concatenate([total.astype(BF16), sums.astype(BF16)], axis=0)
    before_shard = outside * jnp.exp(-wide_rate)
    sums = sums.astype(BF16)

    assert lax.axis_size("dp") == 2
    partner = swapped(sums, "dp", 1)
    (grad_li_value,) = call(
        value_kernel, "value", [chunk, wide, wide, wide], [wide], [wide_half]
    )(before_shard, after, z2, grad)

    residue_full = jax.ShapeDtypeStruct((LANES, TILE), F32)
    grad_filter, grad_residue = call(
        last_kernel, "last", [whole(sums)] * 2,
        [whole(table_full), whole(residue_full)], [table_full, residue_full], grid=1,
    )(sums, partner)
    return (
        grad_query[None],
        grad_key[None],
        grad_mr_value[None],
        grad_li_key[None],
        grad_li_value[None],
        grad_filter,
        grad_residue[:, :groups].T,
    )


def solution(mesh):
    streams = (P("dp", "chan", "seq"),)
    tables = (P("chan", None),)
    return jax.shard_map(
        per_device,
        mesh=mesh,
        in_specs=streams * 6 + tables * 3,
        out_specs=streams * 5 + tables * 2,
        check_vma=False,
    )
```

```python
import functools

import jax
import jax.numpy as jnp
from jax import lax
from jax.experimental import pallas as pl
from jax.experimental.pallas import tpu as pltpu
from jax.sharding import PartitionSpec as P

F32 = jnp.float32
BF16 = jnp.bfloat16
TILE = 128
LANES = 16
PACK = TILE // LANES
CHUNK = 32
STEPS = 4
VMEM_LIMIT = 24 * 1024 * 1024


def nn(lhs, rhs):
    return lax.dot_general(lhs, rhs, (((1,), (0,)), ((), ())), preferred_element_type=F32)


def nt(lhs, rhs):
    return lax.dot_general(lhs, rhs, (((1,), (1,)), ((), ())), preferred_element_type=F32)


def iotas():
    rows = lax.broadcasted_iota(jnp.int32, (TILE, TILE), 0)
    cols = lax.broadcasted_iota(jnp.int32, (TILE, TILE), 1)
    return rows, cols


def ones_where(mask):
    return jnp.where(mask, 1.0, 0.0).astype(BF16)


def column(turned, mask):
    wide = jnp.concatenate([turned] * PACK, axis=0)
    return jnp.sum(jnp.where(mask, wide, 0.0), axis=1, keepdims=True)


def squeeze_groups(wide, mask):
    kept = jnp.where(mask, wide, 0.0)
    total = kept[:LANES]
    for g in range(1, PACK):
        total = total + kept[g * LANES : (g + 1) * LANES]
    return total


def spread_groups(narrow, mask):
    return jnp.where(mask, jnp.concatenate([narrow] * PACK, axis=0), 0.0)


def circulant(row):
    base = jnp.broadcast_to(row, (LANES, TILE))
    base = pltpu.roll(base, 0, 1, stride=1, stride_axis=0).astype(BF16)
    return jnp.concatenate(
        [base] + [pltpu.roll(base, LANES * j, 1) for j in range(1, PACK)], axis=0
    )


def reversal():
    rows, cols = iotas()
    return ones_where((rows + cols) % TILE == 0)


def one_minus_exp(value):
    series = jnp.full_like(value, 1.0)
    for order in (7, 6, 5, 4, 3, 2):
        series = 1.0 - value * series / order
    return jnp.where(value < 0.125, value * series, 1.0 - jnp.exp(-value))


def chunk_mask(shape, bit):
    return (lax.broadcasted_iota(jnp.int32, shape, 1) // CHUNK) & bit == 0


def pair_chunks(turned):
    parts = [turned[CHUNK * j : CHUNK * (j + 1), :] for j in range(TILE // CHUNK)]
    for bit in (1, 2):
        keep = chunk_mask((CHUNK, TILE), bit)
        for j in range(len(parts)):
            if j & bit == 0:
                low, high = parts[j], parts[j + bit]
                parts[j] = jnp.where(keep, low, pltpu.roll(high, CHUNK * bit, 1))
                parts[j + bit] = jnp.where(keep, pltpu.roll(low, TILE - CHUNK * bit, 1), high)
    return parts


def windows(before, now):
    lanes = lax.broadcasted_iota(jnp.int32, now.shape, 1)
    none = jnp.zeros_like(now)
    first, second = [none if before is None else before], [now]
    for j in range(1, TILE // CHUNK):
        left = TILE - CHUNK * j
        moved = pltpu.roll(now, left, 1)
        older = none if before is None else pltpu.roll(before, left, 1)
        first.append(jnp.where(lanes < left, older, moved))
        second.append(moved)
    return jnp.concatenate(
        [jnp.concatenate(first, axis=0), jnp.concatenate(second, axis=0)], axis=1
    )


def beside(first, second):
    return jnp.concatenate([first, second], axis=1)


def above(first, second):
    return jnp.concatenate([first, second], axis=0)


def apart(first, second):
    none = jnp.zeros_like(first)
    return above(beside(first, none), beside(none, second))


def lag_rows(chunks, shifted_rows, own_rows):
    wide = nn(above(*[chunks * own for own in own_rows]), shifted_rows)
    rows = lax.broadcasted_iota(jnp.int32, (2 * CHUNK, TILE), 0) % CHUNK
    lanes = lax.broadcasted_iota(jnp.int32, (2 * CHUNK, TILE), 1)
    sums = jnp.where(lanes + rows < CHUNK, wide[:, TILE:], wide[:, :TILE])
    sums = [
        pltpu.roll(sums[CHUNK * i : CHUNK * (i + 1)], 0, 1, stride=1, stride_axis=0)
        for i in range(2)
    ]
    return above(*[jnp.sum(part, axis=0, keepdims=True) for part in sums])


def now_and_before(now, before, rows, half):
    both = beside(now, before)
    pieces = []
    for g in range(0, PACK, 2):
        circs = beside(*[circulant(rows[h : h + 1, :]) for h in (g, g + 1)])
        w_now = circs * half
        wide = nn(both[g * LANES : (g + 2) * LANES, :], above(w_now, circs - w_now))
        pieces += [wide[:LANES, :TILE], wide[LANES:, TILE:]]
    return jnp.concatenate(pieces, axis=0)


def within_shard(array, rows, half):
    pieces = []
    for g in range(0, PACK, 4):
        weights = [
            beside(*[circulant(rows[h : h + 1, :]) for h in (k, k + 1)]) * half
            for k in (g, g + 2)
        ]
        parts = [array[k * LANES : (k + 2) * LANES, :] for k in (g, g + 2)]
        wide = nn(apart(*parts), above(*weights))
        for k in range(4):
            column_at = (k % 2) * TILE
            pieces.append(wide[k * LANES : (k + 1) * LANES, column_at : column_at + TILE])
    return jnp.concatenate(pieces, axis=0)


def block_groups(at, blocks, block):
    rows, cols = iotas()
    return cols == rows // LANES + (at * blocks + block) * PACK


def gate_kernel(query, key, product, held, made, arrived, left):
    size = held.shape[1] // STEPS

    def fetch(array, step):
        span = pl.ds(step * size, size)
        return pltpu.make_async_copy(
            (query, key)[array].at[span, :], held.at[array, span, :], arrived.at[array, step]
        )

    def store(step):
        span = pl.ds(step * size, size)
        return pltpu.make_async_copy(made.at[span, :], product.at[span, :], left.at[step])

    for step in range(STEPS):
        for array in range(2):
            fetch(array, step).start()
    for step in range(STEPS):
        for array in range(2):
            fetch(array, step).wait()
        span = pl.ds(step * size, size)
        made[span, :] = held[0, span, :] * held[1, span, :]
        store(step).start()
    for step in range(STEPS):
        store(step).wait()


def state_kernel(grad, value, rate, product, state):
    rows, cols = iotas()
    offsets = cols.astype(F32)
    mask = rows // LANES == cols // LANES
    at = pl.program_id(0)
    blocks = state.shape[0]
    for block in range(blocks):
        span = pl.ds(block * TILE, TILE)
        rates = column(rate[...], block_groups(at, blocks, block))
        powers = jnp.exp(-rates * offsets).astype(BF16)
        dz2 = grad[span, :] * value[span, :]
        state[block] = squeeze_groups(nt(powers, dz2), mask).astype(BF16)


def table_kernel(rate, residue, to_next, after, to_end, power, taps, turned, wide_rate):
    rows, cols = iotas()
    mask = rows // LANES == cols // LANES
    offsets = cols.astype(F32)
    lags = ((CHUNK - 1 - cols) % TILE).astype(F32)
    at = pl.program_id(0)
    blocks = power.shape[0] // TILE
    coeffs = residue[...] * jnp.sqrt(one_minus_exp(2.0 * rate[...]))
    filters = []
    for block in range(blocks):
        span = pl.ds(block * TILE, TILE)
        own = block_groups(at, blocks, block)
        rates = column(rate[...], own)
        scale = column(coeffs, own)
        wide_rate[block] = squeeze_groups(jnp.broadcast_to(rates, (TILE, TILE)), mask)
        powers = jnp.exp(-rates * offsets)
        scaled = powers * scale
        ends = jnp.exp(-rates * (TILE - 1 - offsets))
        power[span, :] = jnp.exp(-rates * lags).astype(BF16)
        to_end[span, :] = ends.astype(BF16)
        after[span, :] = scaled.astype(BF16)
        to_next[span, :] = (ends * scale).astype(BF16)
        filters.append(jnp.sum(scaled.reshape(PACK, LANES, TILE), axis=1))
    filters = jnp.concatenate(filters, axis=0)
    taps[...] = filters
    turned[...] = nn(filters.astype(BF16), reversal())


def local_kernel(grad, value, turned, du2):
    rows, cols = iotas()
    lower = ones_where(rows >= cols)
    lower_half = beside(lower, lower)
    for block in range(grad.shape[0] // TILE):
        span = pl.ds(block * TILE, TILE)
        dz2 = grad[span, :] * value[span, :]
        du2[span, :] = within_shard(dz2, turned[pl.ds(block * PACK, PACK), :], lower_half)


def middle_kernel(states, local, to_next, li_key, value, before, dz1, du2):
    rows, cols = iotas()
    mask = rows // LANES == cols // LANES
    for block in range(local.shape[0] // TILE):
        span = pl.ds(block * TILE, TILE)
        wide = spread_groups(states[block], mask).T.astype(BF16)
        total = local[span, :] + nn(wide, to_next[span, :])
        du2[span, :] = total
        dy1 = total * li_key[span, :].astype(F32)
        dz1[span, :] = (dy1 * value[span, :].astype(F32)).astype(BF16)


def forward_kernel(
    before, now, filters, value, li_key, to_end, du2, grad_value, grad_key, u2, state
):
    rows, cols = iotas()
    mask = rows // LANES == cols // LANES
    upper = ones_where(cols >= rows)
    upper_half = beside(upper, upper)
    for block in range(now.shape[0] // TILE):
        span = pl.ds(block * TILE, TILE)
        filt = filters[pl.ds(block * PACK, PACK), :].astype(F32)
        z1 = now_and_before(now[span, :], before[span, :], filt, upper_half)
        y1 = (value[span, :].astype(F32) * z1).astype(BF16).astype(F32)
        key_two = li_key[span, :].astype(F32)
        u2_half = (y1 * key_two).astype(BF16)
        u2[span, :] = u2_half
        state[block] = squeeze_groups(nt(to_end[span, :], u2_half), mask).astype(BF16)
        du2_here = du2[span, :]
        grad_key[span, :] = (du2_here * y1).astype(BF16)
        grad_value[span, :] = (du2_here * key_two * z1).astype(BF16)


def sums_kernel(
    before, now, u2, dz1, grad, li_value, power, state, after_shard, rate,
    packed, filter_sums, within_sums, across_sums,
):
    rows, cols = iotas()
    turn = ones_where(cols == rows - rows % CHUNK + (CHUNK - 1 - rows % CHUNK))
    lanes = lax.broadcasted_iota(jnp.int32, (CHUNK, TILE), 1)
    own_rows = [ones_where((lanes // LANES) % 2 == i) for i in range(2)]
    at = pl.program_id(0)
    blocks = now.shape[0] // TILE

    @pl.when(at == 0)
    def _():
        within_sums[...] = jnp.zeros_like(within_sums)
        across_sums[...] = jnp.zeros_like(across_sums)

    for block in range(blocks):
        span = pl.ds(block * TILE, TILE)
        dz2 = grad[span, :] * li_value[span, :]
        turned = nt(turn, jnp.concatenate([dz1[span, :], dz2], axis=0)).astype(BF16)
        lag_chunks = pair_chunks(turned[:, :TILE])
        energy_chunks = pair_chunks(turned[:, TILE:])
        lags, energies = [], []
        for p in range(TILE // CHUNK):
            pair = pl.ds(block * TILE + p * CHUNK, CHUNK)
            lags.append(lag_rows(lag_chunks[p], windows(before[pair, :], now[pair, :]), own_rows))
            energies.append(lag_rows(energy_chunks[p], windows(None, u2[pair, :]), own_rows))
        few = pl.ds(pl.multiple_of((at * blocks + block) * PACK, PACK), PACK)
        filter_sums[few, :] = jnp.concatenate(lags, axis=0)
        energies = jnp.concatenate(energies, axis=0).astype(BF16)
        energies = jnp.concatenate([energies] * LANES, axis=0)
        own = block_groups(at, blocks, block)
        within_sums[...] += squeeze_groups(nt(power[span, :], energies), own)
        packed[at * blocks + block] = state[block]
        across = state[block].astype(F32) * after_shard[block]
        across_sums[...] += nn(across.astype(BF16), ones_where(own))

    @pl.when(at == STEPS - 1)
    def _():
        place = ones_where((rows + cols) % TILE == CHUNK - 1)
        sums = nn(filter_sums[...].astype(BF16), place).astype(BF16)
        for chunk in range(filter_sums.shape[0] // LANES):
            packed[STEPS * blocks + chunk] = sums[chunk * LANES : (chunk + 1) * LANES]
        gains = jnp.sqrt(one_minus_exp(2.0 * rate[...]))
        total = gains * (within_sums[...] + across_sums[...])
        packed[STEPS * blocks + filter_sums.shape[0] // LANES] = total.astype(BF16)


def within_kernel(bits, u2, taps, wide_rate, later, z2, zeros, *weights):
    zeros[...] = jnp.zeros_like(zeros)
    place = lax.axis_index("seq")
    rates = wide_rate[...]
    weights = list(weights)
    for bit in bits:
        high = (place & bit) != 0
        passed = TILE * (place & (bit - 1)) + 1
        reach = jnp.exp(-rates * passed.astype(F32))
        weights.pop(0)[...] = jnp.where(high, reach, 0.0)
        if bit != bits[-1]:
            run = jnp.exp(-rates * (TILE * bit))
            one = jnp.ones_like(run)
            weights.pop(0)[...] = jnp.where(high, run, one)
            weights.pop(0)[...] = jnp.where(high, one, run)
    rows, cols = iotas()
    upper = ones_where(cols >= rows)
    upper_half = beside(upper, upper)
    for block in range(u2.shape[0] // TILE):
        span = pl.ds(block * TILE, TILE)
        z2[span, :] = within_shard(u2[span, :], taps[pl.ds(block * PACK, PACK), :], upper_half)


def last_kernel(half, other, grad_filter, grad_residue):
    chunks = half.shape[0] - 1
    for chunk in range(chunks):
        grad_filter[pl.ds(chunk * LANES, LANES), :] = half[chunk].astype(F32) + other[chunk].astype(F32)
    grad_residue[...] = half[chunks].astype(F32) + other[chunks].astype(F32)


def product_kernel(dz1, later, filters, query, key, grad_query, grad_key, nothing):
    nothing[...] = jnp.zeros_like(nothing)
    rows, cols = iotas()
    lower = ones_where(rows >= cols)
    lower_half = beside(lower, lower)
    turned = nn(filters[...], reversal())
    for block in range(dz1.shape[0] // TILE):
        span = pl.ds(block * TILE, TILE)
        filt = turned[block * PACK : (block + 1) * PACK]
        du1 = now_and_before(dz1[span, :], later[span, :], filt, lower_half)
        grad_query[span, :] = (du1 * key[span, :].astype(F32)).astype(BF16)
        grad_key[span, :] = (du1 * query[span, :].astype(F32)).astype(BF16)


def value_kernel(states, after, z2, grad, grad_value):
    rows, cols = iotas()
    mask = rows // LANES == cols // LANES
    for block in range(z2.shape[0] // TILE):
        span = pl.ds(block * TILE, TILE)
        wide = spread_groups(states[block], mask).T.astype(BF16)
        total = z2[span, :] + nn(wide, after[span, :])
        grad_value[span, :] = (grad[span, :].astype(F32) * total).astype(BF16)


def shifted(value, axis, steps):
    count = lax.axis_size(axis)
    first, last = max(0, -steps), min(count, count - steps)
    return lax.ppermute(value, axis, [(source, source + steps) for source in range(first, last)])


def swapped(value, axis, bit):
    count = lax.axis_size(axis)
    return lax.ppermute(value, axis, [(source, source ^ bit) for source in range(count)])


def scan_bits():
    count, bit, bits = lax.axis_size("seq"), 1, []
    assert count & (count - 1) == 0
    while bit < count:
        bits.append(bit)
        bit *= 2
    return bits


def per_device(
    mr_query, mr_key, mr_value, li_key, li_value, grad_out, mr_filter, li_residue, li_rate
):
    query, key, value, key_two, value_two, grad = (
        array[0] for array in (mr_query, mr_key, mr_value, li_key, li_value, grad_out)
    )
    groups, filt_len = mr_filter.shape
    channels, seq_local = query.shape
    assert filt_len == TILE and seq_local == TILE and groups <= TILE
    assert channels == groups * LANES and li_rate.shape[1] == LANES
    rows = channels // STEPS
    few = groups // STEPS
    spare = ((0, 0), (0, TILE - groups))
    rate = jnp.pad(li_rate.T, spare)
    residue = jnp.pad(li_residue.T, spare)

    blocks = channels // TILE

    wide = pl.BlockSpec((rows, TILE), lambda i: (i, 0))
    table = pl.BlockSpec((few, TILE), lambda i: (i, 0))
    chunk = pl.BlockSpec((blocks // STEPS, LANES, TILE), lambda i: (i, 0, 0))
    modes = pl.BlockSpec((LANES, TILE), lambda i: (0, 0))
    distant = pl.BlockSpec(memory_space=pltpu.HBM)
    anywhere = pl.BlockSpec(memory_space=pl.ANY)
    wide_half = jax.ShapeDtypeStruct((channels, TILE), BF16)
    wide_full = jax.ShapeDtypeStruct((channels, TILE), F32)
    table_full = jax.ShapeDtypeStruct((groups, TILE), F32)
    chunk_half = jax.ShapeDtypeStruct((blocks, LANES, TILE), BF16)
    chunk_full = jax.ShapeDtypeStruct((blocks, LANES, TILE), F32)

    def call(kernel, name, in_specs, out_specs, out_shape, scratch=(), grid=STEPS, limit=VMEM_LIMIT, work=0):
        return pl.pallas_call(
            kernel,
            grid=(grid,),
            in_specs=in_specs,
            out_specs=out_specs,
            out_shape=out_shape,
            scratch_shapes=scratch,
            name=name,
            cost_estimate=pl.CostEstimate(
                flops=2 * work * channels * TILE * TILE, bytes_accessed=1, transcendentals=0
            ),
            compiler_params=pltpu.CompilerParams(vmem_limit_bytes=limit),
        )

    def whole(leaf):
        return pl.BlockSpec(leaf.shape, lambda i: (0,) * len(leaf.shape))

    (product,) = call(
        gate_kernel, "gate", [distant] * 2, [distant], [wide_half],
        [
            pltpu.VMEM((2, channels, TILE), BF16), pltpu.VMEM((channels, TILE), BF16),
            pltpu.SemaphoreType.DMA((2, STEPS)), pltpu.SemaphoreType.DMA((STEPS,)),
        ],
        grid=1, limit=60 * 1024 * 1024,
    )(query, key)
    product_before = shifted(product, "seq", 1)

    (back,) = call(
        state_kernel, "state", [wide, wide, modes, anywhere], [chunk], [chunk_half]
    )(grad, value_two, rate, product)

    later_backs = [shifted(back, "seq", -gap) for gap in range(1, lax.axis_size("seq"))]
    to_next, after, to_end, power, taps, turned, wide_rate = call(
        table_kernel, "table", [modes, modes], [wide] * 4 + [table] * 2 + [chunk],
        [wide_half] * 4 + [table_full] * 2 + [chunk_full],
    )(rate, residue)
    fade = jnp.exp(-TILE * wide_rate)
    after_shard = later_backs[-1].astype(F32)
    for other in later_backs[-2::-1]:
        after_shard = other.astype(F32) + fade * after_shard
    after_shard = after_shard * jnp.exp(-wide_rate)

    (du2_local,) = call(
        local_kernel, "local", [wide, wide, table], [wide], [wide_full]
    )(
        grad, value_two, turned
    )

    dz1, du2 = call(
        middle_kernel, "middle", [chunk, wide, wide, wide, wide, anywhere], [wide, wide],
        [wide_half, wide_full],
    )(after_shard, du2_local, to_next, key_two, value, product_before)
    dz1_later = shifted(dz1, "seq", -1)

    grad_mr_value, grad_li_key, u2, state = call(
        forward_kernel, "forward",
        [wide, wide, table, wide, wide, wide, wide],
        [wide, wide, wide, chunk], [wide_half] * 3 + [chunk_half],
    )(product_before, product, mr_filter, value, key_two, to_end, du2)

    filter_chunks = groups // LANES
    packed_shape = jax.ShapeDtypeStruct((blocks + filter_chunks + 1, LANES, TILE), BF16)
    (packed,) = call(
        sums_kernel, "sums",
        [wide] * 7 + [chunk, chunk, modes],
        [whole(packed_shape)], [packed_shape],
        [pltpu.VMEM((groups, TILE), F32)] + [pltpu.VMEM((LANES, TILE), F32)] * 2,
    )(product_before, product, u2, dz1, grad, value_two, power, state, after_shard, rate)

    bits = scan_bits()
    few_full = jax.ShapeDtypeStruct((filter_chunks + 1, LANES, TILE), F32)
    factors = 3 * len(bits) - 2
    z2, within_zeros, *weights = call(
        functools.partial(within_kernel, bits), "within",
        [wide, table, chunk, anywhere], [wide, whole(few_full)] + [chunk] * factors,
        [wide_full, few_full] + [chunk_full] * factors,
    )(u2, taps, wide_rate, dz1_later)

    grad_query, grad_key, product_zeros = call(
        product_kernel, "product",
        [wide, wide, table, wide, wide], [wide, wide, whole(few_full)],
        [wide_half, wide_half, few_full],
    )(dz1, dz1_later, mr_filter, query, key)

    zeros = [within_zeros, product_zeros]
    before_shard = jnp.zeros(back.shape, F32)
    for bit in bits:
        other = swapped(packed, "seq", bit)
        sums = packed[blocks:].astype(F32) + other[blocks:].astype(F32)
        if zeros:
            sums = sums + zeros.pop(0)
        mine, theirs = packed[:blocks].astype(F32), other[:blocks].astype(F32)
        before_shard = before_shard + weights.pop(0) * theirs
        if bit != bits[-1]:
            total = weights.pop(0) * theirs + weights.pop(0) * mine
            packed = jnp.concatenate([total.astype(BF16), sums.astype(BF16)], axis=0)
    sums = sums.astype(BF16)

    assert lax.axis_size("dp") == 2
    partner = swapped(sums, "dp", 1)
    (grad_li_value,) = call(
        value_kernel, "value", [chunk, wide, wide, wide], [wide], [wide_half]
    )(before_shard, after, z2, grad)

    residue_full = jax.ShapeDtypeStruct((LANES, TILE), F32)
    grad_filter, grad_residue = call(
        last_kernel, "last", [whole(sums)] * 2,
        [whole(table_full), whole(residue_full)], [table_full, residue_full], grid=1,
    )(sums, partner)
    return (
        grad_query[None],
        grad_key[None],
        grad_mr_value[None],
        grad_li_key[None],
        grad_li_value[None],
        grad_filter,
        grad_residue[:, :groups].T,
    )


def solution(mesh):
    streams = (P("dp", "chan", "seq"),)
    tables = (P("chan", None),)
    return jax.shard_map(
        per_device,
        mesh=mesh,
        in_specs=streams * 6 + tables * 3,
        out_specs=streams * 5 + tables * 2,
        check_vma=False,
    )
```

```python
import functools

import jax
import jax.numpy as jnp
from jax import lax
from jax.experimental import pallas as pl
from jax.experimental.pallas import tpu as pltpu
from jax.sharding import PartitionSpec as P

F32 = jnp.float32
BF16 = jnp.bfloat16
TILE = 128
LANES = 16
PACK = TILE // LANES
CHUNK = 32
STEPS = 4
VMEM_LIMIT = 24 * 1024 * 1024


def nn(lhs, rhs):
    return lax.dot_general(lhs, rhs, (((1,), (0,)), ((), ())), preferred_element_type=F32)


def nt(lhs, rhs):
    return lax.dot_general(lhs, rhs, (((1,), (1,)), ((), ())), preferred_element_type=F32)


def iotas():
    rows = lax.broadcasted_iota(jnp.int32, (TILE, TILE), 0)
    cols = lax.broadcasted_iota(jnp.int32, (TILE, TILE), 1)
    return rows, cols


def ones_where(mask):
    return jnp.where(mask, 1.0, 0.0).astype(BF16)


def column(turned, mask):
    wide = jnp.concatenate([turned] * PACK, axis=0)
    return jnp.sum(jnp.where(mask, wide, 0.0), axis=1, keepdims=True)


def squeeze_groups(wide, mask):
    kept = jnp.where(mask, wide, 0.0)
    total = kept[:LANES]
    for g in range(1, PACK):
        total = total + kept[g * LANES : (g + 1) * LANES]
    return total


def spread_groups(narrow, mask):
    return jnp.where(mask, jnp.concatenate([narrow] * PACK, axis=0), 0.0)


def circulant(row):
    base = jnp.broadcast_to(row, (LANES, TILE))
    base = pltpu.roll(base, 0, 1, stride=1, stride_axis=0).astype(BF16)
    return jnp.concatenate(
        [base] + [pltpu.roll(base, LANES * j, 1) for j in range(1, PACK)], axis=0
    )


def reversal():
    rows, cols = iotas()
    return ones_where((rows + cols) % TILE == 0)


def one_minus_exp(value):
    series = jnp.full_like(value, 1.0)
    for order in (7, 6, 5, 4, 3, 2):
        series = 1.0 - value * series / order
    return jnp.where(value < 0.125, value * series, 1.0 - jnp.exp(-value))


def chunk_mask(shape, bit):
    return (lax.broadcasted_iota(jnp.int32, shape, 1) // CHUNK) & bit == 0


def pair_chunks(turned):
    parts = [turned[CHUNK * j : CHUNK * (j + 1), :] for j in range(TILE // CHUNK)]
    for bit in (1, 2):
        keep = chunk_mask((CHUNK, TILE), bit)
        for j in range(len(parts)):
            if j & bit == 0:
                low, high = parts[j], parts[j + bit]
                parts[j] = jnp.where(keep, low, pltpu.roll(high, CHUNK * bit, 1))
                parts[j + bit] = jnp.where(keep, pltpu.roll(low, TILE - CHUNK * bit, 1), high)
    return parts


def windows(before, now):
    lanes = lax.broadcasted_iota(jnp.int32, now.shape, 1)
    none = jnp.zeros_like(now)
    first, second = [none if before is None else before], [now]
    for j in range(1, TILE // CHUNK):
        left = TILE - CHUNK * j
        moved = pltpu.roll(now, left, 1)
        older = none if before is None else pltpu.roll(before, left, 1)
        first.append(jnp.where(lanes < left, older, moved))
        second.append(moved)
    return jnp.concatenate(
        [jnp.concatenate(first, axis=0), jnp.concatenate(second, axis=0)], axis=1
    )


def beside(first, second):
    return jnp.concatenate([first, second], axis=1)


def above(*arrays):
    return jnp.concatenate(arrays, axis=0)


def apart(first, second):
    none = jnp.zeros_like(first)
    return above(beside(first, none), beside(none, second))


def lag_rows(chunks, shifted_rows, own_rows):
    wide = nn(above(*[chunks * own for own in own_rows]), shifted_rows)
    rows = lax.broadcasted_iota(jnp.int32, (2 * CHUNK, TILE), 0) % CHUNK
    lanes = lax.broadcasted_iota(jnp.int32, (2 * CHUNK, TILE), 1)
    sums = jnp.where(lanes + rows < CHUNK, wide[:, TILE:], wide[:, :TILE])
    sums = [
        pltpu.roll(sums[CHUNK * i : CHUNK * (i + 1)], 0, 1, stride=1, stride_axis=0)
        for i in range(2)
    ]
    return above(*[jnp.sum(part, axis=0, keepdims=True) for part in sums])


def now_and_before(now, before, rows, half):
    both = beside(now, before)
    pieces = []
    for g in range(0, PACK, 2):
        circs = beside(*[circulant(rows[h : h + 1, :]) for h in (g, g + 1)])
        w_now = circs * half
        wide = nn(both[g * LANES : (g + 2) * LANES, :], above(w_now, circs - w_now))
        pieces += [wide[:LANES, :TILE], wide[LANES:, TILE:]]
    return jnp.concatenate(pieces, axis=0)


def within_shard(array, rows, half):
    pieces = []
    for g in range(0, PACK, 4):
        weights = [
            beside(*[circulant(rows[h : h + 1, :]) for h in (k, k + 1)]) * half
            for k in (g, g + 2)
        ]
        parts = [array[k * LANES : (k + 2) * LANES, :] for k in (g, g + 2)]
        wide = nn(apart(*parts), above(*weights))
        for k in range(4):
            column_at = (k % 2) * TILE
            pieces.append(wide[k * LANES : (k + 1) * LANES, column_at : column_at + TILE])
    return jnp.concatenate(pieces, axis=0)


def block_groups(at, blocks, block):
    rows, cols = iotas()
    return cols == rows // LANES + (at * blocks + block) * PACK


def gate_kernel(query, key, product, held, made, arrived, left):
    size = held.shape[1] // STEPS

    def fetch(array, step):
        span = pl.ds(step * size, size)
        return pltpu.make_async_copy(
            (query, key)[array].at[span, :], held.at[array, span, :], arrived.at[array, step]
        )

    def store(step):
        span = pl.ds(step * size, size)
        return pltpu.make_async_copy(made.at[span, :], product.at[span, :], left.at[step])

    for step in range(STEPS):
        for array in range(2):
            fetch(array, step).start()
    for step in range(STEPS):
        for array in range(2):
            fetch(array, step).wait()
        span = pl.ds(step * size, size)
        made[span, :] = held[0, span, :] * held[1, span, :]
        store(step).start()
    for step in range(STEPS):
        store(step).wait()


def state_kernel(grad, value, rate, product, state):
    rows, cols = iotas()
    offsets = cols.astype(F32)
    mask = rows // LANES == cols // LANES
    at = pl.program_id(0)
    blocks = state.shape[0]
    for block in range(blocks):
        span = pl.ds(block * TILE, TILE)
        rates = column(rate[...], block_groups(at, blocks, block))
        powers = jnp.exp(-rates * offsets).astype(BF16)
        dz2 = grad[span, :] * value[span, :]
        state[block] = squeeze_groups(nt(powers, dz2), mask).astype(BF16)


def table_kernel(rate, residue, to_next, to_end, power, taps, turned, wide_rate):
    rows, cols = iotas()
    mask = rows // LANES == cols // LANES
    offsets = cols.astype(F32)
    lags = ((CHUNK - 1 - cols) % TILE).astype(F32)
    at = pl.program_id(0)
    blocks = power.shape[0] // TILE
    coeffs = residue[...] * jnp.sqrt(one_minus_exp(2.0 * rate[...]))
    filters = []
    for block in range(blocks):
        span = pl.ds(block * TILE, TILE)
        own = block_groups(at, blocks, block)
        rates = column(rate[...], own)
        scale = column(coeffs, own)
        wide_rate[block] = squeeze_groups(jnp.broadcast_to(rates, (TILE, TILE)), mask)
        powers = jnp.exp(-rates * offsets)
        scaled = powers * scale
        ends = jnp.exp(-rates * (TILE - 1 - offsets))
        power[span, :] = jnp.exp(-rates * lags).astype(BF16)
        to_end[span, :] = ends.astype(BF16)
        to_next[span, :] = (ends * scale).astype(BF16)
        filters.append(jnp.sum(scaled.reshape(PACK, LANES, TILE), axis=1))
    filters = jnp.concatenate(filters, axis=0)
    taps[...] = filters
    turned[...] = nn(filters.astype(BF16), reversal())


def spans(array):
    return [pl.ds(block * TILE, TILE) for block in range(array.shape[0] // TILE)]


def group_rows(table, block):
    return table[pl.ds(block * PACK, PACK), :]


def local_kernel(grad, value, turned, du2):
    rows, cols = iotas()
    lower = ones_where(rows >= cols)
    lower_half = beside(lower, lower)
    results = [
        within_shard(grad[span, :] * value[span, :], group_rows(turned, block), lower_half)
        for block, span in enumerate(spans(grad))
    ]
    for span, result in zip(spans(grad), results):
        du2[span, :] = result


def middle_kernel(states, local, to_next, li_key, value, before, dz1, du2):
    rows, cols = iotas()
    mask = rows // LANES == cols // LANES
    wides = [spread_groups(states[block], mask).T.astype(BF16) for block in range(states.shape[0])]
    totals = [
        local[span, :] + nn(wide, to_next[span, :]) for span, wide in zip(spans(local), wides)
    ]
    for span, total in zip(spans(local), totals):
        du2[span, :] = total
        dy1 = total * li_key[span, :].astype(F32)
        dz1[span, :] = (dy1 * value[span, :].astype(F32)).astype(BF16)


def forward_kernel(
    before, now, filters, value, li_key, to_end, du2, grad_value, grad_key, u2, state
):
    rows, cols = iotas()
    mask = rows // LANES == cols // LANES
    upper = ones_where(cols >= rows)
    upper_half = beside(upper, upper)
    z1s = [
        now_and_before(
            now[span, :], before[span, :], group_rows(filters, block).astype(F32), upper_half
        )
        for block, span in enumerate(spans(now))
    ]
    results = []
    for span, z1 in zip(spans(now), z1s):
        y1 = (value[span, :].astype(F32) * z1).astype(BF16).astype(F32)
        key_two = li_key[span, :].astype(F32)
        u2_half = (y1 * key_two).astype(BF16)
        du2_here = du2[span, :]
        results.append(
            ((du2_here * y1).astype(BF16), (du2_here * key_two * z1).astype(BF16), u2_half)
        )
    ends = [nt(to_end[span, :], result[2]) for span, result in zip(spans(now), results)]
    for block, (span, result) in enumerate(zip(spans(now), results)):
        grad_key[span, :], grad_value[span, :], u2[span, :] = result
        state[block] = squeeze_groups(ends[block], mask).astype(BF16)


def sums_kernel(
    before, now, u2, dz1, grad, li_value, power, state, after_shard, rate,
    packed, filter_sums, within_sums, across_sums,
):
    rows, cols = iotas()
    turn = ones_where(cols == rows - rows % CHUNK + (CHUNK - 1 - rows % CHUNK))
    lanes = lax.broadcasted_iota(jnp.int32, (CHUNK, TILE), 1)
    own_rows = [ones_where((lanes // LANES) % 2 == i) for i in range(2)]
    at = pl.program_id(0)
    blocks = now.shape[0] // TILE

    @pl.when(at == 0)
    def _():
        within_sums[...] = jnp.zeros_like(within_sums)
        across_sums[...] = jnp.zeros_like(across_sums)

    turned = []
    for span in spans(now):
        dz2 = grad[span, :] * li_value[span, :]
        turned.append(nt(turn, above(dz1[span, :], dz2)).astype(BF16))
    chunks = [(pair_chunks(each[:, :TILE]), pair_chunks(each[:, TILE:])) for each in turned]
    lags, energies = [], []
    for block in range(blocks):
        lag, energy = [], []
        for p in range(TILE // CHUNK):
            pair = pl.ds(block * TILE + p * CHUNK, CHUNK)
            older, newer = before[pair, :], now[pair, :]
            lag.append(lag_rows(chunks[block][0][p], windows(older, newer), own_rows))
            energy.append(lag_rows(chunks[block][1][p], windows(None, u2[pair, :]), own_rows))
        lags.append(above(*lag))
        energies.append(above(*[above(*energy).astype(BF16)] * LANES))
    within, across = jnp.zeros((LANES, TILE), F32), jnp.zeros((LANES, TILE), F32)
    for block, span in enumerate(spans(now)):
        own = block_groups(at, blocks, block)
        within = within + squeeze_groups(nt(power[span, :], energies[block]), own)
        crossing = state[block].astype(F32) * after_shard[block]
        across = across + nn(crossing.astype(BF16), ones_where(own))
        packed[at * blocks + block] = state[block]
    few = blocks * PACK
    filter_sums[pl.ds(pl.multiple_of(at * few, few), few), :] = above(*lags)
    within_sums[...] += within
    across_sums[...] += across

    steps = filter_sums.shape[0] // few

    @pl.when(at == steps - 1)
    def _():
        place = ones_where((rows + cols) % TILE == CHUNK - 1)
        sums = nn(filter_sums[...].astype(BF16), place).astype(BF16)
        for chunk in range(filter_sums.shape[0] // LANES):
            packed[steps * blocks + chunk] = sums[chunk * LANES : (chunk + 1) * LANES]
        gains = jnp.sqrt(one_minus_exp(2.0 * rate[...]))
        total = gains * (within_sums[...] + across_sums[...])
        packed[steps * blocks + filter_sums.shape[0] // LANES] = total.astype(BF16)


def within_kernel(bits, u2, taps, wide_rate, rate, residue, later, z2, after, zeros, *weights):
    zeros[...] = jnp.zeros_like(zeros)
    place = lax.axis_index("seq")
    rates = wide_rate[...]
    weights = list(weights)
    for bit in bits:
        high = (place & bit) != 0
        passed = TILE * (place & (bit - 1)) + 1
        reach = jnp.exp(-rates * passed.astype(F32))
        weights.pop(0)[...] = jnp.where(high, reach, 0.0)
        if bit != bits[-1]:
            run = jnp.exp(-rates * (TILE * bit))
            one = jnp.ones_like(run)
            weights.pop(0)[...] = jnp.where(high, run, one)
            weights.pop(0)[...] = jnp.where(high, one, run)
    rows, cols = iotas()
    upper = ones_where(cols >= rows)
    upper_half = beside(upper, upper)
    results = [
        within_shard(u2[span, :], group_rows(taps, block), upper_half)
        for block, span in enumerate(spans(u2))
    ]
    at = pl.program_id(0)
    coeffs = residue[...] * jnp.sqrt(one_minus_exp(2.0 * rate[...]))
    for block, span in enumerate(spans(u2)):
        own = block_groups(at, len(results), block)
        powers = jnp.exp(-column(rate[...], own) * cols.astype(F32))
        after[span, :] = (powers * column(coeffs, own)).astype(BF16)
        z2[span, :] = results[block]


def last_kernel(half, other, grad_filter, grad_residue):
    chunks = half.shape[0] - 1
    for chunk in range(chunks):
        grad_filter[pl.ds(chunk * LANES, LANES), :] = half[chunk].astype(F32) + other[chunk].astype(F32)
    grad_residue[...] = half[chunks].astype(F32) + other[chunks].astype(F32)


def product_kernel(dz1, later, filters, query, key, grad_query, grad_key, nothing):
    nothing[...] = jnp.zeros_like(nothing)
    rows, cols = iotas()
    lower = ones_where(rows >= cols)
    lower_half = beside(lower, lower)
    turned = nn(filters[...], reversal())
    results = [
        now_and_before(
            dz1[span, :], later[span, :], turned[block * PACK : (block + 1) * PACK], lower_half
        )
        for block, span in enumerate(spans(dz1))
    ]
    for span, du1 in zip(spans(dz1), results):
        grad_query[span, :] = (du1 * key[span, :].astype(F32)).astype(BF16)
        grad_key[span, :] = (du1 * query[span, :].astype(F32)).astype(BF16)


def value_kernel(states, after, z2, grad, grad_value):
    rows, cols = iotas()
    mask = rows // LANES == cols // LANES
    wides = [spread_groups(states[block], mask).T.astype(BF16) for block in range(states.shape[0])]
    totals = [z2[span, :] + nn(wide, after[span, :]) for span, wide in zip(spans(z2), wides)]
    for span, total in zip(spans(z2), totals):
        grad_value[span, :] = (grad[span, :].astype(F32) * total).astype(BF16)


def shifted(value, axis, steps):
    count = lax.axis_size(axis)
    first, last = max(0, -steps), min(count, count - steps)
    return lax.ppermute(value, axis, [(source, source + steps) for source in range(first, last)])


def swapped(value, axis, bit):
    count = lax.axis_size(axis)
    return lax.ppermute(value, axis, [(source, source ^ bit) for source in range(count)])


def scan_bits():
    count, bit, bits = lax.axis_size("seq"), 1, []
    assert count & (count - 1) == 0
    while bit < count:
        bits.append(bit)
        bit *= 2
    return bits


def per_device(
    mr_query, mr_key, mr_value, li_key, li_value, grad_out, mr_filter, li_residue, li_rate
):
    query, key, value, key_two, value_two, grad = (
        array[0] for array in (mr_query, mr_key, mr_value, li_key, li_value, grad_out)
    )
    groups, filt_len = mr_filter.shape
    channels, seq_local = query.shape
    assert filt_len == TILE and seq_local == TILE and groups <= TILE
    assert channels == groups * LANES and li_rate.shape[1] == LANES
    rows = channels // STEPS
    few = groups // STEPS
    spare = ((0, 0), (0, TILE - groups))
    rate = jnp.pad(li_rate.T, spare)
    residue = jnp.pad(li_residue.T, spare)

    blocks = channels // TILE

    wide = pl.BlockSpec((rows, TILE), lambda i: (i, 0))
    table = pl.BlockSpec((few, TILE), lambda i: (i, 0))
    chunk = pl.BlockSpec((blocks // STEPS, LANES, TILE), lambda i: (i, 0, 0))
    modes = pl.BlockSpec((LANES, TILE), lambda i: (0, 0))
    distant = pl.BlockSpec(memory_space=pltpu.HBM)
    anywhere = pl.BlockSpec(memory_space=pl.ANY)
    wide_half = jax.ShapeDtypeStruct((channels, TILE), BF16)
    wide_full = jax.ShapeDtypeStruct((channels, TILE), F32)
    table_full = jax.ShapeDtypeStruct((groups, TILE), F32)
    chunk_half = jax.ShapeDtypeStruct((blocks, LANES, TILE), BF16)
    chunk_full = jax.ShapeDtypeStruct((blocks, LANES, TILE), F32)

    def call(kernel, name, in_specs, out_specs, out_shape, scratch=(), grid=STEPS, limit=VMEM_LIMIT, work=0):
        return pl.pallas_call(
            kernel,
            grid=(grid,),
            in_specs=in_specs,
            out_specs=out_specs,
            out_shape=out_shape,
            scratch_shapes=scratch,
            name=name,
            cost_estimate=pl.CostEstimate(
                flops=2 * work * channels * TILE * TILE, bytes_accessed=1, transcendentals=0
            ),
            compiler_params=pltpu.CompilerParams(vmem_limit_bytes=limit),
        )

    def whole(leaf):
        return pl.BlockSpec(leaf.shape, lambda i: (0,) * len(leaf.shape))

    def twice(spec):
        return pl.BlockSpec((2 * spec.block_shape[0],) + spec.block_shape[1:], spec.index_map)

    (product,) = call(
        gate_kernel, "gate", [distant] * 2, [distant], [wide_half],
        [
            pltpu.VMEM((2, channels, TILE), BF16), pltpu.VMEM((channels, TILE), BF16),
            pltpu.SemaphoreType.DMA((2, STEPS)), pltpu.SemaphoreType.DMA((STEPS,)),
        ],
        grid=1, limit=60 * 1024 * 1024,
    )(query, key)
    product_before = shifted(product, "seq", 1)

    (back,) = call(
        state_kernel, "state", [wide, wide, modes, anywhere], [chunk], [chunk_half]
    )(grad, value_two, rate, product)

    later_backs = [shifted(back, "seq", -gap) for gap in range(1, lax.axis_size("seq"))]
    to_next, to_end, power, taps, turned, wide_rate = call(
        table_kernel, "table", [modes, modes], [wide] * 3 + [table] * 2 + [chunk],
        [wide_half] * 3 + [table_full] * 2 + [chunk_full],
    )(rate, residue)
    fade = jnp.exp(-TILE * wide_rate)
    after_shard = later_backs[-1].astype(F32)
    for other in later_backs[-2::-1]:
        after_shard = other.astype(F32) + fade * after_shard
    after_shard = after_shard * jnp.exp(-wide_rate)

    (du2_local,) = call(
        local_kernel, "local", [wide, wide, table], [wide], [wide_full]
    )(
        grad, value_two, turned
    )

    dz1, du2 = call(
        middle_kernel, "middle", [chunk, wide, wide, wide, wide, anywhere], [wide, wide],
        [wide_half, wide_full],
    )(after_shard, du2_local, to_next, key_two, value, product_before)
    dz1_later = shifted(dz1, "seq", -1)

    grad_mr_value, grad_li_key, u2, state = call(
        forward_kernel, "forward",
        [wide, wide, table, wide, wide, wide, wide],
        [wide, wide, wide, chunk], [wide_half] * 3 + [chunk_half],
    )(product_before, product, mr_filter, value, key_two, to_end, du2)

    filter_chunks = groups // LANES
    packed_shape = jax.ShapeDtypeStruct((blocks + filter_chunks + 1, LANES, TILE), BF16)
    (packed,) = call(
        sums_kernel, "sums",
        [twice(wide)] * 7 + [twice(chunk), twice(chunk), modes],
        [whole(packed_shape)], [packed_shape],
        [pltpu.VMEM((groups, TILE), F32)] + [pltpu.VMEM((LANES, TILE), F32)] * 2,
        grid=STEPS // 2,
    )(product_before, product, u2, dz1, grad, value_two, power, state, after_shard, rate)

    bits = scan_bits()
    few_full = jax.ShapeDtypeStruct((filter_chunks + 1, LANES, TILE), F32)
    factors = 3 * len(bits) - 2
    z2, after, within_zeros, *weights = call(
        functools.partial(within_kernel, bits), "within",
        [wide, table, chunk, modes, modes, anywhere],
        [wide, wide, whole(few_full)] + [chunk] * factors,
        [wide_full, wide_half, few_full] + [chunk_full] * factors,
    )(u2, taps, wide_rate, rate, residue, dz1_later)

    grad_query, grad_key, product_zeros = call(
        product_kernel, "product",
        [wide, wide, table, wide, wide], [wide, wide, whole(few_full)],
        [wide_half, wide_half, few_full],
    )(dz1, dz1_later, mr_filter, query, key)

    zeros = [within_zeros, product_zeros]
    before_shard = jnp.zeros(back.shape, F32)
    for bit in bits:
        other = swapped(packed, "seq", bit)
        sums = packed[blocks:].astype(F32) + other[blocks:].astype(F32)
        if zeros:
            sums = sums + zeros.pop(0)
        mine, theirs = packed[:blocks].astype(F32), other[:blocks].astype(F32)
        before_shard = before_shard + weights.pop(0) * theirs
        if bit != bits[-1]:
            total = weights.pop(0) * theirs + weights.pop(0) * mine
            packed = jnp.concatenate([total.astype(BF16), sums.astype(BF16)], axis=0)
    sums = sums.astype(BF16)

    assert lax.axis_size("dp") == 2
    partner = swapped(sums, "dp", 1)
    (grad_li_value,) = call(
        value_kernel, "value", [chunk, wide, wide, wide], [wide], [wide_half]
    )(before_shard, after, z2, grad)

    residue_full = jax.ShapeDtypeStruct((LANES, TILE), F32)
    grad_filter, grad_residue = call(
        last_kernel, "last", [whole(sums)] * 2,
        [whole(table_full), whole(residue_full)], [table_full, residue_full], grid=1,
    )(sums, partner)
    return (
        grad_query[None],
        grad_key[None],
        grad_mr_value[None],
        grad_li_key[None],
        grad_li_value[None],
        grad_filter,
        grad_residue[:, :groups].T,
    )


def solution(mesh):
    streams = (P("dp", "chan", "seq"),)
    tables = (P("chan", None),)
    return jax.shard_map(
        per_device,
        mesh=mesh,
        in_specs=streams * 6 + tables * 3,
        out_specs=streams * 5 + tables * 2,
        check_vma=False,
    )
```

```python
import functools

import jax
import jax.numpy as jnp
from jax import lax
from jax.experimental import pallas as pl
from jax.experimental.pallas import tpu as pltpu
from jax.sharding import PartitionSpec as P

F32 = jnp.float32
BF16 = jnp.bfloat16
TILE = 128
LANES = 16
PACK = TILE // LANES
CHUNK = 32
HALF = 64
STEPS = 4
VMEM_LIMIT = 24 * 1024 * 1024


def nn(lhs, rhs):
    return lax.dot_general(lhs, rhs, (((1,), (0,)), ((), ())), preferred_element_type=F32)


def nt(lhs, rhs):
    return lax.dot_general(lhs, rhs, (((1,), (1,)), ((), ())), preferred_element_type=F32)


def iotas():
    rows = lax.broadcasted_iota(jnp.int32, (TILE, TILE), 0)
    cols = lax.broadcasted_iota(jnp.int32, (TILE, TILE), 1)
    return rows, cols


def ones_where(mask):
    return jnp.where(mask, 1.0, 0.0).astype(BF16)


def column(turned, mask):
    wide = jnp.concatenate([turned] * PACK, axis=0)
    return jnp.sum(jnp.where(mask, wide, 0.0), axis=1, keepdims=True)


def squeeze_groups(wide, mask):
    kept = jnp.where(mask, wide, 0.0)
    total = kept[:LANES]
    for g in range(1, PACK):
        total = total + kept[g * LANES : (g + 1) * LANES]
    return total


def spread_groups(narrow, mask):
    return jnp.where(mask, jnp.concatenate([narrow] * PACK, axis=0), 0.0)


def left_half(shape):
    return lax.broadcasted_iota(jnp.int32, shape, 1) % TILE < HALF


def turned_rows(row):
    base = jnp.broadcast_to(row, (LANES, TILE))
    return pltpu.roll(base, 0, 1, stride=1, stride_axis=0).astype(BF16)


def circulants(rows):
    left = left_half((LANES, TILE))
    tiles = []
    for pair in (0, 2):
        first, second = (turned_rows(rows[g : g + 1, :]) for g in (pair, pair + 1))
        tiles.append(above(*[
            jnp.where(
                left,
                pltpu.roll(first, LANES * j, 1) if j else first,
                pltpu.roll(second, (LANES * j + HALF) % TILE, 1),
            ) if LANES * j != HALF else jnp.where(left, pltpu.roll(first, HALF, 1), second)
            for j in range(PACK)
        ]))
    return beside(*tiles)


def reversal():
    rows, cols = iotas()
    return ones_where((rows + cols) % TILE == 0)


def one_minus_exp(value):
    series = jnp.full_like(value, 1.0)
    for order in (7, 6, 5, 4, 3, 2):
        series = 1.0 - value * series / order
    return jnp.where(value < 0.125, value * series, 1.0 - jnp.exp(-value))


def chunk_mask(shape, bit):
    return (lax.broadcasted_iota(jnp.int32, shape, 1) // CHUNK) & bit == 0


def pair_chunks(turned):
    parts = [turned[CHUNK * j : CHUNK * (j + 1), :] for j in range(TILE // CHUNK)]
    for bit in (1, 2):
        keep = chunk_mask((CHUNK, TILE), bit)
        for j in range(len(parts)):
            if j & bit == 0:
                low, high = parts[j], parts[j + bit]
                parts[j] = jnp.where(keep, low, pltpu.roll(high, CHUNK * bit, 1))
                parts[j + bit] = jnp.where(keep, pltpu.roll(low, TILE - CHUNK * bit, 1), high)
    return parts


def windows(before, now):
    lanes = lax.broadcasted_iota(jnp.int32, now.shape, 1)
    none = jnp.zeros_like(now)
    first, second = [none if before is None else before], [now]
    for j in range(1, TILE // CHUNK):
        left = TILE - CHUNK * j
        moved = pltpu.roll(now, left, 1)
        older = none if before is None else pltpu.roll(before, left, 1)
        first.append(jnp.where(lanes < left, older, moved))
        second.append(moved)
    return jnp.concatenate(
        [jnp.concatenate(first, axis=0), jnp.concatenate(second, axis=0)], axis=1
    )


def beside(first, second):
    return jnp.concatenate([first, second], axis=1)


def above(*arrays):
    return jnp.concatenate(arrays, axis=0)


def apart(first, second):
    none = jnp.zeros_like(first)
    return above(beside(first, none), beside(none, second))


def lag_rows(chunks, shifted_rows, own_rows):
    wide = nn(above(*[chunks * own for own in own_rows]), shifted_rows)
    rows = lax.broadcasted_iota(jnp.int32, (2 * CHUNK, TILE), 0) % CHUNK
    lanes = lax.broadcasted_iota(jnp.int32, (2 * CHUNK, TILE), 1)
    sums = jnp.where(lanes + rows < CHUNK, wide[:, TILE:], wide[:, :TILE])
    sums = [
        pltpu.roll(sums[CHUNK * i : CHUNK * (i + 1)], 0, 1, stride=1, stride_axis=0)
        for i in range(2)
    ]
    return above(*[jnp.sum(part, axis=0, keepdims=True) for part in sums])


def halves_joined(wide):
    left = left_half((LANES, TILE))
    pieces = []
    for g in range(4):
        lanes = slice((g // 2) * TILE, (g // 2 + 1) * TILE)
        low = wide[g * LANES : (g + 1) * LANES, lanes]
        high = wide[HALF + g * LANES : HALF + (g + 1) * LANES, lanes]
        if g % 2 == 0:
            pieces.append(jnp.where(left, low, pltpu.roll(high, HALF, 1)))
        else:
            pieces.append(jnp.where(left, pltpu.roll(low, HALF, 1), high))
    return pieces


def over_two_shards(first, second, rows, half):
    first_moved, second_moved = pltpu.roll(first, HALF, 1), pltpu.roll(second, HALF, 1)
    low = beside(first, second)[:, : TILE + HALF]
    high = beside(jnp.where(left_half(first.shape), first_moved, second_moved), second_moved)
    high = high[:, : TILE + HALF]
    pieces = []
    for g in range(0, PACK, 4):
        circ = circulants(rows[g : g + 4, :])
        part = slice(g * LANES, (g + 4) * LANES)
        top = circ[:HALF] * half
        weights = above(top, circ[HALF:], circ[:HALF] - top)
        pieces += halves_joined(nn(above(low[part], high[part]), weights))
    return jnp.concatenate(pieces, axis=0)


def within_shard(array, rows, half, earlier):
    moved = pltpu.roll(array, HALF, 1)
    none = jnp.zeros_like(array)
    left = left_half(array.shape)
    if earlier:
        low, high = jnp.where(left, none, moved), array
    else:
        low, high = array, jnp.where(left, moved, none)
    pieces = []
    for g in range(0, PACK, 4):
        circ = circulants(rows[g : g + 4, :])
        part = slice(g * LANES, (g + 4) * LANES)
        top = circ[:HALF] * half
        weights = above(circ[HALF:], top) if earlier else above(top, circ[HALF:])
        pieces += halves_joined(nn(above(low[part], high[part]), weights))
    return jnp.concatenate(pieces, axis=0)


def band_half(later):
    rows = lax.broadcasted_iota(jnp.int32, (HALF, 2 * TILE), 0)
    cols = lax.broadcasted_iota(jnp.int32, (HALF, 2 * TILE), 1) % HALF
    return ones_where(rows >= cols if later else rows > cols)


def block_groups(at, blocks, block):
    rows, cols = iotas()
    return cols == rows // LANES + (at * blocks + block) * PACK


def gate_kernel(query, key, product, held, made, arrived, left):
    size = held.shape[1] // STEPS

    def fetch(array, step):
        span = pl.ds(step * size, size)
        return pltpu.make_async_copy(
            (query, key)[array].at[span, :], held.at[array, span, :], arrived.at[array, step]
        )

    def store(step):
        span = pl.ds(step * size, size)
        return pltpu.make_async_copy(made.at[span, :], product.at[span, :], left.at[step])

    for step in range(STEPS):
        for array in range(2):
            fetch(array, step).start()
    for step in range(STEPS):
        for array in range(2):
            fetch(array, step).wait()
        span = pl.ds(step * size, size)
        made[span, :] = held[0, span, :] * held[1, span, :]
        store(step).start()
    for step in range(STEPS):
        store(step).wait()


def state_kernel(grad, value, rate, state):
    rows, cols = iotas()
    offsets = cols.astype(F32)
    mask = rows // LANES == cols // LANES
    at = pl.program_id(0)
    blocks = state.shape[0]
    for block in range(blocks):
        span = pl.ds(block * TILE, TILE)
        rates = column(rate[...], block_groups(at, blocks, block))
        powers = jnp.exp(-rates * offsets).astype(BF16)
        dz2 = grad[span, :] * value[span, :]
        state[block] = squeeze_groups(nt(powers, dz2), mask).astype(BF16)


def table_kernel(
    rate, residue, filters, to_next, after, to_end, power, taps, turned, mr_turned, wide_rate
):
    rows, cols = iotas()
    mask = rows // LANES == cols // LANES
    offsets = cols.astype(F32)
    lags = ((CHUNK - 1 - cols) % TILE).astype(F32)
    at = pl.program_id(0)
    blocks = power.shape[0] // TILE
    coeffs = residue[...] * jnp.sqrt(one_minus_exp(2.0 * rate[...]))
    sums = []
    for block in range(blocks):
        span = pl.ds(block * TILE, TILE)
        own = block_groups(at, blocks, block)
        rates = column(rate[...], own)
        scale = column(coeffs, own)
        wide_rate[block] = squeeze_groups(jnp.broadcast_to(rates, (TILE, TILE)), mask)
        powers = jnp.exp(-rates * offsets)
        scaled = powers * scale
        ends = jnp.exp(-rates * (TILE - 1 - offsets))
        power[span, :] = jnp.exp(-rates * lags).astype(BF16)
        to_end[span, :] = ends.astype(BF16)
        after[span, :] = scaled.astype(BF16)
        to_next[span, :] = (ends * scale).astype(BF16)
        sums.append(jnp.sum(scaled.reshape(PACK, LANES, TILE), axis=1))
    taps[...] = above(*sums)
    turned[...] = nn(above(*sums).astype(BF16), reversal())
    mr_turned[...] = nn(filters[...], reversal())


def spans(array):
    return [pl.ds(block * TILE, TILE) for block in range(array.shape[0] // TILE)]


def group_rows(table, block):
    return table[pl.ds(block * PACK, PACK), :]


def local_kernel(grad, value, turned, du2):
    half = band_half(True)
    results = [
        within_shard(grad[span, :] * value[span, :], group_rows(turned, block), half, False)
        for block, span in enumerate(spans(grad))
    ]
    for span, result in zip(spans(grad), results):
        du2[span, :] = result


def middle_kernel(states, local, to_next, li_key, value, before, dz1, du2):
    rows, cols = iotas()
    mask = rows // LANES == cols // LANES
    wides = [spread_groups(states[block], mask).T.astype(BF16) for block in range(states.shape[0])]
    totals = [
        local[span, :] + nn(wide, to_next[span, :]) for span, wide in zip(spans(local), wides)
    ]
    for span, total in zip(spans(local), totals):
        du2[span, :] = total
        dy1 = total * li_key[span, :].astype(F32)
        dz1[span, :] = (dy1 * value[span, :].astype(F32)).astype(BF16)


def forward_kernel(
    before, now, filters, value, li_key, to_end, du2, grad_value, grad_key, u2, state
):
    rows, cols = iotas()
    mask = rows // LANES == cols // LANES
    half = band_half(False)
    z1s = [
        over_two_shards(
            before[span, :], now[span, :], group_rows(filters, block).astype(F32), half
        )
        for block, span in enumerate(spans(now))
    ]
    results = []
    for span, z1 in zip(spans(now), z1s):
        y1 = (value[span, :].astype(F32) * z1).astype(BF16).astype(F32)
        key_two = li_key[span, :].astype(F32)
        u2_half = (y1 * key_two).astype(BF16)
        du2_here = du2[span, :]
        results.append(
            ((du2_here * y1).astype(BF16), (du2_here * key_two * z1).astype(BF16), u2_half)
        )
    ends = [nt(to_end[span, :], result[2]) for span, result in zip(spans(now), results)]
    for block, (span, result) in enumerate(zip(spans(now), results)):
        grad_key[span, :], grad_value[span, :], u2[span, :] = result
        state[block] = squeeze_groups(ends[block], mask).astype(BF16)


def sums_kernel(
    before, now, u2, dz1, grad, li_value, power, state, after_shard, rate,
    packed, filter_sums, within_sums, across_sums,
):
    rows, cols = iotas()
    turn = ones_where(cols == rows - rows % CHUNK + (CHUNK - 1 - rows % CHUNK))
    lanes = lax.broadcasted_iota(jnp.int32, (CHUNK, TILE), 1)
    own_rows = [ones_where((lanes // LANES) % 2 == i) for i in range(2)]
    at = pl.program_id(0)
    blocks = now.shape[0] // TILE

    @pl.when(at == 0)
    def _():
        within_sums[...] = jnp.zeros_like(within_sums)
        across_sums[...] = jnp.zeros_like(across_sums)

    turned = []
    for span in spans(now):
        dz2 = grad[span, :] * li_value[span, :]
        turned.append(nt(turn, above(dz1[span, :], dz2)).astype(BF16))
    chunks = [(pair_chunks(each[:, :TILE]), pair_chunks(each[:, TILE:])) for each in turned]
    lags, energies = [], []
    for block in range(blocks):
        lag, energy = [], []
        for p in range(TILE // CHUNK):
            pair = pl.ds(block * TILE + p * CHUNK, CHUNK)
            older, newer = before[pair, :], now[pair, :]
            lag.append(lag_rows(chunks[block][0][p], windows(older, newer), own_rows))
            energy.append(lag_rows(chunks[block][1][p], windows(None, u2[pair, :]), own_rows))
        lags.append(above(*lag))
        energies.append(above(*[above(*energy).astype(BF16)] * LANES))
    within, across = jnp.zeros((LANES, TILE), F32), jnp.zeros((LANES, TILE), F32)
    for block, span in enumerate(spans(now)):
        own = block_groups(at, blocks, block)
        within = within + squeeze_groups(nt(power[span, :], energies[block]), own)
        crossing = state[block].astype(F32) * after_shard[block]
        across = across + nn(crossing.astype(BF16), ones_where(own))
        packed[at * blocks + block] = state[block]
    few = blocks * PACK
    filter_sums[pl.ds(pl.multiple_of(at * few, few), few), :] = above(*lags)
    within_sums[...] += within
    across_sums[...] += across

    steps = filter_sums.shape[0] // few

    @pl.when(at == steps - 1)
    def _():
        place = ones_where((rows + cols) % TILE == CHUNK - 1)
        sums = nn(filter_sums[...].astype(BF16), place).astype(BF16)
        for chunk in range(filter_sums.shape[0] // LANES):
            packed[steps * blocks + chunk] = sums[chunk * LANES : (chunk + 1) * LANES]
        gains = jnp.sqrt(one_minus_exp(2.0 * rate[...]))
        total = gains * (within_sums[...] + across_sums[...])
        packed[steps * blocks + filter_sums.shape[0] // LANES] = total.astype(BF16)


def within_kernel(bits, u2, taps, wide_rate, later, z2, zeros, *weights):
    zeros[...] = jnp.zeros_like(zeros)
    place = lax.axis_index("seq")
    rates = wide_rate[...]
    weights = list(weights)
    for bit in bits:
        high = (place & bit) != 0
        passed = TILE * (place & (bit - 1)) + 1
        reach = jnp.exp(-rates * passed.astype(F32))
        weights.pop(0)[...] = jnp.where(high, reach, 0.0)
        if bit != bits[-1]:
            run = jnp.exp(-rates * (TILE * bit))
            one = jnp.ones_like(run)
            weights.pop(0)[...] = jnp.where(high, run, one)
            weights.pop(0)[...] = jnp.where(high, one, run)
    half = jnp.ones((), BF16) - band_half(False)
    results = [
        within_shard(u2[span, :], group_rows(taps, block), half, True)
        for block, span in enumerate(spans(u2))
    ]
    for span, result in zip(spans(u2), results):
        z2[span, :] = result


def last_kernel(half, other, grad_filter, grad_residue):
    chunks = half.shape[0] - 1
    for chunk in range(chunks):
        grad_filter[pl.ds(chunk * LANES, LANES), :] = half[chunk].astype(F32) + other[chunk].astype(F32)
    grad_residue[...] = half[chunks].astype(F32) + other[chunks].astype(F32)


def product_kernel(dz1, later, turned, query, key, grad_query, grad_key, nothing):
    nothing[...] = jnp.zeros_like(nothing)
    half = band_half(True)
    results = [
        over_two_shards(dz1[span, :], later[span, :], group_rows(turned, block), half)
        for block, span in enumerate(spans(dz1))
    ]
    for span, du1 in zip(spans(dz1), results):
        grad_query[span, :] = (du1 * key[span, :].astype(F32)).astype(BF16)
        grad_key[span, :] = (du1 * query[span, :].astype(F32)).astype(BF16)


def value_kernel(states, after, z2, grad, grad_value):
    rows, cols = iotas()
    mask = rows // LANES == cols // LANES
    wides = [spread_groups(states[block], mask).T.astype(BF16) for block in range(states.shape[0])]
    totals = [z2[span, :] + nn(wide, after[span, :]) for span, wide in zip(spans(z2), wides)]
    for span, total in zip(spans(z2), totals):
        grad_value[span, :] = (grad[span, :].astype(F32) * total).astype(BF16)


def shifted(value, axis, steps):
    count = lax.axis_size(axis)
    first, last = max(0, -steps), min(count, count - steps)
    return lax.ppermute(value, axis, [(source, source + steps) for source in range(first, last)])


def swapped(value, axis, bit):
    count = lax.axis_size(axis)
    return lax.ppermute(value, axis, [(source, source ^ bit) for source in range(count)])


def scan_bits():
    count, bit, bits = lax.axis_size("seq"), 1, []
    assert count & (count - 1) == 0
    while bit < count:
        bits.append(bit)
        bit *= 2
    return bits


def per_device(
    mr_query, mr_key, mr_value, li_key, li_value, grad_out, mr_filter, li_residue, li_rate
):
    query, key, value, key_two, value_two, grad = (
        array[0] for array in (mr_query, mr_key, mr_value, li_key, li_value, grad_out)
    )
    groups, filt_len = mr_filter.shape
    channels, seq_local = query.shape
    assert filt_len == TILE and seq_local == TILE and groups <= TILE
    assert channels == groups * LANES and li_rate.shape[1] == LANES
    rows = channels // STEPS
    few = groups // STEPS
    spare = ((0, 0), (0, TILE - groups))
    rate = jnp.pad(li_rate.T, spare)
    residue = jnp.pad(li_residue.T, spare)

    blocks = channels // TILE

    wide = pl.BlockSpec((rows, TILE), lambda i: (i, 0))
    table = pl.BlockSpec((few, TILE), lambda i: (i, 0))
    chunk = pl.BlockSpec((blocks // STEPS, LANES, TILE), lambda i: (i, 0, 0))
    modes = pl.BlockSpec((LANES, TILE), lambda i: (0, 0))
    distant = pl.BlockSpec(memory_space=pltpu.HBM)
    anywhere = pl.BlockSpec(memory_space=pl.ANY)
    wide_half = jax.ShapeDtypeStruct((channels, TILE), BF16)
    wide_full = jax.ShapeDtypeStruct((channels, TILE), F32)
    table_full = jax.ShapeDtypeStruct((groups, TILE), F32)
    chunk_half = jax.ShapeDtypeStruct((blocks, LANES, TILE), BF16)
    chunk_full = jax.ShapeDtypeStruct((blocks, LANES, TILE), F32)

    def call(kernel, name, in_specs, out_specs, out_shape, scratch=(), grid=STEPS, limit=VMEM_LIMIT, work=0):
        return pl.pallas_call(
            kernel,
            grid=(grid,),
            in_specs=in_specs,
            out_specs=out_specs,
            out_shape=out_shape,
            scratch_shapes=scratch,
            name=name,
            cost_estimate=pl.CostEstimate(
                flops=2 * work * channels * TILE * TILE, bytes_accessed=1, transcendentals=0
            ),
            compiler_params=pltpu.CompilerParams(vmem_limit_bytes=limit),
        )

    def whole(leaf):
        return pl.BlockSpec(leaf.shape, lambda i: (0,) * len(leaf.shape))

    def twice(spec):
        return pl.BlockSpec((2 * spec.block_shape[0],) + spec.block_shape[1:], spec.index_map)

    (product,) = call(
        gate_kernel, "gate", [distant] * 2, [distant], [wide_half],
        [
            pltpu.VMEM((2, channels, TILE), BF16), pltpu.VMEM((channels, TILE), BF16),
            pltpu.SemaphoreType.DMA((2, STEPS)), pltpu.SemaphoreType.DMA((STEPS,)),
        ],
        grid=1, limit=60 * 1024 * 1024,
    )(query, key)
    product_before = shifted(product, "seq", 1)

    (back,) = call(state_kernel, "state", [wide, wide, modes], [chunk], [chunk_half])(
        grad, value_two, rate
    )

    later_backs = [shifted(back, "seq", -gap) for gap in range(1, lax.axis_size("seq"))]
    to_next, after, to_end, power, taps, turned, mr_turned, wide_rate = call(
        table_kernel, "table", [modes, modes, table], [wide] * 4 + [table] * 3 + [chunk],
        [wide_half] * 4 + [table_full] * 3 + [chunk_full],
    )(rate, residue, mr_filter)
    fade = jnp.exp(-TILE * wide_rate)
    after_shard = later_backs[-1].astype(F32)
    for other in later_backs[-2::-1]:
        after_shard = other.astype(F32) + fade * after_shard
    after_shard = after_shard * jnp.exp(-wide_rate)

    (du2_local,) = call(
        local_kernel, "local", [wide, wide, table], [wide], [wide_full]
    )(
        grad, value_two, turned
    )

    dz1, du2 = call(
        middle_kernel, "middle", [chunk, wide, wide, wide, wide, anywhere], [wide, wide],
        [wide_half, wide_full],
    )(after_shard, du2_local, to_next, key_two, value, product_before)
    dz1_later = shifted(dz1, "seq", -1)

    grad_mr_value, grad_li_key, u2, state = call(
        forward_kernel, "forward",
        [wide, wide, table, wide, wide, wide, wide],
        [wide, wide, wide, chunk], [wide_half] * 3 + [chunk_half],
    )(product_before, product, mr_filter, value, key_two, to_end, du2)

    filter_chunks = groups // LANES
    packed_shape = jax.ShapeDtypeStruct((blocks + filter_chunks + 1, LANES, TILE), BF16)
    (packed,) = call(
        sums_kernel, "sums",
        [twice(wide)] * 7 + [twice(chunk), twice(chunk), modes],
        [whole(packed_shape)], [packed_shape],
        [pltpu.VMEM((groups, TILE), F32)] + [pltpu.VMEM((LANES, TILE), F32)] * 2,
        grid=STEPS // 2,
    )(product_before, product, u2, dz1, grad, value_two, power, state, after_shard, rate)

    bits = scan_bits()
    few_full = jax.ShapeDtypeStruct((filter_chunks + 1, LANES, TILE), F32)
    factors = 3 * len(bits) - 2
    z2, within_zeros, *weights = call(
        functools.partial(within_kernel, bits), "within",
        [wide, table, chunk, anywhere], [wide, whole(few_full)] + [chunk] * factors,
        [wide_full, few_full] + [chunk_full] * factors,
    )(u2, taps, wide_rate, dz1_later)

    grad_query, grad_key, product_zeros = call(
        product_kernel, "product",
        [wide, wide, table, wide, wide], [wide, wide, whole(few_full)],
        [wide_half, wide_half, few_full],
    )(dz1, dz1_later, mr_turned, query, key)

    zeros = [within_zeros, product_zeros]
    before_shard = jnp.zeros(back.shape, F32)
    for bit in bits:
        other = swapped(packed, "seq", bit)
        sums = packed[blocks:].astype(F32) + other[blocks:].astype(F32)
        if zeros:
            sums = sums + zeros.pop(0)
        mine, theirs = packed[:blocks].astype(F32), other[:blocks].astype(F32)
        before_shard = before_shard + weights.pop(0) * theirs
        if bit != bits[-1]:
            total = weights.pop(0) * theirs + weights.pop(0) * mine
            packed = jnp.concatenate([total.astype(BF16), sums.astype(BF16)], axis=0)
    sums = sums.astype(BF16)

    assert lax.axis_size("dp") == 2
    partner = swapped(sums, "dp", 1)
    (grad_li_value,) = call(
        value_kernel, "value", [chunk, wide, wide, wide], [wide], [wide_half]
    )(before_shard, after, z2, grad)

    residue_full = jax.ShapeDtypeStruct((LANES, TILE), F32)
    grad_filter, grad_residue = call(
        last_kernel, "last", [whole(sums)] * 2,
        [whole(table_full), whole(residue_full)], [table_full, residue_full], grid=1,
    )(sums, partner)
    return (
        grad_query[None],
        grad_key[None],
        grad_mr_value[None],
        grad_li_key[None],
        grad_li_value[None],
        grad_filter,
        grad_residue[:, :groups].T,
    )


def solution(mesh):
    streams = (P("dp", "chan", "seq"),)
    tables = (P("chan", None),)
    return jax.shard_map(
        per_device,
        mesh=mesh,
        in_specs=streams * 6 + tables * 3,
        out_specs=streams * 5 + tables * 2,
        check_vma=False,
    )
```

```python
import functools

import jax
import jax.numpy as jnp
from jax import lax
from jax.experimental import pallas as pl
from jax.experimental.pallas import tpu as pltpu
from jax.sharding import PartitionSpec as P

F32 = jnp.float32
BF16 = jnp.bfloat16
TILE = 128
LANES = 16
PACK = TILE // LANES
CHUNK = 32
STEPS = 4
VMEM_LIMIT = 24 * 1024 * 1024


def nn(lhs, rhs):
    return lax.dot_general(lhs, rhs, (((1,), (0,)), ((), ())), preferred_element_type=F32)


def nt(lhs, rhs):
    return lax.dot_general(lhs, rhs, (((1,), (1,)), ((), ())), preferred_element_type=F32)


def iotas():
    rows = lax.broadcasted_iota(jnp.int32, (TILE, TILE), 0)
    cols = lax.broadcasted_iota(jnp.int32, (TILE, TILE), 1)
    return rows, cols


def ones_where(mask):
    return jnp.where(mask, 1.0, 0.0).astype(BF16)


def column(turned, mask):
    wide = jnp.concatenate([turned] * PACK, axis=0)
    return jnp.sum(jnp.where(mask, wide, 0.0), axis=1, keepdims=True)


def squeeze_groups(wide, mask):
    kept = jnp.where(mask, wide, 0.0)
    total = kept[:LANES]
    for g in range(1, PACK):
        total = total + kept[g * LANES : (g + 1) * LANES]
    return total


def spread_groups(narrow, mask):
    return jnp.where(mask, jnp.concatenate([narrow] * PACK, axis=0), 0.0)


def circulant(row):
    base = jnp.broadcast_to(row, (LANES, TILE))
    base = pltpu.roll(base, 0, 1, stride=1, stride_axis=0).astype(BF16)
    return jnp.concatenate(
        [base] + [pltpu.roll(base, LANES * j, 1) for j in range(1, PACK)], axis=0
    )


def reversal():
    rows, cols = iotas()
    return ones_where((rows + cols) % TILE == 0)


def one_minus_exp(value):
    series = jnp.full_like(value, 1.0)
    for order in (7, 6, 5, 4, 3, 2):
        series = 1.0 - value * series / order
    return jnp.where(value < 0.125, value * series, 1.0 - jnp.exp(-value))


def chunk_mask(shape, bit):
    return (lax.broadcasted_iota(jnp.int32, shape, 1) // CHUNK) & bit == 0


def pair_chunks(turned):
    parts = [turned[CHUNK * j : CHUNK * (j + 1), :] for j in range(TILE // CHUNK)]
    for bit in (1, 2):
        keep = chunk_mask((CHUNK, TILE), bit)
        for j in range(len(parts)):
            if j & bit == 0:
                low, high = parts[j], parts[j + bit]
                parts[j] = jnp.where(keep, low, pltpu.roll(high, CHUNK * bit, 1))
                parts[j + bit] = jnp.where(keep, pltpu.roll(low, TILE - CHUNK * bit, 1), high)
    return parts


def windows(before, now):
    lanes = lax.broadcasted_iota(jnp.int32, now.shape, 1)
    none = jnp.zeros_like(now)
    first, second = [none if before is None else before], [now]
    for j in range(1, TILE // CHUNK):
        left = TILE - CHUNK * j
        moved = pltpu.roll(now, left, 1)
        older = none if before is None else pltpu.roll(before, left, 1)
        first.append(jnp.where(lanes < left, older, moved))
        second.append(moved)
    return jnp.concatenate(
        [jnp.concatenate(first, axis=0), jnp.concatenate(second, axis=0)], axis=1
    )


def beside(first, second):
    return jnp.concatenate([first, second], axis=1)


def above(*arrays):
    return jnp.concatenate(arrays, axis=0)


def apart(first, second):
    none = jnp.zeros_like(first)
    return above(beside(first, none), beside(none, second))


def lag_rows(chunks, shifted_rows, own_rows):
    wide = nn(above(*[chunks * own for own in own_rows]), shifted_rows)
    rows = lax.broadcasted_iota(jnp.int32, (2 * CHUNK, TILE), 0) % CHUNK
    lanes = lax.broadcasted_iota(jnp.int32, (2 * CHUNK, TILE), 1)
    sums = jnp.where(lanes + rows < CHUNK, wide[:, TILE:], wide[:, :TILE])
    parts = []
    for start in (0, CHUNK):
        total = sums[start : start + 8]
        for turn in (8, 16, 24):
            total = total + pltpu.roll(sums[start + turn : start + turn + 8], turn, 1)
        parts.append(pltpu.roll(total, 0, 1, stride=1, stride_axis=0))
    return above(*parts).astype(BF16)


def now_and_before(now, before, rows, half):
    both = beside(now, before)
    pieces = []
    for g in range(0, PACK, 2):
        circs = beside(*[circulant(rows[h : h + 1, :]) for h in (g, g + 1)])
        w_now = circs * half
        wide = nn(both[g * LANES : (g + 2) * LANES, :], above(w_now, circs - w_now))
        pieces += [wide[:LANES, :TILE], wide[LANES:, TILE:]]
    return jnp.concatenate(pieces, axis=0)


def within_shard(array, rows, half):
    pieces = []
    for g in range(0, PACK, 4):
        weights = [
            beside(*[circulant(rows[h : h + 1, :]) for h in (k, k + 1)]) * half
            for k in (g, g + 2)
        ]
        parts = [array[k * LANES : (k + 2) * LANES, :] for k in (g, g + 2)]
        wide = nn(apart(*parts), above(*weights))
        for k in range(4):
            column_at = (k % 2) * TILE
            pieces.append(wide[k * LANES : (k + 1) * LANES, column_at : column_at + TILE])
    return jnp.concatenate(pieces, axis=0)


def block_groups(at, blocks, block):
    rows, cols = iotas()
    return cols == rows // LANES + (at * blocks + block) * PACK


def gate_kernel(query, key, product, held, made, arrived, left):
    size = held.shape[1] // STEPS

    def fetch(array, step):
        span = pl.ds(step * size, size)
        return pltpu.make_async_copy(
            (query, key)[array].at[span, :], held.at[array, span, :], arrived.at[array, step]
        )

    def store(step):
        span = pl.ds(step * size, size)
        return pltpu.make_async_copy(made.at[span, :], product.at[span, :], left.at[step])

    for step in range(STEPS):
        for array in range(2):
            fetch(array, step).start()
    for step in range(STEPS):
        for array in range(2):
            fetch(array, step).wait()
        span = pl.ds(step * size, size)
        made[span, :] = held[0, span, :] * held[1, span, :]
        store(step).start()
    for step in range(STEPS):
        store(step).wait()


def state_kernel(grad, value, rate, state):
    rows, cols = iotas()
    offsets = cols.astype(F32)
    mask = rows // LANES == cols // LANES
    at = pl.program_id(0)
    blocks = state.shape[0]
    for block in range(blocks):
        span = pl.ds(block * TILE, TILE)
        rates = column(rate[...], block_groups(at, blocks, block))
        powers = jnp.exp(-rates * offsets).astype(BF16)
        dz2 = grad[span, :] * value[span, :]
        state[block] = squeeze_groups(nt(powers, dz2), mask).astype(BF16)


def table_kernel(
    rate, residue, filters, to_next, after, to_end, power, taps, turned, mr_turned, wide_rate
):
    rows, cols = iotas()
    mask = rows // LANES == cols // LANES
    offsets = cols.astype(F32)
    lags = ((CHUNK - 1 - cols) % TILE).astype(F32)
    at = pl.program_id(0)
    blocks = power.shape[0] // TILE
    coeffs = residue[...] * jnp.sqrt(one_minus_exp(2.0 * rate[...]))
    sums = []
    for block in range(blocks):
        span = pl.ds(block * TILE, TILE)
        own = block_groups(at, blocks, block)
        rates = column(rate[...], own)
        scale = column(coeffs, own)
        wide_rate[block] = squeeze_groups(jnp.broadcast_to(rates, (TILE, TILE)), mask)
        powers = jnp.exp(-rates * offsets)
        scaled = powers * scale
        ends = jnp.exp(-rates * (TILE - 1 - offsets))
        power[span, :] = jnp.exp(-rates * lags).astype(BF16)
        to_end[span, :] = ends.astype(BF16)
        after[span, :] = scaled.astype(BF16)
        to_next[span, :] = (ends * scale).astype(BF16)
        sums.append(jnp.sum(scaled.reshape(PACK, LANES, TILE), axis=1))
    taps[...] = above(*sums)
    turned[...] = nn(above(*sums).astype(BF16), reversal())
    mr_turned[...] = nn(filters[...], reversal())


def spans(array):
    return [pl.ds(block * TILE, TILE) for block in range(array.shape[0] // TILE)]


def group_rows(table, block):
    return table[pl.ds(block * PACK, PACK), :]


def local_kernel(grad, value, turned, du2):
    rows, cols = iotas()
    lower = ones_where(rows >= cols)
    lower_half = beside(lower, lower)
    results = [
        within_shard(grad[span, :] * value[span, :], group_rows(turned, block), lower_half)
        for block, span in enumerate(spans(grad))
    ]
    for span, result in zip(spans(grad), results):
        du2[span, :] = result


def middle_kernel(states, local, to_next, li_key, value, before, dz1, du2):
    rows, cols = iotas()
    mask = rows // LANES == cols // LANES
    wides = [spread_groups(states[block], mask).T.astype(BF16) for block in range(states.shape[0])]
    totals = [
        local[span, :] + nn(wide, to_next[span, :]) for span, wide in zip(spans(local), wides)
    ]
    for span, total in zip(spans(local), totals):
        du2[span, :] = total
        dy1 = total * li_key[span, :].astype(F32)
        dz1[span, :] = (dy1 * value[span, :].astype(F32)).astype(BF16)


def forward_kernel(before, now, filters, value, li_key, to_end, z1, u2, state):
    rows, cols = iotas()
    mask = rows // LANES == cols // LANES
    upper = ones_where(cols >= rows)
    upper_half = beside(upper, upper)
    results = [
        now_and_before(
            now[span, :], before[span, :], group_rows(filters, block).astype(F32), upper_half
        )
        for block, span in enumerate(spans(now))
    ]
    halves = []
    for span, result in zip(spans(now), results):
        y1 = (value[span, :].astype(F32) * result).astype(BF16).astype(F32)
        halves.append((y1 * li_key[span, :].astype(F32)).astype(BF16))
    ends = [nt(to_end[span, :], half) for span, half in zip(spans(now), halves)]
    for block, span in enumerate(spans(now)):
        z1[span, :] = results[block]
        u2[span, :] = halves[block]
        state[block] = squeeze_groups(ends[block], mask).astype(BF16)


def sums_kernel(
    before, now, u2, dz1, grad, li_value, power, state, after_shard, rate,
    packed, filter_sums, within_sums, across_sums,
):
    rows, cols = iotas()
    turn = ones_where(cols == rows - rows % CHUNK + (CHUNK - 1 - rows % CHUNK))
    lanes = lax.broadcasted_iota(jnp.int32, (CHUNK, TILE), 1)
    own_rows = [ones_where((lanes // LANES) % 2 == i) for i in range(2)]
    at = pl.program_id(0)
    blocks = now.shape[0] // TILE

    @pl.when(at == 0)
    def _():
        within_sums[...] = jnp.zeros_like(within_sums)
        across_sums[...] = jnp.zeros_like(across_sums)

    eights = ones_where(
        lax.broadcasted_iota(jnp.int32, (2 * PACK, TILE), 1) // 8
        == lax.broadcasted_iota(jnp.int32, (2 * PACK, TILE), 0)
    )
    turned = []
    for span in spans(now):
        dz2 = grad[span, :] * li_value[span, :]
        turned.append(nt(turn, above(dz1[span, :], dz2)).astype(BF16))
    chunks = [(pair_chunks(each[:, :TILE]), pair_chunks(each[:, TILE:])) for each in turned]
    lags, energies = [], []
    for block in range(blocks):
        lag, energy = [], []
        for p in range(TILE // CHUNK):
            pair = pl.ds(block * TILE + p * CHUNK, CHUNK)
            older, newer = before[pair, :], now[pair, :]
            lag.append(lag_rows(chunks[block][0][p], windows(older, newer), own_rows))
            energy.append(lag_rows(chunks[block][1][p], windows(None, u2[pair, :]), own_rows))
        both = nn(eights, above(*lag, *energy))
        lags.append(both[:PACK])
        energies.append(above(*[both[PACK:].astype(BF16)] * LANES))
    within, across = jnp.zeros((LANES, TILE), F32), jnp.zeros((LANES, TILE), F32)
    for block, span in enumerate(spans(now)):
        own = block_groups(at, blocks, block)
        within = within + squeeze_groups(nt(power[span, :], energies[block]), own)
        crossing = state[block].astype(F32) * after_shard[block]
        across = across + nn(crossing.astype(BF16), ones_where(own))
        packed[at * blocks + block] = state[block]
    few = blocks * PACK
    filter_sums[pl.ds(pl.multiple_of(at * few, few), few), :] = above(*lags)
    within_sums[...] += within
    across_sums[...] += across

    steps = filter_sums.shape[0] // few

    @pl.when(at == steps - 1)
    def _():
        place = ones_where((rows + cols) % TILE == CHUNK - 1)
        sums = nn(filter_sums[...].astype(BF16), place).astype(BF16)
        for chunk in range(filter_sums.shape[0] // LANES):
            packed[steps * blocks + chunk] = sums[chunk * LANES : (chunk + 1) * LANES]
        gains = jnp.sqrt(one_minus_exp(2.0 * rate[...]))
        total = gains * (within_sums[...] + across_sums[...])
        packed[steps * blocks + filter_sums.shape[0] // LANES] = total.astype(BF16)


def within_kernel(
    bits, u2, taps, wide_rate, z1, du2, value, li_key, later,
    z2, grad_value, grad_key, zeros, *weights,
):
    zeros[...] = jnp.zeros_like(zeros)
    place = lax.axis_index("seq")
    rates = wide_rate[...]
    weights = list(weights)
    for bit in bits:
        high = (place & bit) != 0
        passed = TILE * (place & (bit - 1)) + 1
        reach = jnp.exp(-rates * passed.astype(F32))
        weights.pop(0)[...] = jnp.where(high, reach, 0.0)
        if bit != bits[-1]:
            run = jnp.exp(-rates * (TILE * bit))
            one = jnp.ones_like(run)
            weights.pop(0)[...] = jnp.where(high, run, one)
            weights.pop(0)[...] = jnp.where(high, one, run)
    rows, cols = iotas()
    upper = ones_where(cols >= rows)
    upper_half = beside(upper, upper)
    results = [
        within_shard(u2[span, :], group_rows(taps, block), upper_half)
        for block, span in enumerate(spans(u2))
    ]
    for span, result in zip(spans(u2), results):
        z2[span, :] = result
        z1_here, du2_here = z1[span, :], du2[span, :]
        y1 = (value[span, :].astype(F32) * z1_here).astype(BF16).astype(F32)
        grad_key[span, :] = (du2_here * y1).astype(BF16)
        grad_value[span, :] = (du2_here * li_key[span, :].astype(F32) * z1_here).astype(BF16)


def last_kernel(half, other, grad_filter, grad_residue):
    chunks = half.shape[0] - 1
    for chunk in range(chunks):
        grad_filter[pl.ds(chunk * LANES, LANES), :] = half[chunk].astype(F32) + other[chunk].astype(F32)
    grad_residue[...] = half[chunks].astype(F32) + other[chunks].astype(F32)


def product_kernel(dz1, later, turned, query, key, grad_query, grad_key, nothing):
    nothing[...] = jnp.zeros_like(nothing)
    rows, cols = iotas()
    lower = ones_where(rows >= cols)
    lower_half = beside(lower, lower)
    results = [
        now_and_before(
            dz1[span, :], later[span, :], group_rows(turned, block), lower_half
        )
        for block, span in enumerate(spans(dz1))
    ]
    for span, du1 in zip(spans(dz1), results):
        grad_query[span, :] = (du1 * key[span, :].astype(F32)).astype(BF16)
        grad_key[span, :] = (du1 * query[span, :].astype(F32)).astype(BF16)


def value_kernel(states, after, z2, grad, grad_value):
    rows, cols = iotas()
    mask = rows // LANES == cols // LANES
    wides = [spread_groups(states[block], mask).T.astype(BF16) for block in range(states.shape[0])]
    totals = [z2[span, :] + nn(wide, after[span, :]) for span, wide in zip(spans(z2), wides)]
    for span, total in zip(spans(z2), totals):
        grad_value[span, :] = (grad[span, :].astype(F32) * total).astype(BF16)


def shifted(value, axis, steps):
    count = lax.axis_size(axis)
    first, last = max(0, -steps), min(count, count - steps)
    return lax.ppermute(value, axis, [(source, source + steps) for source in range(first, last)])


def swapped(value, axis, bit):
    count = lax.axis_size(axis)
    return lax.ppermute(value, axis, [(source, source ^ bit) for source in range(count)])


def scan_bits():
    count, bit, bits = lax.axis_size("seq"), 1, []
    assert count & (count - 1) == 0
    while bit < count:
        bits.append(bit)
        bit *= 2
    return bits


def per_device(
    mr_query, mr_key, mr_value, li_key, li_value, grad_out, mr_filter, li_residue, li_rate
):
    query, key, value, key_two, value_two, grad = (
        array[0] for array in (mr_query, mr_key, mr_value, li_key, li_value, grad_out)
    )
    groups, filt_len = mr_filter.shape
    channels, seq_local = query.shape
    assert filt_len == TILE and seq_local == TILE and groups <= TILE
    assert channels == groups * LANES and li_rate.shape[1] == LANES
    rows = channels // STEPS
    few = groups // STEPS
    spare = ((0, 0), (0, TILE - groups))
    rate = jnp.pad(li_rate.T, spare)
    residue = jnp.pad(li_residue.T, spare)

    blocks = channels // TILE

    wide = pl.BlockSpec((rows, TILE), lambda i: (i, 0))
    table = pl.BlockSpec((few, TILE), lambda i: (i, 0))
    chunk = pl.BlockSpec((blocks // STEPS, LANES, TILE), lambda i: (i, 0, 0))
    modes = pl.BlockSpec((LANES, TILE), lambda i: (0, 0))
    distant = pl.BlockSpec(memory_space=pltpu.HBM)
    anywhere = pl.BlockSpec(memory_space=pl.ANY)
    wide_half = jax.ShapeDtypeStruct((channels, TILE), BF16)
    wide_full = jax.ShapeDtypeStruct((channels, TILE), F32)
    table_full = jax.ShapeDtypeStruct((groups, TILE), F32)
    chunk_half = jax.ShapeDtypeStruct((blocks, LANES, TILE), BF16)
    chunk_full = jax.ShapeDtypeStruct((blocks, LANES, TILE), F32)

    def call(kernel, name, in_specs, out_specs, out_shape, scratch=(), grid=STEPS, limit=VMEM_LIMIT, work=0):
        return pl.pallas_call(
            kernel,
            grid=(grid,),
            in_specs=in_specs,
            out_specs=out_specs,
            out_shape=out_shape,
            scratch_shapes=scratch,
            name=name,
            cost_estimate=pl.CostEstimate(
                flops=2 * work * channels * TILE * TILE, bytes_accessed=1, transcendentals=0
            ),
            compiler_params=pltpu.CompilerParams(vmem_limit_bytes=limit),
        )

    def whole(leaf):
        return pl.BlockSpec(leaf.shape, lambda i: (0,) * len(leaf.shape))

    def twice(spec):
        return pl.BlockSpec((2 * spec.block_shape[0],) + spec.block_shape[1:], spec.index_map)

    (product,) = call(
        gate_kernel, "gate", [distant] * 2, [distant], [wide_half],
        [
            pltpu.VMEM((2, channels, TILE), BF16), pltpu.VMEM((channels, TILE), BF16),
            pltpu.SemaphoreType.DMA((2, STEPS)), pltpu.SemaphoreType.DMA((STEPS,)),
        ],
        grid=1, limit=60 * 1024 * 1024,
    )(query, key)
    product_before = shifted(product, "seq", 1)

    (back,) = call(state_kernel, "state", [wide, wide, modes], [chunk], [chunk_half])(
        grad, value_two, rate
    )

    later_backs = [shifted(back, "seq", -gap) for gap in range(1, lax.axis_size("seq"))]
    to_next, after, to_end, power, taps, turned, mr_turned, wide_rate = call(
        table_kernel, "table", [modes, modes, table], [wide] * 4 + [table] * 3 + [chunk],
        [wide_half] * 4 + [table_full] * 3 + [chunk_full],
    )(rate, residue, mr_filter)
    fade = jnp.exp(-TILE * wide_rate)
    after_shard = later_backs[-1].astype(F32)
    for other in later_backs[-2::-1]:
        after_shard = other.astype(F32) + fade * after_shard
    after_shard = after_shard * jnp.exp(-wide_rate)

    (du2_local,) = call(
        local_kernel, "local", [wide, wide, table], [wide], [wide_full]
    )(
        grad, value_two, turned
    )

    dz1, du2 = call(
        middle_kernel, "middle", [chunk, wide, wide, wide, wide, anywhere], [wide, wide],
        [wide_half, wide_full],
    )(after_shard, du2_local, to_next, key_two, value, product_before)
    dz1_later = shifted(dz1, "seq", -1)

    z1, u2, state = call(
        forward_kernel, "forward",
        [wide, wide, table, wide, wide, wide],
        [wide, wide, chunk], [wide_full, wide_half, chunk_half],
    )(product_before, product, mr_filter, value, key_two, to_end)

    filter_chunks = groups // LANES
    packed_shape = jax.ShapeDtypeStruct((blocks + filter_chunks + 1, LANES, TILE), BF16)
    (packed,) = call(
        sums_kernel, "sums",
        [twice(wide)] * 7 + [twice(chunk), twice(chunk), modes],
        [whole(packed_shape)], [packed_shape],
        [pltpu.VMEM((groups, TILE), F32)] + [pltpu.VMEM((LANES, TILE), F32)] * 2,
        grid=STEPS // 2,
    )(product_before, product, u2, dz1, grad, value_two, power, state, after_shard, rate)

    bits = scan_bits()
    few_full = jax.ShapeDtypeStruct((filter_chunks + 1, LANES, TILE), F32)
    factors = 3 * len(bits) - 2
    z2, grad_mr_value, grad_li_key, within_zeros, *weights = call(
        functools.partial(within_kernel, bits), "within",
        [wide, table, chunk, wide, wide, wide, wide, anywhere],
        [wide, wide, wide, whole(few_full)] + [chunk] * factors,
        [wide_full, wide_half, wide_half, few_full] + [chunk_full] * factors,
    )(u2, taps, wide_rate, z1, du2, value, key_two, dz1_later)

    grad_query, grad_key, product_zeros = call(
        product_kernel, "product",
        [wide, wide, table, wide, wide], [wide, wide, whole(few_full)],
        [wide_half, wide_half, few_full],
    )(dz1, dz1_later, mr_turned, query, key)

    zeros = [within_zeros, product_zeros]
    before_shard = jnp.zeros(back.shape, F32)
    for bit in bits:
        other = swapped(packed, "seq", bit)
        sums = packed[blocks:].astype(F32) + other[blocks:].astype(F32)
        if zeros:
            sums = sums + zeros.pop(0)
        mine, theirs = packed[:blocks].astype(F32), other[:blocks].astype(F32)
        before_shard = before_shard + weights.pop(0) * theirs
        if bit != bits[-1]:
            total = weights.pop(0) * theirs + weights.pop(0) * mine
            packed = jnp.concatenate([total.astype(BF16), sums.astype(BF16)], axis=0)
    sums = sums.astype(BF16)

    assert lax.axis_size("dp") == 2
    partner = swapped(sums, "dp", 1)
    (grad_li_value,) = call(
        value_kernel, "value", [chunk, wide, wide, wide], [wide], [wide_half]
    )(before_shard, after, z2, grad)

    residue_full = jax.ShapeDtypeStruct((LANES, TILE), F32)
    grad_filter, grad_residue = call(
        last_kernel, "last", [whole(sums)] * 2,
        [whole(table_full), whole(residue_full)], [table_full, residue_full], grid=1,
    )(sums, partner)
    return (
        grad_query[None],
        grad_key[None],
        grad_mr_value[None],
        grad_li_key[None],
        grad_li_value[None],
        grad_filter,
        grad_residue[:, :groups].T,
    )


def solution(mesh):
    streams = (P("dp", "chan", "seq"),)
    tables = (P("chan", None),)
    return jax.shard_map(
        per_device,
        mesh=mesh,
        in_specs=streams * 6 + tables * 3,
        out_specs=streams * 5 + tables * 2,
        check_vma=False,
    )
```

```python
import functools

import jax
import jax.numpy as jnp
from jax import lax
from jax.experimental import pallas as pl
from jax.experimental.pallas import tpu as pltpu
from jax.sharding import PartitionSpec as P

F32 = jnp.float32
BF16 = jnp.bfloat16
TILE = 128
LANES = 16
PACK = TILE // LANES
CHUNK = 32
STEPS = 4
VMEM_LIMIT = 24 * 1024 * 1024


def nn(lhs, rhs):
    return lax.dot_general(lhs, rhs, (((1,), (0,)), ((), ())), preferred_element_type=F32)


def nt(lhs, rhs):
    return lax.dot_general(lhs, rhs, (((1,), (1,)), ((), ())), preferred_element_type=F32)


def iotas():
    rows = lax.broadcasted_iota(jnp.int32, (TILE, TILE), 0)
    cols = lax.broadcasted_iota(jnp.int32, (TILE, TILE), 1)
    return rows, cols


def ones_where(mask):
    return jnp.where(mask, 1.0, 0.0).astype(BF16)


def column(turned, mask):
    wide = jnp.concatenate([turned] * PACK, axis=0)
    return jnp.sum(jnp.where(mask, wide, 0.0), axis=1, keepdims=True)


def squeeze_groups(wide, mask):
    kept = jnp.where(mask, wide, 0.0)
    total = kept[:LANES]
    for g in range(1, PACK):
        total = total + kept[g * LANES : (g + 1) * LANES]
    return total


def spread_groups(narrow, mask):
    return jnp.where(mask, jnp.concatenate([narrow] * PACK, axis=0), 0.0)


def circulant(row):
    base = jnp.broadcast_to(row, (LANES, TILE))
    base = pltpu.roll(base, 0, 1, stride=1, stride_axis=0).astype(BF16)
    return jnp.concatenate(
        [base] + [pltpu.roll(base, LANES * j, 1) for j in range(1, PACK)], axis=0
    )


def reversal():
    rows, cols = iotas()
    return ones_where((rows + cols) % TILE == 0)


def one_minus_exp(value):
    series = jnp.full_like(value, 1.0)
    for order in (7, 6, 5, 4, 3, 2):
        series = 1.0 - value * series / order
    return jnp.where(value < 0.125, value * series, 1.0 - jnp.exp(-value))


def chunk_mask(shape, bit):
    return (lax.broadcasted_iota(jnp.int32, shape, 1) // CHUNK) & bit == 0


def pair_chunks(turned):
    parts = [turned[CHUNK * j : CHUNK * (j + 1), :] for j in range(TILE // CHUNK)]
    for bit in (1, 2):
        keep = chunk_mask((CHUNK, TILE), bit)
        for j in range(len(parts)):
            if j & bit == 0:
                low, high = parts[j], parts[j + bit]
                parts[j] = jnp.where(keep, low, pltpu.roll(high, CHUNK * bit, 1))
                parts[j + bit] = jnp.where(keep, pltpu.roll(low, TILE - CHUNK * bit, 1), high)
    return parts


def windows(before, now):
    lanes = lax.broadcasted_iota(jnp.int32, now.shape, 1)
    none = jnp.zeros_like(now)
    first, second = [none if before is None else before], [now]
    for j in range(1, TILE // CHUNK):
        left = TILE - CHUNK * j
        moved = pltpu.roll(now, left, 1)
        older = none if before is None else pltpu.roll(before, left, 1)
        first.append(jnp.where(lanes < left, older, moved))
        second.append(moved)
    return jnp.concatenate(
        [jnp.concatenate(first, axis=0), jnp.concatenate(second, axis=0)], axis=1
    )


def beside(first, second):
    return jnp.concatenate([first, second], axis=1)


def above(*arrays):
    return jnp.concatenate(arrays, axis=0)


def apart(first, second):
    none = jnp.zeros_like(first)
    return above(beside(first, none), beside(none, second))


def lag_rows(chunks, shifted_rows, own_rows):
    wide = nn(above(*[chunks * own for own in own_rows]), shifted_rows)
    rows = lax.broadcasted_iota(jnp.int32, (2 * CHUNK, TILE), 0) % CHUNK
    lanes = lax.broadcasted_iota(jnp.int32, (2 * CHUNK, TILE), 1)
    sums = jnp.where(lanes + rows < CHUNK, wide[:, TILE:], wide[:, :TILE])
    parts = []
    for start in (0, CHUNK):
        part = pltpu.roll(sums[start : start + CHUNK], 0, 1, stride=1, stride_axis=0)
        parts.append(part[:8] + part[8:16] + part[16:24] + part[24:])
    return above(*parts).astype(BF16)


def now_and_before(now, before, rows, half):
    both = beside(now, before)
    pieces = []
    for g in range(0, PACK, 2):
        circs = beside(*[circulant(rows[h : h + 1, :]) for h in (g, g + 1)])
        w_now = circs * half
        wide = nn(both[g * LANES : (g + 2) * LANES, :], above(w_now, circs - w_now))
        pieces += [wide[:LANES, :TILE], wide[LANES:, TILE:]]
    return jnp.concatenate(pieces, axis=0)


def within_shard(array, rows, half):
    pieces = []
    for g in range(0, PACK, 4):
        weights = [
            beside(*[circulant(rows[h : h + 1, :]) for h in (k, k + 1)]) * half
            for k in (g, g + 2)
        ]
        parts = [array[k * LANES : (k + 2) * LANES, :] for k in (g, g + 2)]
        wide = nn(apart(*parts), above(*weights))
        for k in range(4):
            column_at = (k % 2) * TILE
            pieces.append(wide[k * LANES : (k + 1) * LANES, column_at : column_at + TILE])
    return jnp.concatenate(pieces, axis=0)


def block_groups(at, blocks, block):
    rows, cols = iotas()
    return cols == rows // LANES + (at * blocks + block) * PACK


def gate_kernel(query, key, product, held, made, arrived, left):
    size = held.shape[1] // STEPS

    def fetch(array, step):
        span = pl.ds(step * size, size)
        return pltpu.make_async_copy(
            (query, key)[array].at[span, :], held.at[array, span, :], arrived.at[array, step]
        )

    def store(step):
        span = pl.ds(step * size, size)
        return pltpu.make_async_copy(made.at[span, :], product.at[span, :], left.at[step])

    for step in range(STEPS):
        for array in range(2):
            fetch(array, step).start()
    for step in range(STEPS):
        for array in range(2):
            fetch(array, step).wait()
        span = pl.ds(step * size, size)
        made[span, :] = held[0, span, :] * held[1, span, :]
        store(step).start()
    for step in range(STEPS):
        store(step).wait()


def state_kernel(grad, value, rate, state):
    rows, cols = iotas()
    offsets = cols.astype(F32)
    mask = rows // LANES == cols // LANES
    at = pl.program_id(0)
    blocks = state.shape[0]
    for block in range(blocks):
        span = pl.ds(block * TILE, TILE)
        rates = column(rate[...], block_groups(at, blocks, block))
        powers = jnp.exp(-rates * offsets).astype(BF16)
        dz2 = grad[span, :] * value[span, :]
        state[block] = squeeze_groups(nt(powers, dz2), mask).astype(BF16)


def table_kernel(
    rate, residue, filters, to_next, after, to_end, power, taps, turned, mr_turned, wide_rate
):
    rows, cols = iotas()
    mask = rows // LANES == cols // LANES
    offsets = cols.astype(F32)
    lags = ((CHUNK - 1 - cols) % TILE).astype(F32)
    at = pl.program_id(0)
    blocks = power.shape[0] // TILE
    coeffs = residue[...] * jnp.sqrt(one_minus_exp(2.0 * rate[...]))
    sums = []
    for block in range(blocks):
        span = pl.ds(block * TILE, TILE)
        own = block_groups(at, blocks, block)
        rates = column(rate[...], own)
        scale = column(coeffs, own)
        wide_rate[block] = squeeze_groups(jnp.broadcast_to(rates, (TILE, TILE)), mask)
        powers = jnp.exp(-rates * offsets)
        scaled = powers * scale
        ends = jnp.exp(-rates * (TILE - 1 - offsets))
        power[span, :] = jnp.exp(-rates * lags).astype(BF16)
        to_end[span, :] = ends.astype(BF16)
        after[span, :] = scaled.astype(BF16)
        to_next[span, :] = (ends * scale).astype(BF16)
        sums.append(jnp.sum(scaled.reshape(PACK, LANES, TILE), axis=1))
    taps[...] = above(*sums)
    turned[...] = nn(above(*sums).astype(BF16), reversal())
    mr_turned[...] = nn(filters[...], reversal())


def spans(array):
    return [pl.ds(block * TILE, TILE) for block in range(array.shape[0] // TILE)]


def group_rows(table, block):
    return table[pl.ds(block * PACK, PACK), :]


def local_kernel(grad, value, turned, du2):
    rows, cols = iotas()
    lower = ones_where(rows >= cols)
    lower_half = beside(lower, lower)
    results = [
        within_shard(grad[span, :] * value[span, :], group_rows(turned, block), lower_half)
        for block, span in enumerate(spans(grad))
    ]
    for span, result in zip(spans(grad), results):
        du2[span, :] = result


def middle_kernel(states, local, to_next, li_key, value, before, dz1, du2):
    rows, cols = iotas()
    mask = rows // LANES == cols // LANES
    wides = [spread_groups(states[block], mask).T.astype(BF16) for block in range(states.shape[0])]
    totals = [
        local[span, :] + nn(wide, to_next[span, :]) for span, wide in zip(spans(local), wides)
    ]
    for span, total in zip(spans(local), totals):
        du2[span, :] = total
        dy1 = total * li_key[span, :].astype(F32)
        dz1[span, :] = (dy1 * value[span, :].astype(F32)).astype(BF16)


def forward_kernel(
    before, now, filters, value, li_key, to_end, dz1, grad, li_value, power, after_shard, rate,
    z1, u2, packed, filter_sums, within_sums, across_sums,
):
    rows, cols = iotas()
    mask = rows // LANES == cols // LANES
    upper = ones_where(cols >= rows)
    upper_half = beside(upper, upper)
    turn = ones_where(cols == rows - rows % CHUNK + (CHUNK - 1 - rows % CHUNK))
    lanes = lax.broadcasted_iota(jnp.int32, (CHUNK, TILE), 1)
    own_rows = [ones_where((lanes // LANES) % 2 == i) for i in range(2)]
    eights = ones_where(
        lax.broadcasted_iota(jnp.int32, (2 * PACK, TILE), 1) // 8
        == lax.broadcasted_iota(jnp.int32, (2 * PACK, TILE), 0)
    )
    at = pl.program_id(0)
    blocks = now.shape[0] // TILE

    @pl.when(at == 0)
    def _():
        within_sums[...] = jnp.zeros_like(within_sums)
        across_sums[...] = jnp.zeros_like(across_sums)

    turned = []
    for span in spans(now):
        dz2 = grad[span, :] * li_value[span, :]
        turned.append(nt(turn, above(dz1[span, :], dz2)).astype(BF16))
    chunks = [(pair_chunks(each[:, :TILE]), pair_chunks(each[:, TILE:])) for each in turned]
    results = [
        now_and_before(
            now[span, :], before[span, :], group_rows(filters, block).astype(F32), upper_half
        )
        for block, span in enumerate(spans(now))
    ]
    halves = []
    for span, result in zip(spans(now), results):
        z1[span, :] = result
        y1 = (value[span, :].astype(F32) * result).astype(BF16).astype(F32)
        halves.append((y1 * li_key[span, :].astype(F32)).astype(BF16))
        u2[span, :] = halves[-1]
    ends = [nt(to_end[span, :], half) for span, half in zip(spans(now), halves)]

    lags = []
    for block in range(blocks):
        lag, energy = [], []
        for p in range(TILE // CHUNK):
            pair = pl.ds(block * TILE + p * CHUNK, CHUNK)
            older, newer = before[pair, :], now[pair, :]
            later = halves[block][p * CHUNK : (p + 1) * CHUNK]
            lag.append(lag_rows(chunks[block][0][p], windows(older, newer), own_rows))
            energy.append(lag_rows(chunks[block][1][p], windows(None, later), own_rows))
        lags.append(above(*lag, *energy))
    lags = [nn(eights, each) for each in lags]
    within, across = jnp.zeros((LANES, TILE), F32), jnp.zeros((LANES, TILE), F32)
    for block, span in enumerate(spans(now)):
        own = block_groups(at, blocks, block)
        energies = above(*[lags[block][PACK:].astype(BF16)] * LANES)
        within = within + squeeze_groups(nt(power[span, :], energies), own)
        state = squeeze_groups(ends[block], mask).astype(BF16)
        crossing = state.astype(F32) * after_shard[block]
        across = across + nn(crossing.astype(BF16), ones_where(own))
        packed[at * blocks + block] = state
    lags = [each[:PACK] for each in lags]
    few = blocks * PACK
    filter_sums[pl.ds(pl.multiple_of(at * few, few), few), :] = above(*lags)
    within_sums[...] += within
    across_sums[...] += across

    steps = filter_sums.shape[0] // few

    @pl.when(at == steps - 1)
    def _():
        place = ones_where((rows + cols) % TILE == CHUNK - 1)
        sums = nn(filter_sums[...].astype(BF16), place).astype(BF16)
        for chunk in range(filter_sums.shape[0] // LANES):
            packed[steps * blocks + chunk] = sums[chunk * LANES : (chunk + 1) * LANES]
        gains = jnp.sqrt(one_minus_exp(2.0 * rate[...]))
        total = gains * (within_sums[...] + across_sums[...])
        packed[steps * blocks + filter_sums.shape[0] // LANES] = total.astype(BF16)


def within_kernel(
    bits, u2, taps, wide_rate, z1, du2, value, li_key, later,
    z2, grad_value, grad_key, zeros, *weights,
):
    zeros[...] = jnp.zeros_like(zeros)
    place = lax.axis_index("seq")
    rates = wide_rate[...]
    weights = list(weights)
    for bit in bits:
        high = (place & bit) != 0
        passed = TILE * (place & (bit - 1)) + 1
        reach = jnp.exp(-rates * passed.astype(F32))
        weights.pop(0)[...] = jnp.where(high, reach, 0.0)
        if bit != bits[-1]:
            run = jnp.exp(-rates * (TILE * bit))
            one = jnp.ones_like(run)
            weights.pop(0)[...] = jnp.where(high, run, one)
            weights.pop(0)[...] = jnp.where(high, one, run)
    rows, cols = iotas()
    upper = ones_where(cols >= rows)
    upper_half = beside(upper, upper)
    results = [
        within_shard(u2[span, :], group_rows(taps, block), upper_half)
        for block, span in enumerate(spans(u2))
    ]
    for span, result in zip(spans(u2), results):
        z2[span, :] = result
        z1_here, du2_here = z1[span, :], du2[span, :]
        y1 = (value[span, :].astype(F32) * z1_here).astype(BF16).astype(F32)
        grad_key[span, :] = (du2_here * y1).astype(BF16)
        grad_value[span, :] = (du2_here * li_key[span, :].astype(F32) * z1_here).astype(BF16)


def last_kernel(half, other, grad_filter, grad_residue):
    chunks = half.shape[0] - 1
    for chunk in range(chunks):
        grad_filter[pl.ds(chunk * LANES, LANES), :] = half[chunk].astype(F32) + other[chunk].astype(F32)
    grad_residue[...] = half[chunks].astype(F32) + other[chunks].astype(F32)


def product_kernel(dz1, later, turned, query, key, grad_query, grad_key, nothing):
    nothing[...] = jnp.zeros_like(nothing)
    rows, cols = iotas()
    lower = ones_where(rows >= cols)
    lower_half = beside(lower, lower)
    results = [
        now_and_before(
            dz1[span, :], later[span, :], group_rows(turned, block), lower_half
        )
        for block, span in enumerate(spans(dz1))
    ]
    for span, du1 in zip(spans(dz1), results):
        grad_query[span, :] = (du1 * key[span, :].astype(F32)).astype(BF16)
        grad_key[span, :] = (du1 * query[span, :].astype(F32)).astype(BF16)


def value_kernel(states, after, z2, grad, grad_value, made, left):
    rows, cols = iotas()
    mask = rows // LANES == cols // LANES
    at = pl.program_id(0)
    size = z2.shape[0]

    def store(step):
        span = pl.ds(pl.multiple_of(step * size, size), size)
        return pltpu.make_async_copy(made.at[span, :], grad_value.at[span, :], left.at[step])

    wides = [spread_groups(states[block], mask).T.astype(BF16) for block in range(states.shape[0])]
    totals = [z2[span, :] + nn(wide, after[span, :]) for span, wide in zip(spans(z2), wides)]
    for block, (span, total) in enumerate(zip(spans(z2), totals)):
        here = pl.ds(pl.multiple_of(at * size + block * TILE, TILE), TILE)
        made[here, :] = (grad[span, :].astype(F32) * total).astype(BF16)
    store(at).start()

    @pl.when(at == STEPS - 1)
    def _():
        for step in range(STEPS):
            store(step).wait()


def shifted(value, axis, steps):
    count = lax.axis_size(axis)
    first, last = max(0, -steps), min(count, count - steps)
    return lax.ppermute(value, axis, [(source, source + steps) for source in range(first, last)])


def swapped(value, axis, bit):
    count = lax.axis_size(axis)
    return lax.ppermute(value, axis, [(source, source ^ bit) for source in range(count)])


def scan_bits():
    count, bit, bits = lax.axis_size("seq"), 1, []
    assert count & (count - 1) == 0
    while bit < count:
        bits.append(bit)
        bit *= 2
    return bits


def per_device(
    mr_query, mr_key, mr_value, li_key, li_value, grad_out, mr_filter, li_residue, li_rate
):
    query, key, value, key_two, value_two, grad = (
        array[0] for array in (mr_query, mr_key, mr_value, li_key, li_value, grad_out)
    )
    groups, filt_len = mr_filter.shape
    channels, seq_local = query.shape
    assert filt_len == TILE and seq_local == TILE and groups <= TILE
    assert channels == groups * LANES and li_rate.shape[1] == LANES
    rows = channels // STEPS
    few = groups // STEPS
    spare = ((0, 0), (0, TILE - groups))
    rate = jnp.pad(li_rate.T, spare)
    residue = jnp.pad(li_residue.T, spare)

    blocks = channels // TILE

    wide = pl.BlockSpec((rows, TILE), lambda i: (i, 0))
    table = pl.BlockSpec((few, TILE), lambda i: (i, 0))
    chunk = pl.BlockSpec((blocks // STEPS, LANES, TILE), lambda i: (i, 0, 0))
    modes = pl.BlockSpec((LANES, TILE), lambda i: (0, 0))
    distant = pl.BlockSpec(memory_space=pltpu.HBM)
    anywhere = pl.BlockSpec(memory_space=pl.ANY)
    wide_half = jax.ShapeDtypeStruct((channels, TILE), BF16)
    wide_full = jax.ShapeDtypeStruct((channels, TILE), F32)
    table_full = jax.ShapeDtypeStruct((groups, TILE), F32)
    chunk_half = jax.ShapeDtypeStruct((blocks, LANES, TILE), BF16)
    chunk_full = jax.ShapeDtypeStruct((blocks, LANES, TILE), F32)

    def call(kernel, name, in_specs, out_specs, out_shape, scratch=(), grid=STEPS, limit=VMEM_LIMIT, work=0):
        return pl.pallas_call(
            kernel,
            grid=(grid,),
            in_specs=in_specs,
            out_specs=out_specs,
            out_shape=out_shape,
            scratch_shapes=scratch,
            name=name,
            cost_estimate=pl.CostEstimate(
                flops=2 * work * channels * TILE * TILE, bytes_accessed=1, transcendentals=0
            ),
            compiler_params=pltpu.CompilerParams(vmem_limit_bytes=limit),
        )

    def whole(leaf):
        return pl.BlockSpec(leaf.shape, lambda i: (0,) * len(leaf.shape))

    def twice(spec):
        return pl.BlockSpec((2 * spec.block_shape[0],) + spec.block_shape[1:], spec.index_map)

    (product,) = call(
        gate_kernel, "gate", [distant] * 2, [distant], [wide_half],
        [
            pltpu.VMEM((2, channels, TILE), BF16), pltpu.VMEM((channels, TILE), BF16),
            pltpu.SemaphoreType.DMA((2, STEPS)), pltpu.SemaphoreType.DMA((STEPS,)),
        ],
        grid=1, limit=60 * 1024 * 1024,
    )(query, key)
    product_before = shifted(product, "seq", 1)

    (back,) = call(state_kernel, "state", [wide, wide, modes], [chunk], [chunk_half])(
        grad, value_two, rate
    )

    later_backs = [shifted(back, "seq", -gap) for gap in range(1, lax.axis_size("seq"))]
    to_next, after, to_end, power, taps, turned, mr_turned, wide_rate = call(
        table_kernel, "table", [modes, modes, table], [wide] * 4 + [table] * 3 + [chunk],
        [wide_half] * 4 + [table_full] * 3 + [chunk_full],
    )(rate, residue, mr_filter)
    fade = jnp.exp(-TILE * wide_rate)
    after_shard = later_backs[-1].astype(F32)
    for other in later_backs[-2::-1]:
        after_shard = other.astype(F32) + fade * after_shard
    after_shard = after_shard * jnp.exp(-wide_rate)

    (du2_local,) = call(
        local_kernel, "local", [wide, wide, table], [wide], [wide_full]
    )(
        grad, value_two, turned
    )

    dz1, du2 = call(
        middle_kernel, "middle", [chunk, wide, wide, wide, wide, anywhere], [wide, wide],
        [wide_half, wide_full],
    )(after_shard, du2_local, to_next, key_two, value, product_before)
    dz1_later = shifted(dz1, "seq", -1)

    filter_chunks = groups // LANES
    packed_shape = jax.ShapeDtypeStruct((blocks + filter_chunks + 1, LANES, TILE), BF16)
    z1, u2, packed = call(
        forward_kernel, "forward",
        [twice(spec) for spec in [wide, wide, table] + [wide] * 7 + [chunk]] + [modes],
        [twice(wide), twice(wide), whole(packed_shape)], [wide_full, wide_half, packed_shape],
        [pltpu.VMEM((groups, TILE), F32)] + [pltpu.VMEM((LANES, TILE), F32)] * 2,
        grid=STEPS // 2,
    )(
        product_before, product, mr_filter, value, key_two, to_end, dz1, grad, value_two, power,
        after_shard, rate,
    )

    bits = scan_bits()
    few_full = jax.ShapeDtypeStruct((filter_chunks + 1, LANES, TILE), F32)
    factors = 3 * len(bits) - 2
    z2, grad_mr_value, grad_li_key, within_zeros, *weights = call(
        functools.partial(within_kernel, bits), "within",
        [wide, table, chunk, wide, wide, wide, wide, anywhere],
        [wide, wide, wide, whole(few_full)] + [chunk] * factors,
        [wide_full, wide_half, wide_half, few_full] + [chunk_full] * factors,
    )(u2, taps, wide_rate, z1, du2, value, key_two, dz1_later)

    grad_query, grad_key, product_zeros = call(
        product_kernel, "product",
        [wide, wide, table, wide, wide], [wide, wide, whole(few_full)],
        [wide_half, wide_half, few_full],
    )(dz1, dz1_later, mr_turned, query, key)

    zeros = [within_zeros, product_zeros]
    before_shard = jnp.zeros(back.shape, F32)
    for bit in bits:
        other = swapped(packed, "seq", bit)
        sums = packed[blocks:].astype(F32) + other[blocks:].astype(F32)
        if zeros:
            sums = sums + zeros.pop(0)
        mine, theirs = packed[:blocks].astype(F32), other[:blocks].astype(F32)
        before_shard = before_shard + weights.pop(0) * theirs
        if bit != bits[-1]:
            total = weights.pop(0) * theirs + weights.pop(0) * mine
            packed = jnp.concatenate([total.astype(BF16), sums.astype(BF16)], axis=0)
    sums = sums.astype(BF16)

    assert lax.axis_size("dp") == 2
    partner = swapped(sums, "dp", 1)
    (grad_li_value,) = call(
        value_kernel, "value", [chunk, wide, wide, wide], [distant], [wide_half],
        [pltpu.VMEM((channels, TILE), BF16), pltpu.SemaphoreType.DMA((STEPS,))],
    )(before_shard, after, z2, grad)

    residue_full = jax.ShapeDtypeStruct((LANES, TILE), F32)
    grad_filter, grad_residue = call(
        last_kernel, "last", [whole(sums)] * 2,
        [whole(table_full), whole(residue_full)], [table_full, residue_full], grid=1,
    )(sums, partner)
    return (
        grad_query[None],
        grad_key[None],
        grad_mr_value[None],
        grad_li_key[None],
        grad_li_value[None],
        grad_filter,
        grad_residue[:, :groups].T,
    )


def solution(mesh):
    streams = (P("dp", "chan", "seq"),)
    tables = (P("chan", None),)
    return jax.shard_map(
        per_device,
        mesh=mesh,
        in_specs=streams * 6 + tables * 3,
        out_specs=streams * 5 + tables * 2,
        check_vma=False,
    )
```

```python
import functools

import jax
import jax.numpy as jnp
from jax import lax
from jax.experimental import pallas as pl
from jax.experimental.pallas import tpu as pltpu
from jax.sharding import PartitionSpec as P

F32 = jnp.float32
BF16 = jnp.bfloat16
TILE = 128
LANES = 16
PACK = TILE // LANES
CHUNK = 32
STEPS = 4
VMEM_LIMIT = 24 * 1024 * 1024


def nn(lhs, rhs):
    return lax.dot_general(lhs, rhs, (((1,), (0,)), ((), ())), preferred_element_type=F32)


def nt(lhs, rhs):
    return lax.dot_general(lhs, rhs, (((1,), (1,)), ((), ())), preferred_element_type=F32)


def iotas():
    rows = lax.broadcasted_iota(jnp.int32, (TILE, TILE), 0)
    cols = lax.broadcasted_iota(jnp.int32, (TILE, TILE), 1)
    return rows, cols


def ones_where(mask):
    return jnp.where(mask, 1.0, 0.0).astype(BF16)


def column(turned, mask):
    wide = jnp.concatenate([turned] * PACK, axis=0)
    return jnp.sum(jnp.where(mask, wide, 0.0), axis=1, keepdims=True)


def squeeze_groups(wide, mask):
    kept = jnp.where(mask, wide, 0.0)
    total = kept[:LANES]
    for g in range(1, PACK):
        total = total + kept[g * LANES : (g + 1) * LANES]
    return total


def spread_groups(narrow, mask):
    return jnp.where(mask, jnp.concatenate([narrow] * PACK, axis=0), 0.0)


def circulant(row):
    base = jnp.broadcast_to(row, (LANES, TILE))
    base = pltpu.roll(base, 0, 1, stride=1, stride_axis=0).astype(BF16)
    return jnp.concatenate(
        [base] + [pltpu.roll(base, LANES * j, 1) for j in range(1, PACK)], axis=0
    )


def reversal():
    rows, cols = iotas()
    return ones_where((rows + cols) % TILE == 0)


def one_minus_exp(value):
    series = jnp.full_like(value, 1.0)
    for order in (7, 6, 5, 4, 3, 2):
        series = 1.0 - value * series / order
    return jnp.where(value < 0.125, value * series, 1.0 - jnp.exp(-value))


def chunk_mask(shape, bit):
    return (lax.broadcasted_iota(jnp.int32, shape, 1) // CHUNK) & bit == 0


def pair_chunks(turned):
    parts = [turned[CHUNK * j : CHUNK * (j + 1), :] for j in range(TILE // CHUNK)]
    for bit in (1, 2):
        keep = chunk_mask((CHUNK, TILE), bit)
        for j in range(len(parts)):
            if j & bit == 0:
                low, high = parts[j], parts[j + bit]
                parts[j] = jnp.where(keep, low, pltpu.roll(high, CHUNK * bit, 1))
                parts[j + bit] = jnp.where(keep, pltpu.roll(low, TILE - CHUNK * bit, 1), high)
    return parts


def windows(before, now):
    lanes = lax.broadcasted_iota(jnp.int32, now.shape, 1)
    none = jnp.zeros_like(now)
    first, second = [none if before is None else before], [now]
    for j in range(1, TILE // CHUNK):
        left = TILE - CHUNK * j
        moved = pltpu.roll(now, left, 1)
        older = none if before is None else pltpu.roll(before, left, 1)
        first.append(jnp.where(lanes < left, older, moved))
        second.append(moved)
    return jnp.concatenate(
        [jnp.concatenate(first, axis=0), jnp.concatenate(second, axis=0)], axis=1
    )


def beside(first, second):
    return jnp.concatenate([first, second], axis=1)


def above(*arrays):
    return jnp.concatenate(arrays, axis=0)


def apart(first, second):
    none = jnp.zeros_like(first)
    return above(beside(first, none), beside(none, second))


def lag_rows(chunks, shifted_rows, own_rows):
    wide = nn(above(*[chunks * own for own in own_rows]), shifted_rows)
    rows = lax.broadcasted_iota(jnp.int32, (2 * CHUNK, TILE), 0) % CHUNK
    lanes = lax.broadcasted_iota(jnp.int32, (2 * CHUNK, TILE), 1)
    sums = jnp.where(lanes + rows < CHUNK, wide[:, TILE:], wide[:, :TILE])
    parts = []
    for start in (0, CHUNK):
        part = pltpu.roll(sums[start : start + CHUNK], 0, 1, stride=1, stride_axis=0)
        parts.append(part[:8] + part[8:16] + part[16:24] + part[24:])
    return above(*parts).astype(BF16)


def now_and_before(now, before, rows, half):
    both = beside(now, before)
    pieces = []
    for g in range(0, PACK, 2):
        circs = beside(*[circulant(rows[h : h + 1, :]) for h in (g, g + 1)])
        w_now = circs * half
        wide = nn(both[g * LANES : (g + 2) * LANES, :], above(w_now, circs - w_now))
        pieces += [wide[:LANES, :TILE], wide[LANES:, TILE:]]
    return jnp.concatenate(pieces, axis=0)


def within_shard(array, rows, half):
    pieces = []
    for g in range(0, PACK, 4):
        weights = [
            beside(*[circulant(rows[h : h + 1, :]) for h in (k, k + 1)]) * half
            for k in (g, g + 2)
        ]
        parts = [array[k * LANES : (k + 2) * LANES, :] for k in (g, g + 2)]
        wide = nn(apart(*parts), above(*weights))
        for k in range(4):
            column_at = (k % 2) * TILE
            pieces.append(wide[k * LANES : (k + 1) * LANES, column_at : column_at + TILE])
    return jnp.concatenate(pieces, axis=0)


def block_groups(at, blocks, block):
    rows, cols = iotas()
    return cols == rows // LANES + (at * blocks + block) * PACK


def gate_kernel(query, key, product, mark, held, made, arrived, left):
    mark[...] = jnp.zeros_like(mark)
    size = held.shape[1] // STEPS

    def fetch(array, step):
        span = pl.ds(step * size, size)
        return pltpu.make_async_copy(
            (query, key)[array].at[span, :], held.at[array, span, :], arrived.at[array, step]
        )

    def store(step):
        span = pl.ds(step * size, size)
        return pltpu.make_async_copy(made.at[span, :], product.at[span, :], left.at[step])

    for step in range(STEPS):
        for array in range(2):
            fetch(array, step).start()
    for step in range(STEPS):
        for array in range(2):
            fetch(array, step).wait()
        span = pl.ds(step * size, size)
        made[span, :] = held[0, span, :] * held[1, span, :]
        store(step).start()
    for step in range(STEPS):
        store(step).wait()


def state_kernel(grad, value, rate, mark, state):
    rows, cols = iotas()
    offsets = cols.astype(F32)
    mask = rows // LANES == cols // LANES
    at = pl.program_id(0)
    blocks = state.shape[0]
    for block in range(blocks):
        span = pl.ds(block * TILE, TILE)
        rates = column(rate[...], block_groups(at, blocks, block))
        powers = jnp.exp(-rates * offsets).astype(BF16)
        dz2 = grad[span, :] * value[span, :]
        state[block] = squeeze_groups(nt(powers, dz2), mask).astype(BF16)


def table_kernel(
    rate, residue, filters, to_next, after, to_end, power, taps, turned, mr_turned, wide_rate
):
    rows, cols = iotas()
    mask = rows // LANES == cols // LANES
    offsets = cols.astype(F32)
    lags = ((CHUNK - 1 - cols) % TILE).astype(F32)
    at = pl.program_id(0)
    blocks = power.shape[0] // TILE
    coeffs = residue[...] * jnp.sqrt(one_minus_exp(2.0 * rate[...]))
    sums = []
    for block in range(blocks):
        span = pl.ds(block * TILE, TILE)
        own = block_groups(at, blocks, block)
        rates = column(rate[...], own)
        scale = column(coeffs, own)
        wide_rate[block] = squeeze_groups(jnp.broadcast_to(rates, (TILE, TILE)), mask)
        powers = jnp.exp(-rates * offsets)
        scaled = powers * scale
        ends = jnp.exp(-rates * (TILE - 1 - offsets))
        power[span, :] = jnp.exp(-rates * lags).astype(BF16)
        to_end[span, :] = ends.astype(BF16)
        after[span, :] = scaled.astype(BF16)
        to_next[span, :] = (ends * scale).astype(BF16)
        sums.append(jnp.sum(scaled.reshape(PACK, LANES, TILE), axis=1))
    taps[...] = above(*sums)
    turned[...] = nn(above(*sums).astype(BF16), reversal())
    mr_turned[...] = nn(filters[...], reversal())


def spans(array):
    return [pl.ds(block * TILE, TILE) for block in range(array.shape[0] // TILE)]


def group_rows(table, block):
    return table[pl.ds(block * PACK, PACK), :]


def local_kernel(grad, value, turned, du2):
    rows, cols = iotas()
    lower = ones_where(rows >= cols)
    lower_half = beside(lower, lower)
    results = [
        within_shard(grad[span, :] * value[span, :], group_rows(turned, block), lower_half)
        for block, span in enumerate(spans(grad))
    ]
    for span, result in zip(spans(grad), results):
        du2[span, :] = result


def middle_kernel(states, local, to_next, li_key, value, dz1, du2):
    rows, cols = iotas()
    mask = rows // LANES == cols // LANES
    wides = [spread_groups(states[block], mask).T.astype(BF16) for block in range(states.shape[0])]
    totals = [
        local[span, :] + nn(wide, to_next[span, :]) for span, wide in zip(spans(local), wides)
    ]
    for span, total in zip(spans(local), totals):
        du2[span, :] = total
        dy1 = total * li_key[span, :].astype(F32)
        dz1[span, :] = (dy1 * value[span, :].astype(F32)).astype(BF16)


def forward_kernel(
    before, now, filters, value, li_key, to_end, dz1, grad, li_value, power, after_shard, rate,
    z1, u2, packed, filter_sums, within_sums, across_sums,
):
    rows, cols = iotas()
    mask = rows // LANES == cols // LANES
    upper = ones_where(cols >= rows)
    upper_half = beside(upper, upper)
    turn = ones_where(cols == rows - rows % CHUNK + (CHUNK - 1 - rows % CHUNK))
    lanes = lax.broadcasted_iota(jnp.int32, (CHUNK, TILE), 1)
    own_rows = [ones_where((lanes // LANES) % 2 == i) for i in range(2)]
    eights = ones_where(
        lax.broadcasted_iota(jnp.int32, (2 * PACK, TILE), 1) // 8
        == lax.broadcasted_iota(jnp.int32, (2 * PACK, TILE), 0)
    )
    at = pl.program_id(0)
    blocks = now.shape[0] // TILE

    @pl.when(at == 0)
    def _():
        within_sums[...] = jnp.zeros_like(within_sums)
        across_sums[...] = jnp.zeros_like(across_sums)

    turned = []
    for span in spans(now):
        dz2 = grad[span, :] * li_value[span, :]
        turned.append(nt(turn, above(dz1[span, :], dz2)).astype(BF16))
    chunks = [(pair_chunks(each[:, :TILE]), pair_chunks(each[:, TILE:])) for each in turned]
    results = [
        now_and_before(
            now[span, :], before[span, :], group_rows(filters, block).astype(F32), upper_half
        )
        for block, span in enumerate(spans(now))
    ]
    halves = []
    for span, result in zip(spans(now), results):
        z1[span, :] = result
        y1 = (value[span, :].astype(F32) * result).astype(BF16).astype(F32)
        halves.append((y1 * li_key[span, :].astype(F32)).astype(BF16))
        u2[span, :] = halves[-1]
    ends = [nt(to_end[span, :], half) for span, half in zip(spans(now), halves)]

    lags = []
    for block in range(blocks):
        lag, energy = [], []
        for p in range(TILE // CHUNK):
            pair = pl.ds(block * TILE + p * CHUNK, CHUNK)
            older, newer = before[pair, :], now[pair, :]
            later = halves[block][p * CHUNK : (p + 1) * CHUNK]
            lag.append(lag_rows(chunks[block][0][p], windows(older, newer), own_rows))
            energy.append(lag_rows(chunks[block][1][p], windows(None, later), own_rows))
        lags.append(above(*lag, *energy))
    lags = [nn(eights, each) for each in lags]
    within, across = jnp.zeros((LANES, TILE), F32), jnp.zeros((LANES, TILE), F32)
    for block, span in enumerate(spans(now)):
        own = block_groups(at, blocks, block)
        energies = above(*[lags[block][PACK:].astype(BF16)] * LANES)
        within = within + squeeze_groups(nt(power[span, :], energies), own)
        state = squeeze_groups(ends[block], mask).astype(BF16)
        crossing = state.astype(F32) * after_shard[block]
        across = across + nn(crossing.astype(BF16), ones_where(own))
        packed[at * blocks + block] = state
    lags = [each[:PACK] for each in lags]
    few = blocks * PACK
    filter_sums[pl.ds(pl.multiple_of(at * few, few), few), :] = above(*lags)
    within_sums[...] += within
    across_sums[...] += across

    steps = filter_sums.shape[0] // few

    @pl.when(at == steps - 1)
    def _():
        place = ones_where((rows + cols) % TILE == CHUNK - 1)
        sums = nn(filter_sums[...].astype(BF16), place).astype(BF16)
        for chunk in range(filter_sums.shape[0] // LANES):
            packed[steps * blocks + chunk] = sums[chunk * LANES : (chunk + 1) * LANES]
        gains = jnp.sqrt(one_minus_exp(2.0 * rate[...]))
        total = gains * (within_sums[...] + across_sums[...])
        packed[steps * blocks + filter_sums.shape[0] // LANES] = total.astype(BF16)


def factor_kernel(bits, wide_rate, later, zeros, *weights):
    zeros[...] = jnp.zeros_like(zeros)
    place = lax.axis_index("seq")
    rates = wide_rate[...]
    weights = list(weights)
    for bit in bits:
        high = (place & bit) != 0
        passed = TILE * (place & (bit - 1)) + 1
        reach = jnp.exp(-rates * passed.astype(F32))
        weights.pop(0)[...] = jnp.where(high, reach, 0.0)
        if bit != bits[-1]:
            run = jnp.exp(-rates * (TILE * bit))
            one = jnp.ones_like(run)
            weights.pop(0)[...] = jnp.where(high, run, one)
            weights.pop(0)[...] = jnp.where(high, one, run)


def within_kernel(u2, taps, z1, du2, value, li_key, z2, grad_value, grad_key, zeros):
    zeros[...] = jnp.zeros_like(zeros)
    rows, cols = iotas()
    upper = ones_where(cols >= rows)
    upper_half = beside(upper, upper)
    results = [
        within_shard(u2[span, :], group_rows(taps, block), upper_half)
        for block, span in enumerate(spans(u2))
    ]
    for span, result in zip(spans(u2), results):
        z2[span, :] = result
        z1_here, du2_here = z1[span, :], du2[span, :]
        y1 = (value[span, :].astype(F32) * z1_here).astype(BF16).astype(F32)
        grad_key[span, :] = (du2_here * y1).astype(BF16)
        grad_value[span, :] = (du2_here * li_key[span, :].astype(F32) * z1_here).astype(BF16)


def last_kernel(half, other, grad_filter, grad_residue):
    chunks = half.shape[0] - 1
    for chunk in range(chunks):
        grad_filter[pl.ds(chunk * LANES, LANES), :] = half[chunk].astype(F32) + other[chunk].astype(F32)
    grad_residue[...] = half[chunks].astype(F32) + other[chunks].astype(F32)


def product_kernel(dz1, later, turned, query, key, grad_query, grad_key, nothing):
    nothing[...] = jnp.zeros_like(nothing)
    rows, cols = iotas()
    lower = ones_where(rows >= cols)
    lower_half = beside(lower, lower)
    results = [
        now_and_before(
            dz1[span, :], later[span, :], group_rows(turned, block), lower_half
        )
        for block, span in enumerate(spans(dz1))
    ]
    for span, du1 in zip(spans(dz1), results):
        grad_query[span, :] = (du1 * key[span, :].astype(F32)).astype(BF16)
        grad_key[span, :] = (du1 * query[span, :].astype(F32)).astype(BF16)


def value_kernel(states, after, z2, grad, grad_value, made, left):
    rows, cols = iotas()
    mask = rows // LANES == cols // LANES
    at = pl.program_id(0)
    size = z2.shape[0]

    def store(step):
        span = pl.ds(pl.multiple_of(step * size, size), size)
        return pltpu.make_async_copy(made.at[span, :], grad_value.at[span, :], left.at[step])

    wides = [spread_groups(states[block], mask).T.astype(BF16) for block in range(states.shape[0])]
    totals = [z2[span, :] + nn(wide, after[span, :]) for span, wide in zip(spans(z2), wides)]
    for block, (span, total) in enumerate(zip(spans(z2), totals)):
        here = pl.ds(pl.multiple_of(at * size + block * TILE, TILE), TILE)
        made[here, :] = (grad[span, :].astype(F32) * total).astype(BF16)
    store(at).start()

    @pl.when(at == STEPS - 1)
    def _():
        for step in range(STEPS):
            store(step).wait()


def shifted(value, axis, steps):
    count = lax.axis_size(axis)
    first, last = max(0, -steps), min(count, count - steps)
    return lax.ppermute(value, axis, [(source, source + steps) for source in range(first, last)])


def swapped(value, axis, bit):
    count = lax.axis_size(axis)
    return lax.ppermute(value, axis, [(source, source ^ bit) for source in range(count)])


def scan_bits():
    count, bit, bits = lax.axis_size("seq"), 1, []
    assert count & (count - 1) == 0
    while bit < count:
        bits.append(bit)
        bit *= 2
    return bits


def per_device(
    mr_query, mr_key, mr_value, li_key, li_value, grad_out, mr_filter, li_residue, li_rate
):
    query, key, value, key_two, value_two, grad = (
        array[0] for array in (mr_query, mr_key, mr_value, li_key, li_value, grad_out)
    )
    groups, filt_len = mr_filter.shape
    channels, seq_local = query.shape
    assert filt_len == TILE and seq_local == TILE and groups <= TILE
    assert channels == groups * LANES and li_rate.shape[1] == LANES
    rows = channels // STEPS
    few = groups // STEPS
    spare = ((0, 0), (0, TILE - groups))
    rate = jnp.pad(li_rate.T, spare)
    residue = jnp.pad(li_residue.T, spare)

    blocks = channels // TILE

    wide = pl.BlockSpec((rows, TILE), lambda i: (i, 0))
    table = pl.BlockSpec((few, TILE), lambda i: (i, 0))
    chunk = pl.BlockSpec((blocks // STEPS, LANES, TILE), lambda i: (i, 0, 0))
    modes = pl.BlockSpec((LANES, TILE), lambda i: (0, 0))
    distant = pl.BlockSpec(memory_space=pltpu.HBM)
    anywhere = pl.BlockSpec(memory_space=pl.ANY)
    wide_half = jax.ShapeDtypeStruct((channels, TILE), BF16)
    wide_full = jax.ShapeDtypeStruct((channels, TILE), F32)
    table_full = jax.ShapeDtypeStruct((groups, TILE), F32)
    chunk_half = jax.ShapeDtypeStruct((blocks, LANES, TILE), BF16)
    chunk_full = jax.ShapeDtypeStruct((blocks, LANES, TILE), F32)

    def call(kernel, name, in_specs, out_specs, out_shape, scratch=(), grid=STEPS, limit=VMEM_LIMIT, work=0):
        return pl.pallas_call(
            kernel,
            grid=(grid,),
            in_specs=in_specs,
            out_specs=out_specs,
            out_shape=out_shape,
            scratch_shapes=scratch,
            name=name,
            cost_estimate=pl.CostEstimate(
                flops=2 * work * channels * TILE * TILE, bytes_accessed=1, transcendentals=0
            ),
            compiler_params=pltpu.CompilerParams(vmem_limit_bytes=limit),
        )

    def whole(leaf):
        return pl.BlockSpec(leaf.shape, lambda i: (0,) * len(leaf.shape))

    def twice(spec):
        return pl.BlockSpec((2 * spec.block_shape[0],) + spec.block_shape[1:], spec.index_map)

    small = jax.ShapeDtypeStruct((8, TILE), F32)
    product, mark = call(
        gate_kernel, "gate", [distant] * 2, [distant, whole(small)], [wide_half, small],
        [
            pltpu.VMEM((2, channels, TILE), BF16), pltpu.VMEM((channels, TILE), BF16),
            pltpu.SemaphoreType.DMA((2, STEPS)), pltpu.SemaphoreType.DMA((STEPS,)),
        ],
        grid=1, limit=60 * 1024 * 1024,
    )(query, key)
    product_before = shifted(product, "seq", 1)

    (back,) = call(state_kernel, "state", [wide, wide, modes, anywhere], [chunk], [chunk_half])(
        grad, value_two, rate, mark
    )

    to_next, after, to_end, power, taps, turned, mr_turned, wide_rate = call(
        table_kernel, "table", [modes, modes, table], [wide] * 4 + [table] * 3 + [chunk],
        [wide_half] * 4 + [table_full] * 3 + [chunk_full],
    )(rate, residue, mr_filter)
    outside, total = None, back.astype(F32)
    for bit in scan_bits():
        other = shifted(total.astype(BF16), "seq", -bit).astype(F32)
        reach = jnp.exp(-TILE * (bit - 1) * wide_rate) * other if bit > 1 else other
        outside = reach if outside is None else outside + reach
        total = total + jnp.exp(-TILE * bit * wide_rate) * other
    after_shard = outside * jnp.exp(-wide_rate)

    (du2_local,) = call(
        local_kernel, "local", [wide, wide, table], [wide], [wide_full]
    )(
        grad, value_two, turned
    )

    dz1, du2 = call(
        middle_kernel, "middle", [chunk, wide, wide, wide, wide], [wide, wide],
        [wide_half, wide_full],
    )(after_shard, du2_local, to_next, key_two, value)
    dz1_later = shifted(dz1, "seq", -1)

    filter_chunks = groups // LANES
    packed_shape = jax.ShapeDtypeStruct((blocks + filter_chunks + 1, LANES, TILE), BF16)
    z1, u2, packed = call(
        forward_kernel, "forward",
        [twice(spec) for spec in [wide, wide, table] + [wide] * 7 + [chunk]] + [modes],
        [twice(wide), twice(wide), whole(packed_shape)], [wide_full, wide_half, packed_shape],
        [pltpu.VMEM((groups, TILE), F32)] + [pltpu.VMEM((LANES, TILE), F32)] * 2,
        grid=STEPS // 2,
    )(
        product_before, product, mr_filter, value, key_two, to_end, dz1, grad, value_two, power,
        after_shard, rate,
    )

    bits = scan_bits()
    few_full = jax.ShapeDtypeStruct((filter_chunks + 1, LANES, TILE), F32)
    factors = 3 * len(bits) - 2
    z2, grad_mr_value, grad_li_key, within_zeros = call(
        within_kernel, "within",
        [twice(spec) for spec in (wide, table, wide, wide, wide, wide)],
        [twice(wide)] * 3 + [whole(few_full)],
        [wide_full, wide_half, wide_half, few_full], grid=STEPS // 2,
    )(u2, taps, z1, du2, value, key_two)

    factor_zeros, *weights = call(
        functools.partial(factor_kernel, bits), "factor", [whole(chunk_full), anywhere],
        [whole(few_full)] + [whole(chunk_full)] * factors, [few_full] + [chunk_full] * factors,
        grid=1,
    )(wide_rate, dz1_later)

    grad_query, grad_key, product_zeros = call(
        product_kernel, "product",
        [twice(spec) for spec in (wide, wide, table, wide, wide)],
        [twice(wide), twice(wide), whole(few_full)], [wide_half, wide_half, few_full],
        grid=STEPS // 2,
    )(dz1, dz1_later, mr_turned, query, key)

    zeros = [within_zeros + factor_zeros, product_zeros]
    before_shard = jnp.zeros(back.shape, F32)
    for bit in bits:
        other = swapped(packed, "seq", bit)
        sums = packed[blocks:].astype(F32) + other[blocks:].astype(F32)
        if zeros:
            sums = sums + zeros.pop(0)
        mine, theirs = packed[:blocks].astype(F32), other[:blocks].astype(F32)
        before_shard = before_shard + weights.pop(0) * theirs
        if bit != bits[-1]:
            total = weights.pop(0) * theirs + weights.pop(0) * mine
            packed = jnp.concatenate([total.astype(BF16), sums.astype(BF16)], axis=0)
    sums = sums.astype(BF16)

    assert lax.axis_size("dp") == 2
    partner = swapped(sums, "dp", 1)
    (grad_li_value,) = call(
        value_kernel, "value", [chunk, wide, wide, wide], [distant], [wide_half],
        [pltpu.VMEM((channels, TILE), BF16), pltpu.SemaphoreType.DMA((STEPS,))],
    )(before_shard, after, z2, grad)

    residue_full = jax.ShapeDtypeStruct((LANES, TILE), F32)
    grad_filter, grad_residue = call(
        last_kernel, "last", [whole(sums)] * 2,
        [whole(table_full), whole(residue_full)], [table_full, residue_full], grid=1,
    )(sums, partner)
    return (
        grad_query[None],
        grad_key[None],
        grad_mr_value[None],
        grad_li_key[None],
        grad_li_value[None],
        grad_filter,
        grad_residue[:, :groups].T,
    )


def solution(mesh):
    streams = (P("dp", "chan", "seq"),)
    tables = (P("chan", None),)
    return jax.shard_map(
        per_device,
        mesh=mesh,
        in_specs=streams * 6 + tables * 3,
        out_specs=streams * 5 + tables * 2,
        check_vma=False,
    )
```

```python
import functools

import jax
import jax.numpy as jnp
from jax import lax
from jax.experimental import pallas as pl
from jax.experimental.pallas import tpu as pltpu
from jax.sharding import PartitionSpec as P

F32 = jnp.float32
BF16 = jnp.bfloat16
TILE = 128
LANES = 16
PACK = TILE // LANES
CHUNK = 32
STEPS = 4
VMEM_LIMIT = 24 * 1024 * 1024


def nn(lhs, rhs):
    return lax.dot_general(lhs, rhs, (((1,), (0,)), ((), ())), preferred_element_type=F32)


def nt(lhs, rhs):
    return lax.dot_general(lhs, rhs, (((1,), (1,)), ((), ())), preferred_element_type=F32)


def iotas():
    rows = lax.broadcasted_iota(jnp.int32, (TILE, TILE), 0)
    cols = lax.broadcasted_iota(jnp.int32, (TILE, TILE), 1)
    return rows, cols


def ones_where(mask):
    return jnp.where(mask, 1.0, 0.0).astype(BF16)


def column(turned, mask):
    wide = jnp.concatenate([turned] * PACK, axis=0)
    return jnp.sum(jnp.where(mask, wide, 0.0), axis=1, keepdims=True)


def squeeze_groups(wide, mask):
    kept = jnp.where(mask, wide, 0.0)
    total = kept[:LANES]
    for g in range(1, PACK):
        total = total + kept[g * LANES : (g + 1) * LANES]
    return total


def spread_groups(narrow, mask):
    return jnp.where(mask, jnp.concatenate([narrow] * PACK, axis=0), 0.0)


def circulant(row):
    base = jnp.broadcast_to(row, (LANES, TILE))
    base = pltpu.roll(base, 0, 1, stride=1, stride_axis=0).astype(BF16)
    return jnp.concatenate(
        [base] + [pltpu.roll(base, LANES * j, 1) for j in range(1, PACK)], axis=0
    )


def reversal():
    rows, cols = iotas()
    return ones_where((rows + cols) % TILE == 0)


def one_minus_exp(value):
    series = jnp.full_like(value, 1.0)
    for order in (7, 6, 5, 4, 3, 2):
        series = 1.0 - value * series / order
    return jnp.where(value < 0.125, value * series, 1.0 - jnp.exp(-value))


def chunk_mask(shape, bit):
    return (lax.broadcasted_iota(jnp.int32, shape, 1) // CHUNK) & bit == 0


def pair_chunks(turned):
    parts = [turned[CHUNK * j : CHUNK * (j + 1), :] for j in range(TILE // CHUNK)]
    for bit in (1, 2):
        keep = chunk_mask((CHUNK, TILE), bit)
        for j in range(len(parts)):
            if j & bit == 0:
                low, high = parts[j], parts[j + bit]
                parts[j] = jnp.where(keep, low, pltpu.roll(high, CHUNK * bit, 1))
                parts[j + bit] = jnp.where(keep, pltpu.roll(low, TILE - CHUNK * bit, 1), high)
    return parts


def windows(before, now):
    lanes = lax.broadcasted_iota(jnp.int32, now.shape, 1)
    none = jnp.zeros_like(now)
    first, second = [none if before is None else before], [now]
    for j in range(1, TILE // CHUNK):
        left = TILE - CHUNK * j
        moved = pltpu.roll(now, left, 1)
        older = none if before is None else pltpu.roll(before, left, 1)
        first.append(jnp.where(lanes < left, older, moved))
        second.append(moved)
    return jnp.concatenate(
        [jnp.concatenate(first, axis=0), jnp.concatenate(second, axis=0)], axis=1
    )


def beside(first, second):
    return jnp.concatenate([first, second], axis=1)


def above(*arrays):
    return jnp.concatenate(arrays, axis=0)


def apart(first, second):
    none = jnp.zeros_like(first)
    return above(beside(first, none), beside(none, second))


def lag_rows(chunks, shifted_rows, own_rows):
    wide = nn(above(*[chunks * own for own in own_rows]), shifted_rows)
    rows = lax.broadcasted_iota(jnp.int32, (2 * CHUNK, TILE), 0) % CHUNK
    lanes = lax.broadcasted_iota(jnp.int32, (2 * CHUNK, TILE), 1)
    sums = jnp.where(lanes + rows < CHUNK, wide[:, TILE:], wide[:, :TILE])
    parts = []
    for start in (0, CHUNK):
        part = pltpu.roll(sums[start : start + CHUNK], 0, 1, stride=1, stride_axis=0)
        parts.append(part[:8] + part[8:16] + part[16:24] + part[24:])
    return above(*parts).astype(BF16)


def now_and_before(now, before, rows, half):
    both = beside(now, before)
    pieces = []
    for g in range(0, PACK, 2):
        circs = beside(*[circulant(rows[h : h + 1, :]) for h in (g, g + 1)])
        w_now = circs * half
        wide = nn(both[g * LANES : (g + 2) * LANES, :], above(w_now, circs - w_now))
        pieces += [wide[:LANES, :TILE], wide[LANES:, TILE:]]
    return jnp.concatenate(pieces, axis=0)


def within_shard(array, rows, half):
    pieces = []
    for g in range(0, PACK, 4):
        weights = [
            beside(*[circulant(rows[h : h + 1, :]) for h in (k, k + 1)]) * half
            for k in (g, g + 2)
        ]
        parts = [array[k * LANES : (k + 2) * LANES, :] for k in (g, g + 2)]
        wide = nn(apart(*parts), above(*weights))
        for k in range(4):
            column_at = (k % 2) * TILE
            pieces.append(wide[k * LANES : (k + 1) * LANES, column_at : column_at + TILE])
    return jnp.concatenate(pieces, axis=0)


def block_groups(at, blocks, block):
    rows, cols = iotas()
    return cols == rows // LANES + (at * blocks + block) * PACK


def gate_kernel(query, key, product, held, made, arrived, left):
    size = held.shape[1] // STEPS

    def fetch(array, step):
        span = pl.ds(step * size, size)
        return pltpu.make_async_copy(
            (query, key)[array].at[span, :], held.at[array, span, :], arrived.at[array, step]
        )

    def store(step):
        span = pl.ds(step * size, size)
        return pltpu.make_async_copy(made.at[span, :], product.at[span, :], left.at[step])

    for step in range(STEPS):
        for array in range(2):
            fetch(array, step).start()
    for step in range(STEPS):
        for array in range(2):
            fetch(array, step).wait()
        span = pl.ds(step * size, size)
        made[span, :] = held[0, span, :] * held[1, span, :]
        store(step).start()
    for step in range(STEPS):
        store(step).wait()


def state_kernel(grad, value, rate, state):
    rows, cols = iotas()
    offsets = cols.astype(F32)
    mask = rows // LANES == cols // LANES
    at = pl.program_id(0)
    blocks = state.shape[0]
    for block in range(blocks):
        span = pl.ds(block * TILE, TILE)
        rates = column(rate[...], block_groups(at, blocks, block))
        powers = jnp.exp(-rates * offsets).astype(BF16)
        dz2 = grad[span, :] * value[span, :]
        state[block] = squeeze_groups(nt(powers, dz2), mask).astype(BF16)


def table_kernel(
    rate, residue, filters, to_next, after, to_end, power, taps, turned, mr_turned, wide_rate
):
    rows, cols = iotas()
    mask = rows // LANES == cols // LANES
    offsets = cols.astype(F32)
    lags = ((CHUNK - 1 - cols) % TILE).astype(F32)
    at = pl.program_id(0)
    blocks = power.shape[0] // TILE
    coeffs = residue[...] * jnp.sqrt(one_minus_exp(2.0 * rate[...]))
    sums = []
    for block in range(blocks):
        span = pl.ds(block * TILE, TILE)
        own = block_groups(at, blocks, block)
        rates = column(rate[...], own)
        scale = column(coeffs, own)
        wide_rate[block] = squeeze_groups(jnp.broadcast_to(rates, (TILE, TILE)), mask)
        powers = jnp.exp(-rates * offsets)
        scaled = powers * scale
        ends = jnp.exp(-rates * (TILE - 1 - offsets))
        power[span, :] = jnp.exp(-rates * lags).astype(BF16)
        to_end[span, :] = ends.astype(BF16)
        after[span, :] = scaled.astype(BF16)
        to_next[span, :] = (ends * scale).astype(BF16)
        sums.append(jnp.sum(scaled.reshape(PACK, LANES, TILE), axis=1))
    taps[...] = above(*sums)
    turned[...] = nn(above(*sums).astype(BF16), reversal())
    mr_turned[...] = nn(filters[...], reversal())


def spans(array):
    return [pl.ds(block * TILE, TILE) for block in range(array.shape[0] // TILE)]


def group_rows(table, block):
    return table[pl.ds(block * PACK, PACK), :]


def local_kernel(grad, value, turned, du2):
    rows, cols = iotas()
    lower = ones_where(rows >= cols)
    lower_half = beside(lower, lower)
    results = [
        within_shard(grad[span, :] * value[span, :], group_rows(turned, block), lower_half)
        for block, span in enumerate(spans(grad))
    ]
    for span, result in zip(spans(grad), results):
        du2[span, :] = result


def middle_kernel(states, local, to_next, li_key, value, before, dz1, du2):
    rows, cols = iotas()
    mask = rows // LANES == cols // LANES
    wides = [spread_groups(states[block], mask).T.astype(BF16) for block in range(states.shape[0])]
    totals = [
        local[span, :] + nn(wide, to_next[span, :]) for span, wide in zip(spans(local), wides)
    ]
    for span, total in zip(spans(local), totals):
        du2[span, :] = total
        dy1 = total * li_key[span, :].astype(F32)
        dz1[span, :] = (dy1 * value[span, :].astype(F32)).astype(BF16)


def forward_kernel(
    before, now, filters, value, li_key, to_end, dz1, grad, li_value, power, after_shard, rate,
    z1, u2, packed, filter_sums, within_sums, across_sums,
):
    rows, cols = iotas()
    mask = rows // LANES == cols // LANES
    upper = ones_where(cols >= rows)
    upper_half = beside(upper, upper)
    turn = ones_where(cols == rows - rows % CHUNK + (CHUNK - 1 - rows % CHUNK))
    lanes = lax.broadcasted_iota(jnp.int32, (CHUNK, TILE), 1)
    own_rows = [ones_where((lanes // LANES) % 2 == i) for i in range(2)]
    eights = ones_where(
        lax.broadcasted_iota(jnp.int32, (2 * PACK, TILE), 1) // 8
        == lax.broadcasted_iota(jnp.int32, (2 * PACK, TILE), 0)
    )
    at = pl.program_id(0)
    blocks = now.shape[0] // TILE

    @pl.when(at == 0)
    def _():
        within_sums[...] = jnp.zeros_like(within_sums)
        across_sums[...] = jnp.zeros_like(across_sums)

    turned = []
    for span in spans(now):
        dz2 = grad[span, :] * li_value[span, :]
        turned.append(nt(turn, above(dz1[span, :], dz2)).astype(BF16))
    chunks = [(pair_chunks(each[:, :TILE]), pair_chunks(each[:, TILE:])) for each in turned]
    results = [
        now_and_before(
            now[span, :], before[span, :], group_rows(filters, block).astype(F32), upper_half
        )
        for block, span in enumerate(spans(now))
    ]
    halves = []
    for span, result in zip(spans(now), results):
        z1[span, :] = result
        y1 = (value[span, :].astype(F32) * result).astype(BF16).astype(F32)
        halves.append((y1 * li_key[span, :].astype(F32)).astype(BF16))
        u2[span, :] = halves[-1]
    ends = [nt(to_end[span, :], half) for span, half in zip(spans(now), halves)]

    lags = []
    for block in range(blocks):
        lag, energy = [], []
        for p in range(TILE // CHUNK):
            pair = pl.ds(block * TILE + p * CHUNK, CHUNK)
            older, newer = before[pair, :], now[pair, :]
            later = halves[block][p * CHUNK : (p + 1) * CHUNK]
            lag.append(lag_rows(chunks[block][0][p], windows(older, newer), own_rows))
            energy.append(lag_rows(chunks[block][1][p], windows(None, later), own_rows))
        lags.append(above(*lag, *energy))
    lags = [nn(eights, each) for each in lags]
    within, across = jnp.zeros((LANES, TILE), F32), jnp.zeros((LANES, TILE), F32)
    for block, span in enumerate(spans(now)):
        own = block_groups(at, blocks, block)
        energies = above(*[lags[block][PACK:].astype(BF16)] * LANES)
        within = within + squeeze_groups(nt(power[span, :], energies), own)
        state = squeeze_groups(ends[block], mask).astype(BF16)
        crossing = state.astype(F32) * after_shard[block]
        across = across + nn(crossing.astype(BF16), ones_where(own))
        packed[at * blocks + block] = state
    lags = [each[:PACK] for each in lags]
    few = blocks * PACK
    filter_sums[pl.ds(pl.multiple_of(at * few, few), few), :] = above(*lags)
    within_sums[...] += within
    across_sums[...] += across

    steps = filter_sums.shape[0] // few

    @pl.when(at == steps - 1)
    def _():
        place = ones_where((rows + cols) % TILE == CHUNK - 1)
        sums = nn(filter_sums[...].astype(BF16), place).astype(BF16)
        for chunk in range(filter_sums.shape[0] // LANES):
            packed[steps * blocks + chunk] = sums[chunk * LANES : (chunk + 1) * LANES]
        gains = jnp.sqrt(one_minus_exp(2.0 * rate[...]))
        total = gains * (within_sums[...] + across_sums[...])
        packed[steps * blocks + filter_sums.shape[0] // LANES] = total.astype(BF16)


def factor_kernel(bits, wide_rate, later, zeros, *weights):
    zeros[...] = jnp.zeros_like(zeros)
    place = lax.axis_index("seq")
    rates = wide_rate[...]
    weights = list(weights)
    for bit in bits:
        high = (place & bit) != 0
        passed = TILE * (place & (bit - 1)) + 1
        reach = jnp.exp(-rates * passed.astype(F32))
        weights.pop(0)[...] = jnp.where(high, reach, 0.0)
        if bit != bits[-1]:
            run = jnp.exp(-rates * (TILE * bit))
            one = jnp.ones_like(run)
            weights.pop(0)[...] = jnp.where(high, run, one)
            weights.pop(0)[...] = jnp.where(high, one, run)


def within_kernel(u2, taps, z1, du2, value, li_key, z2, grad_value, grad_key, zeros):
    zeros[...] = jnp.zeros_like(zeros)
    rows, cols = iotas()
    upper = ones_where(cols >= rows)
    upper_half = beside(upper, upper)
    results = [
        within_shard(u2[span, :], group_rows(taps, block), upper_half)
        for block, span in enumerate(spans(u2))
    ]
    for span, result in zip(spans(u2), results):
        z2[span, :] = result
        z1_here, du2_here = z1[span, :], du2[span, :]
        y1 = (value[span, :].astype(F32) * z1_here).astype(BF16).astype(F32)
        grad_key[span, :] = (du2_here * y1).astype(BF16)
        grad_value[span, :] = (du2_here * li_key[span, :].astype(F32) * z1_here).astype(BF16)


def last_kernel(half, other, grad_filter, grad_residue):
    chunks = half.shape[0] - 1
    for chunk in range(chunks):
        grad_filter[pl.ds(chunk * LANES, LANES), :] = half[chunk].astype(F32) + other[chunk].astype(F32)
    grad_residue[...] = half[chunks].astype(F32) + other[chunks].astype(F32)


def product_kernel(dz1, later, turned, query, key, grad_query, grad_key, nothing):
    nothing[...] = jnp.zeros_like(nothing)
    rows, cols = iotas()
    lower = ones_where(rows >= cols)
    lower_half = beside(lower, lower)
    results = [
        now_and_before(
            dz1[span, :], later[span, :], group_rows(turned, block), lower_half
        )
        for block, span in enumerate(spans(dz1))
    ]
    for span, du1 in zip(spans(dz1), results):
        grad_query[span, :] = (du1 * key[span, :].astype(F32)).astype(BF16)
        grad_key[span, :] = (du1 * query[span, :].astype(F32)).astype(BF16)


def value_kernel(states, after, z2, grad, grad_value, made, left):
    rows, cols = iotas()
    mask = rows // LANES == cols // LANES
    at = pl.program_id(0)
    size = z2.shape[0]

    def store(step):
        span = pl.ds(pl.multiple_of(step * size, size), size)
        return pltpu.make_async_copy(made.at[span, :], grad_value.at[span, :], left.at[step])

    wides = [spread_groups(states[block], mask).T.astype(BF16) for block in range(states.shape[0])]
    totals = [z2[span, :] + nn(wide, after[span, :]) for span, wide in zip(spans(z2), wides)]
    for block, (span, total) in enumerate(zip(spans(z2), totals)):
        here = pl.ds(pl.multiple_of(at * size + block * TILE, TILE), TILE)
        made[here, :] = (grad[span, :].astype(F32) * total).astype(BF16)
    store(at).start()

    @pl.when(at == STEPS - 1)
    def _():
        for step in range(STEPS):
            store(step).wait()


def shifted(value, axis, steps):
    count = lax.axis_size(axis)
    first, last = max(0, -steps), min(count, count - steps)
    return lax.ppermute(value, axis, [(source, source + steps) for source in range(first, last)])


def swapped(value, axis, bit):
    count = lax.axis_size(axis)
    return lax.ppermute(value, axis, [(source, source ^ bit) for source in range(count)])


def scan_bits():
    count, bit, bits = lax.axis_size("seq"), 1, []
    assert count & (count - 1) == 0
    while bit < count:
        bits.append(bit)
        bit *= 2
    return bits


def per_device(
    mr_query, mr_key, mr_value, li_key, li_value, grad_out, mr_filter, li_residue, li_rate
):
    query, key, value, key_two, value_two, grad = (
        array[0] for array in (mr_query, mr_key, mr_value, li_key, li_value, grad_out)
    )
    groups, filt_len = mr_filter.shape
    channels, seq_local = query.shape
    assert filt_len == TILE and seq_local == TILE and groups <= TILE
    assert channels == groups * LANES and li_rate.shape[1] == LANES
    rows = channels // STEPS
    few = groups // STEPS
    spare = ((0, 0), (0, TILE - groups))
    rate = jnp.pad(li_rate.T, spare)
    residue = jnp.pad(li_residue.T, spare)

    blocks = channels // TILE

    wide = pl.BlockSpec((rows, TILE), lambda i: (i, 0))
    table = pl.BlockSpec((few, TILE), lambda i: (i, 0))
    chunk = pl.BlockSpec((blocks // STEPS, LANES, TILE), lambda i: (i, 0, 0))
    modes = pl.BlockSpec((LANES, TILE), lambda i: (0, 0))
    distant = pl.BlockSpec(memory_space=pltpu.HBM)
    anywhere = pl.BlockSpec(memory_space=pl.ANY)
    wide_half = jax.ShapeDtypeStruct((channels, TILE), BF16)
    wide_full = jax.ShapeDtypeStruct((channels, TILE), F32)
    table_full = jax.ShapeDtypeStruct((groups, TILE), F32)
    chunk_half = jax.ShapeDtypeStruct((blocks, LANES, TILE), BF16)
    chunk_full = jax.ShapeDtypeStruct((blocks, LANES, TILE), F32)

    def call(kernel, name, in_specs, out_specs, out_shape, scratch=(), grid=STEPS, limit=VMEM_LIMIT, work=0):
        return pl.pallas_call(
            kernel,
            grid=(grid,),
            in_specs=in_specs,
            out_specs=out_specs,
            out_shape=out_shape,
            scratch_shapes=scratch,
            name=name,
            cost_estimate=pl.CostEstimate(
                flops=2 * work * channels * TILE * TILE, bytes_accessed=1, transcendentals=0
            ),
            compiler_params=pltpu.CompilerParams(vmem_limit_bytes=limit),
        )

    def whole(leaf):
        return pl.BlockSpec(leaf.shape, lambda i: (0,) * len(leaf.shape))

    def twice(spec):
        return pl.BlockSpec((2 * spec.block_shape[0],) + spec.block_shape[1:], spec.index_map)

    (product,) = call(
        gate_kernel, "gate", [distant] * 2, [distant], [wide_half],
        [
            pltpu.VMEM((2, channels, TILE), BF16), pltpu.VMEM((channels, TILE), BF16),
            pltpu.SemaphoreType.DMA((2, STEPS)), pltpu.SemaphoreType.DMA((STEPS,)),
        ],
        grid=1, limit=60 * 1024 * 1024,
    )(query, key)
    product_before = shifted(product, "seq", 1)

    (back,) = call(state_kernel, "state", [wide, wide, modes], [chunk], [chunk_half])(
        grad, value_two, rate
    )

    later_backs = [shifted(back, "seq", -gap) for gap in range(1, lax.axis_size("seq"))]
    to_next, after, to_end, power, taps, turned, mr_turned, wide_rate = call(
        table_kernel, "table", [modes, modes, table], [wide] * 4 + [table] * 3 + [chunk],
        [wide_half] * 4 + [table_full] * 3 + [chunk_full],
    )(rate, residue, mr_filter)
    fade = jnp.exp(-TILE * wide_rate)
    after_shard = later_backs[-1].astype(F32)
    for other in later_backs[-2::-1]:
        after_shard = other.astype(F32) + fade * after_shard
    after_shard = after_shard * jnp.exp(-wide_rate)

    (du2_local,) = call(
        local_kernel, "local", [wide, wide, table], [wide], [wide_full]
    )(
        grad, value_two, turned
    )

    dz1, du2 = call(
        middle_kernel, "middle", [chunk, wide, wide, wide, wide, anywhere], [wide, wide],
        [wide_half, wide_full],
    )(after_shard, du2_local, to_next, key_two, value, product_before)
    dz1_later = shifted(dz1, "seq", -1)

    filter_chunks = groups // LANES
    packed_shape = jax.ShapeDtypeStruct((blocks + filter_chunks + 1, LANES, TILE), BF16)
    z1, u2, packed = call(
        forward_kernel, "forward",
        [twice(spec) for spec in [wide, wide, table] + [wide] * 7 + [chunk]] + [modes],
        [twice(wide), twice(wide), whole(packed_shape)], [wide_full, wide_half, packed_shape],
        [pltpu.VMEM((groups, TILE), F32)] + [pltpu.VMEM((LANES, TILE), F32)] * 2,
        grid=STEPS // 2,
    )(
        product_before, product, mr_filter, value, key_two, to_end, dz1, grad, value_two, power,
        after_shard, rate,
    )

    bits = scan_bits()
    few_full = jax.ShapeDtypeStruct((filter_chunks + 1, LANES, TILE), F32)
    factors = 3 * len(bits) - 2
    z2, grad_mr_value, grad_li_key, within_zeros = call(
        within_kernel, "within",
        [wide, table, wide, wide, wide, wide], [wide] * 3 + [whole(few_full)],
        [wide_full, wide_half, wide_half, few_full],
    )(u2, taps, z1, du2, value, key_two)

    factor_zeros, *weights = call(
        functools.partial(factor_kernel, bits), "factor", [whole(chunk_full), anywhere],
        [whole(few_full)] + [whole(chunk_full)] * factors, [few_full] + [chunk_full] * factors,
        grid=1,
    )(wide_rate, dz1_later)

    grad_query, grad_key, product_zeros = call(
        product_kernel, "product",
        [twice(spec) for spec in (wide, wide, table, wide, wide)],
        [twice(wide), twice(wide), whole(few_full)], [wide_half, wide_half, few_full],
        grid=STEPS // 2,
    )(dz1, dz1_later, mr_turned, query, key)

    zeros = [within_zeros + factor_zeros, product_zeros]
    before_shard = jnp.zeros(back.shape, F32)
    for bit in bits:
        other = swapped(packed, "seq", bit)
        sums = packed[blocks:].astype(F32) + other[blocks:].astype(F32)
        if zeros:
            sums = sums + zeros.pop(0)
        mine, theirs = packed[:blocks].astype(F32), other[:blocks].astype(F32)
        before_shard = before_shard + weights.pop(0) * theirs
        if bit != bits[-1]:
            total = weights.pop(0) * theirs + weights.pop(0) * mine
            packed = jnp.concatenate([total.astype(BF16), sums.astype(BF16)], axis=0)
    sums = sums.astype(BF16)

    assert lax.axis_size("dp") == 2
    partner = swapped(sums, "dp", 1)
    (grad_li_value,) = call(
        value_kernel, "value", [chunk, wide, wide, wide], [distant], [wide_half],
        [pltpu.VMEM((channels, TILE), BF16), pltpu.SemaphoreType.DMA((STEPS,))],
    )(before_shard, after, z2, grad)

    residue_full = jax.ShapeDtypeStruct((LANES, TILE), F32)
    grad_filter, grad_residue = call(
        last_kernel, "last", [whole(sums)] * 2,
        [whole(table_full), whole(residue_full)], [table_full, residue_full], grid=1,
    )(sums, partner)
    return (
        grad_query[None],
        grad_key[None],
        grad_mr_value[None],
        grad_li_key[None],
        grad_li_value[None],
        grad_filter,
        grad_residue[:, :groups].T,
    )


def solution(mesh):
    streams = (P("dp", "chan", "seq"),)
    tables = (P("chan", None),)
    return jax.shard_map(
        per_device,
        mesh=mesh,
        in_specs=streams * 6 + tables * 3,
        out_specs=streams * 5 + tables * 2,
        check_vma=False,
    )
```

```python
import functools

import jax
import jax.numpy as jnp
from jax import lax
from jax.experimental import pallas as pl
from jax.experimental.pallas import tpu as pltpu
from jax.sharding import PartitionSpec as P

F32 = jnp.float32
BF16 = jnp.bfloat16
TILE = 128
LANES = 16
PACK = TILE // LANES
CHUNK = 32
STEPS = 4
PIECES = 8
VMEM_LIMIT = 24 * 1024 * 1024


def nn(lhs, rhs):
    return lax.dot_general(lhs, rhs, (((1,), (0,)), ((), ())), preferred_element_type=F32)


def nt(lhs, rhs):
    return lax.dot_general(lhs, rhs, (((1,), (1,)), ((), ())), preferred_element_type=F32)


def iotas():
    rows = lax.broadcasted_iota(jnp.int32, (TILE, TILE), 0)
    cols = lax.broadcasted_iota(jnp.int32, (TILE, TILE), 1)
    return rows, cols


def ones_where(mask):
    return jnp.where(mask, 1.0, 0.0).astype(BF16)


def column(turned, mask):
    wide = jnp.concatenate([turned] * PACK, axis=0)
    return jnp.sum(jnp.where(mask, wide, 0.0), axis=1, keepdims=True)


def squeeze_groups(wide, mask):
    kept = jnp.where(mask, wide, 0.0)
    total = kept[:LANES]
    for g in range(1, PACK):
        total = total + kept[g * LANES : (g + 1) * LANES]
    return total


def spread_groups(narrow, mask):
    return jnp.where(mask, jnp.concatenate([narrow] * PACK, axis=0), 0.0)


def circulant(row):
    base = jnp.broadcast_to(row, (LANES, TILE))
    base = pltpu.roll(base, 0, 1, stride=1, stride_axis=0).astype(BF16)
    return jnp.concatenate(
        [base] + [pltpu.roll(base, LANES * j, 1) for j in range(1, PACK)], axis=0
    )


def reversal():
    rows, cols = iotas()
    return ones_where((rows + cols) % TILE == 0)


def one_minus_exp(value):
    series = jnp.full_like(value, 1.0)
    for order in (7, 6, 5, 4, 3, 2):
        series = 1.0 - value * series / order
    return jnp.where(value < 0.125, value * series, 1.0 - jnp.exp(-value))


def chunk_mask(shape, bit):
    return (lax.broadcasted_iota(jnp.int32, shape, 1) // CHUNK) & bit == 0


def pair_chunks(turned):
    parts = [turned[CHUNK * j : CHUNK * (j + 1), :] for j in range(TILE // CHUNK)]
    for bit in (1, 2):
        keep = chunk_mask((CHUNK, TILE), bit)
        for j in range(len(parts)):
            if j & bit == 0:
                low, high = parts[j], parts[j + bit]
                parts[j] = jnp.where(keep, low, pltpu.roll(high, CHUNK * bit, 1))
                parts[j + bit] = jnp.where(keep, pltpu.roll(low, TILE - CHUNK * bit, 1), high)
    return parts


def windows(before, now):
    lanes = lax.broadcasted_iota(jnp.int32, now.shape, 1)
    none = jnp.zeros_like(now)
    first, second = [none if before is None else before], [now]
    for j in range(1, TILE // CHUNK):
        left = TILE - CHUNK * j
        moved = pltpu.roll(now, left, 1)
        older = none if before is None else pltpu.roll(before, left, 1)
        first.append(jnp.where(lanes < left, older, moved))
        second.append(moved)
    return jnp.concatenate(
        [jnp.concatenate(first, axis=0), jnp.concatenate(second, axis=0)], axis=1
    )


def beside(first, second):
    return jnp.concatenate([first, second], axis=1)


def above(*arrays):
    return jnp.concatenate(arrays, axis=0)


def apart(first, second):
    none = jnp.zeros_like(first)
    return above(beside(first, none), beside(none, second))


def lag_rows(chunks, shifted_rows, own_rows):
    wide = nn(above(*[chunks * own for own in own_rows]), shifted_rows)
    rows = lax.broadcasted_iota(jnp.int32, (2 * CHUNK, TILE), 0) % CHUNK
    lanes = lax.broadcasted_iota(jnp.int32, (2 * CHUNK, TILE), 1)
    sums = jnp.where(lanes + rows < CHUNK, wide[:, TILE:], wide[:, :TILE])
    parts = []
    for start in (0, CHUNK):
        part = pltpu.roll(sums[start : start + CHUNK], 0, 1, stride=1, stride_axis=0)
        parts.append(part[:8] + part[8:16] + part[16:24] + part[24:])
    return above(*parts).astype(BF16)


def now_and_before(now, before, rows, half):
    both = beside(now, before)
    pieces = []
    for g in range(0, PACK, 2):
        circs = beside(*[circulant(rows[h : h + 1, :]) for h in (g, g + 1)])
        w_now = circs * half
        wide = nn(both[g * LANES : (g + 2) * LANES, :], above(w_now, circs - w_now))
        pieces += [wide[:LANES, :TILE], wide[LANES:, TILE:]]
    return jnp.concatenate(pieces, axis=0)


def within_shard(array, rows, half):
    pieces = []
    for g in range(0, PACK, 4):
        weights = [
            beside(*[circulant(rows[h : h + 1, :]) for h in (k, k + 1)]) * half
            for k in (g, g + 2)
        ]
        parts = [array[k * LANES : (k + 2) * LANES, :] for k in (g, g + 2)]
        wide = nn(apart(*parts), above(*weights))
        for k in range(4):
            column_at = (k % 2) * TILE
            pieces.append(wide[k * LANES : (k + 1) * LANES, column_at : column_at + TILE])
    return jnp.concatenate(pieces, axis=0)


def block_groups(at, blocks, block):
    rows, cols = iotas()
    return cols == rows // LANES + (at * blocks + block) * PACK


def gate_kernel(query, key, product, held, made, arrived, left):
    size = held.shape[1] // PIECES

    def fetch(array, step):
        span = pl.ds(step * size, size)
        return pltpu.make_async_copy(
            (query, key)[array].at[span, :], held.at[array, span, :], arrived.at[array, step]
        )

    def store(step):
        span = pl.ds(step * size, size)
        return pltpu.make_async_copy(made.at[span, :], product.at[span, :], left.at[step])

    for step in range(PIECES):
        for array in range(2):
            fetch(array, step).start()
    for step in range(PIECES):
        for array in range(2):
            fetch(array, step).wait()
        span = pl.ds(step * size, size)
        made[span, :] = held[0, span, :] * held[1, span, :]
        store(step).start()
    for step in range(PIECES):
        store(step).wait()


def state_kernel(grad, value, rate, state):
    rows, cols = iotas()
    offsets = cols.astype(F32)
    mask = rows // LANES == cols // LANES
    at = pl.program_id(0)
    blocks = state.shape[0]
    for block in range(blocks):
        span = pl.ds(block * TILE, TILE)
        rates = column(rate[...], block_groups(at, blocks, block))
        powers = jnp.exp(-rates * offsets).astype(BF16)
        dz2 = grad[span, :] * value[span, :]
        state[block] = squeeze_groups(nt(powers, dz2), mask).astype(BF16)


def local_kernel(
    grad, value, rate, residue, filters, du2, to_next, after, to_end, power, taps, mr_turned, wide_rate
):
    rows, cols = iotas()
    mask = rows // LANES == cols // LANES
    offsets = cols.astype(F32)
    lags = ((CHUNK - 1 - cols) % TILE).astype(F32)
    at = pl.program_id(0)
    blocks = power.shape[0] // TILE
    coeffs = residue[...] * jnp.sqrt(one_minus_exp(2.0 * rate[...]))
    sums = []
    for block in range(blocks):
        span = pl.ds(block * TILE, TILE)
        own = block_groups(at, blocks, block)
        rates = column(rate[...], own)
        scale = column(coeffs, own)
        wide_rate[block] = squeeze_groups(jnp.broadcast_to(rates, (TILE, TILE)), mask)
        powers = jnp.exp(-rates * offsets)
        scaled = powers * scale
        ends = jnp.exp(-rates * (TILE - 1 - offsets))
        power[span, :] = jnp.exp(-rates * lags).astype(BF16)
        to_end[span, :] = ends.astype(BF16)
        after[span, :] = scaled.astype(BF16)
        to_next[span, :] = (ends * scale).astype(BF16)
        sums.append(jnp.sum(scaled.reshape(PACK, LANES, TILE), axis=1))
    taps[...] = above(*sums)
    turned = nn(above(*sums).astype(BF16), reversal())
    mr_turned[...] = nn(filters[...], reversal())
    lower = ones_where(rows >= cols)
    lower_half = beside(lower, lower)
    results = [
        within_shard(
            grad[span, :] * value[span, :], turned[block * PACK : (block + 1) * PACK], lower_half
        )
        for block, span in enumerate(spans(grad))
    ]
    for span, result in zip(spans(grad), results):
        du2[span, :] = result


def spans(array):
    return [pl.ds(block * TILE, TILE) for block in range(array.shape[0] // TILE)]


def group_rows(table, block):
    return table[pl.ds(block * PACK, PACK), :]


def middle_kernel(states, local, to_next, li_key, value, dz1, du2):
    rows, cols = iotas()
    mask = rows // LANES == cols // LANES
    wides = [spread_groups(states[block], mask).T.astype(BF16) for block in range(states.shape[0])]
    totals = [
        local[span, :] + nn(wide, to_next[span, :]) for span, wide in zip(spans(local), wides)
    ]
    for span, total in zip(spans(local), totals):
        du2[span, :] = total
        dy1 = total * li_key[span, :].astype(F32)
        dz1[span, :] = (dy1 * value[span, :].astype(F32)).astype(BF16)


def forward_kernel(
    before, now, filters, value, li_key, to_end, dz1, grad, li_value, power, after_shard, rate,
    z1, u2, packed, filter_sums, within_sums, across_sums,
):
    rows, cols = iotas()
    mask = rows // LANES == cols // LANES
    upper = ones_where(cols >= rows)
    upper_half = beside(upper, upper)
    turn = ones_where(cols == rows - rows % CHUNK + (CHUNK - 1 - rows % CHUNK))
    lanes = lax.broadcasted_iota(jnp.int32, (CHUNK, TILE), 1)
    own_rows = [ones_where((lanes // LANES) % 2 == i) for i in range(2)]
    eights = ones_where(
        lax.broadcasted_iota(jnp.int32, (2 * PACK, TILE), 1) // 8
        == lax.broadcasted_iota(jnp.int32, (2 * PACK, TILE), 0)
    )
    at = pl.program_id(0)
    blocks = now.shape[0] // TILE

    @pl.when(at == 0)
    def _():
        within_sums[...] = jnp.zeros_like(within_sums)
        across_sums[...] = jnp.zeros_like(across_sums)

    turned = []
    for span in spans(now):
        dz2 = grad[span, :] * li_value[span, :]
        turned.append(nt(turn, above(dz1[span, :], dz2)).astype(BF16))
    chunks = [(pair_chunks(each[:, :TILE]), pair_chunks(each[:, TILE:])) for each in turned]
    results = [
        now_and_before(
            now[span, :], before[span, :], group_rows(filters, block).astype(F32), upper_half
        )
        for block, span in enumerate(spans(now))
    ]
    halves = []
    for span, result in zip(spans(now), results):
        z1[span, :] = result
        y1 = (value[span, :].astype(F32) * result).astype(BF16).astype(F32)
        halves.append((y1 * li_key[span, :].astype(F32)).astype(BF16))
        u2[span, :] = halves[-1]
    ends = [nt(to_end[span, :], half) for span, half in zip(spans(now), halves)]

    lags = []
    for block in range(blocks):
        lag, energy = [], []
        for p in range(TILE // CHUNK):
            pair = pl.ds(block * TILE + p * CHUNK, CHUNK)
            older, newer = before[pair, :], now[pair, :]
            later = halves[block][p * CHUNK : (p + 1) * CHUNK]
            lag.append(lag_rows(chunks[block][0][p], windows(older, newer), own_rows))
            energy.append(lag_rows(chunks[block][1][p], windows(None, later), own_rows))
        lags.append(above(*lag, *energy))
    lags = [nn(eights, each) for each in lags]
    within, across = jnp.zeros((LANES, TILE), F32), jnp.zeros((LANES, TILE), F32)
    for block, span in enumerate(spans(now)):
        own = block_groups(at, blocks, block)
        energies = above(*[lags[block][PACK:].astype(BF16)] * LANES)
        within = within + squeeze_groups(nt(power[span, :], energies), own)
        state = squeeze_groups(ends[block], mask).astype(BF16)
        crossing = state.astype(F32) * after_shard[block]
        across = across + nn(crossing.astype(BF16), ones_where(own))
        packed[at * blocks + block] = state
    lags = [each[:PACK] for each in lags]
    few = blocks * PACK
    filter_sums[pl.ds(pl.multiple_of(at * few, few), few), :] = above(*lags)
    within_sums[...] += within
    across_sums[...] += across

    steps = filter_sums.shape[0] // few

    @pl.when(at == steps - 1)
    def _():
        place = ones_where((rows + cols) % TILE == CHUNK - 1)
        sums = nn(filter_sums[...].astype(BF16), place).astype(BF16)
        for chunk in range(filter_sums.shape[0] // LANES):
            packed[steps * blocks + chunk] = sums[chunk * LANES : (chunk + 1) * LANES]
        gains = jnp.sqrt(one_minus_exp(2.0 * rate[...]))
        total = gains * (within_sums[...] + across_sums[...])
        packed[steps * blocks + filter_sums.shape[0] // LANES] = total.astype(BF16)


def factor_kernel(bits, wide_rate, later, zeros, *weights):
    zeros[...] = jnp.zeros_like(zeros)
    place = lax.axis_index("seq")
    rates = wide_rate[...]
    weights = list(weights)
    for bit in bits:
        high = (place & bit) != 0
        passed = TILE * (place & (bit - 1)) + 1
        reach = jnp.exp(-rates * passed.astype(F32))
        weights.pop(0)[...] = jnp.where(high, reach, 0.0)
        if bit != bits[-1]:
            run = jnp.exp(-rates * (TILE * bit))
            one = jnp.ones_like(run)
            weights.pop(0)[...] = jnp.where(high, run, one)
            weights.pop(0)[...] = jnp.where(high, one, run)


def within_kernel(u2, taps, z1, du2, value, li_key, z2, grad_value, grad_key, zeros):
    zeros[...] = jnp.zeros_like(zeros)
    rows, cols = iotas()
    upper = ones_where(cols >= rows)
    upper_half = beside(upper, upper)
    results = [
        within_shard(u2[span, :], group_rows(taps, block), upper_half)
        for block, span in enumerate(spans(u2))
    ]
    for span, result in zip(spans(u2), results):
        z2[span, :] = result
        z1_here, du2_here = z1[span, :], du2[span, :]
        y1 = (value[span, :].astype(F32) * z1_here).astype(BF16).astype(F32)
        grad_key[span, :] = (du2_here * y1).astype(BF16)
        grad_value[span, :] = (du2_here * li_key[span, :].astype(F32) * z1_here).astype(BF16)


def product_kernel(dz1, later, turned, query, key, grad_query, grad_key):
    rows, cols = iotas()
    lower = ones_where(rows >= cols)
    lower_half = beside(lower, lower)
    results = [
        now_and_before(
            dz1[span, :], later[span, :], group_rows(turned, block), lower_half
        )
        for block, span in enumerate(spans(dz1))
    ]
    for span, du1 in zip(spans(dz1), results):
        grad_query[span, :] = (du1 * key[span, :].astype(F32)).astype(BF16)
        grad_key[span, :] = (du1 * query[span, :].astype(F32)).astype(BF16)


def value_kernel(
    states, after, z2, grad, half, other, grad_value, grad_filter, grad_residue, made, left
):
    chunks = half.shape[0] - 1
    for chunk in range(chunks):
        both = half[chunk].astype(F32) + other[chunk].astype(F32)
        grad_filter[pl.ds(chunk * LANES, LANES), :] = both
    grad_residue[...] = half[chunks].astype(F32) + other[chunks].astype(F32)
    rows, cols = iotas()
    mask = rows // LANES == cols // LANES
    at = pl.program_id(0)
    size = z2.shape[0]

    def store(step):
        span = pl.ds(pl.multiple_of(step * size, size), size)
        return pltpu.make_async_copy(made.at[span, :], grad_value.at[span, :], left.at[step])

    wides = [spread_groups(states[block], mask).T.astype(BF16) for block in range(states.shape[0])]
    totals = [z2[span, :] + nn(wide, after[span, :]) for span, wide in zip(spans(z2), wides)]
    for block, (span, total) in enumerate(zip(spans(z2), totals)):
        here = pl.ds(pl.multiple_of(at * size + block * TILE, TILE), TILE)
        made[here, :] = (grad[span, :].astype(F32) * total).astype(BF16)
    store(at).start()

    @pl.when(at == STEPS - 1)
    def _():
        for step in range(STEPS):
            store(step).wait()


def shifted(value, axis, steps):
    count = lax.axis_size(axis)
    first, last = max(0, -steps), min(count, count - steps)
    return lax.ppermute(value, axis, [(source, source + steps) for source in range(first, last)])


def swapped(value, axis, bit):
    count = lax.axis_size(axis)
    return lax.ppermute(value, axis, [(source, source ^ bit) for source in range(count)])


def scan_bits():
    count, bit, bits = lax.axis_size("seq"), 1, []
    assert count & (count - 1) == 0
    while bit < count:
        bits.append(bit)
        bit *= 2
    return bits


def per_device(
    mr_query, mr_key, mr_value, li_key, li_value, grad_out, mr_filter, li_residue, li_rate
):
    query, key, value, key_two, value_two, grad = (
        array[0] for array in (mr_query, mr_key, mr_value, li_key, li_value, grad_out)
    )
    groups, filt_len = mr_filter.shape
    channels, seq_local = query.shape
    assert filt_len == TILE and seq_local == TILE and groups <= TILE
    assert channels == groups * LANES and li_rate.shape[1] == LANES
    rows = channels // STEPS
    few = groups // STEPS
    spare = ((0, 0), (0, TILE - groups))
    rate = jnp.pad(li_rate.T, spare)
    residue = jnp.pad(li_residue.T, spare)

    blocks = channels // TILE

    wide = pl.BlockSpec((rows, TILE), lambda i: (i, 0))
    table = pl.BlockSpec((few, TILE), lambda i: (i, 0))
    chunk = pl.BlockSpec((blocks // STEPS, LANES, TILE), lambda i: (i, 0, 0))
    modes = pl.BlockSpec((LANES, TILE), lambda i: (0, 0))
    distant = pl.BlockSpec(memory_space=pltpu.HBM)
    anywhere = pl.BlockSpec(memory_space=pl.ANY)
    wide_half = jax.ShapeDtypeStruct((channels, TILE), BF16)
    wide_full = jax.ShapeDtypeStruct((channels, TILE), F32)
    table_full = jax.ShapeDtypeStruct((groups, TILE), F32)
    chunk_half = jax.ShapeDtypeStruct((blocks, LANES, TILE), BF16)
    chunk_full = jax.ShapeDtypeStruct((blocks, LANES, TILE), F32)

    def call(kernel, name, in_specs, out_specs, out_shape, scratch=(), grid=STEPS, limit=VMEM_LIMIT, work=0):
        return pl.pallas_call(
            kernel,
            grid=(grid,),
            in_specs=in_specs,
            out_specs=out_specs,
            out_shape=out_shape,
            scratch_shapes=scratch,
            name=name,
            cost_estimate=pl.CostEstimate(
                flops=2 * work * channels * TILE * TILE, bytes_accessed=1, transcendentals=0
            ),
            compiler_params=pltpu.CompilerParams(vmem_limit_bytes=limit),
        )

    def whole(leaf):
        return pl.BlockSpec(leaf.shape, lambda i: (0,) * len(leaf.shape))

    def twice(spec):
        return pl.BlockSpec((2 * spec.block_shape[0],) + spec.block_shape[1:], spec.index_map)

    (product,) = call(
        gate_kernel, "gate", [distant] * 2, [distant], [wide_half],
        [
            pltpu.VMEM((2, channels, TILE), BF16), pltpu.VMEM((channels, TILE), BF16),
            pltpu.SemaphoreType.DMA((2, PIECES)), pltpu.SemaphoreType.DMA((PIECES,)),
        ],
        grid=1, limit=60 * 1024 * 1024,
    )(query, key)
    product_before = shifted(product, "seq", 1)

    (back,) = call(state_kernel, "state", [wide, wide, modes], [chunk], [chunk_half])(
        grad, value_two, rate
    )

    later_backs = [shifted(back, "seq", -gap) for gap in range(1, lax.axis_size("seq"))]
    du2_local, to_next, after, to_end, power, taps, mr_turned, wide_rate = call(
        local_kernel, "local",
        [twice(wide), twice(wide), modes, modes, twice(table)],
        [twice(wide)] * 5 + [twice(table)] * 2 + [twice(chunk)],
        [wide_full] + [wide_half] * 4 + [table_full] * 2 + [chunk_full], grid=STEPS // 2,
    )(grad, value_two, rate, residue, mr_filter)
    fade = jnp.exp(-TILE * wide_rate)
    after_shard = later_backs[-1].astype(F32)
    for other in later_backs[-2::-1]:
        after_shard = other.astype(F32) + fade * after_shard
    after_shard = after_shard * jnp.exp(-wide_rate)

    dz1, du2 = call(
        middle_kernel, "middle", [twice(chunk)] + [twice(wide)] * 4, [twice(wide)] * 2,
        [wide_half, wide_full], grid=STEPS // 2,
    )(after_shard, du2_local, to_next, key_two, value)
    dz1_later = shifted(dz1, "seq", -1)

    filter_chunks = groups // LANES
    packed_shape = jax.ShapeDtypeStruct((blocks + filter_chunks + 1, LANES, TILE), BF16)
    z1, u2, packed = call(
        forward_kernel, "forward",
        [twice(spec) for spec in [wide, wide, table] + [wide] * 7 + [chunk]] + [modes],
        [twice(wide), twice(wide), whole(packed_shape)], [wide_full, wide_half, packed_shape],
        [pltpu.VMEM((groups, TILE), F32)] + [pltpu.VMEM((LANES, TILE), F32)] * 2,
        grid=STEPS // 2,
    )(
        product_before, product, mr_filter, value, key_two, to_end, dz1, grad, value_two, power,
        after_shard, rate,
    )

    bits = scan_bits()
    few_full = jax.ShapeDtypeStruct((filter_chunks + 1, LANES, TILE), F32)
    factors = 3 * len(bits) - 2
    z2, grad_mr_value, grad_li_key, within_zeros = call(
        within_kernel, "within",
        [wide, table, wide, wide, wide, wide], [wide] * 3 + [whole(few_full)],
        [wide_full, wide_half, wide_half, few_full],
    )(u2, taps, z1, du2, value, key_two)

    factor_zeros, *weights = call(
        functools.partial(factor_kernel, bits), "factor", [whole(chunk_full), anywhere],
        [whole(few_full)] + [whole(chunk_full)] * factors, [few_full] + [chunk_full] * factors,
        grid=1,
    )(wide_rate, dz1_later)

    grad_query, grad_key = call(
        product_kernel, "product",
        [twice(spec) for spec in (wide, wide, table, wide, wide)],
        [twice(wide), twice(wide)], [wide_half, wide_half], grid=STEPS // 2,
    )(dz1, dz1_later, mr_turned, query, key)

    assert lax.axis_size("dp") == 2
    half = packed[blocks:]
    sums = half.astype(F32) + swapped(half, "dp", 1).astype(F32) + within_zeros
    packed = jnp.concatenate([packed[:blocks], sums.astype(BF16)], axis=0)
    zeros = [factor_zeros]
    before_shard = jnp.zeros(back.shape, F32)
    for bit in bits:
        other = swapped(packed, "seq", bit)
        mine, theirs = packed[:blocks].astype(F32), other[:blocks].astype(F32)
        before_shard = before_shard + weights.pop(0) * theirs
        half, partner = packed[blocks:], other[blocks:]
        if bit != bits[-1]:
            sums = half.astype(F32) + partner.astype(F32)
            if zeros:
                sums = sums + zeros.pop(0)
            total = weights.pop(0) * theirs + weights.pop(0) * mine
            packed = jnp.concatenate([total.astype(BF16), sums.astype(BF16)], axis=0)
    residue_full = jax.ShapeDtypeStruct((LANES, TILE), F32)
    grad_li_value, grad_filter, grad_residue = call(
        value_kernel, "value",
        [chunk, wide, wide, wide, whole(half), whole(half)],
        [distant, whole(table_full), whole(residue_full)],
        [wide_half, table_full, residue_full],
        [pltpu.VMEM((channels, TILE), BF16), pltpu.SemaphoreType.DMA((STEPS,))],
    )(before_shard, after, z2, grad, half, partner)

    return (
        grad_query[None],
        grad_key[None],
        grad_mr_value[None],
        grad_li_key[None],
        grad_li_value[None],
        grad_filter,
        grad_residue[:, :groups].T,
    )


def solution(mesh):
    streams = (P("dp", "chan", "seq"),)
    tables = (P("chan", None),)
    return jax.shard_map(
        per_device,
        mesh=mesh,
        in_specs=streams * 6 + tables * 3,
        out_specs=streams * 5 + tables * 2,
        check_vma=False,
    )
```

```python
import functools

import jax
import jax.numpy as jnp
from jax import lax
from jax.experimental import pallas as pl
from jax.experimental.pallas import tpu as pltpu
from jax.sharding import PartitionSpec as P

F32 = jnp.float32
BF16 = jnp.bfloat16
TILE = 128
LANES = 16
PACK = TILE // LANES
CHUNK = 32
STEPS = 4
PIECES = 8
VMEM_LIMIT = 24 * 1024 * 1024


def nn(lhs, rhs):
    return lax.dot_general(lhs, rhs, (((1,), (0,)), ((), ())), preferred_element_type=F32)


def nt(lhs, rhs):
    return lax.dot_general(lhs, rhs, (((1,), (1,)), ((), ())), preferred_element_type=F32)


def iotas():
    rows = lax.broadcasted_iota(jnp.int32, (TILE, TILE), 0)
    cols = lax.broadcasted_iota(jnp.int32, (TILE, TILE), 1)
    return rows, cols


def ones_where(mask):
    return jnp.where(mask, 1.0, 0.0).astype(BF16)


def column(turned, mask):
    wide = jnp.concatenate([turned] * PACK, axis=0)
    return jnp.sum(jnp.where(mask, wide, 0.0), axis=1, keepdims=True)


def squeeze_groups(wide, mask):
    kept = jnp.where(mask, wide, 0.0)
    total = kept[:LANES]
    for g in range(1, PACK):
        total = total + kept[g * LANES : (g + 1) * LANES]
    return total


def spread_groups(narrow, mask):
    return jnp.where(mask, jnp.concatenate([narrow] * PACK, axis=0), 0.0)


def circulant(row):
    base = jnp.broadcast_to(row, (LANES, TILE))
    base = pltpu.roll(base, 0, 1, stride=1, stride_axis=0).astype(BF16)
    return jnp.concatenate(
        [base] + [pltpu.roll(base, LANES * j, 1) for j in range(1, PACK)], axis=0
    )


def reversal():
    rows, cols = iotas()
    return ones_where((rows + cols) % TILE == 0)


def one_minus_exp(value):
    series = jnp.full_like(value, 1.0)
    for order in (7, 6, 5, 4, 3, 2):
        series = 1.0 - value * series / order
    return jnp.where(value < 0.125, value * series, 1.0 - jnp.exp(-value))


def chunk_mask(shape, bit):
    return (lax.broadcasted_iota(jnp.int32, shape, 1) // CHUNK) & bit == 0


def pair_chunks(turned):
    parts = [turned[CHUNK * j : CHUNK * (j + 1), :] for j in range(TILE // CHUNK)]
    for bit in (1, 2):
        keep = chunk_mask((CHUNK, TILE), bit)
        for j in range(len(parts)):
            if j & bit == 0:
                low, high = parts[j], parts[j + bit]
                parts[j] = jnp.where(keep, low, pltpu.roll(high, CHUNK * bit, 1))
                parts[j + bit] = jnp.where(keep, pltpu.roll(low, TILE - CHUNK * bit, 1), high)
    return parts


def windows(before, now):
    lanes = lax.broadcasted_iota(jnp.int32, now.shape, 1)
    none = jnp.zeros_like(now)
    first, second = [none if before is None else before], [now]
    for j in range(1, TILE // CHUNK):
        left = TILE - CHUNK * j
        moved = pltpu.roll(now, left, 1)
        older = none if before is None else pltpu.roll(before, left, 1)
        first.append(jnp.where(lanes < left, older, moved))
        second.append(moved)
    return jnp.concatenate(
        [jnp.concatenate(first, axis=0), jnp.concatenate(second, axis=0)], axis=1
    )


def beside(first, second):
    return jnp.concatenate([first, second], axis=1)


def above(*arrays):
    return jnp.concatenate(arrays, axis=0)


def apart(first, second):
    none = jnp.zeros_like(first)
    return above(beside(first, none), beside(none, second))


def lag_rows(chunks, shifted_rows, own_rows):
    wide = nn(above(*[chunks * own for own in own_rows]), shifted_rows)
    rows = lax.broadcasted_iota(jnp.int32, (2 * CHUNK, TILE), 0) % CHUNK
    lanes = lax.broadcasted_iota(jnp.int32, (2 * CHUNK, TILE), 1)
    sums = jnp.where(lanes + rows < CHUNK, wide[:, TILE:], wide[:, :TILE])
    parts = []
    for start in (0, CHUNK):
        part = pltpu.roll(sums[start : start + CHUNK], 0, 1, stride=1, stride_axis=0)
        parts.append(part[:8] + part[8:16] + part[16:24] + part[24:])
    return above(*parts).astype(BF16)


def now_and_before(now, before, rows, half):
    both = beside(now, before)
    pieces = []
    for g in range(0, PACK, 2):
        circs = beside(*[circulant(rows[h : h + 1, :]) for h in (g, g + 1)])
        w_now = circs * half
        wide = nn(both[g * LANES : (g + 2) * LANES, :], above(w_now, circs - w_now))
        pieces += [wide[:LANES, :TILE], wide[LANES:, TILE:]]
    return jnp.concatenate(pieces, axis=0)


def within_shard(array, rows, half):
    pieces = []
    for g in range(0, PACK, 4):
        weights = [
            beside(*[circulant(rows[h : h + 1, :]) for h in (k, k + 1)]) * half
            for k in (g, g + 2)
        ]
        parts = [array[k * LANES : (k + 2) * LANES, :] for k in (g, g + 2)]
        wide = nn(apart(*parts), above(*weights))
        for k in range(4):
            column_at = (k % 2) * TILE
            pieces.append(wide[k * LANES : (k + 1) * LANES, column_at : column_at + TILE])
    return jnp.concatenate(pieces, axis=0)


def block_groups(at, blocks, block):
    rows, cols = iotas()
    return cols == rows // LANES + (at * blocks + block) * PACK


def gate_kernel(query, key, product, held, made, arrived, left):
    size = held.shape[1] // PIECES

    def fetch(array, step):
        span = pl.ds(step * size, size)
        return pltpu.make_async_copy(
            (query, key)[array].at[span, :], held.at[array, span, :], arrived.at[array, step]
        )

    def store(step):
        span = pl.ds(step * size, size)
        return pltpu.make_async_copy(made.at[span, :], product.at[span, :], left.at[step])

    for step in range(PIECES):
        for array in range(2):
            fetch(array, step).start()
    for step in range(PIECES):
        for array in range(2):
            fetch(array, step).wait()
        span = pl.ds(step * size, size)
        made[span, :] = held[0, span, :] * held[1, span, :]
        store(step).start()
    for step in range(PIECES):
        store(step).wait()


def state_kernel(grad, value, rate, state):
    rows, cols = iotas()
    offsets = cols.astype(F32)
    mask = rows // LANES == cols // LANES
    at = pl.program_id(0)
    blocks = state.shape[0]
    for block in range(blocks):
        span = pl.ds(block * TILE, TILE)
        rates = column(rate[...], block_groups(at, blocks, block))
        powers = jnp.exp(-rates * offsets).astype(BF16)
        dz2 = grad[span, :] * value[span, :]
        state[block] = squeeze_groups(nt(powers, dz2), mask).astype(BF16)


def spans(array):
    return [pl.ds(block * TILE, TILE) for block in range(array.shape[0] // TILE)]


def group_rows(table, block):
    return table[pl.ds(block * PACK, PACK), :]


def local_kernel(grad, value, rate, residue, du2, to_next, taps, wide_rate):
    rows, cols = iotas()
    mask = rows // LANES == cols // LANES
    offsets = cols.astype(F32)
    at = pl.program_id(0)
    blocks = wide_rate.shape[0]
    coeffs = residue[...] * jnp.sqrt(one_minus_exp(2.0 * rate[...]))
    owns = [block_groups(at, blocks, block) for block in range(blocks)]
    rates = [column(rate[...], own) for own in owns]
    scales = [column(coeffs, own) for own in owns]
    sums = [
        jnp.sum((jnp.exp(-each * offsets) * scale).reshape(PACK, LANES, TILE), axis=1)
        for each, scale in zip(rates, scales)
    ]
    taps[...] = above(*sums)
    turned = nn(above(*sums).astype(BF16), reversal())
    lower = ones_where(rows >= cols)
    lower_half = beside(lower, lower)
    for block, span in enumerate(spans(grad)):
        wide_rate[block] = squeeze_groups(jnp.broadcast_to(rates[block], (TILE, TILE)), mask)
        ends = jnp.exp(-rates[block] * (TILE - 1 - offsets))
        to_next[span, :] = (ends * scales[block]).astype(BF16)
    results = [
        within_shard(
            grad[span, :] * value[span, :], turned[block * PACK : (block + 1) * PACK], lower_half
        )
        for block, span in enumerate(spans(grad))
    ]
    for span, result in zip(spans(grad), results):
        du2[span, :] = result


def middle_kernel(states, local, to_next, li_key, value, dz1, du2):
    rows, cols = iotas()
    mask = rows // LANES == cols // LANES
    wides = [spread_groups(states[block], mask).T.astype(BF16) for block in range(states.shape[0])]
    totals = [
        local[span, :] + nn(wide, to_next[span, :]) for span, wide in zip(spans(local), wides)
    ]
    for span, total in zip(spans(local), totals):
        du2[span, :] = total
        dy1 = total * li_key[span, :].astype(F32)
        dz1[span, :] = (dy1 * value[span, :].astype(F32)).astype(BF16)


def forward_kernel(
    before, now, filters, value, li_key, dz1, grad, li_value, after_shard, rate,
    z1, u2, packed, filter_sums, within_sums, across_sums,
):
    rows, cols = iotas()
    mask = rows // LANES == cols // LANES
    upper = ones_where(cols >= rows)
    upper_half = beside(upper, upper)
    turn = ones_where(cols == rows - rows % CHUNK + (CHUNK - 1 - rows % CHUNK))
    lanes = lax.broadcasted_iota(jnp.int32, (CHUNK, TILE), 1)
    own_rows = [ones_where((lanes // LANES) % 2 == i) for i in range(2)]
    eights = ones_where(
        lax.broadcasted_iota(jnp.int32, (2 * PACK, TILE), 1) // 8
        == lax.broadcasted_iota(jnp.int32, (2 * PACK, TILE), 0)
    )
    at = pl.program_id(0)
    blocks = now.shape[0] // TILE

    @pl.when(at == 0)
    def _():
        within_sums[...] = jnp.zeros_like(within_sums)
        across_sums[...] = jnp.zeros_like(across_sums)

    turned = []
    for span in spans(now):
        dz2 = grad[span, :] * li_value[span, :]
        turned.append(nt(turn, above(dz1[span, :], dz2)).astype(BF16))
    chunks = [(pair_chunks(each[:, :TILE]), pair_chunks(each[:, TILE:])) for each in turned]
    results = [
        now_and_before(
            now[span, :], before[span, :], group_rows(filters, block).astype(F32), upper_half
        )
        for block, span in enumerate(spans(now))
    ]
    halves = []
    for span, result in zip(spans(now), results):
        z1[span, :] = result
        y1 = (value[span, :].astype(F32) * result).astype(BF16).astype(F32)
        halves.append((y1 * li_key[span, :].astype(F32)).astype(BF16))
        u2[span, :] = halves[-1]
    owns = [block_groups(at, blocks, block) for block in range(blocks)]
    rates = [column(rate[...], own) for own in owns]
    offsets = cols.astype(F32)
    ends = [
        nt(jnp.exp(-each * (TILE - 1 - offsets)).astype(BF16), half)
        for each, half in zip(rates, halves)
    ]

    lags = []
    for block in range(blocks):
        lag, energy = [], []
        for p in range(TILE // CHUNK):
            pair = pl.ds(block * TILE + p * CHUNK, CHUNK)
            older, newer = before[pair, :], now[pair, :]
            later = halves[block][p * CHUNK : (p + 1) * CHUNK]
            lag.append(lag_rows(chunks[block][0][p], windows(older, newer), own_rows))
            energy.append(lag_rows(chunks[block][1][p], windows(None, later), own_rows))
        lags.append(above(*lag, *energy))
    lags = [nn(eights, each) for each in lags]
    lag_places = ((CHUNK - 1 - cols) % TILE).astype(F32)
    within, across = jnp.zeros((LANES, TILE), F32), jnp.zeros((LANES, TILE), F32)
    for block, span in enumerate(spans(now)):
        own = owns[block]
        power = jnp.exp(-rates[block] * lag_places).astype(BF16)
        energies = above(*[lags[block][PACK:].astype(BF16)] * LANES)
        within = within + squeeze_groups(nt(power, energies), own)
        state = squeeze_groups(ends[block], mask).astype(BF16)
        crossing = state.astype(F32) * after_shard[block]
        across = across + nn(crossing.astype(BF16), ones_where(own))
        packed[at * blocks + block] = state
    lags = [each[:PACK] for each in lags]
    few = blocks * PACK
    filter_sums[pl.ds(pl.multiple_of(at * few, few), few), :] = above(*lags)
    within_sums[...] += within
    across_sums[...] += across

    steps = filter_sums.shape[0] // few

    @pl.when(at == steps - 1)
    def _():
        place = ones_where((rows + cols) % TILE == CHUNK - 1)
        sums = nn(filter_sums[...].astype(BF16), place).astype(BF16)
        for chunk in range(filter_sums.shape[0] // LANES):
            packed[steps * blocks + chunk] = sums[chunk * LANES : (chunk + 1) * LANES]
        gains = jnp.sqrt(one_minus_exp(2.0 * rate[...]))
        total = gains * (within_sums[...] + across_sums[...])
        packed[steps * blocks + filter_sums.shape[0] // LANES] = total.astype(BF16)


def factor_kernel(
    bits, wide_rate, rate, residue, filters, later, zeros, after, mr_turned, *weights
):
    zeros[...] = jnp.zeros_like(zeros)
    place = lax.axis_index("seq")
    rates = wide_rate[...]
    weights = list(weights)
    for bit in bits:
        high = (place & bit) != 0
        passed = TILE * (place & (bit - 1)) + 1
        reach = jnp.exp(-rates * passed.astype(F32))
        weights.pop(0)[...] = jnp.where(high, reach, 0.0)
        if bit != bits[-1]:
            run = jnp.exp(-rates * (TILE * bit))
            one = jnp.ones_like(run)
            weights.pop(0)[...] = jnp.where(high, run, one)
            weights.pop(0)[...] = jnp.where(high, one, run)
    mr_turned[...] = nn(filters[...], reversal())
    _, cols = iotas()
    coeffs = residue[...] * jnp.sqrt(one_minus_exp(2.0 * rate[...]))
    for block, span in enumerate(spans(after)):
        own = block_groups(0, 0, block)
        powers = jnp.exp(-column(rate[...], own) * cols.astype(F32))
        after[span, :] = (powers * column(coeffs, own)).astype(BF16)


def within_kernel(u2, taps, z1, du2, value, li_key, z2, grad_value, grad_key, zeros):
    zeros[...] = jnp.zeros_like(zeros)
    rows, cols = iotas()
    upper = ones_where(cols >= rows)
    upper_half = beside(upper, upper)
    results = [
        within_shard(u2[span, :], group_rows(taps, block), upper_half)
        for block, span in enumerate(spans(u2))
    ]
    for span, result in zip(spans(u2), results):
        z2[span, :] = result
        z1_here, du2_here = z1[span, :], du2[span, :]
        y1 = (value[span, :].astype(F32) * z1_here).astype(BF16).astype(F32)
        grad_key[span, :] = (du2_here * y1).astype(BF16)
        grad_value[span, :] = (du2_here * li_key[span, :].astype(F32) * z1_here).astype(BF16)


def product_kernel(dz1, later, turned, query, key, grad_query, grad_key):
    rows, cols = iotas()
    lower = ones_where(rows >= cols)
    lower_half = beside(lower, lower)
    results = [
        now_and_before(
            dz1[span, :], later[span, :], group_rows(turned, block), lower_half
        )
        for block, span in enumerate(spans(dz1))
    ]
    for span, du1 in zip(spans(dz1), results):
        grad_query[span, :] = (du1 * key[span, :].astype(F32)).astype(BF16)
        grad_key[span, :] = (du1 * query[span, :].astype(F32)).astype(BF16)


def value_kernel(
    states, after, z2, grad, half, other, grad_value, grad_filter, grad_residue,
    made, filter_sum, residue_sum, left, done,
):
    rows, cols = iotas()
    mask = rows // LANES == cols // LANES
    at = pl.program_id(0)
    size = z2.shape[0]
    sums = [
        pltpu.make_async_copy(filter_sum, grad_filter, done.at[0]),
        pltpu.make_async_copy(residue_sum, grad_residue, done.at[1]),
    ]

    @pl.when(at == 0)
    def _():
        chunks = half.shape[0] - 1
        for chunk in range(chunks):
            both = half[chunk].astype(F32) + other[chunk].astype(F32)
            filter_sum[pl.ds(chunk * LANES, LANES), :] = both
        residue_sum[...] = half[chunks].astype(F32) + other[chunks].astype(F32)
        for copy in sums:
            copy.start()

    def store(step):
        span = pl.ds(pl.multiple_of(step * size, size), size)
        return pltpu.make_async_copy(made.at[span, :], grad_value.at[span, :], left.at[step])

    wides = [spread_groups(states[block], mask).T.astype(BF16) for block in range(states.shape[0])]
    totals = [z2[span, :] + nn(wide, after[span, :]) for span, wide in zip(spans(z2), wides)]
    for block, (span, total) in enumerate(zip(spans(z2), totals)):
        here = pl.ds(pl.multiple_of(at * size + block * TILE, TILE), TILE)
        made[here, :] = (grad[span, :].astype(F32) * total).astype(BF16)
    store(at).start()

    @pl.when(at == STEPS - 1)
    def _():
        for copy in sums:
            copy.wait()
        for step in range(STEPS):
            store(step).wait()


def shifted(value, axis, steps):
    count = lax.axis_size(axis)
    first, last = max(0, -steps), min(count, count - steps)
    return lax.ppermute(value, axis, [(source, source + steps) for source in range(first, last)])


def swapped(value, axis, bit):
    count = lax.axis_size(axis)
    return lax.ppermute(value, axis, [(source, source ^ bit) for source in range(count)])


def scan_bits():
    count, bit, bits = lax.axis_size("seq"), 1, []
    assert count & (count - 1) == 0
    while bit < count:
        bits.append(bit)
        bit *= 2
    return bits


def per_device(
    mr_query, mr_key, mr_value, li_key, li_value, grad_out, mr_filter, li_residue, li_rate
):
    query, key, value, key_two, value_two, grad = (
        array[0] for array in (mr_query, mr_key, mr_value, li_key, li_value, grad_out)
    )
    groups, filt_len = mr_filter.shape
    channels, seq_local = query.shape
    assert filt_len == TILE and seq_local == TILE and groups <= TILE
    assert channels == groups * LANES and li_rate.shape[1] == LANES
    rows = channels // STEPS
    few = groups // STEPS
    spare = ((0, 0), (0, TILE - groups))
    rate = jnp.pad(li_rate.T, spare)
    residue = jnp.pad(li_residue.T, spare)

    blocks = channels // TILE

    wide = pl.BlockSpec((rows, TILE), lambda i: (i, 0))
    table = pl.BlockSpec((few, TILE), lambda i: (i, 0))
    chunk = pl.BlockSpec((blocks // STEPS, LANES, TILE), lambda i: (i, 0, 0))
    modes = pl.BlockSpec((LANES, TILE), lambda i: (0, 0))
    distant = pl.BlockSpec(memory_space=pltpu.HBM)
    anywhere = pl.BlockSpec(memory_space=pl.ANY)
    wide_half = jax.ShapeDtypeStruct((channels, TILE), BF16)
    wide_full = jax.ShapeDtypeStruct((channels, TILE), F32)
    table_full = jax.ShapeDtypeStruct((groups, TILE), F32)
    chunk_half = jax.ShapeDtypeStruct((blocks, LANES, TILE), BF16)
    chunk_full = jax.ShapeDtypeStruct((blocks, LANES, TILE), F32)

    def call(kernel, name, in_specs, out_specs, out_shape, scratch=(), grid=STEPS, limit=VMEM_LIMIT, work=0):
        return pl.pallas_call(
            kernel,
            grid=(grid,),
            in_specs=in_specs,
            out_specs=out_specs,
            out_shape=out_shape,
            scratch_shapes=scratch,
            name=name,
            cost_estimate=pl.CostEstimate(
                flops=2 * work * channels * TILE * TILE, bytes_accessed=1, transcendentals=0
            ),
            compiler_params=pltpu.CompilerParams(vmem_limit_bytes=limit),
        )

    def whole(leaf):
        return pl.BlockSpec(leaf.shape, lambda i: (0,) * len(leaf.shape))

    def twice(spec):
        return pl.BlockSpec((2 * spec.block_shape[0],) + spec.block_shape[1:], spec.index_map)

    (product,) = call(
        gate_kernel, "gate", [distant] * 2, [distant], [wide_half],
        [
            pltpu.VMEM((2, channels, TILE), BF16), pltpu.VMEM((channels, TILE), BF16),
            pltpu.SemaphoreType.DMA((2, PIECES)), pltpu.SemaphoreType.DMA((PIECES,)),
        ],
        grid=1, limit=60 * 1024 * 1024,
    )(query, key)
    product_before = shifted(product, "seq", 1)

    (back,) = call(state_kernel, "state", [wide, wide, modes], [chunk], [chunk_half])(
        grad, value_two, rate
    )

    later_backs = [shifted(back, "seq", -gap) for gap in range(1, lax.axis_size("seq"))]
    du2_local, to_next, taps, wide_rate = call(
        local_kernel, "local", [wide, wide, modes, modes], [wide, wide, table, chunk],
        [wide_full, wide_half, table_full, chunk_full],
    )(grad, value_two, rate, residue)
    fade = jnp.exp(-TILE * wide_rate)
    after_shard = later_backs[-1].astype(F32)
    for other in later_backs[-2::-1]:
        after_shard = other.astype(F32) + fade * after_shard
    after_shard = after_shard * jnp.exp(-wide_rate)

    dz1, du2 = call(
        middle_kernel, "middle", [twice(chunk)] + [twice(wide)] * 4, [twice(wide)] * 2,
        [wide_half, wide_full], grid=STEPS // 2,
    )(after_shard, du2_local, to_next, key_two, value)
    dz1_later = shifted(dz1, "seq", -1)

    filter_chunks = groups // LANES
    packed_shape = jax.ShapeDtypeStruct((blocks + filter_chunks + 1, LANES, TILE), BF16)
    z1, u2, packed = call(
        forward_kernel, "forward",
        [twice(spec) for spec in [wide, wide, table] + [wide] * 5 + [chunk]] + [modes],
        [twice(wide), twice(wide), whole(packed_shape)], [wide_full, wide_half, packed_shape],
        [pltpu.VMEM((groups, TILE), F32)] + [pltpu.VMEM((LANES, TILE), F32)] * 2,
        grid=STEPS // 2,
    )(
        product_before, product, mr_filter, value, key_two, dz1, grad, value_two, after_shard, rate,
    )

    bits = scan_bits()
    few_full = jax.ShapeDtypeStruct((filter_chunks + 1, LANES, TILE), F32)
    factors = 3 * len(bits) - 2
    z2, grad_mr_value, grad_li_key, within_zeros = call(
        within_kernel, "within",
        [wide, table, wide, wide, wide, wide], [wide] * 3 + [whole(few_full)],
        [wide_full, wide_half, wide_half, few_full],
    )(u2, taps, z1, du2, value, key_two)

    factor_shapes = [few_full, wide_half, table_full] + [chunk_full] * factors
    factor_zeros, after, mr_turned, *weights = call(
        functools.partial(factor_kernel, bits), "factor",
        [whole(chunk_full), modes, modes, whole(mr_filter), anywhere],
        [whole(leaf) for leaf in factor_shapes], factor_shapes, grid=1,
    )(wide_rate, rate, residue, mr_filter, dz1_later)

    grad_query, grad_key = call(
        product_kernel, "product",
        [twice(spec) for spec in (wide, wide, table, wide, wide)],
        [twice(wide), twice(wide)], [wide_half, wide_half], grid=STEPS // 2,
    )(dz1, dz1_later, mr_turned, query, key)

    assert lax.axis_size("dp") == 2
    half = packed[blocks:]
    sums = half.astype(F32) + swapped(half, "dp", 1).astype(F32) + within_zeros
    packed = jnp.concatenate([packed[:blocks], sums.astype(BF16)], axis=0)
    zeros = [factor_zeros]
    before_shard = jnp.zeros(back.shape, F32)
    for bit in bits:
        other = swapped(packed, "seq", bit)
        mine, theirs = packed[:blocks].astype(F32), other[:blocks].astype(F32)
        before_shard = before_shard + weights.pop(0) * theirs
        half, partner = packed[blocks:], other[blocks:]
        if bit != bits[-1]:
            sums = half.astype(F32) + partner.astype(F32)
            if zeros:
                sums = sums + zeros.pop(0)
            total = weights.pop(0) * theirs + weights.pop(0) * mine
            packed = jnp.concatenate([total.astype(BF16), sums.astype(BF16)], axis=0)
    residue_full = jax.ShapeDtypeStruct((LANES, TILE), F32)
    grad_li_value, grad_filter, grad_residue = call(
        value_kernel, "value",
        [chunk, wide, wide, wide, whole(half), whole(half)],
        [distant] * 3, [wide_half, table_full, residue_full],
        [
            pltpu.VMEM((channels, TILE), BF16), pltpu.VMEM((groups, TILE), F32),
            pltpu.VMEM((LANES, TILE), F32),
            pltpu.SemaphoreType.DMA((STEPS,)), pltpu.SemaphoreType.DMA((2,)),
        ],
    )(before_shard, after, z2, grad, half, partner)

    return (
        grad_query[None],
        grad_key[None],
        grad_mr_value[None],
        grad_li_key[None],
        grad_li_value[None],
        grad_filter,
        grad_residue[:, :groups].T,
    )


def solution(mesh):
    streams = (P("dp", "chan", "seq"),)
    tables = (P("chan", None),)
    return jax.shard_map(
        per_device,
        mesh=mesh,
        in_specs=streams * 6 + tables * 3,
        out_specs=streams * 5 + tables * 2,
        check_vma=False,
    )
```

```python
import functools

import jax
import jax.numpy as jnp
from jax import lax
from jax.experimental import pallas as pl
from jax.experimental.pallas import tpu as pltpu
from jax.sharding import PartitionSpec as P

F32 = jnp.float32
BF16 = jnp.bfloat16
TILE = 128
LANES = 16
PACK = TILE // LANES
CHUNK = 32
STEPS = 4
PIECES = 8
VMEM_LIMIT = 24 * 1024 * 1024


def nn(lhs, rhs):
    return lax.dot_general(lhs, rhs, (((1,), (0,)), ((), ())), preferred_element_type=F32)


def nt(lhs, rhs):
    return lax.dot_general(lhs, rhs, (((1,), (1,)), ((), ())), preferred_element_type=F32)


def iotas():
    rows = lax.broadcasted_iota(jnp.int32, (TILE, TILE), 0)
    cols = lax.broadcasted_iota(jnp.int32, (TILE, TILE), 1)
    return rows, cols


def ones_where(mask):
    return jnp.where(mask, 1.0, 0.0).astype(BF16)


def column(turned, mask):
    wide = jnp.concatenate([turned] * PACK, axis=0)
    return jnp.sum(jnp.where(mask, wide, 0.0), axis=1, keepdims=True)


def squeeze_groups(wide, mask):
    kept = jnp.where(mask, wide, 0.0)
    total = kept[:LANES]
    for g in range(1, PACK):
        total = total + kept[g * LANES : (g + 1) * LANES]
    return total


def spread_groups(narrow, mask):
    return jnp.where(mask, jnp.concatenate([narrow] * PACK, axis=0), 0.0)


def circulant(row):
    base = jnp.broadcast_to(row, (LANES, TILE))
    base = pltpu.roll(base, 0, 1, stride=1, stride_axis=0).astype(BF16)
    return jnp.concatenate(
        [base] + [pltpu.roll(base, LANES * j, 1) for j in range(1, PACK)], axis=0
    )


def reversal():
    rows, cols = iotas()
    return ones_where((rows + cols) % TILE == 0)


def one_minus_exp(value):
    series = jnp.full_like(value, 1.0)
    for order in (7, 6, 5, 4, 3, 2):
        series = 1.0 - value * series / order
    return jnp.where(value < 0.125, value * series, 1.0 - jnp.exp(-value))


def chunk_mask(shape, bit):
    return (lax.broadcasted_iota(jnp.int32, shape, 1) // CHUNK) & bit == 0


def pair_chunks(turned):
    parts = [turned[CHUNK * j : CHUNK * (j + 1), :] for j in range(TILE // CHUNK)]
    for bit in (1, 2):
        keep = chunk_mask((CHUNK, TILE), bit)
        for j in range(len(parts)):
            if j & bit == 0:
                low, high = parts[j], parts[j + bit]
                parts[j] = jnp.where(keep, low, pltpu.roll(high, CHUNK * bit, 1))
                parts[j + bit] = jnp.where(keep, pltpu.roll(low, TILE - CHUNK * bit, 1), high)
    return parts


def windows(before, now):
    lanes = lax.broadcasted_iota(jnp.int32, now.shape, 1)
    none = jnp.zeros_like(now)
    first, second = [none if before is None else before], [now]
    for j in range(1, TILE // CHUNK):
        left = TILE - CHUNK * j
        moved = pltpu.roll(now, left, 1)
        older = none if before is None else pltpu.roll(before, left, 1)
        first.append(jnp.where(lanes < left, older, moved))
        second.append(moved)
    return jnp.concatenate(
        [jnp.concatenate(first, axis=0), jnp.concatenate(second, axis=0)], axis=1
    )


def beside(first, second):
    return jnp.concatenate([first, second], axis=1)


def above(*arrays):
    return jnp.concatenate(arrays, axis=0)


def apart(first, second):
    none = jnp.zeros_like(first)
    return above(beside(first, none), beside(none, second))


def lag_rows(chunks, shifted_rows, own_rows):
    wide = nn(above(*[chunks * own for own in own_rows]), shifted_rows)
    rows = lax.broadcasted_iota(jnp.int32, (2 * CHUNK, TILE), 0) % CHUNK
    lanes = lax.broadcasted_iota(jnp.int32, (2 * CHUNK, TILE), 1)
    sums = jnp.where(lanes + rows < CHUNK, wide[:, TILE:], wide[:, :TILE])
    parts = []
    for start in (0, CHUNK):
        part = pltpu.roll(sums[start : start + CHUNK], 0, 1, stride=1, stride_axis=0)
        parts.append(part[:8] + part[8:16] + part[16:24] + part[24:])
    return above(*parts).astype(BF16)


def now_and_before(now, before, rows, half):
    both = beside(now, before)
    pieces = []
    for g in range(0, PACK, 2):
        circs = beside(*[circulant(rows[h : h + 1, :]) for h in (g, g + 1)])
        w_now = circs * half
        wide = nn(both[g * LANES : (g + 2) * LANES, :], above(w_now, circs - w_now))
        pieces += [wide[:LANES, :TILE], wide[LANES:, TILE:]]
    return jnp.concatenate(pieces, axis=0)


def within_shard(array, rows, half):
    pieces = []
    for g in range(0, PACK, 4):
        weights = [
            beside(*[circulant(rows[h : h + 1, :]) for h in (k, k + 1)]) * half
            for k in (g, g + 2)
        ]
        parts = [array[k * LANES : (k + 2) * LANES, :] for k in (g, g + 2)]
        wide = nn(apart(*parts), above(*weights))
        for k in range(4):
            column_at = (k % 2) * TILE
            pieces.append(wide[k * LANES : (k + 1) * LANES, column_at : column_at + TILE])
    return jnp.concatenate(pieces, axis=0)


def block_groups(at, blocks, block):
    rows, cols = iotas()
    return cols == rows // LANES + (at * blocks + block) * PACK


def gate_kernel(query, key, product, held, made, arrived, left):
    size = held.shape[1] // PIECES

    def fetch(array, step):
        span = pl.ds(step * size, size)
        return pltpu.make_async_copy(
            (query, key)[array].at[span, :], held.at[array, span, :], arrived.at[array, step]
        )

    def store(step):
        span = pl.ds(step * size, size)
        return pltpu.make_async_copy(made.at[span, :], product.at[span, :], left.at[step])

    for step in range(PIECES):
        for array in range(2):
            fetch(array, step).start()
    for step in range(PIECES):
        for array in range(2):
            fetch(array, step).wait()
        span = pl.ds(step * size, size)
        made[span, :] = held[0, span, :] * held[1, span, :]
        store(step).start()
    for step in range(PIECES):
        store(step).wait()


def state_kernel(grad, value, rate, state):
    rows, cols = iotas()
    offsets = cols.astype(F32)
    mask = rows // LANES == cols // LANES
    at = pl.program_id(0)
    blocks = state.shape[0]
    for block in range(blocks):
        span = pl.ds(block * TILE, TILE)
        rates = column(rate[...], block_groups(at, blocks, block))
        powers = jnp.exp(-rates * offsets).astype(BF16)
        dz2 = grad[span, :] * value[span, :]
        state[block] = squeeze_groups(nt(powers, dz2), mask).astype(BF16)


def spans(array):
    return [pl.ds(block * TILE, TILE) for block in range(array.shape[0] // TILE)]


def group_rows(table, block):
    return table[pl.ds(block * PACK, PACK), :]


def local_kernel(grad, value, rate, residue, du2, to_next, taps, wide_rate):
    rows, cols = iotas()
    mask = rows // LANES == cols // LANES
    offsets = cols.astype(F32)
    at = pl.program_id(0)
    blocks = wide_rate.shape[0]
    coeffs = residue[...] * jnp.sqrt(one_minus_exp(2.0 * rate[...]))
    owns = [block_groups(at, blocks, block) for block in range(blocks)]
    rates = [column(rate[...], own) for own in owns]
    scales = [column(coeffs, own) for own in owns]
    sums = [
        jnp.sum((jnp.exp(-each * offsets) * scale).reshape(PACK, LANES, TILE), axis=1)
        for each, scale in zip(rates, scales)
    ]
    taps[...] = above(*sums)
    turned = nn(above(*sums).astype(BF16), reversal())
    lower = ones_where(rows >= cols)
    lower_half = beside(lower, lower)
    for block, span in enumerate(spans(grad)):
        wide_rate[block] = squeeze_groups(jnp.broadcast_to(rates[block], (TILE, TILE)), mask)
        ends = jnp.exp(-rates[block] * (TILE - 1 - offsets))
        to_next[span, :] = (ends * scales[block]).astype(BF16)
    results = [
        within_shard(
            grad[span, :] * value[span, :], turned[block * PACK : (block + 1) * PACK], lower_half
        )
        for block, span in enumerate(spans(grad))
    ]
    for span, result in zip(spans(grad), results):
        du2[span, :] = result


def table_kernel(rate, dz1, to_end, power):
    _, cols = iotas()
    offsets = cols.astype(F32)
    lags = ((CHUNK - 1 - cols) % TILE).astype(F32)
    at = pl.program_id(0)
    blocks = power.shape[0] // TILE
    for block, span in enumerate(spans(power)):
        rates = column(rate[...], block_groups(at, blocks, block))
        power[span, :] = jnp.exp(-rates * lags).astype(BF16)
        to_end[span, :] = jnp.exp(-rates * (TILE - 1 - offsets)).astype(BF16)


def middle_kernel(states, local, to_next, li_key, value, dz1, du2):
    rows, cols = iotas()
    mask = rows // LANES == cols // LANES
    wides = [spread_groups(states[block], mask).T.astype(BF16) for block in range(states.shape[0])]
    totals = [
        local[span, :] + nn(wide, to_next[span, :]) for span, wide in zip(spans(local), wides)
    ]
    for span, total in zip(spans(local), totals):
        du2[span, :] = total
        dy1 = total * li_key[span, :].astype(F32)
        dz1[span, :] = (dy1 * value[span, :].astype(F32)).astype(BF16)


def forward_kernel(
    before, now, filters, value, li_key, to_end, dz1, grad, li_value, power, after_shard, rate,
    z1, u2, packed, filter_sums, within_sums, across_sums,
):
    rows, cols = iotas()
    mask = rows // LANES == cols // LANES
    upper = ones_where(cols >= rows)
    upper_half = beside(upper, upper)
    turn = ones_where(cols == rows - rows % CHUNK + (CHUNK - 1 - rows % CHUNK))
    lanes = lax.broadcasted_iota(jnp.int32, (CHUNK, TILE), 1)
    own_rows = [ones_where((lanes // LANES) % 2 == i) for i in range(2)]
    eights = ones_where(
        lax.broadcasted_iota(jnp.int32, (2 * PACK, TILE), 1) // 8
        == lax.broadcasted_iota(jnp.int32, (2 * PACK, TILE), 0)
    )
    at = pl.program_id(0)
    blocks = now.shape[0] // TILE

    @pl.when(at == 0)
    def _():
        within_sums[...] = jnp.zeros_like(within_sums)
        across_sums[...] = jnp.zeros_like(across_sums)

    turned = []
    for span in spans(now):
        dz2 = grad[span, :] * li_value[span, :]
        turned.append(nt(turn, above(dz1[span, :], dz2)).astype(BF16))
    chunks = [(pair_chunks(each[:, :TILE]), pair_chunks(each[:, TILE:])) for each in turned]
    results = [
        now_and_before(
            now[span, :], before[span, :], group_rows(filters, block).astype(F32), upper_half
        )
        for block, span in enumerate(spans(now))
    ]
    halves = []
    for span, result in zip(spans(now), results):
        z1[span, :] = result
        y1 = (value[span, :].astype(F32) * result).astype(BF16).astype(F32)
        halves.append((y1 * li_key[span, :].astype(F32)).astype(BF16))
        u2[span, :] = halves[-1]
    ends = [nt(to_end[span, :], half) for span, half in zip(spans(now), halves)]

    lags = []
    for block in range(blocks):
        lag, energy = [], []
        for p in range(TILE // CHUNK):
            pair = pl.ds(block * TILE + p * CHUNK, CHUNK)
            older, newer = before[pair, :], now[pair, :]
            later = halves[block][p * CHUNK : (p + 1) * CHUNK]
            lag.append(lag_rows(chunks[block][0][p], windows(older, newer), own_rows))
            energy.append(lag_rows(chunks[block][1][p], windows(None, later), own_rows))
        lags.append(above(*lag, *energy))
    lags = [nn(eights, each) for each in lags]
    within, across = jnp.zeros((LANES, TILE), F32), jnp.zeros((LANES, TILE), F32)
    for block, span in enumerate(spans(now)):
        own = block_groups(at, blocks, block)
        energies = above(*[lags[block][PACK:].astype(BF16)] * LANES)
        within = within + squeeze_groups(nt(power[span, :], energies), own)
        state = squeeze_groups(ends[block], mask).astype(BF16)
        crossing = state.astype(F32) * after_shard[block]
        across = across + nn(crossing.astype(BF16), ones_where(own))
        packed[at * blocks + block] = state
    lags = [each[:PACK] for each in lags]
    few = blocks * PACK
    filter_sums[pl.ds(pl.multiple_of(at * few, few), few), :] = above(*lags)
    within_sums[...] += within
    across_sums[...] += across

    steps = filter_sums.shape[0] // few

    @pl.when(at == steps - 1)
    def _():
        place = ones_where((rows + cols) % TILE == CHUNK - 1)
        sums = nn(filter_sums[...].astype(BF16), place).astype(BF16)
        for chunk in range(filter_sums.shape[0] // LANES):
            packed[steps * blocks + chunk] = sums[chunk * LANES : (chunk + 1) * LANES]
        gains = jnp.sqrt(one_minus_exp(2.0 * rate[...]))
        total = gains * (within_sums[...] + across_sums[...])
        packed[steps * blocks + filter_sums.shape[0] // LANES] = total.astype(BF16)


def factor_kernel(
    bits, wide_rate, rate, residue, filters, later, zeros, after, mr_turned, *weights
):
    zeros[...] = jnp.zeros_like(zeros)
    place = lax.axis_index("seq")
    rates = wide_rate[...]
    weights = list(weights)
    for bit in bits:
        high = (place & bit) != 0
        passed = TILE * (place & (bit - 1)) + 1
        reach = jnp.exp(-rates * passed.astype(F32))
        weights.pop(0)[...] = jnp.where(high, reach, 0.0)
        if bit != bits[-1]:
            run = jnp.exp(-rates * (TILE * bit))
            one = jnp.ones_like(run)
            weights.pop(0)[...] = jnp.where(high, run, one)
            weights.pop(0)[...] = jnp.where(high, one, run)
    mr_turned[...] = nn(filters[...], reversal())
    _, cols = iotas()
    coeffs = residue[...] * jnp.sqrt(one_minus_exp(2.0 * rate[...]))
    for block, span in enumerate(spans(after)):
        own = block_groups(0, 0, block)
        powers = jnp.exp(-column(rate[...], own) * cols.astype(F32))
        after[span, :] = (powers * column(coeffs, own)).astype(BF16)


def within_kernel(u2, taps, z1, du2, value, li_key, z2, grad_value, grad_key, zeros):
    zeros[...] = jnp.zeros_like(zeros)
    rows, cols = iotas()
    upper = ones_where(cols >= rows)
    upper_half = beside(upper, upper)
    results = [
        within_shard(u2[span, :], group_rows(taps, block), upper_half)
        for block, span in enumerate(spans(u2))
    ]
    for span, result in zip(spans(u2), results):
        z2[span, :] = result
        z1_here, du2_here = z1[span, :], du2[span, :]
        y1 = (value[span, :].astype(F32) * z1_here).astype(BF16).astype(F32)
        grad_key[span, :] = (du2_here * y1).astype(BF16)
        grad_value[span, :] = (du2_here * li_key[span, :].astype(F32) * z1_here).astype(BF16)


def product_kernel(dz1, later, turned, query, key, grad_query, grad_key):
    rows, cols = iotas()
    lower = ones_where(rows >= cols)
    lower_half = beside(lower, lower)
    results = [
        now_and_before(
            dz1[span, :], later[span, :], group_rows(turned, block), lower_half
        )
        for block, span in enumerate(spans(dz1))
    ]
    for span, du1 in zip(spans(dz1), results):
        grad_query[span, :] = (du1 * key[span, :].astype(F32)).astype(BF16)
        grad_key[span, :] = (du1 * query[span, :].astype(F32)).astype(BF16)


def value_kernel(
    states, after, z2, grad, half, other, grad_value, grad_filter, grad_residue,
    made, filter_sum, residue_sum, left, done,
):
    rows, cols = iotas()
    mask = rows // LANES == cols // LANES
    at = pl.program_id(0)
    size = z2.shape[0]
    sums = [
        pltpu.make_async_copy(filter_sum, grad_filter, done.at[0]),
        pltpu.make_async_copy(residue_sum, grad_residue, done.at[1]),
    ]

    @pl.when(at == 0)
    def _():
        chunks = half.shape[0] - 1
        for chunk in range(chunks):
            both = half[chunk].astype(F32) + other[chunk].astype(F32)
            filter_sum[pl.ds(chunk * LANES, LANES), :] = both
        residue_sum[...] = half[chunks].astype(F32) + other[chunks].astype(F32)
        for copy in sums:
            copy.start()

    def store(step):
        span = pl.ds(pl.multiple_of(step * size, size), size)
        return pltpu.make_async_copy(made.at[span, :], grad_value.at[span, :], left.at[step])

    wides = [spread_groups(states[block], mask).T.astype(BF16) for block in range(states.shape[0])]
    totals = [z2[span, :] + nn(wide, after[span, :]) for span, wide in zip(spans(z2), wides)]
    for block, (span, total) in enumerate(zip(spans(z2), totals)):
        here = pl.ds(pl.multiple_of(at * size + block * TILE, TILE), TILE)
        made[here, :] = (grad[span, :].astype(F32) * total).astype(BF16)
    store(at).start()

    @pl.when(at == STEPS - 1)
    def _():
        for copy in sums:
            copy.wait()
        for step in range(STEPS):
            store(step).wait()


def shifted(value, axis, steps):
    count = lax.axis_size(axis)
    first, last = max(0, -steps), min(count, count - steps)
    return lax.ppermute(value, axis, [(source, source + steps) for source in range(first, last)])


def swapped(value, axis, bit):
    count = lax.axis_size(axis)
    return lax.ppermute(value, axis, [(source, source ^ bit) for source in range(count)])


def scan_bits():
    count, bit, bits = lax.axis_size("seq"), 1, []
    assert count & (count - 1) == 0
    while bit < count:
        bits.append(bit)
        bit *= 2
    return bits


def per_device(
    mr_query, mr_key, mr_value, li_key, li_value, grad_out, mr_filter, li_residue, li_rate
):
    query, key, value, key_two, value_two, grad = (
        array[0] for array in (mr_query, mr_key, mr_value, li_key, li_value, grad_out)
    )
    groups, filt_len = mr_filter.shape
    channels, seq_local = query.shape
    assert filt_len == TILE and seq_local == TILE and groups <= TILE
    assert channels == groups * LANES and li_rate.shape[1] == LANES
    rows = channels // STEPS
    few = groups // STEPS
    spare = ((0, 0), (0, TILE - groups))
    rate = jnp.pad(li_rate.T, spare)
    residue = jnp.pad(li_residue.T, spare)

    blocks = channels // TILE

    wide = pl.BlockSpec((rows, TILE), lambda i: (i, 0))
    table = pl.BlockSpec((few, TILE), lambda i: (i, 0))
    chunk = pl.BlockSpec((blocks // STEPS, LANES, TILE), lambda i: (i, 0, 0))
    modes = pl.BlockSpec((LANES, TILE), lambda i: (0, 0))
    distant = pl.BlockSpec(memory_space=pltpu.HBM)
    anywhere = pl.BlockSpec(memory_space=pl.ANY)
    wide_half = jax.ShapeDtypeStruct((channels, TILE), BF16)
    wide_full = jax.ShapeDtypeStruct((channels, TILE), F32)
    table_full = jax.ShapeDtypeStruct((groups, TILE), F32)
    chunk_half = jax.ShapeDtypeStruct((blocks, LANES, TILE), BF16)
    chunk_full = jax.ShapeDtypeStruct((blocks, LANES, TILE), F32)

    def call(kernel, name, in_specs, out_specs, out_shape, scratch=(), grid=STEPS, limit=VMEM_LIMIT, work=0):
        return pl.pallas_call(
            kernel,
            grid=(grid,),
            in_specs=in_specs,
            out_specs=out_specs,
            out_shape=out_shape,
            scratch_shapes=scratch,
            name=name,
            cost_estimate=pl.CostEstimate(
                flops=2 * work * channels * TILE * TILE, bytes_accessed=1, transcendentals=0
            ),
            compiler_params=pltpu.CompilerParams(vmem_limit_bytes=limit),
        )

    def whole(leaf):
        return pl.BlockSpec(leaf.shape, lambda i: (0,) * len(leaf.shape))

    def twice(spec):
        return pl.BlockSpec((2 * spec.block_shape[0],) + spec.block_shape[1:], spec.index_map)

    (product,) = call(
        gate_kernel, "gate", [distant] * 2, [distant], [wide_half],
        [
            pltpu.VMEM((2, channels, TILE), BF16), pltpu.VMEM((channels, TILE), BF16),
            pltpu.SemaphoreType.DMA((2, PIECES)), pltpu.SemaphoreType.DMA((PIECES,)),
        ],
        grid=1, limit=60 * 1024 * 1024,
    )(query, key)
    product_before = shifted(product, "seq", 1)

    (back,) = call(state_kernel, "state", [wide, wide, modes], [chunk], [chunk_half])(
        grad, value_two, rate
    )

    later_backs = [shifted(back, "seq", -gap) for gap in range(1, lax.axis_size("seq"))]
    du2_local, to_next, taps, wide_rate = call(
        local_kernel, "local", [wide, wide, modes, modes], [wide, wide, table, chunk],
        [wide_full, wide_half, table_full, chunk_full],
    )(grad, value_two, rate, residue)
    fade = jnp.exp(-TILE * wide_rate)
    after_shard = later_backs[-1].astype(F32)
    for other in later_backs[-2::-1]:
        after_shard = other.astype(F32) + fade * after_shard
    after_shard = after_shard * jnp.exp(-wide_rate)

    dz1, du2 = call(
        middle_kernel, "middle", [twice(chunk)] + [twice(wide)] * 4, [twice(wide)] * 2,
        [wide_half, wide_full], grid=STEPS // 2,
    )(after_shard, du2_local, to_next, key_two, value)
    dz1_later = shifted(dz1, "seq", -1)
    to_end, power = call(
        table_kernel, "table", [modes, anywhere], [wide, wide], [wide_half, wide_half]
    )(rate, dz1)

    filter_chunks = groups // LANES
    packed_shape = jax.ShapeDtypeStruct((blocks + filter_chunks + 1, LANES, TILE), BF16)
    z1, u2, packed = call(
        forward_kernel, "forward",
        [twice(spec) for spec in [wide, wide, table] + [wide] * 7 + [chunk]] + [modes],
        [twice(wide), twice(wide), whole(packed_shape)], [wide_full, wide_half, packed_shape],
        [pltpu.VMEM((groups, TILE), F32)] + [pltpu.VMEM((LANES, TILE), F32)] * 2,
        grid=STEPS // 2,
    )(
        product_before, product, mr_filter, value, key_two, to_end, dz1, grad, value_two, power,
        after_shard, rate,
    )

    bits = scan_bits()
    few_full = jax.ShapeDtypeStruct((filter_chunks + 1, LANES, TILE), F32)
    factors = 3 * len(bits) - 2
    z2, grad_mr_value, grad_li_key, within_zeros = call(
        within_kernel, "within",
        [wide, table, wide, wide, wide, wide], [wide] * 3 + [whole(few_full)],
        [wide_full, wide_half, wide_half, few_full],
    )(u2, taps, z1, du2, value, key_two)

    factor_shapes = [few_full, wide_half, table_full] + [chunk_full] * factors
    factor_zeros, after, mr_turned, *weights = call(
        functools.partial(factor_kernel, bits), "factor",
        [whole(chunk_full), modes, modes, whole(mr_filter), anywhere],
        [whole(leaf) for leaf in factor_shapes], factor_shapes, grid=1,
    )(wide_rate, rate, residue, mr_filter, dz1_later)

    grad_query, grad_key = call(
        product_kernel, "product",
        [twice(spec) for spec in (wide, wide, table, wide, wide)],
        [twice(wide), twice(wide)], [wide_half, wide_half], grid=STEPS // 2,
    )(dz1, dz1_later, mr_turned, query, key)

    assert lax.axis_size("dp") == 2
    half = packed[blocks:]
    sums = half.astype(F32) + swapped(half, "dp", 1).astype(F32) + within_zeros
    packed = jnp.concatenate([packed[:blocks], sums.astype(BF16)], axis=0)
    zeros = [factor_zeros]
    before_shard = jnp.zeros(back.shape, F32)
    for bit in bits:
        other = swapped(packed, "seq", bit)
        mine, theirs = packed[:blocks].astype(F32), other[:blocks].astype(F32)
        before_shard = before_shard + weights.pop(0) * theirs
        half, partner = packed[blocks:], other[blocks:]
        if bit != bits[-1]:
            sums = half.astype(F32) + partner.astype(F32)
            if zeros:
                sums = sums + zeros.pop(0)
            total = weights.pop(0) * theirs + weights.pop(0) * mine
            packed = jnp.concatenate([total.astype(BF16), sums.astype(BF16)], axis=0)
    residue_full = jax.ShapeDtypeStruct((LANES, TILE), F32)
    grad_li_value, grad_filter, grad_residue = call(
        value_kernel, "value",
        [chunk, wide, wide, wide, whole(half), whole(half)],
        [distant] * 3, [wide_half, table_full, residue_full],
        [
            pltpu.VMEM((channels, TILE), BF16), pltpu.VMEM((groups, TILE), F32),
            pltpu.VMEM((LANES, TILE), F32),
            pltpu.SemaphoreType.DMA((STEPS,)), pltpu.SemaphoreType.DMA((2,)),
        ],
    )(before_shard, after, z2, grad, half, partner)

    return (
        grad_query[None],
        grad_key[None],
        grad_mr_value[None],
        grad_li_key[None],
        grad_li_value[None],
        grad_filter,
        grad_residue[:, :groups].T,
    )


def solution(mesh):
    streams = (P("dp", "chan", "seq"),)
    tables = (P("chan", None),)
    return jax.shard_map(
        per_device,
        mesh=mesh,
        in_specs=streams * 6 + tables * 3,
        out_specs=streams * 5 + tables * 2,
        check_vma=False,
    )
```

```python
import functools

import jax
import jax.numpy as jnp
from jax import lax
from jax.experimental import pallas as pl
from jax.experimental.pallas import tpu as pltpu
from jax.sharding import PartitionSpec as P

F32 = jnp.float32
BF16 = jnp.bfloat16
TILE = 128
LANES = 16
PACK = TILE // LANES
CHUNK = 32
STEPS = 4
PIECES = 8
VMEM_LIMIT = 24 * 1024 * 1024


def nn(lhs, rhs):
    return lax.dot_general(lhs, rhs, (((1,), (0,)), ((), ())), preferred_element_type=F32)


def nt(lhs, rhs):
    return lax.dot_general(lhs, rhs, (((1,), (1,)), ((), ())), preferred_element_type=F32)


def iotas():
    rows = lax.broadcasted_iota(jnp.int32, (TILE, TILE), 0)
    cols = lax.broadcasted_iota(jnp.int32, (TILE, TILE), 1)
    return rows, cols


def ones_where(mask):
    return jnp.where(mask, 1.0, 0.0).astype(BF16)


def column(turned, mask):
    wide = jnp.concatenate([turned] * PACK, axis=0)
    return jnp.sum(jnp.where(mask, wide, 0.0), axis=1, keepdims=True)


def squeeze_groups(wide, mask):
    kept = jnp.where(mask, wide, 0.0)
    total = kept[:LANES]
    for g in range(1, PACK):
        total = total + kept[g * LANES : (g + 1) * LANES]
    return total


def spread_groups(narrow, mask):
    return jnp.where(mask, jnp.concatenate([narrow] * PACK, axis=0), 0.0)


def circulant(row):
    base = jnp.broadcast_to(row, (LANES, TILE))
    base = pltpu.roll(base, 0, 1, stride=1, stride_axis=0).astype(BF16)
    return jnp.concatenate(
        [base] + [pltpu.roll(base, LANES * j, 1) for j in range(1, PACK)], axis=0
    )


def reversal():
    rows, cols = iotas()
    return ones_where((rows + cols) % TILE == 0)


def one_minus_exp(value):
    series = jnp.full_like(value, 1.0)
    for order in (7, 6, 5, 4, 3, 2):
        series = 1.0 - value * series / order
    return jnp.where(value < 0.125, value * series, 1.0 - jnp.exp(-value))


def chunk_mask(shape, bit):
    return (lax.broadcasted_iota(jnp.int32, shape, 1) // CHUNK) & bit == 0


def pair_chunks(turned):
    parts = [turned[CHUNK * j : CHUNK * (j + 1), :] for j in range(TILE // CHUNK)]
    for bit in (1, 2):
        keep = chunk_mask((CHUNK, TILE), bit)
        for j in range(len(parts)):
            if j & bit == 0:
                low, high = parts[j], parts[j + bit]
                parts[j] = jnp.where(keep, low, pltpu.roll(high, CHUNK * bit, 1))
                parts[j + bit] = jnp.where(keep, pltpu.roll(low, TILE - CHUNK * bit, 1), high)
    return parts


def windows(before, now):
    lanes = lax.broadcasted_iota(jnp.int32, now.shape, 1)
    none = jnp.zeros_like(now)
    first, second = [none if before is None else before], [now]
    for j in range(1, TILE // CHUNK):
        left = TILE - CHUNK * j
        moved = pltpu.roll(now, left, 1)
        older = none if before is None else pltpu.roll(before, left, 1)
        first.append(jnp.where(lanes < left, older, moved))
        second.append(moved)
    return jnp.concatenate(
        [jnp.concatenate(first, axis=0), jnp.concatenate(second, axis=0)], axis=1
    )


def beside(first, second):
    return jnp.concatenate([first, second], axis=1)


def above(*arrays):
    return jnp.concatenate(arrays, axis=0)


def apart(first, second):
    none = jnp.zeros_like(first)
    return above(beside(first, none), beside(none, second))


def lag_rows(chunks, shifted_rows, own_rows):
    wide = nn(above(*[chunks * own for own in own_rows]), shifted_rows)
    rows = lax.broadcasted_iota(jnp.int32, (2 * CHUNK, TILE), 0) % CHUNK
    lanes = lax.broadcasted_iota(jnp.int32, (2 * CHUNK, TILE), 1)
    sums = jnp.where(lanes + rows < CHUNK, wide[:, TILE:], wide[:, :TILE])
    parts = []
    for start in (0, CHUNK):
        part = pltpu.roll(sums[start : start + CHUNK], 0, 1, stride=1, stride_axis=0)
        parts.append(part[:8] + part[8:16] + part[16:24] + part[24:])
    return above(*parts).astype(BF16)


def now_and_before(now, before, rows, half):
    both = beside(now, before)
    pieces = []
    for g in range(0, PACK, 2):
        circs = beside(*[circulant(rows[h : h + 1, :]) for h in (g, g + 1)])
        w_now = circs * half
        wide = nn(both[g * LANES : (g + 2) * LANES, :], above(w_now, circs - w_now))
        pieces += [wide[:LANES, :TILE], wide[LANES:, TILE:]]
    return jnp.concatenate(pieces, axis=0)


def within_shard(array, rows, half):
    pieces = []
    for g in range(0, PACK, 4):
        weights = [
            beside(*[circulant(rows[h : h + 1, :]) for h in (k, k + 1)]) * half
            for k in (g, g + 2)
        ]
        parts = [array[k * LANES : (k + 2) * LANES, :] for k in (g, g + 2)]
        wide = nn(apart(*parts), above(*weights))
        for k in range(4):
            column_at = (k % 2) * TILE
            pieces.append(wide[k * LANES : (k + 1) * LANES, column_at : column_at + TILE])
    return jnp.concatenate(pieces, axis=0)


def block_groups(at, blocks, block):
    rows, cols = iotas()
    return cols == rows // LANES + (at * blocks + block) * PACK


def gate_kernel(query, key, product, held, made, arrived, left):
    size = held.shape[1] // PIECES

    def fetch(array, step):
        span = pl.ds(step * size, size)
        return pltpu.make_async_copy(
            (query, key)[array].at[span, :], held.at[array, span, :], arrived.at[array, step]
        )

    def store(step):
        span = pl.ds(step * size, size)
        return pltpu.make_async_copy(made.at[span, :], product.at[span, :], left.at[step])

    for step in range(PIECES):
        for array in range(2):
            fetch(array, step).start()
    for step in range(PIECES):
        for array in range(2):
            fetch(array, step).wait()
        span = pl.ds(step * size, size)
        made[span, :] = held[0, span, :] * held[1, span, :]
        store(step).start()
    for step in range(PIECES):
        store(step).wait()


def state_kernel(grad, value, rate, state):
    rows, cols = iotas()
    offsets = cols.astype(F32)
    mask = rows // LANES == cols // LANES
    at = pl.program_id(0)
    blocks = state.shape[0]
    for block in range(blocks):
        span = pl.ds(block * TILE, TILE)
        rates = column(rate[...], block_groups(at, blocks, block))
        powers = jnp.exp(-rates * offsets).astype(BF16)
        dz2 = grad[span, :] * value[span, :]
        state[block] = squeeze_groups(nt(powers, dz2), mask).astype(BF16)


def spans(array):
    return [pl.ds(block * TILE, TILE) for block in range(array.shape[0] // TILE)]


def group_rows(table, block):
    return table[pl.ds(block * PACK, PACK), :]


def table_kernel(rate, residue, to_next, to_end, power, taps, turned, wide_rate):
    rows, cols = iotas()
    mask = rows // LANES == cols // LANES
    offsets = cols.astype(F32)
    lags = ((CHUNK - 1 - cols) % TILE).astype(F32)
    at = pl.program_id(0)
    blocks = power.shape[0] // TILE
    coeffs = residue[...] * jnp.sqrt(one_minus_exp(2.0 * rate[...]))
    sums = []
    for block in range(blocks):
        span = pl.ds(block * TILE, TILE)
        own = block_groups(at, blocks, block)
        rates = column(rate[...], own)
        scale = column(coeffs, own)
        wide_rate[block] = squeeze_groups(jnp.broadcast_to(rates, (TILE, TILE)), mask)
        scaled = jnp.exp(-rates * offsets) * scale
        ends = jnp.exp(-rates * (TILE - 1 - offsets))
        power[span, :] = jnp.exp(-rates * lags).astype(BF16)
        to_end[span, :] = ends.astype(BF16)
        to_next[span, :] = (ends * scale).astype(BF16)
        sums.append(jnp.sum(scaled.reshape(PACK, LANES, TILE), axis=1))
    taps[...] = above(*sums)
    turned[...] = nn(above(*sums).astype(BF16), reversal())


def local_kernel(grad, value, turned, du2):
    rows, cols = iotas()
    lower = ones_where(rows >= cols)
    lower_half = beside(lower, lower)
    results = [
        within_shard(grad[span, :] * value[span, :], group_rows(turned, block), lower_half)
        for block, span in enumerate(spans(grad))
    ]
    for span, result in zip(spans(grad), results):
        du2[span, :] = result


def middle_kernel(states, local, to_next, li_key, value, before, dz1, du2):
    rows, cols = iotas()
    mask = rows // LANES == cols // LANES
    wides = [spread_groups(states[block], mask).T.astype(BF16) for block in range(states.shape[0])]
    totals = [
        local[span, :] + nn(wide, to_next[span, :]) for span, wide in zip(spans(local), wides)
    ]
    for span, total in zip(spans(local), totals):
        du2[span, :] = total
        dy1 = total * li_key[span, :].astype(F32)
        dz1[span, :] = (dy1 * value[span, :].astype(F32)).astype(BF16)


def forward_kernel(
    before, now, filters, value, li_key, to_end, dz1, grad, li_value, power, after_shard, rate,
    z1, u2, packed, filter_sums, within_sums, across_sums,
):
    rows, cols = iotas()
    mask = rows // LANES == cols // LANES
    upper = ones_where(cols >= rows)
    upper_half = beside(upper, upper)
    turn = ones_where(cols == rows - rows % CHUNK + (CHUNK - 1 - rows % CHUNK))
    lanes = lax.broadcasted_iota(jnp.int32, (CHUNK, TILE), 1)
    own_rows = [ones_where((lanes // LANES) % 2 == i) for i in range(2)]
    eights = ones_where(
        lax.broadcasted_iota(jnp.int32, (2 * PACK, TILE), 1) // 8
        == lax.broadcasted_iota(jnp.int32, (2 * PACK, TILE), 0)
    )
    at = pl.program_id(0)
    blocks = now.shape[0] // TILE

    @pl.when(at == 0)
    def _():
        within_sums[...] = jnp.zeros_like(within_sums)
        across_sums[...] = jnp.zeros_like(across_sums)

    turned = []
    for span in spans(now):
        dz2 = grad[span, :] * li_value[span, :]
        turned.append(nt(turn, above(dz1[span, :], dz2)).astype(BF16))
    chunks = [(pair_chunks(each[:, :TILE]), pair_chunks(each[:, TILE:])) for each in turned]
    results = [
        now_and_before(
            now[span, :], before[span, :], group_rows(filters, block).astype(F32), upper_half
        )
        for block, span in enumerate(spans(now))
    ]
    halves = []
    for span, result in zip(spans(now), results):
        z1[span, :] = result
        y1 = (value[span, :].astype(F32) * result).astype(BF16).astype(F32)
        halves.append((y1 * li_key[span, :].astype(F32)).astype(BF16))
        u2[span, :] = halves[-1]
    ends = [nt(to_end[span, :], half) for span, half in zip(spans(now), halves)]

    lags = []
    for block in range(blocks):
        lag, energy = [], []
        for p in range(TILE // CHUNK):
            pair = pl.ds(block * TILE + p * CHUNK, CHUNK)
            older, newer = before[pair, :], now[pair, :]
            later = halves[block][p * CHUNK : (p + 1) * CHUNK]
            lag.append(lag_rows(chunks[block][0][p], windows(older, newer), own_rows))
            energy.append(lag_rows(chunks[block][1][p], windows(None, later), own_rows))
        lags.append(above(*lag, *energy))
    lags = [nn(eights, each) for each in lags]
    within, across = jnp.zeros((LANES, TILE), F32), jnp.zeros((LANES, TILE), F32)
    for block, span in enumerate(spans(now)):
        own = block_groups(at, blocks, block)
        energies = above(*[lags[block][PACK:].astype(BF16)] * LANES)
        within = within + squeeze_groups(nt(power[span, :], energies), own)
        state = squeeze_groups(ends[block], mask).astype(BF16)
        crossing = state.astype(F32) * after_shard[block]
        across = across + nn(crossing.astype(BF16), ones_where(own))
        packed[at * blocks + block] = state
    lags = [each[:PACK] for each in lags]
    few = blocks * PACK
    filter_sums[pl.ds(pl.multiple_of(at * few, few), few), :] = above(*lags)
    within_sums[...] += within
    across_sums[...] += across

    steps = filter_sums.shape[0] // few

    @pl.when(at == steps - 1)
    def _():
        place = ones_where((rows + cols) % TILE == CHUNK - 1)
        sums = nn(filter_sums[...].astype(BF16), place).astype(BF16)
        for chunk in range(filter_sums.shape[0] // LANES):
            packed[steps * blocks + chunk] = sums[chunk * LANES : (chunk + 1) * LANES]
        gains = jnp.sqrt(one_minus_exp(2.0 * rate[...]))
        total = gains * (within_sums[...] + across_sums[...])
        packed[steps * blocks + filter_sums.shape[0] // LANES] = total.astype(BF16)


def factor_kernel(
    bits, wide_rate, rate, residue, filters, later, zeros, after, mr_turned, *weights
):
    zeros[...] = jnp.zeros_like(zeros)
    place = lax.axis_index("seq")
    rates = wide_rate[...]
    weights = list(weights)
    for bit in bits:
        high = (place & bit) != 0
        passed = TILE * (place & (bit - 1)) + 1
        reach = jnp.exp(-rates * passed.astype(F32))
        weights.pop(0)[...] = jnp.where(high, reach, 0.0)
        if bit != bits[-1]:
            run = jnp.exp(-rates * (TILE * bit))
            one = jnp.ones_like(run)
            weights.pop(0)[...] = jnp.where(high, run, one)
            weights.pop(0)[...] = jnp.where(high, one, run)
    mr_turned[...] = nn(filters[...], reversal())
    _, cols = iotas()
    coeffs = residue[...] * jnp.sqrt(one_minus_exp(2.0 * rate[...]))
    for block, span in enumerate(spans(after)):
        own = block_groups(0, 0, block)
        powers = jnp.exp(-column(rate[...], own) * cols.astype(F32))
        after[span, :] = (powers * column(coeffs, own)).astype(BF16)


def within_kernel(u2, taps, z1, du2, value, li_key, z2, grad_value, grad_key, zeros):
    zeros[...] = jnp.zeros_like(zeros)
    rows, cols = iotas()
    upper = ones_where(cols >= rows)
    upper_half = beside(upper, upper)
    results = [
        within_shard(u2[span, :], group_rows(taps, block), upper_half)
        for block, span in enumerate(spans(u2))
    ]
    for span, result in zip(spans(u2), results):
        z2[span, :] = result
        z1_here, du2_here = z1[span, :], du2[span, :]
        y1 = (value[span, :].astype(F32) * z1_here).astype(BF16).astype(F32)
        grad_key[span, :] = (du2_here * y1).astype(BF16)
        grad_value[span, :] = (du2_here * li_key[span, :].astype(F32) * z1_here).astype(BF16)


def product_kernel(dz1, later, turned, query, key, grad_query, grad_key):
    rows, cols = iotas()
    lower = ones_where(rows >= cols)
    lower_half = beside(lower, lower)
    results = [
        now_and_before(
            dz1[span, :], later[span, :], group_rows(turned, block), lower_half
        )
        for block, span in enumerate(spans(dz1))
    ]
    for span, du1 in zip(spans(dz1), results):
        grad_query[span, :] = (du1 * key[span, :].astype(F32)).astype(BF16)
        grad_key[span, :] = (du1 * query[span, :].astype(F32)).astype(BF16)


def value_kernel(
    states, after, z2, grad, half, other, grad_value, grad_filter, grad_residue,
    made, filter_sum, residue_sum, left, done,
):
    rows, cols = iotas()
    mask = rows // LANES == cols // LANES
    at = pl.program_id(0)
    size = z2.shape[0]
    sums = [
        pltpu.make_async_copy(filter_sum, grad_filter, done.at[0]),
        pltpu.make_async_copy(residue_sum, grad_residue, done.at[1]),
    ]

    @pl.when(at == 0)
    def _():
        chunks = half.shape[0] - 1
        for chunk in range(chunks):
            both = half[chunk].astype(F32) + other[chunk].astype(F32)
            filter_sum[pl.ds(chunk * LANES, LANES), :] = both
        residue_sum[...] = half[chunks].astype(F32) + other[chunks].astype(F32)
        for copy in sums:
            copy.start()

    def store(step):
        span = pl.ds(pl.multiple_of(step * size, size), size)
        return pltpu.make_async_copy(made.at[span, :], grad_value.at[span, :], left.at[step])

    wides = [spread_groups(states[block], mask).T.astype(BF16) for block in range(states.shape[0])]
    totals = [z2[span, :] + nn(wide, after[span, :]) for span, wide in zip(spans(z2), wides)]
    for block, (span, total) in enumerate(zip(spans(z2), totals)):
        here = pl.ds(pl.multiple_of(at * size + block * TILE, TILE), TILE)
        made[here, :] = (grad[span, :].astype(F32) * total).astype(BF16)
    store(at).start()

    @pl.when(at == STEPS - 1)
    def _():
        for copy in sums:
            copy.wait()
        for step in range(STEPS):
            store(step).wait()


def shifted(value, axis, steps):
    count = lax.axis_size(axis)
    first, last = max(0, -steps), min(count, count - steps)
    return lax.ppermute(value, axis, [(source, source + steps) for source in range(first, last)])


def swapped(value, axis, bit):
    count = lax.axis_size(axis)
    return lax.ppermute(value, axis, [(source, source ^ bit) for source in range(count)])


def scan_bits():
    count, bit, bits = lax.axis_size("seq"), 1, []
    assert count & (count - 1) == 0
    while bit < count:
        bits.append(bit)
        bit *= 2
    return bits


def per_device(
    mr_query, mr_key, mr_value, li_key, li_value, grad_out, mr_filter, li_residue, li_rate
):
    query, key, value, key_two, value_two, grad = (
        array[0] for array in (mr_query, mr_key, mr_value, li_key, li_value, grad_out)
    )
    groups, filt_len = mr_filter.shape
    channels, seq_local = query.shape
    assert filt_len == TILE and seq_local == TILE and groups <= TILE
    assert channels == groups * LANES and li_rate.shape[1] == LANES
    rows = channels // STEPS
    few = groups // STEPS
    spare = ((0, 0), (0, TILE - groups))
    rate = jnp.pad(li_rate.T, spare)
    residue = jnp.pad(li_residue.T, spare)

    blocks = channels // TILE

    wide = pl.BlockSpec((rows, TILE), lambda i: (i, 0))
    table = pl.BlockSpec((few, TILE), lambda i: (i, 0))
    chunk = pl.BlockSpec((blocks // STEPS, LANES, TILE), lambda i: (i, 0, 0))
    modes = pl.BlockSpec((LANES, TILE), lambda i: (0, 0))
    distant = pl.BlockSpec(memory_space=pltpu.HBM)
    anywhere = pl.BlockSpec(memory_space=pl.ANY)
    wide_half = jax.ShapeDtypeStruct((channels, TILE), BF16)
    wide_full = jax.ShapeDtypeStruct((channels, TILE), F32)
    table_full = jax.ShapeDtypeStruct((groups, TILE), F32)
    chunk_half = jax.ShapeDtypeStruct((blocks, LANES, TILE), BF16)
    chunk_full = jax.ShapeDtypeStruct((blocks, LANES, TILE), F32)

    def call(kernel, name, in_specs, out_specs, out_shape, scratch=(), grid=STEPS, limit=VMEM_LIMIT, work=0):
        return pl.pallas_call(
            kernel,
            grid=(grid,),
            in_specs=in_specs,
            out_specs=out_specs,
            out_shape=out_shape,
            scratch_shapes=scratch,
            name=name,
            cost_estimate=pl.CostEstimate(
                flops=2 * work * channels * TILE * TILE, bytes_accessed=1, transcendentals=0
            ),
            compiler_params=pltpu.CompilerParams(vmem_limit_bytes=limit),
        )

    def whole(leaf):
        return pl.BlockSpec(leaf.shape, lambda i: (0,) * len(leaf.shape))

    def twice(spec):
        return pl.BlockSpec((2 * spec.block_shape[0],) + spec.block_shape[1:], spec.index_map)

    (product,) = call(
        gate_kernel, "gate", [distant] * 2, [distant], [wide_half],
        [
            pltpu.VMEM((2, channels, TILE), BF16), pltpu.VMEM((channels, TILE), BF16),
            pltpu.SemaphoreType.DMA((2, PIECES)), pltpu.SemaphoreType.DMA((PIECES,)),
        ],
        grid=1, limit=60 * 1024 * 1024,
    )(query, key)
    product_before = shifted(product, "seq", 1)

    (back,) = call(state_kernel, "state", [wide, wide, modes], [chunk], [chunk_half])(
        grad, value_two, rate
    )

    later_backs = [shifted(back, "seq", -gap) for gap in range(1, lax.axis_size("seq"))]
    to_next, to_end, power, taps, turned, wide_rate = call(
        table_kernel, "table", [modes, modes], [wide] * 3 + [table] * 2 + [chunk],
        [wide_half] * 3 + [table_full] * 2 + [chunk_full],
    )(rate, residue)
    (du2_local,) = call(local_kernel, "local", [wide, wide, table], [wide], [wide_full])(
        grad, value_two, turned
    )
    fade = jnp.exp(-TILE * wide_rate)
    after_shard = later_backs[-1].astype(F32)
    for other in later_backs[-2::-1]:
        after_shard = other.astype(F32) + fade * after_shard
    after_shard = after_shard * jnp.exp(-wide_rate)

    dz1, du2 = call(
        middle_kernel, "middle", [twice(chunk)] + [twice(wide)] * 4 + [anywhere],
        [twice(wide)] * 2,
        [wide_half, wide_full], grid=STEPS // 2,
    )(after_shard, du2_local, to_next, key_two, value, product_before)
    dz1_later = shifted(dz1, "seq", -1)

    filter_chunks = groups // LANES
    packed_shape = jax.ShapeDtypeStruct((blocks + filter_chunks + 1, LANES, TILE), BF16)
    z1, u2, packed = call(
        forward_kernel, "forward",
        [twice(spec) for spec in [wide, wide, table] + [wide] * 7 + [chunk]] + [modes],
        [twice(wide), twice(wide), whole(packed_shape)], [wide_full, wide_half, packed_shape],
        [pltpu.VMEM((groups, TILE), F32)] + [pltpu.VMEM((LANES, TILE), F32)] * 2,
        grid=STEPS // 2,
    )(
        product_before, product, mr_filter, value, key_two, to_end, dz1, grad, value_two, power,
        after_shard, rate,
    )

    bits = scan_bits()
    few_full = jax.ShapeDtypeStruct((filter_chunks + 1, LANES, TILE), F32)
    factors = 3 * len(bits) - 2
    z2, grad_mr_value, grad_li_key, within_zeros = call(
        within_kernel, "within",
        [wide, table, wide, wide, wide, wide], [wide] * 3 + [whole(few_full)],
        [wide_full, wide_half, wide_half, few_full],
    )(u2, taps, z1, du2, value, key_two)

    factor_shapes = [few_full, wide_half, table_full] + [chunk_full] * factors
    factor_zeros, after, mr_turned, *weights = call(
        functools.partial(factor_kernel, bits), "factor",
        [whole(chunk_full), modes, modes, whole(mr_filter), anywhere],
        [whole(leaf) for leaf in factor_shapes], factor_shapes, grid=1,
    )(wide_rate, rate, residue, mr_filter, dz1_later)

    grad_query, grad_key = call(
        product_kernel, "product",
        [twice(spec) for spec in (wide, wide, table, wide, wide)],
        [twice(wide), twice(wide)], [wide_half, wide_half], grid=STEPS // 2,
    )(dz1, dz1_later, mr_turned, query, key)

    assert lax.axis_size("dp") == 2
    half = packed[blocks:]
    sums = half.astype(F32) + swapped(half, "dp", 1).astype(F32) + within_zeros
    packed = jnp.concatenate([packed[:blocks], sums.astype(BF16)], axis=0)
    zeros = [factor_zeros]
    before_shard = jnp.zeros(back.shape, F32)
    for bit in bits:
        other = swapped(packed, "seq", bit)
        mine, theirs = packed[:blocks].astype(F32), other[:blocks].astype(F32)
        before_shard = before_shard + weights.pop(0) * theirs
        half, partner = packed[blocks:], other[blocks:]
        if bit != bits[-1]:
            sums = half.astype(F32) + partner.astype(F32)
            if zeros:
                sums = sums + zeros.pop(0)
            total = weights.pop(0) * theirs + weights.pop(0) * mine
            packed = jnp.concatenate([total.astype(BF16), sums.astype(BF16)], axis=0)
    residue_full = jax.ShapeDtypeStruct((LANES, TILE), F32)
    grad_li_value, grad_filter, grad_residue = call(
        value_kernel, "value",
        [chunk, wide, wide, wide, whole(half), whole(half)],
        [distant] * 3, [wide_half, table_full, residue_full],
        [
            pltpu.VMEM((channels, TILE), BF16), pltpu.VMEM((groups, TILE), F32),
            pltpu.VMEM((LANES, TILE), F32),
            pltpu.SemaphoreType.DMA((STEPS,)), pltpu.SemaphoreType.DMA((2,)),
        ],
    )(before_shard, after, z2, grad, half, partner)

    return (
        grad_query[None],
        grad_key[None],
        grad_mr_value[None],
        grad_li_key[None],
        grad_li_value[None],
        grad_filter,
        grad_residue[:, :groups].T,
    )


def solution(mesh):
    streams = (P("dp", "chan", "seq"),)
    tables = (P("chan", None),)
    return jax.shard_map(
        per_device,
        mesh=mesh,
        in_specs=streams * 6 + tables * 3,
        out_specs=streams * 5 + tables * 2,
        check_vma=False,
    )
```

```python
import functools

import jax
import jax.numpy as jnp
from jax import lax
from jax.experimental import pallas as pl
from jax.experimental.pallas import tpu as pltpu
from jax.sharding import PartitionSpec as P

F32 = jnp.float32
BF16 = jnp.bfloat16
TILE = 128
LANES = 16
PACK = TILE // LANES
CHUNK = 32
STEPS = 4
PIECES = 8
VMEM_LIMIT = 24 * 1024 * 1024


def nn(lhs, rhs):
    return lax.dot_general(lhs, rhs, (((1,), (0,)), ((), ())), preferred_element_type=F32)


def nt(lhs, rhs):
    return lax.dot_general(lhs, rhs, (((1,), (1,)), ((), ())), preferred_element_type=F32)


def iotas():
    rows = lax.broadcasted_iota(jnp.int32, (TILE, TILE), 0)
    cols = lax.broadcasted_iota(jnp.int32, (TILE, TILE), 1)
    return rows, cols


def ones_where(mask):
    return jnp.where(mask, 1.0, 0.0).astype(BF16)


def column(turned, mask):
    wide = jnp.concatenate([turned] * PACK, axis=0)
    return jnp.sum(jnp.where(mask, wide, 0.0), axis=1, keepdims=True)


def squeeze_groups(wide, mask):
    kept = jnp.where(mask, wide, 0.0)
    total = kept[:LANES]
    for g in range(1, PACK):
        total = total + kept[g * LANES : (g + 1) * LANES]
    return total


def spread_groups(narrow, mask):
    return jnp.where(mask, jnp.concatenate([narrow] * PACK, axis=0), 0.0)


def circulant(row):
    base = jnp.broadcast_to(row, (LANES, TILE))
    base = pltpu.roll(base, 0, 1, stride=1, stride_axis=0).astype(BF16)
    return jnp.concatenate(
        [base] + [pltpu.roll(base, LANES * j, 1) for j in range(1, PACK)], axis=0
    )


def reversal():
    rows, cols = iotas()
    return ones_where((rows + cols) % TILE == 0)


def one_minus_exp(value):
    series = jnp.full_like(value, 1.0)
    for order in (7, 6, 5, 4, 3, 2):
        series = 1.0 - value * series / order
    return jnp.where(value < 0.125, value * series, 1.0 - jnp.exp(-value))


def chunk_mask(shape, bit):
    return (lax.broadcasted_iota(jnp.int32, shape, 1) // CHUNK) & bit == 0


def pair_chunks(turned):
    parts = [turned[CHUNK * j : CHUNK * (j + 1), :] for j in range(TILE // CHUNK)]
    for bit in (1, 2):
        keep = chunk_mask((CHUNK, TILE), bit)
        for j in range(len(parts)):
            if j & bit == 0:
                low, high = parts[j], parts[j + bit]
                parts[j] = jnp.where(keep, low, pltpu.roll(high, CHUNK * bit, 1))
                parts[j + bit] = jnp.where(keep, pltpu.roll(low, TILE - CHUNK * bit, 1), high)
    return parts


def windows(before, now):
    lanes = lax.broadcasted_iota(jnp.int32, now.shape, 1)
    none = jnp.zeros_like(now)
    first, second = [none if before is None else before], [now]
    for j in range(1, TILE // CHUNK):
        left = TILE - CHUNK * j
        moved = pltpu.roll(now, left, 1)
        older = none if before is None else pltpu.roll(before, left, 1)
        first.append(jnp.where(lanes < left, older, moved))
        second.append(moved)
    return jnp.concatenate(
        [jnp.concatenate(first, axis=0), jnp.concatenate(second, axis=0)], axis=1
    )


def beside(first, second):
    return jnp.concatenate([first, second], axis=1)


def above(*arrays):
    return jnp.concatenate(arrays, axis=0)


def apart(first, second):
    none = jnp.zeros_like(first)
    return above(beside(first, none), beside(none, second))


def lag_rows(chunks, shifted_rows, own_rows):
    wide = nn(above(*[chunks * own for own in own_rows]), shifted_rows)
    rows = lax.broadcasted_iota(jnp.int32, (2 * CHUNK, TILE), 0) % CHUNK
    lanes = lax.broadcasted_iota(jnp.int32, (2 * CHUNK, TILE), 1)
    sums = jnp.where(lanes + rows < CHUNK, wide[:, TILE:], wide[:, :TILE])
    parts = []
    for start in (0, CHUNK):
        part = pltpu.roll(sums[start : start + CHUNK], 0, 1, stride=1, stride_axis=0)
        parts.append(part[:8] + part[8:16] + part[16:24] + part[24:])
    return above(*parts).astype(BF16)


def now_and_before(now, before, rows, half):
    both = beside(now, before)
    pieces = []
    for g in range(0, PACK, 2):
        circs = beside(*[circulant(rows[h : h + 1, :]) for h in (g, g + 1)])
        w_now = circs * half
        wide = nn(both[g * LANES : (g + 2) * LANES, :], above(w_now, circs - w_now))
        pieces += [wide[:LANES, :TILE], wide[LANES:, TILE:]]
    return jnp.concatenate(pieces, axis=0)


def within_shard(array, rows, half):
    pieces = []
    for g in range(0, PACK, 4):
        weights = [
            beside(*[circulant(rows[h : h + 1, :]) for h in (k, k + 1)]) * half
            for k in (g, g + 2)
        ]
        parts = [array[k * LANES : (k + 2) * LANES, :] for k in (g, g + 2)]
        wide = nn(apart(*parts), above(*weights))
        for k in range(4):
            column_at = (k % 2) * TILE
            pieces.append(wide[k * LANES : (k + 1) * LANES, column_at : column_at + TILE])
    return jnp.concatenate(pieces, axis=0)


def block_groups(at, blocks, block):
    rows, cols = iotas()
    return cols == rows // LANES + (at * blocks + block) * PACK


def gate_kernel(query, key, product, held, made, arrived, left):
    size = held.shape[1] // PIECES

    def fetch(array, step):
        span = pl.ds(step * size, size)
        return pltpu.make_async_copy(
            (query, key)[array].at[span, :], held.at[array, span, :], arrived.at[array, step]
        )

    def store(step):
        span = pl.ds(step * size, size)
        return pltpu.make_async_copy(made.at[span, :], product.at[span, :], left.at[step])

    for step in range(PIECES):
        for array in range(2):
            fetch(array, step).start()
    for step in range(PIECES):
        for array in range(2):
            fetch(array, step).wait()
        span = pl.ds(step * size, size)
        made[span, :] = held[0, span, :] * held[1, span, :]
        store(step).start()
    for step in range(PIECES):
        store(step).wait()


def state_kernel(grad, value, rate, state):
    rows, cols = iotas()
    offsets = cols.astype(F32)
    mask = rows // LANES == cols // LANES
    at = pl.program_id(0)
    blocks = state.shape[0]
    for block in range(blocks):
        span = pl.ds(block * TILE, TILE)
        rates = column(rate[...], block_groups(at, blocks, block))
        powers = jnp.exp(-rates * offsets).astype(BF16)
        dz2 = grad[span, :] * value[span, :]
        state[block] = squeeze_groups(nt(powers, dz2), mask).astype(BF16)


def spans(array):
    return [pl.ds(block * TILE, TILE) for block in range(array.shape[0] // TILE)]


def group_rows(table, block):
    return table[pl.ds(block * PACK, PACK), :]


def table_kernel(rate, residue, to_next, to_end, power, taps, turned, wide_rate):
    rows, cols = iotas()
    mask = rows // LANES == cols // LANES
    offsets = cols.astype(F32)
    lags = ((CHUNK - 1 - cols) % TILE).astype(F32)
    at = pl.program_id(0)
    blocks = power.shape[0] // TILE
    coeffs = residue[...] * jnp.sqrt(one_minus_exp(2.0 * rate[...]))
    sums = []
    for block in range(blocks):
        span = pl.ds(block * TILE, TILE)
        own = block_groups(at, blocks, block)
        rates = column(rate[...], own)
        scale = column(coeffs, own)
        wide_rate[block] = squeeze_groups(jnp.broadcast_to(rates, (TILE, TILE)), mask)
        scaled = jnp.exp(-rates * offsets) * scale
        ends = jnp.exp(-rates * (TILE - 1 - offsets))
        power[span, :] = jnp.exp(-rates * lags).astype(BF16)
        to_end[span, :] = ends.astype(BF16)
        to_next[span, :] = (ends * scale).astype(BF16)
        sums.append(jnp.sum(scaled.reshape(PACK, LANES, TILE), axis=1))
    taps[...] = above(*sums)
    turned[...] = nn(above(*sums).astype(BF16), reversal())


def local_kernel(grad, value, turned, du2):
    rows, cols = iotas()
    lower = ones_where(rows >= cols)
    lower_half = beside(lower, lower)
    results = [
        within_shard(grad[span, :] * value[span, :], group_rows(turned, block), lower_half)
        for block, span in enumerate(spans(grad))
    ]
    for span, result in zip(spans(grad), results):
        du2[span, :] = result


def middle_kernel(states, local, to_next, li_key, value, before, dz1, du2):
    rows, cols = iotas()
    mask = rows // LANES == cols // LANES
    wides = [spread_groups(states[block], mask).T.astype(BF16) for block in range(states.shape[0])]
    totals = [
        local[span, :] + nn(wide, to_next[span, :]) for span, wide in zip(spans(local), wides)
    ]
    for span, total in zip(spans(local), totals):
        du2[span, :] = total
        dy1 = total * li_key[span, :].astype(F32)
        dz1[span, :] = (dy1 * value[span, :].astype(F32)).astype(BF16)


def forward_kernel(
    before, now, filters, value, li_key, to_end, dz1, grad, li_value, power, after_shard, rate,
    z1, u2, packed, filter_sums, within_sums, across_sums,
):
    rows, cols = iotas()
    mask = rows // LANES == cols // LANES
    upper = ones_where(cols >= rows)
    upper_half = beside(upper, upper)
    turn = ones_where(cols == rows - rows % CHUNK + (CHUNK - 1 - rows % CHUNK))
    lanes = lax.broadcasted_iota(jnp.int32, (CHUNK, TILE), 1)
    own_rows = [ones_where((lanes // LANES) % 2 == i) for i in range(2)]
    eights = ones_where(
        lax.broadcasted_iota(jnp.int32, (2 * PACK, TILE), 1) // 8
        == lax.broadcasted_iota(jnp.int32, (2 * PACK, TILE), 0)
    )
    at = pl.program_id(0)
    blocks = now.shape[0] // TILE

    @pl.when(at == 0)
    def _():
        within_sums[...] = jnp.zeros_like(within_sums)
        across_sums[...] = jnp.zeros_like(across_sums)

    turned = []
    for span in spans(now):
        dz2 = grad[span, :] * li_value[span, :]
        turned.append(nt(turn, above(dz1[span, :], dz2)).astype(BF16))
    chunks = [(pair_chunks(each[:, :TILE]), pair_chunks(each[:, TILE:])) for each in turned]
    results = [
        now_and_before(
            now[span, :], before[span, :], group_rows(filters, block).astype(F32), upper_half
        )
        for block, span in enumerate(spans(now))
    ]
    halves = []
    for span, result in zip(spans(now), results):
        z1[span, :] = result
        y1 = (value[span, :].astype(F32) * result).astype(BF16).astype(F32)
        halves.append((y1 * li_key[span, :].astype(F32)).astype(BF16))
        u2[span, :] = halves[-1]
    ends = [nt(to_end[span, :], half) for span, half in zip(spans(now), halves)]

    lags = []
    for block in range(blocks):
        lag, energy = [], []
        for p in range(TILE // CHUNK):
            pair = pl.ds(block * TILE + p * CHUNK, CHUNK)
            older, newer = before[pair, :], now[pair, :]
            later = halves[block][p * CHUNK : (p + 1) * CHUNK]
            lag.append(lag_rows(chunks[block][0][p], windows(older, newer), own_rows))
            energy.append(lag_rows(chunks[block][1][p], windows(None, later), own_rows))
        lags.append(above(*lag, *energy))
    lags = [nn(eights, each) for each in lags]
    within, across = jnp.zeros((LANES, TILE), F32), jnp.zeros((LANES, TILE), F32)
    for block, span in enumerate(spans(now)):
        own = block_groups(at, blocks, block)
        energies = above(*[lags[block][PACK:].astype(BF16)] * LANES)
        within = within + squeeze_groups(nt(power[span, :], energies), own)
        state = squeeze_groups(ends[block], mask).astype(BF16)
        crossing = state.astype(F32) * after_shard[block]
        across = across + nn(crossing.astype(BF16), ones_where(own))
        packed[at * blocks + block] = state
    lags = [each[:PACK] for each in lags]
    few = blocks * PACK
    filter_sums[pl.ds(pl.multiple_of(at * few, few), few), :] = above(*lags)
    within_sums[...] += within
    across_sums[...] += across

    steps = filter_sums.shape[0] // few

    @pl.when(at == steps - 1)
    def _():
        place = ones_where((rows + cols) % TILE == CHUNK - 1)
        sums = nn(filter_sums[...].astype(BF16), place).astype(BF16)
        for chunk in range(filter_sums.shape[0] // LANES):
            packed[steps * blocks + chunk] = sums[chunk * LANES : (chunk + 1) * LANES]
        gains = jnp.sqrt(one_minus_exp(2.0 * rate[...]))
        total = gains * (within_sums[...] + across_sums[...])
        packed[steps * blocks + filter_sums.shape[0] // LANES] = total.astype(BF16)


def factor_kernel(
    bits, wide_rate, rate, residue, filters, later, zeros, after, mr_turned, *weights
):
    zeros[...] = jnp.zeros_like(zeros)
    place = lax.axis_index("seq")
    rates = wide_rate[...]
    weights = list(weights)
    for bit in bits:
        low = (place & bit) == 0
        one = jnp.ones_like(rates)
        weights.pop(0)[...] = jnp.where(low, one, 0.0)
        weights.pop(0)[...] = jnp.where(low, jnp.exp(-rates * (2 * TILE * bit)), one)
    mr_turned[...] = nn(filters[...], reversal())
    _, cols = iotas()
    coeffs = residue[...] * jnp.sqrt(one_minus_exp(2.0 * rate[...]))
    for block, span in enumerate(spans(after)):
        own = block_groups(0, 0, block)
        powers = jnp.exp(-column(rate[...], own) * cols.astype(F32))
        after[span, :] = (powers * column(coeffs, own)).astype(BF16)


def within_kernel(u2, taps, z1, du2, value, li_key, z2, grad_value, grad_key, zeros):
    zeros[...] = jnp.zeros_like(zeros)
    rows, cols = iotas()
    upper = ones_where(cols >= rows)
    upper_half = beside(upper, upper)
    results = [
        within_shard(u2[span, :], group_rows(taps, block), upper_half)
        for block, span in enumerate(spans(u2))
    ]
    for span, result in zip(spans(u2), results):
        z2[span, :] = result
        z1_here, du2_here = z1[span, :], du2[span, :]
        y1 = (value[span, :].astype(F32) * z1_here).astype(BF16).astype(F32)
        grad_key[span, :] = (du2_here * y1).astype(BF16)
        grad_value[span, :] = (du2_here * li_key[span, :].astype(F32) * z1_here).astype(BF16)


def product_kernel(dz1, later, turned, query, key, grad_query, grad_key):
    rows, cols = iotas()
    lower = ones_where(rows >= cols)
    lower_half = beside(lower, lower)
    results = [
        now_and_before(
            dz1[span, :], later[span, :], group_rows(turned, block), lower_half
        )
        for block, span in enumerate(spans(dz1))
    ]
    for span, du1 in zip(spans(dz1), results):
        grad_query[span, :] = (du1 * key[span, :].astype(F32)).astype(BF16)
        grad_key[span, :] = (du1 * query[span, :].astype(F32)).astype(BF16)


def value_kernel(
    states, after, z2, grad, half, other, grad_value, grad_filter, grad_residue,
    made, filter_sum, residue_sum, left, done,
):
    rows, cols = iotas()
    mask = rows // LANES == cols // LANES
    at = pl.program_id(0)
    size = z2.shape[0]
    sums = [
        pltpu.make_async_copy(filter_sum, grad_filter, done.at[0]),
        pltpu.make_async_copy(residue_sum, grad_residue, done.at[1]),
    ]

    @pl.when(at == 0)
    def _():
        chunks = half.shape[0] - 1
        for chunk in range(chunks):
            both = half[chunk].astype(F32) + other[chunk].astype(F32)
            filter_sum[pl.ds(chunk * LANES, LANES), :] = both
        residue_sum[...] = half[chunks].astype(F32) + other[chunks].astype(F32)
        for copy in sums:
            copy.start()

    def store(step):
        span = pl.ds(pl.multiple_of(step * size, size), size)
        return pltpu.make_async_copy(made.at[span, :], grad_value.at[span, :], left.at[step])

    wides = [spread_groups(states[block], mask).T.astype(BF16) for block in range(states.shape[0])]
    totals = [z2[span, :] + nn(wide, after[span, :]) for span, wide in zip(spans(z2), wides)]
    for block, (span, total) in enumerate(zip(spans(z2), totals)):
        here = pl.ds(pl.multiple_of(at * size + block * TILE, TILE), TILE)
        made[here, :] = (grad[span, :].astype(F32) * total).astype(BF16)
    store(at).start()

    @pl.when(at == STEPS - 1)
    def _():
        for copy in sums:
            copy.wait()
        for step in range(STEPS):
            store(step).wait()


def shifted(value, axis, steps):
    count = lax.axis_size(axis)
    first, last = max(0, -steps), min(count, count - steps)
    return lax.ppermute(value, axis, [(source, source + steps) for source in range(first, last)])


def swapped(value, axis, bit):
    count = lax.axis_size(axis)
    return lax.ppermute(value, axis, [(source, source ^ bit) for source in range(count)])


def scan_bits():
    count, bit, bits = lax.axis_size("seq"), 1, []
    assert count & (count - 1) == 0
    while bit < count:
        bits.append(bit)
        bit *= 2
    return bits


def per_device(
    mr_query, mr_key, mr_value, li_key, li_value, grad_out, mr_filter, li_residue, li_rate
):
    query, key, value, key_two, value_two, grad = (
        array[0] for array in (mr_query, mr_key, mr_value, li_key, li_value, grad_out)
    )
    groups, filt_len = mr_filter.shape
    channels, seq_local = query.shape
    assert filt_len == TILE and seq_local == TILE and groups <= TILE
    assert channels == groups * LANES and li_rate.shape[1] == LANES
    rows = channels // STEPS
    few = groups // STEPS
    spare = ((0, 0), (0, TILE - groups))
    rate = jnp.pad(li_rate.T, spare)
    residue = jnp.pad(li_residue.T, spare)

    blocks = channels // TILE

    wide = pl.BlockSpec((rows, TILE), lambda i: (i, 0))
    table = pl.BlockSpec((few, TILE), lambda i: (i, 0))
    chunk = pl.BlockSpec((blocks // STEPS, LANES, TILE), lambda i: (i, 0, 0))
    modes = pl.BlockSpec((LANES, TILE), lambda i: (0, 0))
    distant = pl.BlockSpec(memory_space=pltpu.HBM)
    anywhere = pl.BlockSpec(memory_space=pl.ANY)
    wide_half = jax.ShapeDtypeStruct((channels, TILE), BF16)
    wide_full = jax.ShapeDtypeStruct((channels, TILE), F32)
    table_full = jax.ShapeDtypeStruct((groups, TILE), F32)
    chunk_half = jax.ShapeDtypeStruct((blocks, LANES, TILE), BF16)
    chunk_full = jax.ShapeDtypeStruct((blocks, LANES, TILE), F32)

    def call(kernel, name, in_specs, out_specs, out_shape, scratch=(), grid=STEPS, limit=VMEM_LIMIT, work=0):
        return pl.pallas_call(
            kernel,
            grid=(grid,),
            in_specs=in_specs,
            out_specs=out_specs,
            out_shape=out_shape,
            scratch_shapes=scratch,
            name=name,
            cost_estimate=pl.CostEstimate(
                flops=2 * work * channels * TILE * TILE, bytes_accessed=1, transcendentals=0
            ),
            compiler_params=pltpu.CompilerParams(vmem_limit_bytes=limit),
        )

    def whole(leaf):
        return pl.BlockSpec(leaf.shape, lambda i: (0,) * len(leaf.shape))

    def twice(spec):
        return pl.BlockSpec((2 * spec.block_shape[0],) + spec.block_shape[1:], spec.index_map)

    (product,) = call(
        gate_kernel, "gate", [distant] * 2, [distant], [wide_half],
        [
            pltpu.VMEM((2, channels, TILE), BF16), pltpu.VMEM((channels, TILE), BF16),
            pltpu.SemaphoreType.DMA((2, PIECES)), pltpu.SemaphoreType.DMA((PIECES,)),
        ],
        grid=1, limit=60 * 1024 * 1024,
    )(query, key)
    product_before = shifted(product, "seq", 1)

    (back,) = call(state_kernel, "state", [wide, wide, modes], [chunk], [chunk_half])(
        grad, value_two, rate
    )

    later_backs = [shifted(back, "seq", -gap) for gap in range(1, lax.axis_size("seq"))]
    to_next, to_end, power, taps, turned, wide_rate = call(
        table_kernel, "table", [modes, modes], [wide] * 3 + [table] * 2 + [chunk],
        [wide_half] * 3 + [table_full] * 2 + [chunk_full],
    )(rate, residue)
    (du2_local,) = call(local_kernel, "local", [wide, wide, table], [wide], [wide_full])(
        grad, value_two, turned
    )
    fade = jnp.exp(-TILE * wide_rate)
    after_shard = later_backs[-1].astype(F32)
    for other in later_backs[-2::-1]:
        after_shard = other.astype(F32) + fade * after_shard
    after_shard = after_shard * jnp.exp(-wide_rate)

    dz1, du2 = call(
        middle_kernel, "middle", [twice(chunk)] + [twice(wide)] * 4 + [anywhere],
        [twice(wide)] * 2,
        [wide_half, wide_full], grid=STEPS // 2,
    )(after_shard, du2_local, to_next, key_two, value, product_before)
    dz1_later = shifted(dz1, "seq", -1)

    filter_chunks = groups // LANES
    packed_shape = jax.ShapeDtypeStruct((blocks + filter_chunks + 1, LANES, TILE), BF16)
    z1, u2, packed = call(
        forward_kernel, "forward",
        [twice(spec) for spec in [wide, wide, table] + [wide] * 7 + [chunk]] + [modes],
        [twice(wide), twice(wide), whole(packed_shape)], [wide_full, wide_half, packed_shape],
        [pltpu.VMEM((groups, TILE), F32)] + [pltpu.VMEM((LANES, TILE), F32)] * 2,
        grid=STEPS // 2,
    )(
        product_before, product, mr_filter, value, key_two, to_end, dz1, grad, value_two, power,
        after_shard, rate,
    )

    bits = scan_bits()[::-1]
    few_full = jax.ShapeDtypeStruct((filter_chunks + 1, LANES, TILE), F32)
    factors = 2 * (len(bits) - 1)
    z2, grad_mr_value, grad_li_key, within_zeros = call(
        within_kernel, "within",
        [wide, table, wide, wide, wide, wide], [wide] * 3 + [whole(few_full)],
        [wide_full, wide_half, wide_half, few_full],
    )(u2, taps, z1, du2, value, key_two)

    factor_shapes = [few_full, wide_half, table_full] + [chunk_full] * factors
    factor_zeros, after, mr_turned, *weights = call(
        functools.partial(factor_kernel, bits[1:]), "factor",
        [whole(chunk_full), modes, modes, whole(mr_filter), anywhere],
        [whole(leaf) for leaf in factor_shapes], factor_shapes, grid=1,
    )(wide_rate, rate, residue, mr_filter, dz1_later)

    grad_query, grad_key = call(
        product_kernel, "product",
        [twice(spec) for spec in (wide, wide, table, wide, wide)],
        [twice(wide), twice(wide)], [wide_half, wide_half], grid=STEPS // 2,
    )(dz1, dz1_later, mr_turned, query, key)

    assert lax.axis_size("dp") == 2
    state, half = packed[:blocks], packed[blocks:]
    reached = shifted(state, "seq", bits[0]).astype(F32)
    sums = half.astype(F32) + swapped(half, "dp", 1).astype(F32) + within_zeros
    half = sums.astype(BF16)
    partner = swapped(half, "seq", bits[0])
    zeros = factor_zeros
    for bit in bits[1:]:
        sums = half.astype(F32) + partner.astype(F32) + zeros
        sent = weights.pop(0) * state.astype(F32) + weights.pop(0) * reached
        packed = jnp.concatenate([sent.astype(BF16), sums.astype(BF16)], axis=0)
        other = swapped(packed, "seq", bit)
        reached = other[:blocks].astype(F32) + jnp.exp(-TILE * bit * wide_rate) * reached
        half, partner = packed[blocks:], other[blocks:]
    before_shard = reached * jnp.exp(-wide_rate)
    residue_full = jax.ShapeDtypeStruct((LANES, TILE), F32)
    grad_li_value, grad_filter, grad_residue = call(
        value_kernel, "value",
        [chunk, wide, wide, wide, whole(half), whole(half)],
        [distant] * 3, [wide_half, table_full, residue_full],
        [
            pltpu.VMEM((channels, TILE), BF16), pltpu.VMEM((groups, TILE), F32),
            pltpu.VMEM((LANES, TILE), F32),
            pltpu.SemaphoreType.DMA((STEPS,)), pltpu.SemaphoreType.DMA((2,)),
        ],
    )(before_shard, after, z2, grad, half, partner)

    return (
        grad_query[None],
        grad_key[None],
        grad_mr_value[None],
        grad_li_key[None],
        grad_li_value[None],
        grad_filter,
        grad_residue[:, :groups].T,
    )


def solution(mesh):
    streams = (P("dp", "chan", "seq"),)
    tables = (P("chan", None),)
    return jax.shard_map(
        per_device,
        mesh=mesh,
        in_specs=streams * 6 + tables * 3,
        out_specs=streams * 5 + tables * 2,
        check_vma=False,
    )
```

```python
import functools

import jax
import jax.numpy as jnp
from jax import lax
from jax.experimental import pallas as pl
from jax.experimental.pallas import tpu as pltpu
from jax.sharding import PartitionSpec as P

F32 = jnp.float32
BF16 = jnp.bfloat16
TILE = 128
LANES = 16
PACK = TILE // LANES
CHUNK = 32
STEPS = 4
PIECES = 8
VMEM_LIMIT = 24 * 1024 * 1024


def nn(lhs, rhs):
    return lax.dot_general(lhs, rhs, (((1,), (0,)), ((), ())), preferred_element_type=F32)


def nt(lhs, rhs):
    return lax.dot_general(lhs, rhs, (((1,), (1,)), ((), ())), preferred_element_type=F32)


def iotas():
    rows = lax.broadcasted_iota(jnp.int32, (TILE, TILE), 0)
    cols = lax.broadcasted_iota(jnp.int32, (TILE, TILE), 1)
    return rows, cols


def ones_where(mask):
    return jnp.where(mask, 1.0, 0.0).astype(BF16)


def column(turned, mask):
    wide = jnp.concatenate([turned] * PACK, axis=0)
    return jnp.sum(jnp.where(mask, wide, 0.0), axis=1, keepdims=True)


def squeeze_groups(wide, mask):
    kept = jnp.where(mask, wide, 0.0)
    total = kept[:LANES]
    for g in range(1, PACK):
        total = total + kept[g * LANES : (g + 1) * LANES]
    return total


def spread_groups(narrow, mask):
    return jnp.where(mask, jnp.concatenate([narrow] * PACK, axis=0), 0.0)


def circulant(row):
    base = jnp.broadcast_to(row, (LANES, TILE))
    base = pltpu.roll(base, 0, 1, stride=1, stride_axis=0).astype(BF16)
    return jnp.concatenate(
        [base] + [pltpu.roll(base, LANES * j, 1) for j in range(1, PACK)], axis=0
    )


def reversal():
    rows, cols = iotas()
    return ones_where((rows + cols) % TILE == 0)


def one_minus_exp(value):
    series = jnp.full_like(value, 1.0)
    for order in (7, 6, 5, 4, 3, 2):
        series = 1.0 - value * series / order
    return jnp.where(value < 0.125, value * series, 1.0 - jnp.exp(-value))


def chunk_mask(shape, bit):
    return (lax.broadcasted_iota(jnp.int32, shape, 1) // CHUNK) & bit == 0


def pair_chunks(turned):
    parts = [turned[CHUNK * j : CHUNK * (j + 1), :] for j in range(TILE // CHUNK)]
    for bit in (1, 2):
        keep = chunk_mask((CHUNK, TILE), bit)
        for j in range(len(parts)):
            if j & bit == 0:
                low, high = parts[j], parts[j + bit]
                parts[j] = jnp.where(keep, low, pltpu.roll(high, CHUNK * bit, 1))
                parts[j + bit] = jnp.where(keep, pltpu.roll(low, TILE - CHUNK * bit, 1), high)
    return parts


def windows(before, now):
    lanes = lax.broadcasted_iota(jnp.int32, now.shape, 1)
    none = jnp.zeros_like(now)
    first, second = [none if before is None else before], [now]
    for j in range(1, TILE // CHUNK):
        left = TILE - CHUNK * j
        moved = pltpu.roll(now, left, 1)
        older = none if before is None else pltpu.roll(before, left, 1)
        first.append(jnp.where(lanes < left, older, moved))
        second.append(moved)
    return jnp.concatenate(
        [jnp.concatenate(first, axis=0), jnp.concatenate(second, axis=0)], axis=1
    )


def beside(first, second):
    return jnp.concatenate([first, second], axis=1)


def above(*arrays):
    return jnp.concatenate(arrays, axis=0)


def apart(first, second):
    none = jnp.zeros_like(first)
    return above(beside(first, none), beside(none, second))


def lag_rows(chunks, shifted_rows, own_rows):
    wide = nn(above(*[chunks * own for own in own_rows]), shifted_rows)
    rows = lax.broadcasted_iota(jnp.int32, (2 * CHUNK, TILE), 0) % CHUNK
    lanes = lax.broadcasted_iota(jnp.int32, (2 * CHUNK, TILE), 1)
    sums = jnp.where(lanes + rows < CHUNK, wide[:, TILE:], wide[:, :TILE])
    parts = []
    for start in (0, CHUNK):
        part = pltpu.roll(sums[start : start + CHUNK], 0, 1, stride=1, stride_axis=0)
        parts.append(part[:8] + part[8:16] + part[16:24] + part[24:])
    return above(*parts).astype(BF16)


def now_and_before(now, before, rows, half):
    both = beside(now, before)
    pieces = []
    for g in range(0, PACK, 2):
        circs = beside(*[circulant(rows[h : h + 1, :]) for h in (g, g + 1)])
        w_now = circs * half
        wide = nn(both[g * LANES : (g + 2) * LANES, :], above(w_now, circs - w_now))
        pieces += [wide[:LANES, :TILE], wide[LANES:, TILE:]]
    return jnp.concatenate(pieces, axis=0)


def within_shard(array, rows, half):
    pieces = []
    for g in range(0, PACK, 4):
        weights = [
            beside(*[circulant(rows[h : h + 1, :]) for h in (k, k + 1)]) * half
            for k in (g, g + 2)
        ]
        parts = [array[k * LANES : (k + 2) * LANES, :] for k in (g, g + 2)]
        wide = nn(apart(*parts), above(*weights))
        for k in range(4):
            column_at = (k % 2) * TILE
            pieces.append(wide[k * LANES : (k + 1) * LANES, column_at : column_at + TILE])
    return jnp.concatenate(pieces, axis=0)


def block_groups(at, blocks, block):
    rows, cols = iotas()
    return cols == rows // LANES + (at * blocks + block) * PACK


def gate_kernel(query, key, product, held, made, arrived, left):
    size = held.shape[1] // PIECES

    def fetch(array, step):
        span = pl.ds(step * size, size)
        return pltpu.make_async_copy(
            (query, key)[array].at[span, :], held.at[array, span, :], arrived.at[array, step]
        )

    def store(step):
        span = pl.ds(step * size, size)
        return pltpu.make_async_copy(made.at[span, :], product.at[span, :], left.at[step])

    for step in range(PIECES):
        for array in range(2):
            fetch(array, step).start()
    for step in range(PIECES):
        for array in range(2):
            fetch(array, step).wait()
        span = pl.ds(step * size, size)
        made[span, :] = held[0, span, :] * held[1, span, :]
        store(step).start()
    for step in range(PIECES):
        store(step).wait()


def state_kernel(grad, value, rate, state):
    rows, cols = iotas()
    offsets = cols.astype(F32)
    mask = rows // LANES == cols // LANES
    at = pl.program_id(0)
    blocks = state.shape[0]
    for block in range(blocks):
        span = pl.ds(block * TILE, TILE)
        rates = column(rate[...], block_groups(at, blocks, block))
        powers = jnp.exp(-rates * offsets).astype(BF16)
        dz2 = grad[span, :] * value[span, :]
        state[block] = squeeze_groups(nt(powers, dz2), mask).astype(BF16)


def spans(array):
    return [pl.ds(block * TILE, TILE) for block in range(array.shape[0] // TILE)]


def group_rows(table, block):
    return table[pl.ds(block * PACK, PACK), :]


def table_kernel(rate, residue, to_next, to_end, power, taps, turned, wide_rate):
    rows, cols = iotas()
    mask = rows // LANES == cols // LANES
    offsets = cols.astype(F32)
    lags = ((CHUNK - 1 - cols) % TILE).astype(F32)
    at = pl.program_id(0)
    blocks = power.shape[0] // TILE
    coeffs = residue[...] * jnp.sqrt(one_minus_exp(2.0 * rate[...]))
    sums = []
    for block in range(blocks):
        span = pl.ds(block * TILE, TILE)
        own = block_groups(at, blocks, block)
        rates = column(rate[...], own)
        scale = column(coeffs, own)
        wide_rate[block] = squeeze_groups(jnp.broadcast_to(rates, (TILE, TILE)), mask)
        scaled = jnp.exp(-rates * offsets) * scale
        ends = jnp.exp(-rates * (TILE - 1 - offsets))
        power[span, :] = jnp.exp(-rates * lags).astype(BF16)
        to_end[span, :] = ends.astype(BF16)
        to_next[span, :] = (ends * scale).astype(BF16)
        sums.append(jnp.sum(scaled.reshape(PACK, LANES, TILE), axis=1))
    taps[...] = above(*sums)
    turned[...] = nn(above(*sums).astype(BF16), reversal())


def local_kernel(grad, value, turned, du2):
    rows, cols = iotas()
    lower = ones_where(rows >= cols)
    lower_half = beside(lower, lower)
    results = [
        within_shard(grad[span, :] * value[span, :], group_rows(turned, block), lower_half)
        for block, span in enumerate(spans(grad))
    ]
    for span, result in zip(spans(grad), results):
        du2[span, :] = result


def middle_kernel(states, local, to_next, li_key, value, before, dz1, du2):
    rows, cols = iotas()
    mask = rows // LANES == cols // LANES
    wides = [spread_groups(states[block], mask).T.astype(BF16) for block in range(states.shape[0])]
    totals = [
        local[span, :] + nn(wide, to_next[span, :]) for span, wide in zip(spans(local), wides)
    ]
    for span, total in zip(spans(local), totals):
        du2[span, :] = total
        dy1 = total * li_key[span, :].astype(F32)
        dz1[span, :] = (dy1 * value[span, :].astype(F32)).astype(BF16)


def forward_kernel(
    before, now, filters, value, li_key, to_end, dz1, grad, li_value, power, after_shard, rate,
    z1, u2, packed, filter_sums, within_sums, across_sums,
):
    rows, cols = iotas()
    mask = rows // LANES == cols // LANES
    upper = ones_where(cols >= rows)
    upper_half = beside(upper, upper)
    turn = ones_where(cols == rows - rows % CHUNK + (CHUNK - 1 - rows % CHUNK))
    lanes = lax.broadcasted_iota(jnp.int32, (CHUNK, TILE), 1)
    own_rows = [ones_where((lanes // LANES) % 2 == i) for i in range(2)]
    eights = ones_where(
        lax.broadcasted_iota(jnp.int32, (2 * PACK, TILE), 1) // 8
        == lax.broadcasted_iota(jnp.int32, (2 * PACK, TILE), 0)
    )
    at = pl.program_id(0)
    blocks = now.shape[0] // TILE

    @pl.when(at == 0)
    def _():
        within_sums[...] = jnp.zeros_like(within_sums)
        across_sums[...] = jnp.zeros_like(across_sums)

    turned = []
    for span in spans(now):
        dz2 = grad[span, :] * li_value[span, :]
        turned.append(nt(turn, above(dz1[span, :], dz2)).astype(BF16))
    chunks = [(pair_chunks(each[:, :TILE]), pair_chunks(each[:, TILE:])) for each in turned]
    results = [
        now_and_before(
            now[span, :], before[span, :], group_rows(filters, block).astype(F32), upper_half
        )
        for block, span in enumerate(spans(now))
    ]
    halves = []
    for span, result in zip(spans(now), results):
        z1[span, :] = result
        y1 = (value[span, :].astype(F32) * result).astype(BF16).astype(F32)
        halves.append((y1 * li_key[span, :].astype(F32)).astype(BF16))
        u2[span, :] = halves[-1]
    ends = [nt(to_end[span, :], half) for span, half in zip(spans(now), halves)]

    lags = []
    for block in range(blocks):
        lag, energy = [], []
        for p in range(TILE // CHUNK):
            pair = pl.ds(block * TILE + p * CHUNK, CHUNK)
            older, newer = before[pair, :], now[pair, :]
            later = halves[block][p * CHUNK : (p + 1) * CHUNK]
            lag.append(lag_rows(chunks[block][0][p], windows(older, newer), own_rows))
            energy.append(lag_rows(chunks[block][1][p], windows(None, later), own_rows))
        lags.append(above(*lag, *energy))
    lags = [nn(eights, each) for each in lags]
    within, across = jnp.zeros((LANES, TILE), F32), jnp.zeros((LANES, TILE), F32)
    for block, span in enumerate(spans(now)):
        own = block_groups(at, blocks, block)
        energies = above(*[lags[block][PACK:].astype(BF16)] * LANES)
        within = within + squeeze_groups(nt(power[span, :], energies), own)
        state = squeeze_groups(ends[block], mask).astype(BF16)
        crossing = state.astype(F32) * after_shard[block]
        across = across + nn(crossing.astype(BF16), ones_where(own))
        packed[at * blocks + block] = state
    lags = [each[:PACK] for each in lags]
    few = blocks * PACK
    filter_sums[pl.ds(pl.multiple_of(at * few, few), few), :] = above(*lags)
    within_sums[...] += within
    across_sums[...] += across

    steps = filter_sums.shape[0] // few

    @pl.when(at == steps - 1)
    def _():
        place = ones_where((rows + cols) % TILE == CHUNK - 1)
        sums = nn(filter_sums[...].astype(BF16), place).astype(BF16)
        for chunk in range(filter_sums.shape[0] // LANES):
            packed[steps * blocks + chunk] = sums[chunk * LANES : (chunk + 1) * LANES]
        gains = jnp.sqrt(one_minus_exp(2.0 * rate[...]))
        total = gains * (within_sums[...] + across_sums[...])
        packed[steps * blocks + filter_sums.shape[0] // LANES] = total.astype(BF16)


def factor_kernel(
    bits, wide_rate, rate, residue, filters, later, zeros, after, mr_turned, *weights
):
    zeros[...] = jnp.zeros_like(zeros)
    place = lax.axis_index("seq")
    rates = wide_rate[...]
    weights = list(weights)
    for bit in bits:
        low = (place & bit) == 0
        one = jnp.ones_like(rates)
        weights.pop(0)[...] = jnp.where(low, one, 0.0)
        weights.pop(0)[...] = jnp.where(low, jnp.exp(-rates * (2 * TILE * bit)), one)
    mr_turned[...] = nn(filters[...], reversal())
    _, cols = iotas()
    coeffs = residue[...] * jnp.sqrt(one_minus_exp(2.0 * rate[...]))
    for block, span in enumerate(spans(after)):
        own = block_groups(0, 0, block)
        powers = jnp.exp(-column(rate[...], own) * cols.astype(F32))
        after[span, :] = (powers * column(coeffs, own)).astype(BF16)


def within_kernel(u2, taps, z1, du2, value, li_key, z2, grad_value, grad_key, zeros):
    zeros[...] = jnp.zeros_like(zeros)
    rows, cols = iotas()
    upper = ones_where(cols >= rows)
    upper_half = beside(upper, upper)
    results = [
        within_shard(u2[span, :], group_rows(taps, block), upper_half)
        for block, span in enumerate(spans(u2))
    ]
    for span, result in zip(spans(u2), results):
        z2[span, :] = result
        z1_here, du2_here = z1[span, :], du2[span, :]
        y1 = (value[span, :].astype(F32) * z1_here).astype(BF16).astype(F32)
        grad_key[span, :] = (du2_here * y1).astype(BF16)
        grad_value[span, :] = (du2_here * li_key[span, :].astype(F32) * z1_here).astype(BF16)


def product_kernel(part, dz1, later, turned, query, key, *refs):
    grad_query, grad_key = refs[2 * part : 2 * part + 2]
    if part == 0:
        refs[2][...] = jnp.zeros_like(refs[2])
    rows, cols = iotas()
    lower = ones_where(rows >= cols)
    lower_half = beside(lower, lower)
    results = [
        now_and_before(
            dz1[span, :], later[span, :], group_rows(turned, block), lower_half
        )
        for block, span in enumerate(spans(dz1))
    ]
    for span, du1 in zip(spans(dz1), results):
        grad_query[span, :] = (du1 * key[span, :].astype(F32)).astype(BF16)
        grad_key[span, :] = (du1 * query[span, :].astype(F32)).astype(BF16)


def value_kernel(
    states, after, z2, grad, half, other, grad_value, grad_filter, grad_residue,
    made, filter_sum, residue_sum, left, done,
):
    rows, cols = iotas()
    mask = rows // LANES == cols // LANES
    at = pl.program_id(0)
    size = z2.shape[0]
    sums = [
        pltpu.make_async_copy(filter_sum, grad_filter, done.at[0]),
        pltpu.make_async_copy(residue_sum, grad_residue, done.at[1]),
    ]

    @pl.when(at == 0)
    def _():
        chunks = half.shape[0] - 1
        for chunk in range(chunks):
            both = half[chunk].astype(F32) + other[chunk].astype(F32)
            filter_sum[pl.ds(chunk * LANES, LANES), :] = both
        residue_sum[...] = half[chunks].astype(F32) + other[chunks].astype(F32)
        for copy in sums:
            copy.start()

    def store(step):
        span = pl.ds(pl.multiple_of(step * size, size), size)
        return pltpu.make_async_copy(made.at[span, :], grad_value.at[span, :], left.at[step])

    wides = [spread_groups(states[block], mask).T.astype(BF16) for block in range(states.shape[0])]
    totals = [z2[span, :] + nn(wide, after[span, :]) for span, wide in zip(spans(z2), wides)]
    for block, (span, total) in enumerate(zip(spans(z2), totals)):
        here = pl.ds(pl.multiple_of(at * size + block * TILE, TILE), TILE)
        made[here, :] = (grad[span, :].astype(F32) * total).astype(BF16)
    store(at).start()

    @pl.when(at == STEPS - 1)
    def _():
        for copy in sums:
            copy.wait()
        for step in range(STEPS):
            store(step).wait()


def shifted(value, axis, steps):
    count = lax.axis_size(axis)
    first, last = max(0, -steps), min(count, count - steps)
    return lax.ppermute(value, axis, [(source, source + steps) for source in range(first, last)])


def swapped(value, axis, bit):
    count = lax.axis_size(axis)
    return lax.ppermute(value, axis, [(source, source ^ bit) for source in range(count)])


def scan_bits():
    count, bit, bits = lax.axis_size("seq"), 1, []
    assert count & (count - 1) == 0
    while bit < count:
        bits.append(bit)
        bit *= 2
    return bits


def per_device(
    mr_query, mr_key, mr_value, li_key, li_value, grad_out, mr_filter, li_residue, li_rate
):
    query, key, value, key_two, value_two, grad = (
        array[0] for array in (mr_query, mr_key, mr_value, li_key, li_value, grad_out)
    )
    groups, filt_len = mr_filter.shape
    channels, seq_local = query.shape
    assert filt_len == TILE and seq_local == TILE and groups <= TILE
    assert channels == groups * LANES and li_rate.shape[1] == LANES
    rows = channels // STEPS
    few = groups // STEPS
    spare = ((0, 0), (0, TILE - groups))
    rate = jnp.pad(li_rate.T, spare)
    residue = jnp.pad(li_residue.T, spare)

    blocks = channels // TILE

    wide = pl.BlockSpec((rows, TILE), lambda i: (i, 0))
    table = pl.BlockSpec((few, TILE), lambda i: (i, 0))
    chunk = pl.BlockSpec((blocks // STEPS, LANES, TILE), lambda i: (i, 0, 0))
    modes = pl.BlockSpec((LANES, TILE), lambda i: (0, 0))
    distant = pl.BlockSpec(memory_space=pltpu.HBM)
    anywhere = pl.BlockSpec(memory_space=pl.ANY)
    wide_half = jax.ShapeDtypeStruct((channels, TILE), BF16)
    wide_full = jax.ShapeDtypeStruct((channels, TILE), F32)
    table_full = jax.ShapeDtypeStruct((groups, TILE), F32)
    chunk_half = jax.ShapeDtypeStruct((blocks, LANES, TILE), BF16)
    chunk_full = jax.ShapeDtypeStruct((blocks, LANES, TILE), F32)

    def call(kernel, name, in_specs, out_specs, out_shape, scratch=(), grid=STEPS, limit=VMEM_LIMIT, aliases={}):
        return pl.pallas_call(
            kernel,
            grid=(grid,),
            in_specs=in_specs,
            out_specs=out_specs,
            out_shape=out_shape,
            scratch_shapes=scratch,
            input_output_aliases=aliases,
            name=name,
            cost_estimate=pl.CostEstimate(flops=1, bytes_accessed=1, transcendentals=0),
            compiler_params=pltpu.CompilerParams(vmem_limit_bytes=limit),
        )

    def whole(leaf):
        return pl.BlockSpec(leaf.shape, lambda i: (0,) * len(leaf.shape))

    def twice(spec):
        return pl.BlockSpec((2 * spec.block_shape[0],) + spec.block_shape[1:], spec.index_map)

    (product,) = call(
        gate_kernel, "gate", [distant] * 2, [distant], [wide_half],
        [
            pltpu.VMEM((2, channels, TILE), BF16), pltpu.VMEM((channels, TILE), BF16),
            pltpu.SemaphoreType.DMA((2, PIECES)), pltpu.SemaphoreType.DMA((PIECES,)),
        ],
        grid=1, limit=60 * 1024 * 1024,
    )(query, key)
    product_before = shifted(product, "seq", 1)

    (back,) = call(state_kernel, "state", [wide, wide, modes], [chunk], [chunk_half])(
        grad, value_two, rate
    )

    later_backs = [shifted(back, "seq", -gap) for gap in range(1, lax.axis_size("seq"))]
    to_next, to_end, power, taps, turned, wide_rate = call(
        table_kernel, "table", [modes, modes], [wide] * 3 + [table] * 2 + [chunk],
        [wide_half] * 3 + [table_full] * 2 + [chunk_full],
    )(rate, residue)
    (du2_local,) = call(local_kernel, "local", [wide, wide, table], [wide], [wide_full])(
        grad, value_two, turned
    )
    fade = jnp.exp(-TILE * wide_rate)
    after_shard = later_backs[-1].astype(F32)
    for other in later_backs[-2::-1]:
        after_shard = other.astype(F32) + fade * after_shard
    after_shard = after_shard * jnp.exp(-wide_rate)

    dz1, du2 = call(
        middle_kernel, "middle", [twice(chunk)] + [twice(wide)] * 4 + [anywhere],
        [twice(wide)] * 2,
        [wide_half, wide_full], grid=STEPS // 2,
    )(after_shard, du2_local, to_next, key_two, value, product_before)
    dz1_later = shifted(dz1, "seq", -1)

    filter_chunks = groups // LANES
    packed_shape = jax.ShapeDtypeStruct((blocks + filter_chunks + 1, LANES, TILE), BF16)
    z1, u2, packed = call(
        forward_kernel, "forward",
        [twice(spec) for spec in [wide, wide, table] + [wide] * 7 + [chunk]] + [modes],
        [twice(wide), twice(wide), whole(packed_shape)], [wide_full, wide_half, packed_shape],
        [pltpu.VMEM((groups, TILE), F32)] + [pltpu.VMEM((LANES, TILE), F32)] * 2,
        grid=STEPS // 2,
    )(
        product_before, product, mr_filter, value, key_two, to_end, dz1, grad, value_two, power,
        after_shard, rate,
    )

    bits = scan_bits()[::-1]
    few_full = jax.ShapeDtypeStruct((filter_chunks + 1, LANES, TILE), F32)
    factors = 2 * (len(bits) - 1)
    z2, grad_mr_value, grad_li_key, within_zeros = call(
        within_kernel, "within",
        [wide, table, wide, wide, wide, wide], [wide] * 3 + [whole(few_full)],
        [wide_full, wide_half, wide_half, few_full],
    )(u2, taps, z1, du2, value, key_two)

    factor_shapes = [few_full, wide_half, table_full] + [chunk_full] * factors
    factor_zeros, after, mr_turned, *weights = call(
        functools.partial(factor_kernel, bits[1:]), "factor",
        [whole(chunk_full), modes, modes, whole(mr_filter), anywhere],
        [whole(leaf) for leaf in factor_shapes], factor_shapes, grid=1,
    )(wide_rate, rate, residue, mr_filter, dz1_later)

    def half_product(part, *made):
        def half_of(spec):
            shape = (spec.block_shape[0] * STEPS // 2,) + spec.block_shape[1:]
            return pl.BlockSpec(shape, lambda i: (part, 0))

        streams = [half_of(spec) for spec in (wide, wide, table, wide, wide)]
        return call(
            functools.partial(product_kernel, part), "product",
            streams + [anywhere] * len(made),
            [half_of(wide)] * 2 + [whole(few_full)] * (1 - part),
            [wide_half] * 2 + [few_full] * (1 - part), grid=1,
            aliases={len(streams) + at: at for at in range(len(made))},
        )(dz1, dz1_later, mr_turned, query, key, *made)

    *products, product_zeros = half_product(0)
    grad_query, grad_key = half_product(1, *products)

    assert lax.axis_size("dp") == 2
    state, half = packed[:blocks], packed[blocks:]
    reached = shifted(state, "seq", bits[0]).astype(F32)
    sums = half.astype(F32) + swapped(half, "dp", 1).astype(F32) + within_zeros
    half = sums.astype(BF16)
    partner = swapped(half, "seq", bits[0])
    zeros = factor_zeros + product_zeros
    for bit in bits[1:]:
        sums = half.astype(F32) + partner.astype(F32) + zeros
        sent = weights.pop(0) * state.astype(F32) + weights.pop(0) * reached
        packed = jnp.concatenate([sent.astype(BF16), sums.astype(BF16)], axis=0)
        other = swapped(packed, "seq", bit)
        reached = other[:blocks].astype(F32) + jnp.exp(-TILE * bit * wide_rate) * reached
        half, partner = packed[blocks:], other[blocks:]
    before_shard = reached * jnp.exp(-wide_rate)
    residue_full = jax.ShapeDtypeStruct((LANES, TILE), F32)
    grad_li_value, grad_filter, grad_residue = call(
        value_kernel, "value",
        [chunk, wide, wide, wide, whole(half), whole(half)],
        [distant] * 3, [wide_half, table_full, residue_full],
        [
            pltpu.VMEM((channels, TILE), BF16), pltpu.VMEM((groups, TILE), F32),
            pltpu.VMEM((LANES, TILE), F32),
            pltpu.SemaphoreType.DMA((STEPS,)), pltpu.SemaphoreType.DMA((2,)),
        ],
    )(before_shard, after, z2, grad, half, partner)

    return (
        grad_query[None],
        grad_key[None],
        grad_mr_value[None],
        grad_li_key[None],
        grad_li_value[None],
        grad_filter,
        grad_residue[:, :groups].T,
    )


def solution(mesh):
    streams = (P("dp", "chan", "seq"),)
    tables = (P("chan", None),)
    return jax.shard_map(
        per_device,
        mesh=mesh,
        in_specs=streams * 6 + tables * 3,
        out_specs=streams * 5 + tables * 2,
        check_vma=False,
    )
```

```python
import functools

import jax
import jax.numpy as jnp
from jax import lax
from jax.experimental import pallas as pl
from jax.experimental.pallas import tpu as pltpu
from jax.sharding import PartitionSpec as P

F32 = jnp.float32
BF16 = jnp.bfloat16
TILE = 128
LANES = 16
PACK = TILE // LANES
CHUNK = 32
STEPS = 4
PIECES = 8
VMEM_LIMIT = 24 * 1024 * 1024


def nn(lhs, rhs):
    return lax.dot_general(lhs, rhs, (((1,), (0,)), ((), ())), preferred_element_type=F32)


def nt(lhs, rhs):
    return lax.dot_general(lhs, rhs, (((1,), (1,)), ((), ())), preferred_element_type=F32)


def iotas():
    rows = lax.broadcasted_iota(jnp.int32, (TILE, TILE), 0)
    cols = lax.broadcasted_iota(jnp.int32, (TILE, TILE), 1)
    return rows, cols


def ones_where(mask):
    return jnp.where(mask, 1.0, 0.0).astype(BF16)


def column(turned, mask):
    wide = jnp.concatenate([turned] * PACK, axis=0)
    return jnp.sum(jnp.where(mask, wide, 0.0), axis=1, keepdims=True)


def squeeze_groups(wide, mask):
    kept = jnp.where(mask, wide, 0.0)
    total = kept[:LANES]
    for g in range(1, PACK):
        total = total + kept[g * LANES : (g + 1) * LANES]
    return total


def spread_groups(narrow, mask):
    return jnp.where(mask, jnp.concatenate([narrow] * PACK, axis=0), 0.0)


def circulant(row):
    base = jnp.broadcast_to(row, (LANES, TILE))
    base = pltpu.roll(base, 0, 1, stride=1, stride_axis=0).astype(BF16)
    return jnp.concatenate(
        [base] + [pltpu.roll(base, LANES * j, 1) for j in range(1, PACK)], axis=0
    )


def reversal():
    rows, cols = iotas()
    return ones_where((rows + cols) % TILE == 0)


def one_minus_exp(value):
    series = jnp.full_like(value, 1.0)
    for order in (7, 6, 5, 4, 3, 2):
        series = 1.0 - value * series / order
    return jnp.where(value < 0.125, value * series, 1.0 - jnp.exp(-value))


def chunk_mask(shape, bit):
    return (lax.broadcasted_iota(jnp.int32, shape, 1) // CHUNK) & bit == 0


def pair_chunks(turned):
    parts = [turned[CHUNK * j : CHUNK * (j + 1), :] for j in range(TILE // CHUNK)]
    for bit in (1, 2):
        keep = chunk_mask((CHUNK, TILE), bit)
        for j in range(len(parts)):
            if j & bit == 0:
                low, high = parts[j], parts[j + bit]
                parts[j] = jnp.where(keep, low, pltpu.roll(high, CHUNK * bit, 1))
                parts[j + bit] = jnp.where(keep, pltpu.roll(low, TILE - CHUNK * bit, 1), high)
    return parts


def windows(before, now):
    lanes = lax.broadcasted_iota(jnp.int32, now.shape, 1)
    none = jnp.zeros_like(now)
    first, second = [none if before is None else before], [now]
    for j in range(1, TILE // CHUNK):
        left = TILE - CHUNK * j
        moved = pltpu.roll(now, left, 1)
        older = none if before is None else pltpu.roll(before, left, 1)
        first.append(jnp.where(lanes < left, older, moved))
        second.append(moved)
    return jnp.concatenate(
        [jnp.concatenate(first, axis=0), jnp.concatenate(second, axis=0)], axis=1
    )


def beside(first, second):
    return jnp.concatenate([first, second], axis=1)


def above(*arrays):
    return jnp.concatenate(arrays, axis=0)


def apart(first, second):
    none = jnp.zeros_like(first)
    return above(beside(first, none), beside(none, second))


def lag_rows(chunks, shifted_rows, own_rows):
    wide = nn(above(*[chunks * own for own in own_rows]), shifted_rows)
    rows = lax.broadcasted_iota(jnp.int32, (2 * CHUNK, TILE), 0) % CHUNK
    lanes = lax.broadcasted_iota(jnp.int32, (2 * CHUNK, TILE), 1)
    sums = jnp.where(lanes + rows < CHUNK, wide[:, TILE:], wide[:, :TILE])
    parts = []
    for start in (0, CHUNK):
        part = pltpu.roll(sums[start : start + CHUNK], 0, 1, stride=1, stride_axis=0)
        parts.append(part[:8] + part[8:16] + part[16:24] + part[24:])
    return above(*parts).astype(BF16)


def now_and_before(now, before, rows, half):
    both = beside(now, before)
    pieces = []
    for g in range(0, PACK, 2):
        circs = beside(*[circulant(rows[h : h + 1, :]) for h in (g, g + 1)])
        w_now = circs * half
        wide = nn(both[g * LANES : (g + 2) * LANES, :], above(w_now, circs - w_now))
        pieces += [wide[:LANES, :TILE], wide[LANES:, TILE:]]
    return jnp.concatenate(pieces, axis=0)


def within_shard(array, rows, half):
    pieces = []
    for g in range(0, PACK, 4):
        weights = [
            beside(*[circulant(rows[h : h + 1, :]) for h in (k, k + 1)]) * half
            for k in (g, g + 2)
        ]
        parts = [array[k * LANES : (k + 2) * LANES, :] for k in (g, g + 2)]
        wide = nn(apart(*parts), above(*weights))
        for k in range(4):
            column_at = (k % 2) * TILE
            pieces.append(wide[k * LANES : (k + 1) * LANES, column_at : column_at + TILE])
    return jnp.concatenate(pieces, axis=0)


def block_groups(at, blocks, block):
    rows, cols = iotas()
    return cols == rows // LANES + (at * blocks + block) * PACK


def gate_kernel(query, key, product, held, made, arrived, left):
    size = held.shape[1] // PIECES

    def fetch(array, step):
        span = pl.ds(step * size, size)
        return pltpu.make_async_copy(
            (query, key)[array].at[span, :], held.at[array, span, :], arrived.at[array, step]
        )

    def store(step):
        span = pl.ds(step * size, size)
        return pltpu.make_async_copy(made.at[span, :], product.at[span, :], left.at[step])

    for step in range(PIECES):
        for array in range(2):
            fetch(array, step).start()
    for step in range(PIECES):
        for array in range(2):
            fetch(array, step).wait()
        span = pl.ds(step * size, size)
        made[span, :] = held[0, span, :] * held[1, span, :]
        store(step).start()
    for step in range(PIECES):
        store(step).wait()


def state_kernel(grad, value, rate, state):
    rows, cols = iotas()
    offsets = cols.astype(F32)
    mask = rows // LANES == cols // LANES
    at = pl.program_id(0)
    blocks = state.shape[0]
    for block in range(blocks):
        span = pl.ds(block * TILE, TILE)
        rates = column(rate[...], block_groups(at, blocks, block))
        powers = jnp.exp(-rates * offsets).astype(BF16)
        dz2 = grad[span, :] * value[span, :]
        state[block] = squeeze_groups(nt(powers, dz2), mask).astype(BF16)


def spans(array):
    return [pl.ds(block * TILE, TILE) for block in range(array.shape[0] // TILE)]


def group_rows(table, block):
    return table[pl.ds(block * PACK, PACK), :]


def table_kernel(rate, residue, to_next, to_end, power, taps, turned, wide_rate):
    rows, cols = iotas()
    mask = rows // LANES == cols // LANES
    offsets = cols.astype(F32)
    lags = ((CHUNK - 1 - cols) % TILE).astype(F32)
    at = pl.program_id(0)
    blocks = power.shape[0] // TILE
    coeffs = residue[...] * jnp.sqrt(one_minus_exp(2.0 * rate[...]))
    sums = []
    for block in range(blocks):
        span = pl.ds(block * TILE, TILE)
        own = block_groups(at, blocks, block)
        rates = column(rate[...], own)
        scale = column(coeffs, own)
        wide_rate[block] = squeeze_groups(jnp.broadcast_to(rates, (TILE, TILE)), mask)
        scaled = jnp.exp(-rates * offsets) * scale
        ends = jnp.exp(-rates * (TILE - 1 - offsets))
        power[span, :] = jnp.exp(-rates * lags).astype(BF16)
        to_end[span, :] = ends.astype(BF16)
        to_next[span, :] = (ends * scale).astype(BF16)
        sums.append(jnp.sum(scaled.reshape(PACK, LANES, TILE), axis=1))
    taps[...] = above(*sums)
    turned[...] = nn(above(*sums).astype(BF16), reversal())


def local_kernel(grad, value, turned, du2):
    rows, cols = iotas()
    lower = ones_where(rows >= cols)
    lower_half = beside(lower, lower)
    results = [
        within_shard(grad[span, :] * value[span, :], group_rows(turned, block), lower_half)
        for block, span in enumerate(spans(grad))
    ]
    for span, result in zip(spans(grad), results):
        du2[span, :] = result


def middle_kernel(states, local, to_next, li_key, value, before, dz1, du2):
    rows, cols = iotas()
    mask = rows // LANES == cols // LANES
    wides = [spread_groups(states[block], mask).T.astype(BF16) for block in range(states.shape[0])]
    totals = [
        local[span, :] + nn(wide, to_next[span, :]) for span, wide in zip(spans(local), wides)
    ]
    for span, total in zip(spans(local), totals):
        du2[span, :] = total
        dy1 = total * li_key[span, :].astype(F32)
        dz1[span, :] = (dy1 * value[span, :].astype(F32)).astype(BF16)


def forward_kernel(
    before, now, filters, value, li_key, to_end, dz1, grad, li_value, power, after_shard, rate,
    z1, u2, packed, filter_sums, within_sums, across_sums,
):
    rows, cols = iotas()
    mask = rows // LANES == cols // LANES
    upper = ones_where(cols >= rows)
    upper_half = beside(upper, upper)
    turn = ones_where(cols == rows - rows % CHUNK + (CHUNK - 1 - rows % CHUNK))
    lanes = lax.broadcasted_iota(jnp.int32, (CHUNK, TILE), 1)
    own_rows = [ones_where((lanes // LANES) % 2 == i) for i in range(2)]
    eights = ones_where(
        lax.broadcasted_iota(jnp.int32, (2 * PACK, TILE), 1) // 8
        == lax.broadcasted_iota(jnp.int32, (2 * PACK, TILE), 0)
    )
    at = pl.program_id(0)
    blocks = now.shape[0] // TILE

    @pl.when(at == 0)
    def _():
        within_sums[...] = jnp.zeros_like(within_sums)
        across_sums[...] = jnp.zeros_like(across_sums)

    turned = []
    for span in spans(now):
        dz2 = grad[span, :] * li_value[span, :]
        turned.append(nt(turn, above(dz1[span, :], dz2)).astype(BF16))
    chunks = [(pair_chunks(each[:, :TILE]), pair_chunks(each[:, TILE:])) for each in turned]
    results = [
        now_and_before(
            now[span, :], before[span, :], group_rows(filters, block).astype(F32), upper_half
        )
        for block, span in enumerate(spans(now))
    ]
    halves = []
    for span, result in zip(spans(now), results):
        z1[span, :] = result
        y1 = (value[span, :].astype(F32) * result).astype(BF16).astype(F32)
        halves.append((y1 * li_key[span, :].astype(F32)).astype(BF16))
        u2[span, :] = halves[-1]
    ends = [nt(to_end[span, :], half) for span, half in zip(spans(now), halves)]

    lags = []
    for block in range(blocks):
        lag, energy = [], []
        for p in range(TILE // CHUNK):
            pair = pl.ds(block * TILE + p * CHUNK, CHUNK)
            older, newer = before[pair, :], now[pair, :]
            later = halves[block][p * CHUNK : (p + 1) * CHUNK]
            lag.append(lag_rows(chunks[block][0][p], windows(older, newer), own_rows))
            energy.append(lag_rows(chunks[block][1][p], windows(None, later), own_rows))
        lags.append(above(*lag, *energy))
    lags = [nn(eights, each) for each in lags]
    within, across = jnp.zeros((LANES, TILE), F32), jnp.zeros((LANES, TILE), F32)
    for block, span in enumerate(spans(now)):
        own = block_groups(at, blocks, block)
        energies = above(*[lags[block][PACK:].astype(BF16)] * LANES)
        within = within + squeeze_groups(nt(power[span, :], energies), own)
        state = squeeze_groups(ends[block], mask).astype(BF16)
        crossing = state.astype(F32) * after_shard[block]
        across = across + nn(crossing.astype(BF16), ones_where(own))
        packed[at * blocks + block] = state
    lags = [each[:PACK] for each in lags]
    few = blocks * PACK
    filter_sums[pl.ds(pl.multiple_of(at * few, few), few), :] = above(*lags)
    within_sums[...] += within
    across_sums[...] += across

    steps = filter_sums.shape[0] // few

    @pl.when(at == steps - 1)
    def _():
        place = ones_where((rows + cols) % TILE == CHUNK - 1)
        sums = nn(filter_sums[...].astype(BF16), place).astype(BF16)
        for chunk in range(filter_sums.shape[0] // LANES):
            packed[steps * blocks + chunk] = sums[chunk * LANES : (chunk + 1) * LANES]
        gains = jnp.sqrt(one_minus_exp(2.0 * rate[...]))
        total = gains * (within_sums[...] + across_sums[...])
        packed[steps * blocks + filter_sums.shape[0] // LANES] = total.astype(BF16)


def factor_kernel(
    bits, wide_rate, rate, residue, filters, later, zeros, after, mr_turned, *weights
):
    zeros[...] = jnp.zeros_like(zeros)
    place = lax.axis_index("seq")
    rates = wide_rate[...]
    weights = list(weights)
    for bit in bits:
        low = (place & bit) == 0
        one = jnp.ones_like(rates)
        weights.pop(0)[...] = jnp.where(low, one, 0.0)
        weights.pop(0)[...] = jnp.where(low, jnp.exp(-rates * (2 * TILE * bit)), one)
    mr_turned[...] = nn(filters[...], reversal())
    _, cols = iotas()
    coeffs = residue[...] * jnp.sqrt(one_minus_exp(2.0 * rate[...]))
    for block, span in enumerate(spans(after)):
        own = block_groups(0, 0, block)
        powers = jnp.exp(-column(rate[...], own) * cols.astype(F32))
        after[span, :] = (powers * column(coeffs, own)).astype(BF16)


def within_kernel(
    u2, taps, z1, du2, value, li_key, states, z2, grad_value, grad_key, zeros, kept
):
    kept[...] = states[...]
    zeros[...] = jnp.zeros_like(zeros)
    rows, cols = iotas()
    upper = ones_where(cols >= rows)
    upper_half = beside(upper, upper)
    results = [
        within_shard(u2[span, :], group_rows(taps, block), upper_half)
        for block, span in enumerate(spans(u2))
    ]
    for span, result in zip(spans(u2), results):
        z2[span, :] = result
        z1_here, du2_here = z1[span, :], du2[span, :]
        y1 = (value[span, :].astype(F32) * z1_here).astype(BF16).astype(F32)
        grad_key[span, :] = (du2_here * y1).astype(BF16)
        grad_value[span, :] = (du2_here * li_key[span, :].astype(F32) * z1_here).astype(BF16)


def product_kernel(part, dz1, later, turned, query, key, *refs):
    grad_query, grad_key = refs[2 * part : 2 * part + 2]
    if part == 0:
        refs[2][...] = jnp.zeros_like(refs[2])
    rows, cols = iotas()
    lower = ones_where(rows >= cols)
    lower_half = beside(lower, lower)
    results = [
        now_and_before(
            dz1[span, :], later[span, :], group_rows(turned, block), lower_half
        )
        for block, span in enumerate(spans(dz1))
    ]
    for span, du1 in zip(spans(dz1), results):
        grad_query[span, :] = (du1 * key[span, :].astype(F32)).astype(BF16)
        grad_key[span, :] = (du1 * query[span, :].astype(F32)).astype(BF16)


def value_kernel(
    states, after, z2, grad, half, other, grad_value, grad_filter, grad_residue,
    made, filter_sum, residue_sum, left, done,
):
    rows, cols = iotas()
    mask = rows // LANES == cols // LANES
    at = pl.program_id(0)
    size = z2.shape[0]
    sums = [
        pltpu.make_async_copy(filter_sum, grad_filter, done.at[0]),
        pltpu.make_async_copy(residue_sum, grad_residue, done.at[1]),
    ]

    @pl.when(at == 0)
    def _():
        chunks = half.shape[0] - 1
        for chunk in range(chunks):
            both = half[chunk].astype(F32) + other[chunk].astype(F32)
            filter_sum[pl.ds(chunk * LANES, LANES), :] = both
        residue_sum[...] = half[chunks].astype(F32) + other[chunks].astype(F32)
        for copy in sums:
            copy.start()

    def store(step):
        span = pl.ds(pl.multiple_of(step * size, size), size)
        return pltpu.make_async_copy(made.at[span, :], grad_value.at[span, :], left.at[step])

    wides = [spread_groups(states[block], mask).T.astype(BF16) for block in range(states.shape[0])]
    totals = [z2[span, :] + nn(wide, after[span, :]) for span, wide in zip(spans(z2), wides)]
    for block, (span, total) in enumerate(zip(spans(z2), totals)):
        here = pl.ds(pl.multiple_of(at * size + block * TILE, TILE), TILE)
        made[here, :] = (grad[span, :].astype(F32) * total).astype(BF16)
    store(at).start()

    @pl.when(at == STEPS - 1)
    def _():
        for copy in sums:
            copy.wait()
        for step in range(STEPS):
            store(step).wait()


def shifted(value, axis, steps):
    count = lax.axis_size(axis)
    first, last = max(0, -steps), min(count, count - steps)
    return lax.ppermute(value, axis, [(source, source + steps) for source in range(first, last)])


def swapped(value, axis, bit):
    count = lax.axis_size(axis)
    return lax.ppermute(value, axis, [(source, source ^ bit) for source in range(count)])


def scan_bits():
    count, bit, bits = lax.axis_size("seq"), 1, []
    assert count & (count - 1) == 0
    while bit < count:
        bits.append(bit)
        bit *= 2
    return bits


def per_device(
    mr_query, mr_key, mr_value, li_key, li_value, grad_out, mr_filter, li_residue, li_rate
):
    query, key, value, key_two, value_two, grad = (
        array[0] for array in (mr_query, mr_key, mr_value, li_key, li_value, grad_out)
    )
    groups, filt_len = mr_filter.shape
    channels, seq_local = query.shape
    assert filt_len == TILE and seq_local == TILE and groups <= TILE
    assert channels == groups * LANES and li_rate.shape[1] == LANES
    rows = channels // STEPS
    few = groups // STEPS
    spare = ((0, 0), (0, TILE - groups))
    rate = jnp.pad(li_rate.T, spare)
    residue = jnp.pad(li_residue.T, spare)

    blocks = channels // TILE

    wide = pl.BlockSpec((rows, TILE), lambda i: (i, 0))
    table = pl.BlockSpec((few, TILE), lambda i: (i, 0))
    chunk = pl.BlockSpec((blocks // STEPS, LANES, TILE), lambda i: (i, 0, 0))
    modes = pl.BlockSpec((LANES, TILE), lambda i: (0, 0))
    distant = pl.BlockSpec(memory_space=pltpu.HBM)
    anywhere = pl.BlockSpec(memory_space=pl.ANY)
    wide_half = jax.ShapeDtypeStruct((channels, TILE), BF16)
    wide_full = jax.ShapeDtypeStruct((channels, TILE), F32)
    table_full = jax.ShapeDtypeStruct((groups, TILE), F32)
    chunk_half = jax.ShapeDtypeStruct((blocks, LANES, TILE), BF16)
    chunk_full = jax.ShapeDtypeStruct((blocks, LANES, TILE), F32)

    def call(kernel, name, in_specs, out_specs, out_shape, scratch=(), grid=STEPS, limit=VMEM_LIMIT, aliases={}):
        return pl.pallas_call(
            kernel,
            grid=(grid,),
            in_specs=in_specs,
            out_specs=out_specs,
            out_shape=out_shape,
            scratch_shapes=scratch,
            input_output_aliases=aliases,
            name=name,
            cost_estimate=pl.CostEstimate(flops=1, bytes_accessed=1, transcendentals=0),
            compiler_params=pltpu.CompilerParams(vmem_limit_bytes=limit),
        )

    def whole(leaf):
        return pl.BlockSpec(leaf.shape, lambda i: (0,) * len(leaf.shape))

    def twice(spec):
        return pl.BlockSpec((2 * spec.block_shape[0],) + spec.block_shape[1:], spec.index_map)

    (product,) = call(
        gate_kernel, "gate", [distant] * 2, [distant], [wide_half],
        [
            pltpu.VMEM((2, channels, TILE), BF16), pltpu.VMEM((channels, TILE), BF16),
            pltpu.SemaphoreType.DMA((2, PIECES)), pltpu.SemaphoreType.DMA((PIECES,)),
        ],
        grid=1, limit=60 * 1024 * 1024,
    )(query, key)
    product_before = shifted(product, "seq", 1)

    (back,) = call(state_kernel, "state", [wide, wide, modes], [chunk], [chunk_half])(
        grad, value_two, rate
    )

    later_backs = [shifted(back, "seq", -gap) for gap in range(1, lax.axis_size("seq"))]
    to_next, to_end, power, taps, turned, wide_rate = call(
        table_kernel, "table", [modes, modes], [wide] * 3 + [table] * 2 + [chunk],
        [wide_half] * 3 + [table_full] * 2 + [chunk_full],
    )(rate, residue)
    (du2_local,) = call(local_kernel, "local", [wide, wide, table], [wide], [wide_full])(
        grad, value_two, turned
    )
    fade = jnp.exp(-TILE * wide_rate)
    after_shard = later_backs[-1].astype(F32)
    for other in later_backs[-2::-1]:
        after_shard = other.astype(F32) + fade * after_shard
    after_shard = after_shard * jnp.exp(-wide_rate)

    dz1, du2 = call(
        middle_kernel, "middle", [twice(chunk)] + [twice(wide)] * 4 + [anywhere],
        [twice(wide)] * 2,
        [wide_half, wide_full], grid=STEPS // 2,
    )(after_shard, du2_local, to_next, key_two, value, product_before)
    dz1_later = shifted(dz1, "seq", -1)

    filter_chunks = groups // LANES
    packed_shape = jax.ShapeDtypeStruct((blocks + filter_chunks + 1, LANES, TILE), BF16)
    z1, u2, packed = call(
        forward_kernel, "forward",
        [twice(spec) for spec in [wide, wide, table] + [wide] * 7 + [chunk]] + [modes],
        [twice(wide), twice(wide), whole(packed_shape)], [wide_full, wide_half, packed_shape],
        [pltpu.VMEM((groups, TILE), F32)] + [pltpu.VMEM((LANES, TILE), F32)] * 2,
        grid=STEPS // 2,
    )(
        product_before, product, mr_filter, value, key_two, to_end, dz1, grad, value_two, power,
        after_shard, rate,
    )

    bits = scan_bits()[::-1]
    few_full = jax.ShapeDtypeStruct((filter_chunks + 1, LANES, TILE), F32)
    factors = 2 * (len(bits) - 1)
    z2, grad_mr_value, grad_li_key, within_zeros, state = call(
        within_kernel, "within",
        [wide, table, wide, wide, wide, wide, chunk], [wide] * 3 + [whole(few_full), chunk],
        [wide_full, wide_half, wide_half, few_full, chunk_half],
    )(u2, taps, z1, du2, value, key_two, packed)

    factor_shapes = [few_full, wide_half, table_full] + [chunk_full] * factors
    factor_zeros, after, mr_turned, *weights = call(
        functools.partial(factor_kernel, bits[1:]), "factor",
        [whole(chunk_full), modes, modes, whole(mr_filter), anywhere],
        [whole(leaf) for leaf in factor_shapes], factor_shapes, grid=1,
    )(wide_rate, rate, residue, mr_filter, dz1_later)

    def half_product(part, *made):
        def half_of(spec):
            shape = (spec.block_shape[0] * STEPS // 2,) + spec.block_shape[1:]
            return pl.BlockSpec(shape, lambda i: (part, 0))

        streams = [half_of(spec) for spec in (wide, wide, table, wide, wide)]
        return call(
            functools.partial(product_kernel, part), "product",
            streams + [anywhere] * len(made),
            [half_of(wide)] * 2 + [whole(few_full)] * (1 - part),
            [wide_half] * 2 + [few_full] * (1 - part), grid=1,
            aliases={len(streams) + at: at for at in range(len(made))},
        )(dz1, dz1_later, mr_turned, query, key, *made)

    *products, product_zeros = half_product(0)
    grad_query, grad_key = half_product(1, *products)

    assert lax.axis_size("dp") == 2
    half = packed[blocks:]
    reached = shifted(state, "seq", bits[0]).astype(F32)
    sums = half.astype(F32) + swapped(half, "dp", 1).astype(F32) + within_zeros
    half = sums.astype(BF16)
    partner = swapped(half, "seq", bits[0])
    zeros = factor_zeros + product_zeros
    for bit in bits[1:]:
        sums = half.astype(F32) + partner.astype(F32) + zeros
        sent = weights.pop(0) * state.astype(F32) + weights.pop(0) * reached
        packed = jnp.concatenate([sent.astype(BF16), sums.astype(BF16)], axis=0)
        other = swapped(packed, "seq", bit)
        reached = other[:blocks].astype(F32) + jnp.exp(-TILE * bit * wide_rate) * reached
        half, partner = packed[blocks:], other[blocks:]
    before_shard = reached * jnp.exp(-wide_rate)
    residue_full = jax.ShapeDtypeStruct((LANES, TILE), F32)
    grad_li_value, grad_filter, grad_residue = call(
        value_kernel, "value",
        [chunk, wide, wide, wide, whole(half), whole(half)],
        [distant] * 3, [wide_half, table_full, residue_full],
        [
            pltpu.VMEM((channels, TILE), BF16), pltpu.VMEM((groups, TILE), F32),
            pltpu.VMEM((LANES, TILE), F32),
            pltpu.SemaphoreType.DMA((STEPS,)), pltpu.SemaphoreType.DMA((2,)),
        ],
    )(before_shard, after, z2, grad, half, partner)

    return (
        grad_query[None],
        grad_key[None],
        grad_mr_value[None],
        grad_li_key[None],
        grad_li_value[None],
        grad_filter,
        grad_residue[:, :groups].T,
    )


def solution(mesh):
    streams = (P("dp", "chan", "seq"),)
    tables = (P("chan", None),)
    return jax.shard_map(
        per_device,
        mesh=mesh,
        in_specs=streams * 6 + tables * 3,
        out_specs=streams * 5 + tables * 2,
        check_vma=False,
    )
```
